32 devices in a mesh: grp: 8 (over z, x), seq: 4 (over y, core).
Axes of the slice: x: 2, y: 2, z: 4, core: 2. Of those that a mesh axis runs over, the one named last changes fastest.
Arguments:
- tokens: bfloat16 [16, 1024, 768], P('grp', 'seq'), may hold values from -6 to 6
- out_grad: bfloat16 [16, 1024, 768], P('grp', 'seq'), may hold values from -6 to 6
- section: int32 [16], P('grp'), may hold values from 0 to 1, as said below
- lengths: int32 [16], P('grp'), may hold values from 256 to 1024, as said below
- ln1_gain: float32 [768], replicated, may hold values from 0.5 to 1.5
- ln1_shift: float32 [768], replicated, may hold values from -1.8 to 1.8
- w_qkv: bfloat16 [768, 2304], replicated, may hold values from -0.21875 to 0.21875
- b_query: float32 [768], replicated, may hold values from -1.8 to 1.8
- b_value: float32 [768], replicated, may hold values from -1.8 to 1.8
- w_proj: bfloat16 [768, 768], replicated, may hold values from -0.625 to 0.625
- b_proj: float32 [768], replicated, may hold values from -1.8 to 1.8
- ln2_gain: float32 [768], replicated, may hold values from 0.5 to 1.5
- ln2_shift: float32 [768], replicated, may hold values from -1.8 to 1.8
- w_fc: bfloat16 [768, 3072], replicated, may hold values from -0.21875 to 0.21875
- b_fc: float32 [3072], replicated, may hold values from -1.8 to 1.8
- w_out: bfloat16 [3072, 768], replicated, may hold values from -0.109375 to 0.109375
- b_out: float32 [768], replicated, may hold values from -1.8 to 1.8
Outputs:
- mixed: bfloat16 [16, 1024, 768], P('grp', 'seq')
- tokens_grad: float32 [16, 1024, 768], P('grp', 'seq')
- grad_ln1_gain: float32 [768], replicated
- grad_ln1_shift: float32 [768], replicated
- grad_w_qkv: float32 [768, 2304], replicated
- grad_b_query: float32 [768], replicated
- grad_b_value: float32 [768], replicated
- grad_w_proj: float32 [768, 768], replicated
- grad_b_proj: float32 [768], replicated
- grad_ln2_gain: float32 [768], replicated
- grad_ln2_shift: float32 [768], replicated
- grad_w_fc: float32 [768, 3072], replicated
- grad_b_fc: float32 [3072], replicated
- grad_w_out: float32 [3072, 768], replicated
- grad_b_out: float32 [768], replicated
The draws below stay inside these ranges and needn't reach their ends.
Inputs may be any that keep to these rules, and one draw needn't show every extreme that they name: Sequences come in groups of 2 consecutive entries; all sequences of one group share a section, and a sequence of section s runs 2 s + 1 passes. The first lengths positions of a sequence are its valid tokens; every group of 2 consecutive sequences holds one of length 1024.
All inputs are finite; a program needn't handle non-finite values.
Results may differ from the reference program's by a relative error of at most 0.013.
Values may be sent and summed in bfloat16 or wider, within the bound.
A program may use at most 320 MiB of HBM per device.

```python
import jax
import jax.numpy as jnp
from jax import lax

D = 768
HEADS = 12
HD = 64
FF = 3072
LEN = 1024
MAXP = 3
SEQ_GRP = 2
SEQS = 16
N_SEQ = 4


def draw_section(key, part):
    key = jax.random.fold_in(key, 11)
    first_key, second_key = jax.random.split(key, 2)
    groups = SEQS // SEQ_GRP
    group_section = jax.random.randint(first_key, (groups,), 0, (MAXP - 1) // 2 + 1)
    order = jax.random.permutation(second_key, groups)
    group_section = group_section.at[order[0]].set((MAXP - 1) // 2)
    group_section = group_section.at[order[1]].set(0)
    return jnp.repeat(group_section, SEQ_GRP, total_repeat_length=SEQS).astype(jnp.int32)


def draw_lengths(key, part):
    key = jax.random.fold_in(key, 23)
    first_key, second_key, third_key = jax.random.split(key, 3)
    groups = SEQS // SEQ_GRP
    drawn = jax.random.randint(first_key, (groups, SEQ_GRP), LEN // 4, LEN + 1)
    full_slot = jax.random.randint(second_key, (groups,), 0, SEQ_GRP)
    slots = lax.broadcasted_iota(jnp.int32, (groups, SEQ_GRP), 1)
    group_ids = lax.broadcasted_iota(jnp.int32, (groups, SEQ_GRP), 0)
    drawn = jnp.where(slots == full_slot[:, None], LEN, drawn)
    short_group = jax.random.randint(third_key, (), 0, groups)
    short_slot = (full_slot[short_group] + 1) % SEQ_GRP
    drawn = jnp.where((group_ids == short_group) & (slots == short_slot), LEN // 4, drawn)
    return drawn.reshape(SEQS).astype(jnp.int32)


def block_levels(stream_key, extent, pieces, low, largest):
    level, own = 1.0, jax.random.fold_in(stream_key, 6)
    for dim, blocks in pieces:
        heights = jnp.exp(jax.random.uniform(jax.random.fold_in(own, dim), (blocks,), jnp.float32, low / len(pieces), largest / len(pieces)))
        level = level * jnp.repeat(heights, extent[dim] // blocks).reshape([-1 if axis == dim else 1 for axis in range(len(extent))])
    return level


def noise(key, dims, deviation, most, pieces=(), kind=jnp.bfloat16):
    values = deviation * jax.random.normal(key, dims, jnp.float32)
    if pieces:
        values = values * block_levels(key, dims, pieces, -0.22, 0.18)
    return jnp.clip(values, -most, most).astype(kind)


def setup_inputs(seed: int = 0) -> dict:
    arg_keys = jax.random.split(jax.random.key(seed), 18)
    return {
        "tokens": noise(arg_keys[0], (SEQS, LEN, D), 1.0, 6.0, ((0, 8), (1, 4))),
        "out_grad": noise(arg_keys[1], (SEQS, LEN, D), 1.0, 6.0, ((0, 8), (1, 4))),
        "section": draw_section(jax.random.fold_in(arg_keys[17], 71), 0),
        "lengths": draw_lengths(jax.random.fold_in(arg_keys[17], 71), 0),
        "ln1_gain": jnp.clip(1.0 + 0.1 * jax.random.normal(arg_keys[4], (D,), jnp.float32), 0.5, 1.5),
        "ln1_shift": noise(arg_keys[5], (D,), 0.3, 1.8, (), jnp.float32),
        "w_qkv": noise(arg_keys[6], (D, 3 * D), D ** -0.5, 0.21875),
        "b_query": noise(arg_keys[7], (D,), 0.3, 1.8, (), jnp.float32),
        "b_value": noise(arg_keys[8], (D,), 0.3, 1.8, (), jnp.float32),
        "w_proj": noise(arg_keys[9], (D, D), (D // 8) ** -0.5, 0.625),
        "b_proj": noise(arg_keys[10], (D,), 0.3, 1.8, (), jnp.float32),
        "ln2_gain": jnp.clip(1.0 + 0.1 * jax.random.normal(arg_keys[11], (D,), jnp.float32), 0.5, 1.5),
        "ln2_shift": noise(arg_keys[12], (D,), 0.3, 1.8, (), jnp.float32),
        "w_fc": noise(arg_keys[13], (D, FF), D ** -0.5, 0.21875),
        "b_fc": noise(arg_keys[14], (FF,), 0.3, 1.8, (), jnp.float32),
        "w_out": noise(arg_keys[15], (FF, D), FF ** -0.5, 0.109375),
        "b_out": noise(arg_keys[16], (D,), 0.3, 1.8, (), jnp.float32),
    }


@jax.custom_vjp
def low(v):
    return lax.optimization_barrier(v.astype(jnp.bfloat16)).astype(jnp.float32)

@jax.custom_vjp
def low_back(v):
    return v

def low_keep(v):
    return (low(v), None)

def low_pass(kept, grad):
    return (grad,)

def back_keep(v):
    return (v, None)

def back_low(kept, grad):
    return (low(grad),)
low.defvjp(low_keep, low_pass)
low_back.defvjp(back_keep, back_low)
EPSILON = 1e-05
GELU_COEF = 0.7978845608028654
MASKED = -1e+30

def layer_norm(hidden, gain, shift):
    average = lax.optimization_barrier(jnp.mean(hidden, axis=-1, keepdims=True))
    centered = hidden - average
    variance = lax.optimization_barrier(jnp.mean(centered * centered, axis=-1, keepdims=True))
    return centered * lax.rsqrt(variance + EPSILON) * gain + shift

def gelu_tanh(pre_act):
    return 0.5 * pre_act * (1.0 + jnp.tanh(GELU_COEF * (pre_act + 0.044715 * pre_act * pre_act * pre_act)))

def matmul(left, right):
    return jnp.dot(left, right, precision=lax.Precision.HIGHEST, preferred_element_type=jnp.float32)

def attend_rows(block_index, query_rows, key_rows, value_rows):
    key_rows = low_back(key_rows)
    value_rows = low_back(value_rows)
    row_count = query_rows.shape[0]
    q_heads = query_rows.reshape(row_count, HEADS, HD)
    k_heads = key_rows.reshape(LEN, HEADS, HD)
    v_heads = value_rows.reshape(LEN, HEADS, HD)
    scores = jnp.einsum('rhd,thd->hrt', q_heads, k_heads, precision=lax.Precision.HIGHEST) * HD ** (-0.5)
    scores = low_back(scores)
    position = block_index * row_count + jnp.arange(row_count, dtype=jnp.int32)
    causal = jnp.arange(LEN, dtype=jnp.int32)[None, :] <= position[:, None]
    scores = jnp.where(causal[None], scores, MASKED)
    row_peak = lax.optimization_barrier(jnp.max(scores, axis=-1, keepdims=True))
    shifted = jnp.exp(scores - row_peak)
    attn_probs = low(shifted / lax.optimization_barrier(jnp.sum(shifted, axis=-1, keepdims=True)))
    attended = jnp.einsum('hrt,thd->rhd', attn_probs, v_heads, precision=lax.Precision.HIGHEST)
    return attended.reshape(row_count, HEADS * HD)

def block_layer(hidden, weights):
    ln1_gain, ln1_shift, w_qkv, b_query, b_value, w_proj, b_proj, ln2_gain, ln2_shift, w_fc, b_fc, w_out, b_out = weights
    normed = low(layer_norm(hidden, ln1_gain, ln1_shift))
    joined_rows = matmul(normed, w_qkv) + jnp.concatenate([b_query, jnp.zeros_like(b_query), b_value])
    joined_rows = low(low_back(joined_rows))
    query_rows = joined_rows[:, :D]
    key_rows = joined_rows[:, D:2 * D]
    value_rows = joined_rows[:, 2 * D:]

    def one_block(items):
        return attend_rows(items[0], items[1], key_rows, value_rows)
    blocked = lax.map(jax.checkpoint(one_block), (jnp.arange(N_SEQ, dtype=jnp.int32), query_rows.reshape(N_SEQ, LEN // N_SEQ, D)))
    attended = low(low_back(blocked.reshape(LEN, D)))
    middle = hidden + low_back(matmul(attended, w_proj) + b_proj)
    normed_two = low(layer_norm(middle, ln2_gain, ln2_shift))
    pre_act = low_back(matmul(normed_two, w_fc) + b_fc)
    activ = low(gelu_tanh(pre_act))
    return middle + low_back(matmul(activ, w_out) + b_out)

def run_passes(start, passes, weights):
    hidden = start
    step_layer = jax.checkpoint(block_layer)
    for pass_index in range(MAXP):
        updated = step_layer(hidden, weights)
        hidden = jnp.where(pass_index < passes, updated, hidden)
    return hidden

def reference(tokens, out_grad, section, lengths, ln1_gain, ln1_shift, w_qkv, b_query, b_value, w_proj, b_proj, ln2_gain, ln2_shift, w_fc, b_fc, w_out, b_out):
    params = (ln1_gain, ln1_shift, w_qkv.astype(jnp.float32), b_query, b_value, w_proj.astype(jnp.float32), b_proj, ln2_gain, ln2_shift, w_fc.astype(jnp.float32), b_fc, w_out.astype(jnp.float32), b_out)
    zeros = jax.tree.map(jnp.zeros_like, params)

    def one_sequence(accum, items):
        source, cotangent, level, length = items
        passes = 2 * level + 1

        def forward(start, weights):
            return run_passes(start, passes, weights)
        final, pull = jax.vjp(forward, source.astype(jnp.float32), params)
        valid = (jnp.arange(LEN, dtype=jnp.int32) < length).astype(jnp.float32)
        start_grad, weight_grads = pull(cotangent.astype(jnp.float32) * valid[:, None])
        accum = jax.tree.map(jnp.add, accum, weight_grads)
        return (accum, (final.astype(jnp.bfloat16), start_grad))
    accum, outputs = lax.scan(one_sequence, zeros, (tokens, out_grad, section, lengths))
    mixed, start_grads = outputs
    count = jnp.sum(lengths).astype(jnp.float32)
    return (mixed, start_grads / count, accum[0] / count, accum[1] / count, accum[2] / count, accum[3] / count, accum[4] / count, accum[5] / count, accum[6] / count, accum[7] / count, accum[8] / count, accum[9] / count, accum[10] / count, accum[11] / count, accum[12] / count)
```

```python
import jax
import jax.numpy as jnp
from jax import lax
from jax.experimental import pallas as pl
from jax.experimental.pallas import tpu as pltpu
from jax.sharding import PartitionSpec as P

HEADS = 12
HD = 64
MAXP = 3


EPSILON = 1e-05
GELU_COEF = 0.7978845608028654
MASKED = -1e30


def layer_norm(hidden, gain, shift):
    average = jnp.mean(hidden, axis=-1, keepdims=True)
    centered = hidden - average
    variance = jnp.mean(centered * centered, axis=-1, keepdims=True)
    return centered * lax.rsqrt(variance + EPSILON) * gain + shift


def gelu_tanh(pre_act):
    return (
        0.5
        * pre_act
        * (1.0 + jnp.tanh(GELU_COEF * (pre_act + 0.044715 * pre_act * pre_act * pre_act)))
    )


def dense(left, right):
    return jnp.einsum("srk,kn->srn", left, right, preferred_element_type=jnp.float32)


def weight_grad(left, right):
    return jnp.einsum("srk,srn->kn", left, right, preferred_element_type=jnp.float32)


def back_dense(grad_rows, right):
    return jnp.einsum("srn,kn->srk", grad_rows, right, preferred_element_type=jnp.float32)


def row_sums(grad_rows):
    return jnp.sum(grad_rows.astype(jnp.float32), axis=(0, 1))


def causal_scores(query_rows, key_all, row_start):
    sample, row_count, width = query_rows.shape
    key_count = key_all.shape[1]
    q_heads = query_rows.reshape(sample, row_count, HEADS, HD)
    k_heads = key_all.reshape(sample, key_count, HEADS, HD)
    scores = jnp.einsum(
        "srhd,sthd->shrt", q_heads, k_heads, preferred_element_type=jnp.float32
    ) * HD ** (-0.5)
    position = row_start + lax.broadcasted_iota(jnp.int32, (row_count, key_count), 0)
    column = lax.broadcasted_iota(jnp.int32, (row_count, key_count), 1)
    return jnp.where(column <= position, scores, MASKED)


def forward_pass(hidden, params, row_start):
    (
        ln1_gain,
        ln1_shift,
        w_qkv,
        b_query,
        b_value,
        w_proj,
        b_proj,
        ln2_gain,
        ln2_shift,
        w_fc,
        b_fc,
        w_out,
        b_out,
    ) = params
    sample, row_count, width = hidden.shape
    normed_low = layer_norm(hidden, ln1_gain, ln1_shift).astype(jnp.bfloat16)
    bias_row = jnp.concatenate([b_query, jnp.zeros_like(b_query), b_value])
    joined_low = (dense(normed_low, w_qkv) + bias_row).astype(jnp.bfloat16)
    query_rows = joined_low[:, :, :width]
    key_rows = joined_low[:, :, width : 2 * width]
    value_rows = joined_low[:, :, 2 * width :]
    key_all, value_all = (
        lax.all_gather(key_rows, "seq", axis=1, tiled=True),
        lax.all_gather(value_rows, "seq", axis=1, tiled=True),
    )
    scores = causal_scores(query_rows, key_all, row_start)
    row_peak = jnp.max(scores, axis=-1, keepdims=True)
    shifted = jnp.exp(scores - row_peak)
    row_total = jnp.sum(shifted, axis=-1, keepdims=True)
    attn_probs = shifted / row_total
    log_total = row_peak + jnp.log(row_total)
    v_heads = value_all.reshape(sample, value_all.shape[1], HEADS, HD)
    attended = jnp.einsum(
        "shrt,sthd->srhd",
        attn_probs.astype(jnp.bfloat16),
        v_heads,
        preferred_element_type=jnp.float32,
    )
    attended_low = attended.reshape(sample, row_count, width).astype(jnp.bfloat16)
    middle = hidden + dense(attended_low, w_proj) + b_proj
    normed_two = layer_norm(middle, ln2_gain, ln2_shift).astype(jnp.bfloat16)
    pre_act = dense(normed_two, w_fc) + b_fc
    activ_low = gelu_tanh(pre_act).astype(jnp.bfloat16)
    output = middle + dense(activ_low, w_out) + b_out
    kept_keys = (key_rows, value_rows)
    kept = (
        hidden,
        normed_low,
        joined_low,
        kept_keys,
        log_total,
        attended_low,
        middle,
        normed_two,
        pre_act,
        activ_low,
    )
    return (output, kept)


def ffn_back(kept, grad_out, params):
    (
        ln1_gain,
        ln1_shift,
        w_qkv,
        b_query,
        b_value,
        w_proj,
        b_proj,
        ln2_gain,
        ln2_shift,
        w_fc,
        b_fc,
        w_out,
        b_out,
    ) = params
    (
        hidden,
        normed_low,
        joined_low,
        kept_keys,
        log_total,
        attended_low,
        middle,
        normed_two,
        pre_act,
        activ_low,
    ) = kept
    grad_low = grad_out.astype(jnp.bfloat16)
    g_w_out = weight_grad(activ_low, grad_low)
    g_b_out = row_sums(grad_low)
    d_activ = back_dense(grad_low, w_out)
    gelu_pull = jax.vjp(gelu_tanh, pre_act)[1]
    d_pre_low = gelu_pull(d_activ)[0].astype(jnp.bfloat16)
    g_w_fc = weight_grad(normed_two, d_pre_low)
    g_b_fc = row_sums(d_pre_low)
    d_normed_two = back_dense(d_pre_low, w_fc)
    norm_pull = jax.vjp(layer_norm, middle, ln2_gain, ln2_shift)[1]
    d_mid_norm, g_ln2_gain, g_ln2_shift = norm_pull(d_normed_two)
    return ((g_ln2_gain, g_ln2_shift, g_w_fc, g_b_fc, g_w_out, g_b_out), grad_out + d_mid_norm)


def attn_back(kept, d_middle, params, row_start):
    (
        ln1_gain,
        ln1_shift,
        w_qkv,
        b_query,
        b_value,
        w_proj,
        b_proj,
        ln2_gain,
        ln2_shift,
        w_fc,
        b_fc,
        w_out,
        b_out,
    ) = params
    (
        hidden,
        normed_low,
        joined_low,
        kept_keys,
        log_total,
        attended_low,
        middle,
        normed_two,
        pre_act,
        activ_low,
    ) = kept
    sample, row_count, width = hidden.shape
    grad_low = d_middle.astype(jnp.bfloat16)
    g_w_proj = weight_grad(attended_low, grad_low)
    g_b_proj = row_sums(grad_low)
    d_att_low = back_dense(grad_low, w_proj).astype(jnp.bfloat16)
    query_rows = joined_low[:, :, :width]
    key_all, value_all = (
        lax.all_gather(kept_keys[0], "seq", axis=1, tiled=True),
        lax.all_gather(kept_keys[1], "seq", axis=1, tiled=True),
    )
    key_count = key_all.shape[1]
    scores = causal_scores(query_rows, key_all, row_start)
    attn_probs = jnp.exp(scores - log_total)
    probs_low = attn_probs.astype(jnp.bfloat16)
    q_heads = query_rows.reshape(sample, row_count, HEADS, HD)
    k_heads = key_all.reshape(sample, key_count, HEADS, HD)
    v_heads = value_all.reshape(sample, key_count, HEADS, HD)
    do_heads = d_att_low.reshape(sample, row_count, HEADS, HD)
    d_probs = jnp.einsum("srhd,sthd->shrt", do_heads, v_heads, preferred_element_type=jnp.float32)
    inner = jnp.sum(d_probs * attn_probs, axis=-1, keepdims=True)
    d_scores = (attn_probs * (d_probs - inner)).astype(jnp.bfloat16)
    scale = HD ** (-0.5)
    d_query = (
        jnp.einsum(
            "shrt,sthd->srhd", d_scores, k_heads, preferred_element_type=jnp.float32
        ).reshape(sample, row_count, width)
        * scale
    )
    d_key_all = (
        jnp.einsum(
            "shrt,srhd->sthd", d_scores, q_heads, preferred_element_type=jnp.float32
        ).reshape(sample, key_count, width)
        * scale
    )
    d_value_all = jnp.einsum(
        "shrt,srhd->sthd", probs_low, do_heads, preferred_element_type=jnp.float32
    ).reshape(sample, key_count, width)
    d_key, d_value = (
        lax.psum_scatter(
            d_key_all.astype(jnp.bfloat16), "seq", scatter_dimension=1, tiled=True
        ).astype(jnp.float32),
        lax.psum_scatter(
            d_value_all.astype(jnp.bfloat16), "seq", scatter_dimension=1, tiled=True
        ).astype(jnp.float32),
    )
    d_joined_low = jnp.concatenate([d_query, d_key, d_value], axis=-1).astype(jnp.bfloat16)
    g_w_qkv = weight_grad(normed_low, d_joined_low)
    g_b_query = row_sums(d_joined_low[:, :, :width])
    g_b_value = row_sums(d_joined_low[:, :, 2 * width :])
    d_normed = back_dense(d_joined_low, w_qkv)
    norm_pull = jax.vjp(layer_norm, hidden, ln1_gain, ln1_shift)[1]
    d_hidden_norm, g_ln1_gain, g_ln1_shift = norm_pull(d_normed)
    terms = (g_ln1_gain, g_ln1_shift, g_w_qkv, g_b_query, g_b_value, g_w_proj, g_b_proj)
    return (terms, d_middle + d_hidden_norm)


def add_terms(accum, terms):
    if accum is None:
        return terms
    return tuple((left_term + right_term for left_term, right_term in zip(accum, terms)))


def on_device(
    tokens,
    out_grad,
    section,
    lengths,
    ln1_gain,
    ln1_shift,
    w_qkv,
    b_query,
    b_value,
    w_proj,
    b_proj,
    ln2_gain,
    ln2_shift,
    w_fc,
    b_fc,
    w_out,
    b_out,
):
    params = (
        ln1_gain,
        ln1_shift,
        w_qkv,
        b_query,
        b_value,
        w_proj,
        b_proj,
        ln2_gain,
        ln2_shift,
        w_fc,
        b_fc,
        w_out,
        b_out,
    )
    sample, row_count, width = tokens.shape
    row_start = lax.axis_index("seq") * row_count
    passes = 2 * section + 1
    position = row_start + lax.broadcasted_iota(jnp.int32, (sample, row_count), 1)
    valid = (position < lengths[:, None]).astype(jnp.float32)
    local_count = jnp.sum(valid)
    hidden = tokens.astype(jnp.float32)
    kept_all = []
    for pass_index in range(MAXP):
        updated, kept = forward_pass(hidden, params, row_start)
        kept_all.append(kept)
        active = (pass_index < passes)[:, None, None]
        hidden = jnp.where(active, updated, hidden)
    mixed = hidden.astype(jnp.bfloat16)
    grad_rows = out_grad.astype(jnp.float32) * valid[:, :, None]
    ffn_acc = None
    attn_acc = None
    for pass_index in reversed(range(MAXP)):
        active_flag = (pass_index < passes).astype(jnp.float32)[:, None, None]
        layer_grad = grad_rows * active_flag
        ffn_terms, d_middle = ffn_back(kept_all[pass_index], layer_grad, params)
        ffn_acc = add_terms(ffn_acc, ffn_terms)
        attn_terms, d_hidden = attn_back(kept_all[pass_index], d_middle, params, row_start)
        attn_acc = add_terms(attn_acc, attn_terms)
        grad_rows = d_hidden + grad_rows * (1.0 - active_flag)
    summed = lax.psum(
        (
            attn_acc[0],
            attn_acc[1],
            attn_acc[2],
            attn_acc[3],
            attn_acc[4],
            attn_acc[5],
            attn_acc[6],
            ffn_acc[0],
            ffn_acc[1],
            ffn_acc[2],
            ffn_acc[3],
            ffn_acc[4],
            ffn_acc[5],
            local_count,
        ),
        ("grp", "seq"),
    )
    attn_sums = summed[0:7]
    ffn_sums = summed[7:13]
    token_total = summed[13]
    return (
        mixed,
        grad_rows / token_total,
        attn_sums[0] / token_total,
        attn_sums[1] / token_total,
        attn_sums[2] / token_total,
        attn_sums[3] / token_total,
        attn_sums[4] / token_total,
        attn_sums[5] / token_total,
        attn_sums[6] / token_total,
        ffn_sums[0] / token_total,
        ffn_sums[1] / token_total,
        ffn_sums[2] / token_total,
        ffn_sums[3] / token_total,
        ffn_sums[4] / token_total,
        ffn_sums[5] / token_total,
    )


BF = jnp.bfloat16
F32 = jnp.float32
MESH_ID = pl.DeviceIdType.MESH
NT = (((1,), (1,)), ((), ()))
TN = (((0,), (0,)), ((), ()))
NN = (((1,), (0,)), ((), ()))
RB = 256
WIDE = 768
HALF = 384
FF = 3072
LEN = 1024
VMEM_BYTES = 60 * 2**20


def mm(left, right, dims):
    return lax.dot_general(left, right, dims, preferred_element_type=F32)


def col_sum(v):
    return jnp.sum(v, axis=0, keepdims=True)


def center(v):
    mean = jnp.mean(v, axis=1, keepdims=True)
    diff = v - mean
    var = jnp.mean(diff * diff, axis=1, keepdims=True)
    return diff, lax.rsqrt(var + EPSILON)


def barrier(partners):
    sem = pltpu.get_barrier_semaphore()
    for seq_index in partners:
        pl.semaphore_signal(sem, inc=1, device_id={"seq": seq_index}, device_id_type=MESH_ID)
    pl.semaphore_wait(sem, len(partners))


def push(src, dst, sems, slot, seq_index):
    return pltpu.make_async_remote_copy(
        src_ref=src,
        dst_ref=dst,
        send_sem=sems.at[0, slot],
        recv_sem=sems.at[1, slot],
        device_id={"seq": seq_index},
        device_id_type=MESH_ID,
    )


def qkv_columns(core, part):
    return pl.ds(pl.multiple_of(part * WIDE + core * HALF, 128), HALF)


def fwd_kernel(
    tokens,
    out_grad,
    info,
    bias_q,
    bias_v,
    vec,
    b_fc,
    w_qkv,
    w_proj,
    w_fc,
    w_out,
    st_h,
    st_norm,
    st_q,
    st_k,
    st_v,
    st_att,
    st_own,
    st_lse,
    st_mid,
    st_norm2,
    st_pre,
    st_act,
    st_og,
    final,
    wq,
    wp,
    wf,
    wo,
    tok,
    h,
    norm,
    q,
    k,
    v,
    att,
    own,
    lse,
    mid,
    norm2,
    pre,
    act,
    fin,
    wsem,
    ssem,
    nsem,
    asem,
    ysem,
):
    me = lax.axis_index("seq")
    core = lax.rem(me, 2)
    chip = me // 2
    partner = me + 1 - 2 * core
    across = lax.rem(me + 2, 4)
    loads = [
        pltpu.make_async_copy(
            w_qkv.at[:, qkv_columns(core, part)],
            wq.at[:, pl.ds(part * HALF, HALF)],
            wsem.at[part],
        )
        for part in range(3)
    ]
    loads += [
        pltpu.make_async_copy(w_proj, wp, wsem.at[3]),
        pltpu.make_async_copy(w_fc, wf, wsem.at[4]),
        pltpu.make_async_copy(w_out, wo, wsem.at[5]),
    ]
    keep = pltpu.make_async_copy(tokens.at[chip], tok.at[chip], wsem.at[6])
    keep.start()
    for load in loads:
        load.start()
    barrier((partner, across))
    give = push(tokens.at[1 - chip], tok.at[chip], ysem, 0, across)
    give.start()
    keep.wait()
    give.wait()
    og_keep = pltpu.make_async_copy(out_grad.at[chip], st_og.at[chip], wsem.at[6])
    og_give = push(out_grad.at[1 - chip], st_og.at[chip], ysem, 1, across)
    og_keep.start()
    og_give.start()
    for j in range(2):
        h[j] = tok[j].astype(F32)
    for load in loads:
        load.wait()

    def one_pass(p, carry):
        norm_send = []
        for j in range(2):
            diff, inv = center(h[j])
            norm[2 * j + core] = (diff * inv * vec[0:1] + vec[1:2]).astype(BF)
            copy = push(norm.at[2 * j + core], norm.at[2 * j + core], nsem, j, partner)
            copy.start()
            norm_send.append(copy)
        save_h = pltpu.make_async_copy(h, st_h.at[p], ssem.at[0])
        save_h.start()

        def project(block):
            rows = norm[block]
            out = mm(rows, wq[...], NN)
            q[block] = (out[:, :HALF] + bias_q[...]).astype(BF)
            k[block] = out[:, HALF : 2 * HALF].astype(BF)
            v[block] = (out[:, 2 * HALF :] + bias_v[...]).astype(BF)

        for j in range(2):
            project(2 * j + core)
        for j in range(2):
            norm_send[j].wait()
            project(2 * j + 1 - core)
        saves = [
            pltpu.make_async_copy(norm, st_norm.at[p], ssem.at[1]),
            pltpu.make_async_copy(q, st_q.at[p], ssem.at[2]),
            pltpu.make_async_copy(k, st_k.at[p], ssem.at[3]),
            pltpu.make_async_copy(v, st_v.at[p], ssem.at[4]),
        ]
        for save in saves:
            save.start()
        lane = lax.broadcasted_iota(jnp.int32, (RB, 128), 1)
        row = lax.broadcasted_iota(jnp.int32, (2 * RB, RB), 0) & (RB - 1)
        causal = lax.broadcasted_iota(jnp.int32, (2 * RB, RB), 1) <= row
        zero = jnp.zeros((RB, 128), BF)
        att_send = []
        for i in (3, 2, 0, 1):
            keys = (i + 1) * RB
            for pair in range(3):
                cs = slice(pair * 128, pair * 128 + 128)
                qi = q[i, :, cs] * jnp.asarray(HD**-0.5, BF)
                both = jnp.concatenate(
                    [jnp.where(lane < HD, qi, zero), jnp.where(lane < HD, zero, qi)], 0
                )
                k_all = k[0 : i + 1, :, cs].reshape(keys, 128)
                v_all = v[0 : i + 1, :, cs].reshape(keys, 128)
                s = mm(both, k_all, NT)
                last = jnp.where(causal, s[:, i * RB :], MASKED)
                s = jnp.concatenate([s[:, : i * RB], last], 1) if i else last
                peak = jnp.max(s, axis=1, keepdims=True)
                e = jnp.exp(s - peak).astype(BF)
                ol = mm(e, jnp.concatenate([v_all, jnp.ones((keys, 128), BF)], 1), NN)
                total = ol[:, 128:]
                o = ol[:, :128] / total
                att[i, :, cs] = jnp.where(lane < HD, o[:RB], o[RB:]).astype(BF)
                ls = peak + jnp.log(total)
                ls = jnp.concatenate([ls[:RB], ls[RB:]], 1).T
                lse[pair, 0:1, i * RB : (i + 1) * RB] = ls[0:1]
                lse[pair, 1:2, i * RB : (i + 1) * RB] = ls[128:129]
            if i == 3:
                saves[0].wait()
            copy = push(att.at[i], own.at[i // 2, core], asem, i // 2, partner)

            @pl.when(core == i % 2)
            def _():
                own[i // 2, core] = att[i]

            @pl.when(core != i % 2)
            def _():
                copy.start()

            if i in (2, 1):
                att_send.append(copy)
        save_att = pltpu.make_async_copy(att, st_att.at[p], ssem.at[1])
        save_lse = pltpu.make_async_copy(lse, st_lse.at[p], ssem.at[5])
        save_att.start()
        save_lse.start()
        for j, copy in ((1, att_send[0]), (0, att_send[1])):
            copy.wait()
            out = mm(own[j, 0], wp[0:HALF, :], NN) + mm(own[j, 1], wp[HALF:, :], NN)
            m = h[j] + out + vec[2:3]
            mid[j] = m
            diff, inv = center(m)
            norm2[j] = (diff * inv * vec[3:4] + vec[4:5]).astype(BF)
        save_rest = [
            pltpu.make_async_copy(own, st_own.at[p], ssem.at[6]),
            pltpu.make_async_copy(mid, st_mid.at[p], ssem.at[7]),
            pltpu.make_async_copy(norm2, st_norm2.at[p], ssem.at[8]),
        ]
        for save in save_rest:
            save.start()
        x = norm2[...].reshape(2 * RB, WIDE)
        for t in range(3):
            cs = slice(t * 1024, (t + 1) * 1024)
            z = mm(x, wf[:, cs], NN) + b_fc[:, cs]
            pre[:, cs] = z.astype(BF)
            act[:, cs] = gelu_tanh(z).astype(BF)
        save_ffn = [
            pltpu.make_async_copy(pre, st_pre.at[p], ssem.at[9]),
            pltpu.make_async_copy(act, st_act.at[p], ssem.at[10]),
        ]
        for save in save_ffn:
            save.start()
        out = mm(act[...], wo[...], NN)
        active = info[pl.ds(p, 1), :]
        save_h.wait()
        for j in range(2):
            new = mid[j] + out[j * RB : (j + 1) * RB] + vec[5:6]
            h[j] = jnp.where(active > 0.5, new, h[j])
        for save in saves[1:] + [save_att, save_lse] + save_rest + save_ffn:
            save.wait()
        return carry

    lax.fori_loop(0, MAXP, one_pass, 0)
    for j in range(2):
        fin[j] = h[j].astype(BF)
    done = pltpu.make_async_copy(fin, final, ssem.at[0])
    done.start()
    og_keep.wait()
    og_give.wait()
    done.wait()


def shape(dims, kind=BF):
    return jax.ShapeDtypeStruct(dims, kind)


def forward_call(tokens, out_grad, info, bias_q, bias_v, vec, b_fc, w_qkv, w_proj, w_fc, w_out):
    vmem = pl.BlockSpec(memory_space=pltpu.VMEM)
    hbm = pl.BlockSpec(memory_space=pl.ANY)
    outs = (
        shape((MAXP, 2, RB, WIDE), F32),
        shape((MAXP, 4, RB, WIDE)),
        shape((MAXP, 4, RB, HALF)),
        shape((MAXP, 4, RB, HALF)),
        shape((MAXP, 4, RB, HALF)),
        shape((MAXP, 4, RB, HALF)),
        shape((MAXP, 2, 2, RB, HALF)),
        shape((MAXP, 3, 2, LEN), F32),
        shape((MAXP, 2, RB, WIDE), F32),
        shape((MAXP, 2, RB, WIDE)),
        shape((MAXP, 2 * RB, FF)),
        shape((MAXP, 2 * RB, FF)),
        shape((2, RB, WIDE)),
        shape((2, RB, WIDE)),
    )
    scratch = [
        pltpu.VMEM((WIDE, 3 * HALF), BF),
        pltpu.VMEM((WIDE, WIDE), BF),
        pltpu.VMEM((WIDE, FF), BF),
        pltpu.VMEM((FF, WIDE), BF),
        pltpu.VMEM((2, RB, WIDE), BF),
        pltpu.VMEM((2, RB, WIDE), F32),
        pltpu.VMEM((4, RB, WIDE), BF),
        pltpu.VMEM((4, RB, HALF), BF),
        pltpu.VMEM((4, RB, HALF), BF),
        pltpu.VMEM((4, RB, HALF), BF),
        pltpu.VMEM((4, RB, HALF), BF),
        pltpu.VMEM((2, 2, RB, HALF), BF),
        pltpu.VMEM((3, 2, LEN), F32),
        pltpu.VMEM((2, RB, WIDE), F32),
        pltpu.VMEM((2, RB, WIDE), BF),
        pltpu.VMEM((2 * RB, FF), BF),
        pltpu.VMEM((2 * RB, FF), BF),
        pltpu.VMEM((2, RB, WIDE), BF),
        pltpu.SemaphoreType.DMA((7,)),
        pltpu.SemaphoreType.DMA((11,)),
        pltpu.SemaphoreType.DMA((2, 2)),
        pltpu.SemaphoreType.DMA((2, 2)),
        pltpu.SemaphoreType.DMA((2, 2)),
    ]
    return pl.pallas_call(
        fwd_kernel,
        out_shape=outs,
        in_specs=[hbm] * 2 + [vmem] * 5 + [hbm] * 4,
        out_specs=(hbm,) * len(outs),
        scratch_shapes=scratch,
        compiler_params=pltpu.CompilerParams(
            collective_id=1, has_side_effects=True, vmem_limit_bytes=VMEM_BYTES
        ),
        name="forward",
    )(tokens, out_grad, info, bias_q, bias_v, vec, b_fc, w_qkv, w_proj, w_fc, w_out)


def gelu_slope(z):
    cubic = 0.044715 * z * z
    t = jnp.tanh(GELU_COEF * (z + cubic * z))
    return 0.5 * (1.0 + t) + (0.5 * GELU_COEF) * z * (1.0 - t * t) * (1.0 + 3.0 * cubic)


def norm_back(v, grad, gain):
    diff, inv = center(v)
    xhat = diff * inv
    qv = grad * gain
    mean = jnp.mean(qv, axis=1, keepdims=True)
    cross = jnp.mean(qv * xhat, axis=1, keepdims=True)
    return inv * (qv - mean - xhat * cross), col_sum(grad * xhat), col_sum(grad)


def bwd_kernel(
    final,
    og,
    info,
    vec,
    w_qkv,
    w_proj,
    w_fc,
    w_out,
    st_h,
    st_q,
    st_k,
    st_v,
    st_att,
    st_lse,
    st_mid,
    st_pre,
    mixed,
    st_e,
    st_dpre,
    st_f,
    st_dfused,
    g_out,
    sums,
    sums_qv,
    sums_fc,
    wq,
    wp,
    wf,
    wo,
    g,
    glow,
    h,
    q,
    k,
    v,
    att,
    lse,
    mid,
    pre,
    dpre,
    dmid,
    flow,
    datt,
    datt_in,
    dfused,
    part,
    part_in,
    dk_acc,
    dv_acc,
    wsem,
    lsem,
    ssem,
    dsem,
    psem,
    ysem,
):
    me = lax.axis_index("seq")
    core = lax.rem(me, 2)
    chip = me // 2
    partner = me + 1 - 2 * core
    across = lax.rem(me + 2, 4)
    loads = [
        pltpu.make_async_copy(w_out, wo, wsem.at[0]),
        pltpu.make_async_copy(w_fc, wf, wsem.at[1]),
        pltpu.make_async_copy(w_proj, wp, wsem.at[2]),
    ]
    loads += [
        pltpu.make_async_copy(
            w_qkv.at[:, qkv_columns(core, third)],
            wq.at[:, pl.ds(third * HALF, HALF)],
            wsem.at[3 + third],
        )
        for third in range(3)
    ]

    def fetch(p):
        return {
            "pre": pltpu.make_async_copy(st_pre.at[p], pre, lsem.at[0]),
            "mid": pltpu.make_async_copy(st_mid.at[p], mid, lsem.at[1]),
            "q": pltpu.make_async_copy(st_q.at[p], q, lsem.at[2]),
            "k": pltpu.make_async_copy(st_k.at[p], k, lsem.at[3]),
            "v": pltpu.make_async_copy(st_v.at[p], v, lsem.at[4]),
            "att": pltpu.make_async_copy(st_att.at[p], att, lsem.at[5]),
            "lse": pltpu.make_async_copy(st_lse.at[p], lse, lsem.at[6]),
            "h": pltpu.make_async_copy(st_h.at[p], h, lsem.at[7]),
        }

    first_g = pltpu.make_async_copy(og, glow, wsem.at[6])
    first_g.start()
    first = fetch(MAXP - 1)
    loads[0].start()
    first["pre"].start()
    loads[1].start()
    for name in ("mid", "q", "k", "v", "att", "lse", "h"):
        first[name].start()
    for load in loads[2:]:
        load.start()
    barrier((partner, across))
    mixed_keep = pltpu.make_async_copy(final.at[chip], mixed.at[chip], wsem.at[7])
    mixed_give = push(final.at[1 - chip], mixed.at[chip], ysem, 0, across)
    mixed_keep.start()
    mixed_give.start()
    sums[...] = jnp.zeros_like(sums)
    sums_qv[...] = jnp.zeros_like(sums_qv)
    sums_fc[...] = jnp.zeros_like(sums_fc)
    first_g.wait()
    for j in range(2):
        pos = (2 * j + core) * RB + lax.broadcasted_iota(jnp.int32, (RB, WIDE), 0)
        valid = pos.astype(F32) < info[3:4]
        g[j] = jnp.where(valid, glow[j].astype(F32), 0.0)
    for load in loads:
        load.wait()

    def one_pass(step, carry):
        p = MAXP - 1 - step
        here = fetch(p)
        ahead = fetch(jnp.maximum(p - 1, 0))

        def prefetch(*names):
            @pl.when(p > 0)
            def _():
                for name in names:
                    ahead[name].start()

        active = info[pl.ds(p, 1), :]
        for j in range(2):
            glow[j] = (g[j] * active).astype(BF)
        save_e = pltpu.make_async_copy(glow, st_e.at[p], ssem.at[0])
        save_e.start()
        e = glow[...].reshape(2 * RB, WIDE)
        sums[5:6] += col_sum(e.astype(F32))
        here["pre"].wait()
        for t in range(3):
            cs = slice(t * 1024, (t + 1) * 1024)
            dact = mm(e, wo[cs, :], NT)
            d = (dact * gelu_slope(pre[:, cs].astype(F32))).astype(BF)
            dpre[:, cs] = d
            sums_fc[:, cs] += col_sum(d.astype(F32))
        prefetch("pre")
        save_dpre = pltpu.make_async_copy(dpre, st_dpre.at[p], ssem.at[1])
        save_dpre.start()
        dnorm2 = mm(dpre[...], wf[...], NT)
        here["mid"].wait()
        for j in range(2):
            d = dnorm2[j * RB : (j + 1) * RB]
            dv_in, dgain, dshift = norm_back(mid[j], d, vec[3:4])
            sums[3:4] += dgain
            sums[4:5] += dshift
            dm = g[j] * active + dv_in
            dmid[j] = dm
            low = dm.astype(BF)
            flow[j] = low
            sums[2:3] += col_sum(low.astype(F32))
        prefetch("mid")
        save_f = pltpu.make_async_copy(flow, st_f.at[p], ssem.at[2])
        save_f.start()
        da = mm(flow[...].reshape(2 * RB, WIDE), wp[...], NT).astype(BF)
        for half in range(2):
            for j in range(2):
                datt[half, j] = da[j * RB : (j + 1) * RB, half * HALF : (half + 1) * HALF]
        datt_send = []
        for j in range(2):
            copy = push(
                datt.at[1 - core, j], datt_in.at[2 * j + core], dsem, j, partner
            )
            copy.start()
            datt_send.append(copy)
            datt_in[2 * j + core] = datt[core, j]
        for name in ("q", "k", "v", "att", "lse"):
            here[name].wait()
        for copy in datt_send:
            copy.wait()
        lane = lax.broadcasted_iota(jnp.int32, (RB, 128), 1)
        zero = jnp.zeros((RB, 128), BF)
        col = lax.broadcasted_iota(jnp.int32, (RB, 2 * RB), 1) & (RB - 1)
        causal = lax.broadcasted_iota(jnp.int32, (RB, 2 * RB), 0) <= col
        sub = lax.broadcasted_iota(jnp.int32, (128, LEN), 0)
        zero_t = jnp.zeros((128, LEN), BF)
        scale = jnp.asarray(HD**-0.5, BF)

        def split(rows):
            return jnp.concatenate(
                [jnp.where(lane < HD, rows, zero), jnp.where(lane < HD, zero, rows)], 0
            )

        for pair in range(3):
            cs = slice(pair * 128, pair * 128 + 128)
            slot = pair % 2
            k_t = k[:, :, cs].reshape(LEN, 128).T
            k_low = jnp.where(sub < HD, k_t, zero_t)
            k_high = jnp.where(sub < HD, zero_t, k_t)
            for i in (3, 2, 1, 0):
                keys = (i + 1) * RB
                rs = slice(i * RB, (i + 1) * RB)
                qm = split(q[i, :, cs] * scale)
                do = datt_in[i, :, cs]
                dm = split(do)
                inner = (do.astype(F32) * att[i, :, cs].astype(F32)).T
                inner = jnp.concatenate([col_sum(inner[:HD]), col_sum(inner[HD:])], 1)
                total = jnp.concatenate([lse[pair, 0:1, rs], lse[pair, 1:2, rs]], 1)
                s = mm(k[0 : i + 1, :, cs].reshape(keys, 128), qm, NT)
                dp = mm(v[0 : i + 1, :, cs].reshape(keys, 128), dm, NT)
                last = jnp.where(causal, s[i * RB :], MASKED)
                s = jnp.concatenate([s[: i * RB], last], 0) if i else last
                prob = jnp.exp(s - total)
                ds = (prob * (dp - inner)).astype(BF)
                dv = mm(prob.astype(BF), dm, NN)
                dk = mm(ds, qm, NN)
                if i == 3:
                    dv_acc[slot] = dv
                    dk_acc[slot] = dk
                else:
                    dv_acc[slot, 0:keys] += dv
                    dk_acc[slot, 0:keys] += dk
                dq = mm(k_low[:, :keys], ds[:, :RB], NN) + mm(k_high[:, :keys], ds[:, RB:], NN)
                dfused[i, :, cs] = (dq.T * HD**-0.5).astype(BF)
            ks = slice(HALF + pair * 128, HALF + pair * 128 + 128)
            vs = slice(2 * HALF + pair * 128, 2 * HALF + pair * 128 + 128)
            dfused[:, :, ks] = dk_acc[slot].astype(BF).reshape(4, RB, 128)
            dfused[:, :, vs] = dv_acc[slot].astype(BF).reshape(4, RB, 128)
        prefetch("q", "k", "v", "att", "lse")
        save_d = pltpu.make_async_copy(dfused, st_dfused.at[p], ssem.at[3])
        save_d.start()
        part_send = []
        for j in range(2):
            block = 2 * j + 1 - core
            part[j] = mm(dfused[block], wq[...], NT).astype(BF)
            copy = push(part.at[j], part_in.at[j], psem, j, partner)
            copy.start()
            part_send.append(copy)
        dq_sum = jnp.zeros((1, HALF), F32)
        dv_sum = jnp.zeros((1, HALF), F32)
        for block in range(4):
            dq_sum += col_sum(dfused[block, :, :HALF].astype(F32))
            dv_sum += col_sum(dfused[block, :, 2 * HALF :].astype(F32))
        sums_qv[0:1] += dq_sum
        sums_qv[1:2] += dv_sum
        mine = [mm(dfused[2 * j + core], wq[...], NT) for j in range(2)]
        here["h"].wait()
        save_e.wait()
        for j in range(2):
            part_send[j].wait()
            d = mine[j] + part_in[j].astype(F32)
            dv_in, dgain, dshift = norm_back(h[j], d, vec[0:1])
            sums[0:1] += dgain
            sums[1:2] += dshift
            g[j] = dmid[j] + dv_in + g[j] * (1.0 - active)
        prefetch("h")
        save_dpre.wait()
        save_f.wait()
        save_d.wait()
        return carry

    lax.fori_loop(0, MAXP, one_pass, 0)
    done = pltpu.make_async_copy(g, g_out, ssem.at[0])
    done.start()
    mixed_keep.wait()
    mixed_give.wait()
    done.wait()


def backward_call(final, og, info, vec, w_qkv, w_proj, w_fc, w_out, *stash):
    vmem = pl.BlockSpec(memory_space=pltpu.VMEM)
    hbm = pl.BlockSpec(memory_space=pl.ANY)
    outs = (
        shape((2, RB, WIDE)),
        shape((MAXP, 2, RB, WIDE)),
        shape((MAXP, 2 * RB, FF)),
        shape((MAXP, 2, RB, WIDE)),
        shape((MAXP, 4, RB, 3 * HALF)),
        shape((2, RB, WIDE), F32),
        shape((8, WIDE), F32),
        shape((2, HALF), F32),
        shape((1, FF), F32),
    )
    scratch = [
        pltpu.VMEM((WIDE, 3 * HALF), BF),
        pltpu.VMEM((WIDE, WIDE), BF),
        pltpu.VMEM((WIDE, FF), BF),
        pltpu.VMEM((FF, WIDE), BF),
        pltpu.VMEM((2, RB, WIDE), F32),
        pltpu.VMEM((2, RB, WIDE), BF),
        pltpu.VMEM((2, RB, WIDE), F32),
        pltpu.VMEM((4, RB, HALF), BF),
        pltpu.VMEM((4, RB, HALF), BF),
        pltpu.VMEM((4, RB, HALF), BF),
        pltpu.VMEM((4, RB, HALF), BF),
        pltpu.VMEM((3, 2, LEN), F32),
        pltpu.VMEM((2, RB, WIDE), F32),
        pltpu.VMEM((2 * RB, FF), BF),
        pltpu.VMEM((2 * RB, FF), BF),
        pltpu.VMEM((2, RB, WIDE), F32),
        pltpu.VMEM((2, RB, WIDE), BF),
        pltpu.VMEM((2, 2, RB, HALF), BF),
        pltpu.VMEM((4, RB, HALF), BF),
        pltpu.VMEM((4, RB, 3 * HALF), BF),
        pltpu.VMEM((2, RB, WIDE), BF),
        pltpu.VMEM((2, RB, WIDE), BF),
        pltpu.VMEM((2, LEN, 128), F32),
        pltpu.VMEM((2, LEN, 128), F32),
        pltpu.SemaphoreType.DMA((8,)),
        pltpu.SemaphoreType.DMA((8,)),
        pltpu.SemaphoreType.DMA((4,)),
        pltpu.SemaphoreType.DMA((2, 2)),
        pltpu.SemaphoreType.DMA((2, 2)),
        pltpu.SemaphoreType.DMA((2, 1)),
    ]
    return pl.pallas_call(
        bwd_kernel,
        out_shape=outs,
        in_specs=[hbm] * 2 + [vmem] * 2 + [hbm] * 12,
        out_specs=(hbm,) * 6 + (vmem,) * 3,
        scratch_shapes=scratch,
        compiler_params=pltpu.CompilerParams(
            collective_id=2, has_side_effects=True, vmem_limit_bytes=VMEM_BYTES
        ),
        name="backward",
    )(final, og, info, vec, w_qkv, w_proj, w_fc, w_out, *stash)


def flat(a):
    return a.reshape(-1, a.shape[-1])


def rows_grad(left, right):
    return lax.dot_general(flat(left), flat(right), TN, preferred_element_type=F32)


def on_chip(
    tokens,
    out_grad,
    section,
    lengths,
    ln1_gain,
    ln1_shift,
    w_qkv,
    b_query,
    b_value,
    w_proj,
    b_proj,
    ln2_gain,
    ln2_shift,
    w_fc,
    b_fc,
    w_out,
    b_out,
):
    me = lax.axis_index("seq")
    core = lax.rem(me, 2)
    chip = me // 2
    passes = 2 * lax.dynamic_index_in_dim(section, chip, keepdims=False) + 1
    length = lax.dynamic_index_in_dim(lengths, chip, keepdims=False)
    step = jnp.arange(8)
    info = jnp.where(step < MAXP, (step < passes).astype(F32), length.astype(F32))
    info = jnp.broadcast_to(info[:, None], (8, WIDE))
    zero = jnp.zeros_like(b_proj)
    vec = jnp.stack([ln1_gain, ln1_shift, b_proj, ln2_gain, ln2_shift, b_out, zero, zero])
    bias_q = lax.dynamic_slice_in_dim(b_query, core * HALF, HALF)[None]
    bias_v = lax.dynamic_slice_in_dim(b_value, core * HALF, HALF)[None]
    kept = forward_call(
        tokens, out_grad, info, bias_q, bias_v, vec, b_fc[None], w_qkv, w_proj, w_fc, w_out
    )
    (h, norm, q, k, v, att, own, lse, mid, norm2, pre, act, og, final) = kept
    back = backward_call(
        final, og, info, vec, w_qkv, w_proj, w_fc, w_out, h, q, k, v, att, lse, mid, pre
    )
    (mixed, e, dpre, f, dfused, g, sums, sums_qv, sums_fc) = back
    g_qkv = rows_grad(norm, dfused)
    g_fc = rows_grad(norm2, dpre)
    g_out = rows_grad(act, e)
    own_rows = own.transpose(0, 1, 3, 2, 4)
    g_proj = lax.dot_general(
        own_rows.reshape(-1, WIDE), flat(f), TN, preferred_element_type=F32
    )
    full = jnp.zeros((WIDE, 3, 2, HALF), F32)
    full = lax.dynamic_update_slice(full, g_qkv.reshape(WIDE, 3, 1, HALF), (0, 0, core, 0))
    g_qkv = full.reshape(WIDE, 3 * WIDE)
    full = jnp.zeros((2, 2, HALF), F32)
    full = lax.dynamic_update_slice(full, sums_qv.reshape(2, 1, HALF), (0, core, 0))
    g_bqv = full.reshape(2, WIDE)
    count = jnp.where(me == 0, jnp.sum(lengths).astype(F32), 0.0)
    big = lax.psum(tuple(a.astype(BF) for a in (g_qkv, g_proj, g_fc, g_out)), ("grp", "seq"))
    sums, g_bqv, sums_fc, count = lax.psum((sums, g_bqv, sums_fc, count), ("grp", "seq"))
    inv = 1.0 / count
    g_qkv, g_proj, g_fc, g_out = (a.astype(F32) * inv for a in big)
    other = lax.dynamic_index_in_dim(g, 1 - chip, keepdims=False)
    same = lax.dynamic_index_in_dim(g, chip, keepdims=False)
    got = lax.ppermute(other, "seq", [(i, (i + 2) % 4) for i in range(4)])
    tokens_grad = jnp.where(chip == 0, jnp.stack([same, got]), jnp.stack([got, same])) * inv
    return (
        mixed,
        tokens_grad,
        sums[0] * inv,
        sums[1] * inv,
        g_qkv,
        g_bqv[0] * inv,
        g_bqv[1] * inv,
        g_proj,
        sums[2] * inv,
        sums[3] * inv,
        sums[4] * inv,
        g_fc,
        sums_fc[0] * inv,
        g_out,
        sums[5] * inv,
    )


def solution(mesh):
    in_specs = (
        P("grp", "seq", None),
        P("grp", "seq", None),
        P("grp"),
        P("grp"),
        P(),
        P(),
        P(),
        P(),
        P(),
        P(),
        P(),
        P(),
        P(),
        P(),
        P(),
        P(),
        P(),
    )
    out_specs = (
        P("grp", "seq", None),
        P("grp", "seq", None),
        P(),
        P(),
        P(),
        P(),
        P(),
        P(),
        P(),
        P(),
        P(),
        P(),
        P(),
        P(),
        P(),
    )
    chosen = on_chip if mesh.shape["seq"] == 4 else on_device
    return jax.shard_map(
        chosen, mesh=mesh, in_specs=in_specs, out_specs=out_specs, check_vma=False
    )
```

```python
import jax
import jax.numpy as jnp
from jax import lax
from jax.experimental import pallas as pl
from jax.experimental.pallas import tpu as pltpu
from jax.sharding import PartitionSpec as P

HEADS = 12
HD = 64
MAXP = 3


EPSILON = 1e-05
GELU_COEF = 0.7978845608028654
MASKED = -1e30


def layer_norm(hidden, gain, shift):
    average = jnp.mean(hidden, axis=-1, keepdims=True)
    centered = hidden - average
    variance = jnp.mean(centered * centered, axis=-1, keepdims=True)
    return centered * lax.rsqrt(variance + EPSILON) * gain + shift


def gelu_tanh(pre_act):
    return (
        0.5
        * pre_act
        * (1.0 + jnp.tanh(GELU_COEF * (pre_act + 0.044715 * pre_act * pre_act * pre_act)))
    )


def dense(left, right):
    return jnp.einsum("srk,kn->srn", left, right, preferred_element_type=jnp.float32)


def weight_grad(left, right):
    return jnp.einsum("srk,srn->kn", left, right, preferred_element_type=jnp.float32)


def back_dense(grad_rows, right):
    return jnp.einsum("srn,kn->srk", grad_rows, right, preferred_element_type=jnp.float32)


def row_sums(grad_rows):
    return jnp.sum(grad_rows.astype(jnp.float32), axis=(0, 1))


def causal_scores(query_rows, key_all, row_start):
    sample, row_count, width = query_rows.shape
    key_count = key_all.shape[1]
    q_heads = query_rows.reshape(sample, row_count, HEADS, HD)
    k_heads = key_all.reshape(sample, key_count, HEADS, HD)
    scores = jnp.einsum(
        "srhd,sthd->shrt", q_heads, k_heads, preferred_element_type=jnp.float32
    ) * HD ** (-0.5)
    position = row_start + lax.broadcasted_iota(jnp.int32, (row_count, key_count), 0)
    column = lax.broadcasted_iota(jnp.int32, (row_count, key_count), 1)
    return jnp.where(column <= position, scores, MASKED)


def forward_pass(hidden, params, row_start):
    (
        ln1_gain,
        ln1_shift,
        w_qkv,
        b_query,
        b_value,
        w_proj,
        b_proj,
        ln2_gain,
        ln2_shift,
        w_fc,
        b_fc,
        w_out,
        b_out,
    ) = params
    sample, row_count, width = hidden.shape
    normed_low = layer_norm(hidden, ln1_gain, ln1_shift).astype(jnp.bfloat16)
    bias_row = jnp.concatenate([b_query, jnp.zeros_like(b_query), b_value])
    joined_low = (dense(normed_low, w_qkv) + bias_row).astype(jnp.bfloat16)
    query_rows = joined_low[:, :, :width]
    key_rows = joined_low[:, :, width : 2 * width]
    value_rows = joined_low[:, :, 2 * width :]
    key_all, value_all = (
        lax.all_gather(key_rows, "seq", axis=1, tiled=True),
        lax.all_gather(value_rows, "seq", axis=1, tiled=True),
    )
    scores = causal_scores(query_rows, key_all, row_start)
    row_peak = jnp.max(scores, axis=-1, keepdims=True)
    shifted = jnp.exp(scores - row_peak)
    row_total = jnp.sum(shifted, axis=-1, keepdims=True)
    attn_probs = shifted / row_total
    log_total = row_peak + jnp.log(row_total)
    v_heads = value_all.reshape(sample, value_all.shape[1], HEADS, HD)
    attended = jnp.einsum(
        "shrt,sthd->srhd",
        attn_probs.astype(jnp.bfloat16),
        v_heads,
        preferred_element_type=jnp.float32,
    )
    attended_low = attended.reshape(sample, row_count, width).astype(jnp.bfloat16)
    middle = hidden + dense(attended_low, w_proj) + b_proj
    normed_two = layer_norm(middle, ln2_gain, ln2_shift).astype(jnp.bfloat16)
    pre_act = dense(normed_two, w_fc) + b_fc
    activ_low = gelu_tanh(pre_act).astype(jnp.bfloat16)
    output = middle + dense(activ_low, w_out) + b_out
    kept_keys = (key_rows, value_rows)
    kept = (
        hidden,
        normed_low,
        joined_low,
        kept_keys,
        log_total,
        attended_low,
        middle,
        normed_two,
        pre_act,
        activ_low,
    )
    return (output, kept)


def ffn_back(kept, grad_out, params):
    (
        ln1_gain,
        ln1_shift,
        w_qkv,
        b_query,
        b_value,
        w_proj,
        b_proj,
        ln2_gain,
        ln2_shift,
        w_fc,
        b_fc,
        w_out,
        b_out,
    ) = params
    (
        hidden,
        normed_low,
        joined_low,
        kept_keys,
        log_total,
        attended_low,
        middle,
        normed_two,
        pre_act,
        activ_low,
    ) = kept
    grad_low = grad_out.astype(jnp.bfloat16)
    g_w_out = weight_grad(activ_low, grad_low)
    g_b_out = row_sums(grad_low)
    d_activ = back_dense(grad_low, w_out)
    gelu_pull = jax.vjp(gelu_tanh, pre_act)[1]
    d_pre_low = gelu_pull(d_activ)[0].astype(jnp.bfloat16)
    g_w_fc = weight_grad(normed_two, d_pre_low)
    g_b_fc = row_sums(d_pre_low)
    d_normed_two = back_dense(d_pre_low, w_fc)
    norm_pull = jax.vjp(layer_norm, middle, ln2_gain, ln2_shift)[1]
    d_mid_norm, g_ln2_gain, g_ln2_shift = norm_pull(d_normed_two)
    return ((g_ln2_gain, g_ln2_shift, g_w_fc, g_b_fc, g_w_out, g_b_out), grad_out + d_mid_norm)


def attn_back(kept, d_middle, params, row_start):
    (
        ln1_gain,
        ln1_shift,
        w_qkv,
        b_query,
        b_value,
        w_proj,
        b_proj,
        ln2_gain,
        ln2_shift,
        w_fc,
        b_fc,
        w_out,
        b_out,
    ) = params
    (
        hidden,
        normed_low,
        joined_low,
        kept_keys,
        log_total,
        attended_low,
        middle,
        normed_two,
        pre_act,
        activ_low,
    ) = kept
    sample, row_count, width = hidden.shape
    grad_low = d_middle.astype(jnp.bfloat16)
    g_w_proj = weight_grad(attended_low, grad_low)
    g_b_proj = row_sums(grad_low)
    d_att_low = back_dense(grad_low, w_proj).astype(jnp.bfloat16)
    query_rows = joined_low[:, :, :width]
    key_all, value_all = (
        lax.all_gather(kept_keys[0], "seq", axis=1, tiled=True),
        lax.all_gather(kept_keys[1], "seq", axis=1, tiled=True),
    )
    key_count = key_all.shape[1]
    scores = causal_scores(query_rows, key_all, row_start)
    attn_probs = jnp.exp(scores - log_total)
    probs_low = attn_probs.astype(jnp.bfloat16)
    q_heads = query_rows.reshape(sample, row_count, HEADS, HD)
    k_heads = key_all.reshape(sample, key_count, HEADS, HD)
    v_heads = value_all.reshape(sample, key_count, HEADS, HD)
    do_heads = d_att_low.reshape(sample, row_count, HEADS, HD)
    d_probs = jnp.einsum("srhd,sthd->shrt", do_heads, v_heads, preferred_element_type=jnp.float32)
    inner = jnp.sum(d_probs * attn_probs, axis=-1, keepdims=True)
    d_scores = (attn_probs * (d_probs - inner)).astype(jnp.bfloat16)
    scale = HD ** (-0.5)
    d_query = (
        jnp.einsum(
            "shrt,sthd->srhd", d_scores, k_heads, preferred_element_type=jnp.float32
        ).reshape(sample, row_count, width)
        * scale
    )
    d_key_all = (
        jnp.einsum(
            "shrt,srhd->sthd", d_scores, q_heads, preferred_element_type=jnp.float32
        ).reshape(sample, key_count, width)
        * scale
    )
    d_value_all = jnp.einsum(
        "shrt,srhd->sthd", probs_low, do_heads, preferred_element_type=jnp.float32
    ).reshape(sample, key_count, width)
    d_key, d_value = (
        lax.psum_scatter(
            d_key_all.astype(jnp.bfloat16), "seq", scatter_dimension=1, tiled=True
        ).astype(jnp.float32),
        lax.psum_scatter(
            d_value_all.astype(jnp.bfloat16), "seq", scatter_dimension=1, tiled=True
        ).astype(jnp.float32),
    )
    d_joined_low = jnp.concatenate([d_query, d_key, d_value], axis=-1).astype(jnp.bfloat16)
    g_w_qkv = weight_grad(normed_low, d_joined_low)
    g_b_query = row_sums(d_joined_low[:, :, :width])
    g_b_value = row_sums(d_joined_low[:, :, 2 * width :])
    d_normed = back_dense(d_joined_low, w_qkv)
    norm_pull = jax.vjp(layer_norm, hidden, ln1_gain, ln1_shift)[1]
    d_hidden_norm, g_ln1_gain, g_ln1_shift = norm_pull(d_normed)
    terms = (g_ln1_gain, g_ln1_shift, g_w_qkv, g_b_query, g_b_value, g_w_proj, g_b_proj)
    return (terms, d_middle + d_hidden_norm)


def add_terms(accum, terms):
    if accum is None:
        return terms
    return tuple((left_term + right_term for left_term, right_term in zip(accum, terms)))


def on_device(
    tokens,
    out_grad,
    section,
    lengths,
    ln1_gain,
    ln1_shift,
    w_qkv,
    b_query,
    b_value,
    w_proj,
    b_proj,
    ln2_gain,
    ln2_shift,
    w_fc,
    b_fc,
    w_out,
    b_out,
):
    params = (
        ln1_gain,
        ln1_shift,
        w_qkv,
        b_query,
        b_value,
        w_proj,
        b_proj,
        ln2_gain,
        ln2_shift,
        w_fc,
        b_fc,
        w_out,
        b_out,
    )
    sample, row_count, width = tokens.shape
    row_start = lax.axis_index("seq") * row_count
    passes = 2 * section + 1
    position = row_start + lax.broadcasted_iota(jnp.int32, (sample, row_count), 1)
    valid = (position < lengths[:, None]).astype(jnp.float32)
    local_count = jnp.sum(valid)
    hidden = tokens.astype(jnp.float32)
    kept_all = []
    for pass_index in range(MAXP):
        updated, kept = forward_pass(hidden, params, row_start)
        kept_all.append(kept)
        active = (pass_index < passes)[:, None, None]
        hidden = jnp.where(active, updated, hidden)
    mixed = hidden.astype(jnp.bfloat16)
    grad_rows = out_grad.astype(jnp.float32) * valid[:, :, None]
    ffn_acc = None
    attn_acc = None
    for pass_index in reversed(range(MAXP)):
        active_flag = (pass_index < passes).astype(jnp.float32)[:, None, None]
        layer_grad = grad_rows * active_flag
        ffn_terms, d_middle = ffn_back(kept_all[pass_index], layer_grad, params)
        ffn_acc = add_terms(ffn_acc, ffn_terms)
        attn_terms, d_hidden = attn_back(kept_all[pass_index], d_middle, params, row_start)
        attn_acc = add_terms(attn_acc, attn_terms)
        grad_rows = d_hidden + grad_rows * (1.0 - active_flag)
    summed = lax.psum(
        (
            attn_acc[0],
            attn_acc[1],
            attn_acc[2],
            attn_acc[3],
            attn_acc[4],
            attn_acc[5],
            attn_acc[6],
            ffn_acc[0],
            ffn_acc[1],
            ffn_acc[2],
            ffn_acc[3],
            ffn_acc[4],
            ffn_acc[5],
            local_count,
        ),
        ("grp", "seq"),
    )
    attn_sums = summed[0:7]
    ffn_sums = summed[7:13]
    token_total = summed[13]
    return (
        mixed,
        grad_rows / token_total,
        attn_sums[0] / token_total,
        attn_sums[1] / token_total,
        attn_sums[2] / token_total,
        attn_sums[3] / token_total,
        attn_sums[4] / token_total,
        attn_sums[5] / token_total,
        attn_sums[6] / token_total,
        ffn_sums[0] / token_total,
        ffn_sums[1] / token_total,
        ffn_sums[2] / token_total,
        ffn_sums[3] / token_total,
        ffn_sums[4] / token_total,
        ffn_sums[5] / token_total,
    )


BF = jnp.bfloat16
F32 = jnp.float32
MESH_ID = pl.DeviceIdType.MESH
NT = (((1,), (1,)), ((), ()))
TN = (((0,), (0,)), ((), ()))
NN = (((1,), (0,)), ((), ()))
RB = 256
WIDE = 768
HALF = 384
FF = 3072
LEN = 1024
VMEM_BYTES = 60 * 2**20


def mm(left, right, dims):
    return lax.dot_general(left, right, dims, preferred_element_type=F32)


def col_sum(v):
    return jnp.sum(v, axis=0, keepdims=True)


def center(v):
    mean = jnp.mean(v, axis=1, keepdims=True)
    diff = v - mean
    var = jnp.mean(diff * diff, axis=1, keepdims=True)
    return diff, lax.rsqrt(var + EPSILON)


def barrier(partners):
    sem = pltpu.get_barrier_semaphore()
    for seq_index in partners:
        pl.semaphore_signal(sem, inc=1, device_id={"seq": seq_index}, device_id_type=MESH_ID)
    pl.semaphore_wait(sem, len(partners))


def push(src, dst, sems, slot, seq_index):
    return pltpu.make_async_remote_copy(
        src_ref=src,
        dst_ref=dst,
        send_sem=sems.at[0, slot],
        recv_sem=sems.at[1, slot],
        device_id={"seq": seq_index},
        device_id_type=MESH_ID,
    )


def qkv_columns(core, part):
    return pl.ds(pl.multiple_of(part * WIDE + core * HALF, 128), HALF)


def fwd_kernel(
    tokens,
    out_grad,
    info,
    bias_q,
    bias_v,
    vec,
    b_fc,
    w_qkv,
    w_proj,
    w_fc,
    w_out,
    st_h,
    st_norm,
    st_q,
    st_k,
    st_v,
    st_att,
    st_own,
    st_lse,
    st_mid,
    st_norm2,
    st_pre,
    st_act,
    st_og,
    final,
    wq,
    wp,
    wf,
    wo,
    tok,
    h,
    norm,
    q,
    k,
    v,
    att,
    own,
    lse,
    mid,
    norm2,
    pre,
    act,
    fin,
    wsem,
    ssem,
    nsem,
    asem,
    ysem,
):
    me = lax.axis_index("seq")
    core = lax.rem(me, 2)
    chip = me // 2
    partner = me + 1 - 2 * core
    across = lax.rem(me + 2, 4)
    loads = [
        pltpu.make_async_copy(
            w_qkv.at[:, qkv_columns(core, part)],
            wq.at[:, pl.ds(part * HALF, HALF)],
            wsem.at[part],
        )
        for part in range(3)
    ]
    loads += [
        pltpu.make_async_copy(w_proj, wp, wsem.at[3]),
        pltpu.make_async_copy(w_fc, wf, wsem.at[4]),
        pltpu.make_async_copy(w_out, wo, wsem.at[5]),
    ]
    keep = pltpu.make_async_copy(tokens.at[chip], tok.at[chip], wsem.at[6])
    keep.start()
    for load in loads:
        load.start()
    barrier((partner, across))
    give = push(tokens.at[1 - chip], tok.at[chip], ysem, 0, across)
    give.start()
    keep.wait()
    give.wait()
    og_keep = pltpu.make_async_copy(out_grad.at[chip], st_og.at[chip], wsem.at[6])
    og_give = push(out_grad.at[1 - chip], st_og.at[chip], ysem, 1, across)
    og_keep.start()
    og_give.start()
    for j in range(2):
        h[j] = tok[j].astype(F32)
    for load in loads:
        load.wait()

    def one_pass(p, carry):
        norm_send = []
        for j in range(2):
            diff, inv = center(h[j])
            norm[2 * j + core] = (diff * inv * vec[0:1] + vec[1:2]).astype(BF)
            copy = push(norm.at[2 * j + core], norm.at[2 * j + core], nsem, j, partner)
            copy.start()
            norm_send.append(copy)
        save_h = pltpu.make_async_copy(h, st_h.at[p], ssem.at[0])
        save_h.start()

        def project(block):
            rows = norm[block]
            out = mm(rows, wq[...], NN)
            q[block] = (out[:, :HALF] + bias_q[...]).astype(BF)
            k[block] = out[:, HALF : 2 * HALF].astype(BF)
            v[block] = (out[:, 2 * HALF :] + bias_v[...]).astype(BF)

        for j in range(2):
            project(2 * j + core)
        for j in range(2):
            norm_send[j].wait()
            project(2 * j + 1 - core)
        saves = [
            pltpu.make_async_copy(norm, st_norm.at[p], ssem.at[1]),
            pltpu.make_async_copy(q, st_q.at[p], ssem.at[2]),
            pltpu.make_async_copy(k, st_k.at[p], ssem.at[3]),
            pltpu.make_async_copy(v, st_v.at[p], ssem.at[4]),
        ]
        for save in saves:
            save.start()
        lane = lax.broadcasted_iota(jnp.int32, (RB, 128), 1)
        row = lax.broadcasted_iota(jnp.int32, (2 * RB, RB), 0) & (RB - 1)
        causal = lax.broadcasted_iota(jnp.int32, (2 * RB, RB), 1) <= row
        zero = jnp.zeros((RB, 128), BF)
        att_send = []
        for i in (3, 2, 0, 1):
            keys = (i + 1) * RB
            for pair in range(3):
                cs = slice(pair * 128, pair * 128 + 128)
                qi = q[i, :, cs] * jnp.asarray(HD**-0.5, BF)
                both = jnp.concatenate(
                    [jnp.where(lane < HD, qi, zero), jnp.where(lane < HD, zero, qi)], 0
                )
                k_all = k[0 : i + 1, :, cs].reshape(keys, 128)
                v_all = v[0 : i + 1, :, cs].reshape(keys, 128)
                s = mm(both, k_all, NT)
                last = jnp.where(causal, s[:, i * RB :], MASKED)
                s = jnp.concatenate([s[:, : i * RB], last], 1) if i else last
                peak = jnp.max(s, axis=1, keepdims=True)
                e = jnp.exp(s - peak).astype(BF)
                ol = mm(e, jnp.concatenate([v_all, jnp.ones((keys, 128), BF)], 1), NN)
                total = ol[:, 128:]
                o = ol[:, :128] / total
                att[i, :, cs] = jnp.where(lane < HD, o[:RB], o[RB:]).astype(BF)
                ls = peak + jnp.log(total)
                ls = jnp.concatenate([ls[:RB], ls[RB:]], 1).T
                lse[pair, 0:1, i * RB : (i + 1) * RB] = ls[0:1]
                lse[pair, 1:2, i * RB : (i + 1) * RB] = ls[128:129]
            if i == 3:
                saves[0].wait()
            copy = push(att.at[i], own.at[i // 2, core], asem, i // 2, partner)

            @pl.when(core == i % 2)
            def _():
                own[i // 2, core] = att[i]

            @pl.when(core != i % 2)
            def _():
                copy.start()

            if i in (2, 1):
                att_send.append(copy)
        save_att = pltpu.make_async_copy(att, st_att.at[p], ssem.at[1])
        save_lse = pltpu.make_async_copy(lse, st_lse.at[p], ssem.at[5])
        save_att.start()
        save_lse.start()
        for j, copy in ((1, att_send[0]), (0, att_send[1])):
            copy.wait()
            out = mm(own[j, 0], wp[0:HALF, :], NN) + mm(own[j, 1], wp[HALF:, :], NN)
            m = h[j] + out + vec[2:3]
            mid[j] = m
            diff, inv = center(m)
            norm2[j] = (diff * inv * vec[3:4] + vec[4:5]).astype(BF)
        save_rest = [
            pltpu.make_async_copy(own, st_own.at[p], ssem.at[6]),
            pltpu.make_async_copy(mid, st_mid.at[p], ssem.at[7]),
            pltpu.make_async_copy(norm2, st_norm2.at[p], ssem.at[8]),
        ]
        for save in save_rest:
            save.start()
        x = norm2[...].reshape(2 * RB, WIDE)
        for t in range(3):
            cs = slice(t * 1024, (t + 1) * 1024)
            z = mm(x, wf[:, cs], NN) + b_fc[:, cs]
            pre[:, cs] = z.astype(BF)
            act[:, cs] = gelu_tanh(z).astype(BF)
        save_ffn = [
            pltpu.make_async_copy(pre, st_pre.at[p], ssem.at[9]),
            pltpu.make_async_copy(act, st_act.at[p], ssem.at[10]),
        ]
        for save in save_ffn:
            save.start()
        out = mm(act[...], wo[...], NN)
        active = info[pl.ds(p, 1), :]
        save_h.wait()
        for j in range(2):
            new = mid[j] + out[j * RB : (j + 1) * RB] + vec[5:6]
            h[j] = jnp.where(active > 0.5, new, h[j])
        for save in saves[1:] + [save_att, save_lse] + save_rest + save_ffn:
            save.wait()
        return carry

    lax.fori_loop(0, MAXP, one_pass, 0)
    for j in range(2):
        fin[j] = h[j].astype(BF)
    done = pltpu.make_async_copy(fin, final, ssem.at[0])
    done.start()
    og_keep.wait()
    og_give.wait()
    done.wait()


def shape(dims, kind=BF):
    return jax.ShapeDtypeStruct(dims, kind)


def forward_call(tokens, out_grad, info, bias_q, bias_v, vec, b_fc, w_qkv, w_proj, w_fc, w_out):
    vmem = pl.BlockSpec(memory_space=pltpu.VMEM)
    hbm = pl.BlockSpec(memory_space=pl.ANY)
    outs = (
        shape((MAXP, 2, RB, WIDE), F32),
        shape((MAXP, 4, RB, WIDE)),
        shape((MAXP, 4, RB, HALF)),
        shape((MAXP, 4, RB, HALF)),
        shape((MAXP, 4, RB, HALF)),
        shape((MAXP, 4, RB, HALF)),
        shape((MAXP, 2, 2, RB, HALF)),
        shape((MAXP, 3, 2, LEN), F32),
        shape((MAXP, 2, RB, WIDE), F32),
        shape((MAXP, 2, RB, WIDE)),
        shape((MAXP, 2 * RB, FF)),
        shape((MAXP, 2 * RB, FF)),
        shape((2, RB, WIDE)),
        shape((2, RB, WIDE)),
    )
    scratch = [
        pltpu.VMEM((WIDE, 3 * HALF), BF),
        pltpu.VMEM((WIDE, WIDE), BF),
        pltpu.VMEM((WIDE, FF), BF),
        pltpu.VMEM((FF, WIDE), BF),
        pltpu.VMEM((2, RB, WIDE), BF),
        pltpu.VMEM((2, RB, WIDE), F32),
        pltpu.VMEM((4, RB, WIDE), BF),
        pltpu.VMEM((4, RB, HALF), BF),
        pltpu.VMEM((4, RB, HALF), BF),
        pltpu.VMEM((4, RB, HALF), BF),
        pltpu.VMEM((4, RB, HALF), BF),
        pltpu.VMEM((2, 2, RB, HALF), BF),
        pltpu.VMEM((3, 2, LEN), F32),
        pltpu.VMEM((2, RB, WIDE), F32),
        pltpu.VMEM((2, RB, WIDE), BF),
        pltpu.VMEM((2 * RB, FF), BF),
        pltpu.VMEM((2 * RB, FF), BF),
        pltpu.VMEM((2, RB, WIDE), BF),
        pltpu.SemaphoreType.DMA((7,)),
        pltpu.SemaphoreType.DMA((11,)),
        pltpu.SemaphoreType.DMA((2, 2)),
        pltpu.SemaphoreType.DMA((2, 2)),
        pltpu.SemaphoreType.DMA((2, 2)),
    ]
    return pl.pallas_call(
        fwd_kernel,
        out_shape=outs,
        in_specs=[hbm] * 2 + [vmem] * 5 + [hbm] * 4,
        out_specs=(hbm,) * len(outs),
        scratch_shapes=scratch,
        compiler_params=pltpu.CompilerParams(
            collective_id=1, has_side_effects=True, vmem_limit_bytes=VMEM_BYTES
        ),
        name="forward",
    )(tokens, out_grad, info, bias_q, bias_v, vec, b_fc, w_qkv, w_proj, w_fc, w_out)


def gelu_slope(z):
    cubic = 0.044715 * z * z
    t = jnp.tanh(GELU_COEF * (z + cubic * z))
    return 0.5 * (1.0 + t) + (0.5 * GELU_COEF) * z * (1.0 - t * t) * (1.0 + 3.0 * cubic)


def norm_back(v, grad, gain):
    diff, inv = center(v)
    xhat = diff * inv
    qv = grad * gain
    mean = jnp.mean(qv, axis=1, keepdims=True)
    cross = jnp.mean(qv * xhat, axis=1, keepdims=True)
    return inv * (qv - mean - xhat * cross), col_sum(grad * xhat), col_sum(grad)


def bwd_kernel(
    final,
    og,
    info,
    vec,
    w_qkv,
    w_proj,
    w_fc,
    w_out,
    st_h,
    st_q,
    st_k,
    st_v,
    st_att,
    st_lse,
    st_mid,
    st_pre,
    mixed,
    st_e,
    st_dpre,
    st_f,
    st_dfused,
    g_out,
    sums,
    wq,
    wp,
    wf,
    wo,
    g,
    glow,
    h,
    q,
    k,
    v,
    att,
    lse,
    mid,
    pre,
    dpre,
    dmid,
    flow,
    datt,
    datt_in,
    dfused,
    part,
    part_in,
    dk_acc,
    dv_acc,
    sums_qv,
    sums_fc,
    wsem,
    lsem,
    ssem,
    dsem,
    psem,
    ysem,
):
    me = lax.axis_index("seq")
    core = lax.rem(me, 2)
    chip = me // 2
    partner = me + 1 - 2 * core
    across = lax.rem(me + 2, 4)
    loads = [
        pltpu.make_async_copy(w_out, wo, wsem.at[0]),
        pltpu.make_async_copy(w_fc, wf, wsem.at[1]),
        pltpu.make_async_copy(w_proj, wp, wsem.at[2]),
    ]
    loads += [
        pltpu.make_async_copy(
            w_qkv.at[:, qkv_columns(core, third)],
            wq.at[:, pl.ds(third * HALF, HALF)],
            wsem.at[3 + third],
        )
        for third in range(3)
    ]

    def fetch(p):
        return {
            "pre": pltpu.make_async_copy(st_pre.at[p], pre, lsem.at[0]),
            "mid": pltpu.make_async_copy(st_mid.at[p], mid, lsem.at[1]),
            "q": pltpu.make_async_copy(st_q.at[p], q, lsem.at[2]),
            "k": pltpu.make_async_copy(st_k.at[p], k, lsem.at[3]),
            "v": pltpu.make_async_copy(st_v.at[p], v, lsem.at[4]),
            "att": pltpu.make_async_copy(st_att.at[p], att, lsem.at[5]),
            "lse": pltpu.make_async_copy(st_lse.at[p], lse, lsem.at[6]),
            "h": pltpu.make_async_copy(st_h.at[p], h, lsem.at[7]),
        }

    first_g = pltpu.make_async_copy(og, glow, wsem.at[6])
    first_g.start()
    first = fetch(MAXP - 1)
    loads[0].start()
    first["pre"].start()
    loads[1].start()
    for name in ("mid", "q", "k", "v", "att", "lse", "h"):
        first[name].start()
    for load in loads[2:]:
        load.start()
    barrier((partner, across))
    mixed_keep = pltpu.make_async_copy(final.at[chip], mixed.at[chip], wsem.at[7])
    mixed_give = push(final.at[1 - chip], mixed.at[chip], ysem, 0, across)
    mixed_keep.start()
    mixed_give.start()
    sums[...] = jnp.zeros_like(sums)
    sums_qv[...] = jnp.zeros_like(sums_qv)
    sums_fc[...] = jnp.zeros_like(sums_fc)
    first_g.wait()
    for j in range(2):
        pos = (2 * j + core) * RB + lax.broadcasted_iota(jnp.int32, (RB, WIDE), 0)
        valid = pos.astype(F32) < info[3:4]
        g[j] = jnp.where(valid, glow[j].astype(F32), 0.0)
    for load in loads:
        load.wait()

    def one_pass(step, carry):
        p = MAXP - 1 - step
        here = fetch(p)
        ahead = fetch(jnp.maximum(p - 1, 0))

        def prefetch(*names):
            @pl.when(p > 0)
            def _():
                for name in names:
                    ahead[name].start()

        active = info[pl.ds(p, 1), :]
        for j in range(2):
            glow[j] = (g[j] * active).astype(BF)
        save_e = pltpu.make_async_copy(glow, st_e.at[p], ssem.at[0])
        save_e.start()
        e = glow[...].reshape(2 * RB, WIDE)
        sums[5:6] += col_sum(e.astype(F32))
        here["pre"].wait()
        for t in range(3):
            cs = slice(t * 1024, (t + 1) * 1024)
            dact = mm(e, wo[cs, :], NT)
            d = (dact * gelu_slope(pre[:, cs].astype(F32))).astype(BF)
            dpre[:, cs] = d
            sums_fc[:, cs] += col_sum(d.astype(F32))
        prefetch("pre")
        save_dpre = pltpu.make_async_copy(dpre, st_dpre.at[p], ssem.at[1])
        save_dpre.start()
        dnorm2 = mm(dpre[...], wf[...], NT)
        here["mid"].wait()
        for j in range(2):
            d = dnorm2[j * RB : (j + 1) * RB]
            dv_in, dgain, dshift = norm_back(mid[j], d, vec[3:4])
            sums[3:4] += dgain
            sums[4:5] += dshift
            dm = g[j] * active + dv_in
            dmid[j] = dm
            low = dm.astype(BF)
            flow[j] = low
            sums[2:3] += col_sum(low.astype(F32))
        prefetch("mid")
        save_f = pltpu.make_async_copy(flow, st_f.at[p], ssem.at[2])
        save_f.start()
        da = mm(flow[...].reshape(2 * RB, WIDE), wp[...], NT).astype(BF)
        for half in range(2):
            for j in range(2):
                datt[half, j] = da[j * RB : (j + 1) * RB, half * HALF : (half + 1) * HALF]
        datt_send = []
        for j in range(2):
            copy = push(
                datt.at[1 - core, j], datt_in.at[2 * j + core], dsem, j, partner
            )
            copy.start()
            datt_send.append(copy)
            datt_in[2 * j + core] = datt[core, j]
        for name in ("q", "k", "v", "att", "lse"):
            here[name].wait()
        for copy in datt_send:
            copy.wait()
        lane = lax.broadcasted_iota(jnp.int32, (RB, 128), 1)
        zero = jnp.zeros((RB, 128), BF)
        col = lax.broadcasted_iota(jnp.int32, (RB, 2 * RB), 1) & (RB - 1)
        causal = lax.broadcasted_iota(jnp.int32, (RB, 2 * RB), 0) <= col
        sub = lax.broadcasted_iota(jnp.int32, (128, LEN), 0)
        zero_t = jnp.zeros((128, LEN), BF)
        scale = jnp.asarray(HD**-0.5, BF)

        def split(rows):
            return jnp.concatenate(
                [jnp.where(lane < HD, rows, zero), jnp.where(lane < HD, zero, rows)], 0
            )

        for pair in range(3):
            cs = slice(pair * 128, pair * 128 + 128)
            slot = pair % 2
            k_t = k[:, :, cs].reshape(LEN, 128).T
            k_low = jnp.where(sub < HD, k_t, zero_t)
            k_high = jnp.where(sub < HD, zero_t, k_t)
            for i in (3, 2, 1, 0):
                keys = (i + 1) * RB
                rs = slice(i * RB, (i + 1) * RB)
                qm = split(q[i, :, cs] * scale)
                do = datt_in[i, :, cs]
                dm = split(do)
                inner = (do.astype(F32) * att[i, :, cs].astype(F32)).T
                inner = jnp.concatenate([col_sum(inner[:HD]), col_sum(inner[HD:])], 1)
                total = jnp.concatenate([lse[pair, 0:1, rs], lse[pair, 1:2, rs]], 1)
                s = mm(k[0 : i + 1, :, cs].reshape(keys, 128), qm, NT)
                dp = mm(v[0 : i + 1, :, cs].reshape(keys, 128), dm, NT)
                last = jnp.where(causal, s[i * RB :], MASKED)
                s = jnp.concatenate([s[: i * RB], last], 0) if i else last
                prob = jnp.exp(s - total)
                ds = (prob * (dp - inner)).astype(BF)
                dv = mm(prob.astype(BF), dm, NN)
                dk = mm(ds, qm, NN)
                if i == 3:
                    dv_acc[slot] = dv
                    dk_acc[slot] = dk
                else:
                    dv_acc[slot, 0:keys] += dv
                    dk_acc[slot, 0:keys] += dk
                dq = mm(k_low[:, :keys], ds[:, :RB], NN) + mm(k_high[:, :keys], ds[:, RB:], NN)
                dfused[i, :, cs] = (dq.T * HD**-0.5).astype(BF)
            ks = slice(HALF + pair * 128, HALF + pair * 128 + 128)
            vs = slice(2 * HALF + pair * 128, 2 * HALF + pair * 128 + 128)
            dfused[:, :, ks] = dk_acc[slot].astype(BF).reshape(4, RB, 128)
            dfused[:, :, vs] = dv_acc[slot].astype(BF).reshape(4, RB, 128)
        prefetch("q", "k", "v", "att", "lse")
        save_d = pltpu.make_async_copy(dfused, st_dfused.at[p], ssem.at[3])
        save_d.start()
        part_send = []
        for j in range(2):
            block = 2 * j + 1 - core
            part[j] = mm(dfused[block], wq[...], NT).astype(BF)
            copy = push(part.at[j], part_in.at[j], psem, j, partner)
            copy.start()
            part_send.append(copy)
        dq_sum = jnp.zeros((1, HALF), F32)
        dv_sum = jnp.zeros((1, HALF), F32)
        for block in range(4):
            dq_sum += col_sum(dfused[block, :, :HALF].astype(F32))
            dv_sum += col_sum(dfused[block, :, 2 * HALF :].astype(F32))
        sums_qv[0:1] += dq_sum
        sums_qv[1:2] += dv_sum
        mine = [mm(dfused[2 * j + core], wq[...], NT) for j in range(2)]
        here["h"].wait()
        save_e.wait()
        for j in range(2):
            part_send[j].wait()
            d = mine[j] + part_in[j].astype(F32)
            dv_in, dgain, dshift = norm_back(h[j], d, vec[0:1])
            sums[0:1] += dgain
            sums[1:2] += dshift
            g[j] = dmid[j] + dv_in + g[j] * (1.0 - active)
        prefetch("h")
        save_dpre.wait()
        save_f.wait()
        save_d.wait()
        return carry

    lax.fori_loop(0, MAXP, one_pass, 0)
    done = pltpu.make_async_copy(g, g_out, ssem.at[0])
    done.start()
    sums[6:7] = jnp.where(core == 0, info[3:4], jnp.zeros_like(info[3:4]))
    for i in range(4):
        sums[8 + i : 9 + i] = sums_fc[:, i * WIDE : (i + 1) * WIDE]
    blank = jnp.zeros((1, HALF), F32)
    for i in range(2):
        part_sum = sums_qv[i : i + 1]
        sums[12 + i : 13 + i] = jnp.concatenate(
            [jnp.where(core == 0, part_sum, blank), jnp.where(core == 0, blank, part_sum)], 1
        )
    mixed_keep.wait()
    mixed_give.wait()
    done.wait()


def backward_call(final, og, info, vec, w_qkv, w_proj, w_fc, w_out, *stash):
    vmem = pl.BlockSpec(memory_space=pltpu.VMEM)
    hbm = pl.BlockSpec(memory_space=pl.ANY)
    outs = (
        shape((2, RB, WIDE)),
        shape((MAXP, 2, RB, WIDE)),
        shape((MAXP, 2 * RB, FF)),
        shape((MAXP, 2, RB, WIDE)),
        shape((MAXP, 4, RB, 3 * HALF)),
        shape((2, RB, WIDE), F32),
        shape((16, WIDE), F32),
    )
    scratch = [
        pltpu.VMEM((WIDE, 3 * HALF), BF),
        pltpu.VMEM((WIDE, WIDE), BF),
        pltpu.VMEM((WIDE, FF), BF),
        pltpu.VMEM((FF, WIDE), BF),
        pltpu.VMEM((2, RB, WIDE), F32),
        pltpu.VMEM((2, RB, WIDE), BF),
        pltpu.VMEM((2, RB, WIDE), F32),
        pltpu.VMEM((4, RB, HALF), BF),
        pltpu.VMEM((4, RB, HALF), BF),
        pltpu.VMEM((4, RB, HALF), BF),
        pltpu.VMEM((4, RB, HALF), BF),
        pltpu.VMEM((3, 2, LEN), F32),
        pltpu.VMEM((2, RB, WIDE), F32),
        pltpu.VMEM((2 * RB, FF), BF),
        pltpu.VMEM((2 * RB, FF), BF),
        pltpu.VMEM((2, RB, WIDE), F32),
        pltpu.VMEM((2, RB, WIDE), BF),
        pltpu.VMEM((2, 2, RB, HALF), BF),
        pltpu.VMEM((4, RB, HALF), BF),
        pltpu.VMEM((4, RB, 3 * HALF), BF),
        pltpu.VMEM((2, RB, WIDE), BF),
        pltpu.VMEM((2, RB, WIDE), BF),
        pltpu.VMEM((2, LEN, 128), F32),
        pltpu.VMEM((2, LEN, 128), F32),
        pltpu.VMEM((2, HALF), F32),
        pltpu.VMEM((1, FF), F32),
        pltpu.SemaphoreType.DMA((8,)),
        pltpu.SemaphoreType.DMA((8,)),
        pltpu.SemaphoreType.DMA((4,)),
        pltpu.SemaphoreType.DMA((2, 2)),
        pltpu.SemaphoreType.DMA((2, 2)),
        pltpu.SemaphoreType.DMA((2, 1)),
    ]
    return pl.pallas_call(
        bwd_kernel,
        out_shape=outs,
        in_specs=[hbm] * 2 + [vmem] * 2 + [hbm] * 12,
        out_specs=(hbm,) * 6 + (vmem,),
        scratch_shapes=scratch,
        compiler_params=pltpu.CompilerParams(
            collective_id=2, has_side_effects=True, vmem_limit_bytes=VMEM_BYTES
        ),
        name="backward",
    )(final, og, info, vec, w_qkv, w_proj, w_fc, w_out, *stash)


CHUNKS = 6
SIDE = 768
ORDER = (
    (0, 0), (1, 0), (0, 1), (2, 0, 0, 0), (2, 0, 1, 0), (1, 1), (0, 2), (2, 1, 0, 0), (2, 1, 1, 0), (1, 2),
    (0, 3), (2, 0, 0, 1), (2, 0, 1, 1), (2, 2, 0, 0), (2, 2, 1, 0), (1, 3), (0, 4), (2, 3, 0, 0),
    (2, 3, 1, 0), (2, 1, 0, 1), (2, 1, 1, 1), (1, 4), (2, 0, 1, 2), (2, 0, 0, 2), (2, 4, 0, 0), (2, 4, 1, 0),
    (0, 5), (1, 5), (2, 5, 0, 0), (2, 5, 1, 0), (2, 0, 1, 3), (2, 2, 0, 1), (2, 2, 1, 1), (2, 0, 0, 3),
    (2, 0, 1, 4), (2, 3, 0, 1), (2, 3, 1, 1), (2, 0, 0, 4), (2, 1, 1, 2), (2, 1, 0, 2), (2, 1, 1, 3),
    (2, 4, 0, 1), (2, 4, 1, 1), (2, 1, 0, 3), (2, 1, 1, 4), (2, 5, 0, 1), (2, 5, 1, 1), (2, 1, 0, 4),
    (2, 2, 1, 2), (2, 2, 0, 2), (2, 0, 1, 5), (2, 3, 0, 2), (2, 2, 1, 3), (2, 3, 1, 2), (2, 0, 0, 5),
    (2, 2, 0, 3), (2, 4, 1, 2), (2, 4, 0, 2), (2, 3, 0, 3), (2, 1, 1, 5), (2, 5, 0, 2), (2, 2, 1, 4),
    (2, 5, 1, 2), (2, 1, 0, 5), (2, 3, 1, 3), (2, 2, 0, 4), (2, 0, 0, 6), (2, 0, 1, 6), (2, 4, 1, 3),
    (2, 2, 1, 5), (2, 4, 0, 3), (2, 1, 1, 6), (2, 3, 0, 4), (2, 1, 0, 6), (2, 2, 0, 5), (2, 5, 0, 3),
    (2, 5, 1, 3), (2, 2, 1, 6), (2, 3, 1, 4), (2, 2, 0, 6), (2, 3, 0, 5), (2, 4, 1, 4), (2, 3, 1, 5),
    (2, 4, 0, 4), (2, 5, 0, 4), (2, 3, 0, 6), (2, 5, 1, 4), (2, 3, 1, 6), (2, 4, 1, 5), (2, 4, 0, 5),
    (2, 5, 1, 5), (2, 5, 0, 5), (2, 4, 0, 6), (2, 4, 1, 6), (2, 5, 0, 6), (2, 5, 1, 6),
)


def mesh_push(src, dst, send, recv, where):
    return pltpu.make_async_remote_copy(
        src_ref=src,
        dst_ref=dst,
        send_sem=send,
        recv_sem=recv,
        device_id=where,
        device_id_type=MESH_ID,
    )


def grad_kernel(
    act,
    e,
    norm2,
    dpre,
    own,
    f,
    norm,
    dfused,
    g,
    vec,
    o_qkv,
    o_proj,
    o_fc,
    o_out,
    o_tok,
    o_vec,
    e_v,
    n2_v,
    own_v,
    f_v,
    norm_v,
    third_v,
    pieces,
    give,
    got,
    work,
    rx1,
    rx2,
    rx3,
    tok,
    tok_low,
    vsend,
    vgot,
    lsem,
    psem,
    tsem,
    csem,
    xsem,
    rsem,
    vsem,
    ysem,
    osem,
):
    me = lax.axis_index("seq")
    group = lax.axis_index("grp")
    core = lax.rem(me, 2)
    y = me // 2
    x = lax.rem(group, 2)
    z = group // 2
    other = 1 - core
    to_core = {"seq": me + 1 - 2 * core}
    to_y = {"seq": lax.rem(me + 2, 4)}
    to_x = {"grp": group + 1 - 2 * x}

    def to_z(step):
        return {"grp": lax.rem(z + step, 4) * 2 + x}

    def to_z_pair(step):
        low = lax.rem(z // step, 2)
        return {"grp": (z + step - 2 * step * low) * 2 + x}

    def half_cols(owner, part):
        return pl.ds(pl.multiple_of(owner * 2 * SIDE + part * SIDE, 128), SIDE)

    stream = []
    for src in (act, dpre):
        for part in range(2):
            for owner in (other, core):
                stream.append((src, half_cols(owner, part)))

    def load_piece(i):
        src, cols = stream[i]
        return pltpu.make_async_copy(src.at[:, :, cols], pieces.at[i % 3], psem.at[i % 3])

    def load_third(i):
        return pltpu.make_async_copy(
            dfused.at[:, :, :, pl.ds(i * HALF, HALF)], third_v.at[i % 2], tsem.at[i % 2]
        )

    load_e = pltpu.make_async_copy(e, e_v, lsem.at[0])
    load_n2 = pltpu.make_async_copy(norm2, n2_v, lsem.at[1])
    load_own = pltpu.make_async_copy(own, own_v, lsem.at[2])
    load_f = pltpu.make_async_copy(f, f_v, lsem.at[3])
    load_norm = pltpu.make_async_copy(norm, norm_v, lsem.at[4])
    load_g = pltpu.make_async_copy(g, tok, lsem.at[5])
    load_piece(0).start()
    load_e.start()
    load_piece(1).start()
    load_g.start()
    load_piece(2).start()
    load_n2.start()
    load_own.start()
    load_f.start()
    load_norm.start()
    load_third(0).start()
    load_third(1).start()

    sem = pltpu.get_barrier_semaphore()
    partners = [to_core, to_y, to_x, to_z(1), to_z(2), to_z(3)]
    for where in partners:
        pl.semaphore_signal(sem, inc=1, device_id=where, device_id_type=MESH_ID)
    pl.semaphore_wait(sem, len(partners))

    load_g.wait()
    tok_low[...] = tok[...].astype(BF)
    tok_give = mesh_push(tok_low.at[1 - y], o_tok.at[y], ysem.at[0], ysem.at[1], to_y)
    tok_keep = pltpu.make_async_copy(tok_low.at[y], o_tok.at[y], lsem.at[5])
    tok_give.start()
    tok_keep.start()

    vec_to = [to_core, to_x, to_y, to_z_pair(1), to_z_pair(2)]

    def vec_copy(k):
        return mesh_push(vsend.at[k], vgot.at[k], vsem.at[0, k], vsem.at[1, k], vec_to[k])

    vsend[0] = vec[...]
    vec_copy(0).start()

    def vec_step(k):
        vec_copy(k).wait()
        vsend[k + 1] = vsend[k] + vgot[k]
        if k < 4:
            vec_copy(k + 1).start()

    def product(n, owner, place):
        if n < 4:
            i = 2 * n + place
            load_piece(i).wait()
            piece = pieces[i % 3].reshape(MAXP * 2 * RB, SIDE)
            if n < 2:
                if i == 0:
                    load_e.wait()
                out = mm(piece, e_v[...].reshape(MAXP * 2 * RB, WIDE), TN)
            else:
                if i == 4:
                    load_n2.wait()
                out = mm(n2_v[...].reshape(MAXP * 2 * RB, WIDE), piece, TN)
            return out
        if place == 0:
            load_own.wait()
            load_f.wait()
        right = f_v[:, :, :, pl.ds(pl.multiple_of(owner * HALF, 128), HALF)]
        right = right.reshape(MAXP * 2 * RB, HALF)
        return jnp.concatenate(
            [mm(own_v[:, :, half].reshape(MAXP * 2 * RB, HALF), right, TN) for half in range(2)], 0
        )

    def after_piece(n, place):
        i = 2 * n + place
        if n < 4 and i + 3 < len(stream):
            load_piece(i + 3).start()

    def core_copy(n):
        width = SIDE if n < 4 else HALF
        return mesh_push(
            give.at[n % 2, :, pl.ds(0, width)],
            got.at[n, :, pl.ds(0, width)],
            csem.at[0, n],
            csem.at[1, n],
            to_core,
        )

    def third(i):
        load_third(i).wait()
        right = third_v[i % 2].reshape(MAXP * LEN, HALF)
        out = mm(norm_v[...].reshape(MAXP * LEN, WIDE), right, TN).astype(BF)
        return out

    def theirs(n):
        if n >= 2:
            core_copy(n - 2).wait_send()
        out = product(n, other, 0).astype(BF)
        if n < 4:
            give[n % 2] = out
        else:
            give[n % 2, :, 0:HALF] = out
        core_copy(n).start()
        after_piece(n, 0)

    def ours(n):
        if n < 5:
            out = product(n, core, 1)
            after_piece(n, 1)
            core_copy(n).wait_recv()
            if n < 4:
                out = (out + got[n].astype(F32)).astype(BF)
                work[n, 0] = out[:, :HALF]
                work[n, 1] = out[:, HALF:]
            else:
                work[n, 0] = (out + got[n, :, 0:HALF].astype(F32)).astype(BF)
                load_norm.wait()
                work[n, 1] = third(0)
                load_third(2).start()
        else:
            work[n, 0] = third(1)
            work[n, 1] = third(2)

    def rows(start, size):
        return pl.ds(pl.multiple_of(start, 16), size)

    def step_copies(n, s, k):
        first, second = ((x, to_x), (y, to_y)) if s == 0 else ((y, to_y), (x, to_x))
        a, to_a = first
        b, to_b = second
        sub = 2 * n + s
        buf = work.at[n, s]
        quarter = a * 384 + b * 192

        def copy(slot, src, dst, where):
            return mesh_push(src, dst, xsem.at[sub, slot], rsem.at[sub, slot], where)

        if k == 0:
            return [copy(0, buf.at[rows((1 - a) * 384, 384)], rx1.at[sub], to_a)]
        if k == 1:
            return [copy(1, buf.at[rows(a * 384 + (1 - b) * 192, 192)], rx2.at[sub], to_b)]
        if k == 2:
            return [
                copy(
                    1 + d,
                    buf.at[rows(quarter + lax.rem(z + d, 4) * 48, 48)],
                    rx3.at[sub, d - 1],
                    to_z(d),
                )
                for d in (1, 2, 3)
            ]
        if n < 2:
            out, start, col = o_out, core * 2 * SIDE + n * SIDE, s * HALF
        elif n < 4:
            out, start, col = o_fc, 0, core * 2 * SIDE + (n - 2) * SIDE + s * HALF
        elif n == 4 and s == 0:
            out, start, col = o_proj, 0, core * HALF
        else:
            out, start, col = o_qkv, 0, (0 if n == 4 else 1 + s) * WIDE + core * HALF

        def place(first_row, size):
            return out.at[rows(start + first_row, size), pl.ds(pl.multiple_of(col, 128), HALF)]

        if k == 3:
            mine = buf.at[rows(quarter + z * 48, 48)]
            dst = place(quarter + z * 48, 48)
            return [copy(4 + d, mine, dst, to_z(d)) for d in (1, 2, 3)] + [
                pltpu.make_async_copy(mine, dst, osem.at[sub])
            ]
        if k == 4:
            return [copy(8, place(quarter, 192), place(quarter, 192), to_b)]
        if k == 5:
            return [copy(9, place(a * 384, 384), place(a * 384, 384), to_a)]
        return [copy(10, place(0, SIDE), place(0, SIDE), to_core)]

    def advance(n, s, k):
        a, b = (x, y) if s == 0 else (y, x)
        sub = 2 * n + s
        if k > 0:
            for copy in step_copies(n, s, k - 1):
                copy.wait()
        if k == 1:
            here = rows(a * 384, 384)
            work[n, s, here] = (work[n, s, here].astype(F32) + rx1[sub].astype(F32)).astype(BF)
        if k == 2:
            here = rows(a * 384 + b * 192, 192)
            work[n, s, here] = (work[n, s, here].astype(F32) + rx2[sub].astype(F32)).astype(BF)
        if k == 3:
            here = rows(a * 384 + b * 192 + z * 48, 48)
            total = work[n, s, here].astype(F32) + rx3[sub, 0].astype(F32)
            total = total + (rx3[sub, 1].astype(F32) + rx3[sub, 2].astype(F32))
            work[n, s, here] = total.astype(BF)
        for copy in step_copies(n, s, k):
            copy.start()

    for entry in ORDER:
        if entry[0] == 0:
            n = entry[1]
            if n < 5:
                theirs(n)
            if n > 0:
                vec_step(n - 1)
        elif entry[0] == 1:
            ours(entry[1])
        else:
            advance(*entry[1:])
    total = vsend[5]
    inv = 1.0 / total[6:7]
    o_vec[...] = total * inv
    o_vec[7:8] = inv
    for n in range(CHUNKS):
        for s in range(2):
            for copy in step_copies(n, s, 6):
                copy.wait()
    for n in (3, 4):
        core_copy(n).wait_send()
    tok_give.wait()
    tok_keep.wait()


def grad_call(*operands):
    vmem = pl.BlockSpec(memory_space=pltpu.VMEM)
    hbm = pl.BlockSpec(memory_space=pl.ANY)
    outs = (
        shape((WIDE, 3 * WIDE)),
        shape((WIDE, WIDE)),
        shape((WIDE, FF)),
        shape((FF, WIDE)),
        shape((2, RB, WIDE)),
        shape((16, WIDE), F32),
    )
    scratch = [
        pltpu.VMEM((MAXP, 2, RB, WIDE), BF),
        pltpu.VMEM((MAXP, 2, RB, WIDE), BF),
        pltpu.VMEM((MAXP, 2, 2, RB, HALF), BF),
        pltpu.VMEM((MAXP, 2, RB, WIDE), BF),
        pltpu.VMEM((MAXP, 4, RB, WIDE), BF),
        pltpu.VMEM((2, MAXP, 4, RB, HALF), BF),
        pltpu.VMEM((3, MAXP, 2 * RB, SIDE), BF),
        pltpu.VMEM((2, SIDE, SIDE), BF),
        pltpu.VMEM((5, SIDE, SIDE), BF),
        pltpu.VMEM((CHUNKS, 2, SIDE, HALF), BF),
        pltpu.VMEM((2 * CHUNKS, 384, HALF), BF),
        pltpu.VMEM((2 * CHUNKS, 192, HALF), BF),
        pltpu.VMEM((2 * CHUNKS, 3, 48, HALF), BF),
        pltpu.VMEM((2, RB, WIDE), F32),
        pltpu.VMEM((2, RB, WIDE), BF),
        pltpu.VMEM((6, 16, WIDE), F32),
        pltpu.VMEM((5, 16, WIDE), F32),
        pltpu.SemaphoreType.DMA((6,)),
        pltpu.SemaphoreType.DMA((3,)),
        pltpu.SemaphoreType.DMA((2,)),
        pltpu.SemaphoreType.DMA((2, 5)),
        pltpu.SemaphoreType.DMA((2 * CHUNKS, 11)),
        pltpu.SemaphoreType.DMA((2 * CHUNKS, 11)),
        pltpu.SemaphoreType.DMA((2, 5)),
        pltpu.SemaphoreType.DMA((2,)),
        pltpu.SemaphoreType.DMA((2 * CHUNKS,)),
    ]
    return pl.pallas_call(
        grad_kernel,
        out_shape=outs,
        in_specs=[hbm] * 9 + [vmem],
        out_specs=(hbm,) * 5 + (vmem,),
        scratch_shapes=scratch,
        compiler_params=pltpu.CompilerParams(
            collective_id=3, has_side_effects=True, vmem_limit_bytes=VMEM_BYTES
        ),
        name="gradients",
    )(*operands)


def on_chip(
    tokens,
    out_grad,
    section,
    lengths,
    ln1_gain,
    ln1_shift,
    w_qkv,
    b_query,
    b_value,
    w_proj,
    b_proj,
    ln2_gain,
    ln2_shift,
    w_fc,
    b_fc,
    w_out,
    b_out,
):
    me = lax.axis_index("seq")
    core = lax.rem(me, 2)
    chip = me // 2
    passes = 2 * lax.dynamic_index_in_dim(section, chip, keepdims=False) + 1
    length = lax.dynamic_index_in_dim(lengths, chip, keepdims=False)
    step = jnp.arange(8)
    info = jnp.where(step < MAXP, (step < passes).astype(F32), length.astype(F32))
    info = jnp.broadcast_to(info[:, None], (8, WIDE))
    zero = jnp.zeros_like(b_proj)
    vec = jnp.stack([ln1_gain, ln1_shift, b_proj, ln2_gain, ln2_shift, b_out, zero, zero])
    bias_q = lax.dynamic_slice_in_dim(b_query, core * HALF, HALF)[None]
    bias_v = lax.dynamic_slice_in_dim(b_value, core * HALF, HALF)[None]
    kept = forward_call(
        tokens, out_grad, info, bias_q, bias_v, vec, b_fc[None], w_qkv, w_proj, w_fc, w_out
    )
    (h, norm, q, k, v, att, own, lse, mid, norm2, pre, act, og, final) = kept
    back = backward_call(
        final, og, info, vec, w_qkv, w_proj, w_fc, w_out, h, q, k, v, att, lse, mid, pre
    )
    (mixed, e, dpre, f, dfused, g, sums) = back
    g_qkv, g_proj, g_fc, g_out, g_tok, s = grad_call(
        act, e, norm2, dpre, own, f, norm, dfused, g, sums
    )
    inv = s[7, 0]
    return (
        mixed,
        g_tok.astype(F32) * inv,
        s[0],
        s[1],
        g_qkv.astype(F32) * inv,
        s[12],
        s[13],
        g_proj.astype(F32) * inv,
        s[2],
        s[3],
        s[4],
        g_fc.astype(F32) * inv,
        s[8:12].reshape(-1),
        g_out.astype(F32) * inv,
        s[5],
    )


def solution(mesh):
    in_specs = (
        P("grp", "seq", None),
        P("grp", "seq", None),
        P("grp"),
        P("grp"),
        P(),
        P(),
        P(),
        P(),
        P(),
        P(),
        P(),
        P(),
        P(),
        P(),
        P(),
        P(),
        P(),
    )
    out_specs = (
        P("grp", "seq", None),
        P("grp", "seq", None),
        P(),
        P(),
        P(),
        P(),
        P(),
        P(),
        P(),
        P(),
        P(),
        P(),
        P(),
        P(),
        P(),
    )
    chosen = on_chip if (mesh.shape["grp"], mesh.shape["seq"]) == (8, 4) else on_device
    return jax.shard_map(
        chosen, mesh=mesh, in_specs=in_specs, out_specs=out_specs, check_vma=False
    )
```

```python
import jax
import jax.numpy as jnp
from jax import lax
from jax.experimental import pallas as pl
from jax.experimental.pallas import tpu as pltpu
from jax.sharding import PartitionSpec as P

HEADS = 12
HD = 64
MAXP = 3


EPSILON = 1e-05
GELU_COEF = 0.7978845608028654
MASKED = -1e30


def layer_norm(hidden, gain, shift):
    average = jnp.mean(hidden, axis=-1, keepdims=True)
    centered = hidden - average
    variance = jnp.mean(centered * centered, axis=-1, keepdims=True)
    return centered * lax.rsqrt(variance + EPSILON) * gain + shift


def gelu_tanh(pre_act):
    return (
        0.5
        * pre_act
        * (1.0 + jnp.tanh(GELU_COEF * (pre_act + 0.044715 * pre_act * pre_act * pre_act)))
    )


def dense(left, right):
    return jnp.einsum("srk,kn->srn", left, right, preferred_element_type=jnp.float32)


def weight_grad(left, right):
    return jnp.einsum("srk,srn->kn", left, right, preferred_element_type=jnp.float32)


def back_dense(grad_rows, right):
    return jnp.einsum("srn,kn->srk", grad_rows, right, preferred_element_type=jnp.float32)


def row_sums(grad_rows):
    return jnp.sum(grad_rows.astype(jnp.float32), axis=(0, 1))


def causal_scores(query_rows, key_all, row_start):
    sample, row_count, width = query_rows.shape
    key_count = key_all.shape[1]
    q_heads = query_rows.reshape(sample, row_count, HEADS, HD)
    k_heads = key_all.reshape(sample, key_count, HEADS, HD)
    scores = jnp.einsum(
        "srhd,sthd->shrt", q_heads, k_heads, preferred_element_type=jnp.float32
    ) * HD ** (-0.5)
    position = row_start + lax.broadcasted_iota(jnp.int32, (row_count, key_count), 0)
    column = lax.broadcasted_iota(jnp.int32, (row_count, key_count), 1)
    return jnp.where(column <= position, scores, MASKED)


def forward_pass(hidden, params, row_start):
    (
        ln1_gain,
        ln1_shift,
        w_qkv,
        b_query,
        b_value,
        w_proj,
        b_proj,
        ln2_gain,
        ln2_shift,
        w_fc,
        b_fc,
        w_out,
        b_out,
    ) = params
    sample, row_count, width = hidden.shape
    normed_low = layer_norm(hidden, ln1_gain, ln1_shift).astype(jnp.bfloat16)
    bias_row = jnp.concatenate([b_query, jnp.zeros_like(b_query), b_value])
    joined_low = (dense(normed_low, w_qkv) + bias_row).astype(jnp.bfloat16)
    query_rows = joined_low[:, :, :width]
    key_rows = joined_low[:, :, width : 2 * width]
    value_rows = joined_low[:, :, 2 * width :]
    key_all, value_all = (
        lax.all_gather(key_rows, "seq", axis=1, tiled=True),
        lax.all_gather(value_rows, "seq", axis=1, tiled=True),
    )
    scores = causal_scores(query_rows, key_all, row_start)
    row_peak = jnp.max(scores, axis=-1, keepdims=True)
    shifted = jnp.exp(scores - row_peak)
    row_total = jnp.sum(shifted, axis=-1, keepdims=True)
    attn_probs = shifted / row_total
    log_total = row_peak + jnp.log(row_total)
    v_heads = value_all.reshape(sample, value_all.shape[1], HEADS, HD)
    attended = jnp.einsum(
        "shrt,sthd->srhd",
        attn_probs.astype(jnp.bfloat16),
        v_heads,
        preferred_element_type=jnp.float32,
    )
    attended_low = attended.reshape(sample, row_count, width).astype(jnp.bfloat16)
    middle = hidden + dense(attended_low, w_proj) + b_proj
    normed_two = layer_norm(middle, ln2_gain, ln2_shift).astype(jnp.bfloat16)
    pre_act = dense(normed_two, w_fc) + b_fc
    activ_low = gelu_tanh(pre_act).astype(jnp.bfloat16)
    output = middle + dense(activ_low, w_out) + b_out
    kept_keys = (key_rows, value_rows)
    kept = (
        hidden,
        normed_low,
        joined_low,
        kept_keys,
        log_total,
        attended_low,
        middle,
        normed_two,
        pre_act,
        activ_low,
    )
    return (output, kept)


def ffn_back(kept, grad_out, params):
    (
        ln1_gain,
        ln1_shift,
        w_qkv,
        b_query,
        b_value,
        w_proj,
        b_proj,
        ln2_gain,
        ln2_shift,
        w_fc,
        b_fc,
        w_out,
        b_out,
    ) = params
    (
        hidden,
        normed_low,
        joined_low,
        kept_keys,
        log_total,
        attended_low,
        middle,
        normed_two,
        pre_act,
        activ_low,
    ) = kept
    grad_low = grad_out.astype(jnp.bfloat16)
    g_w_out = weight_grad(activ_low, grad_low)
    g_b_out = row_sums(grad_low)
    d_activ = back_dense(grad_low, w_out)
    gelu_pull = jax.vjp(gelu_tanh, pre_act)[1]
    d_pre_low = gelu_pull(d_activ)[0].astype(jnp.bfloat16)
    g_w_fc = weight_grad(normed_two, d_pre_low)
    g_b_fc = row_sums(d_pre_low)
    d_normed_two = back_dense(d_pre_low, w_fc)
    norm_pull = jax.vjp(layer_norm, middle, ln2_gain, ln2_shift)[1]
    d_mid_norm, g_ln2_gain, g_ln2_shift = norm_pull(d_normed_two)
    return ((g_ln2_gain, g_ln2_shift, g_w_fc, g_b_fc, g_w_out, g_b_out), grad_out + d_mid_norm)


def attn_back(kept, d_middle, params, row_start):
    (
        ln1_gain,
        ln1_shift,
        w_qkv,
        b_query,
        b_value,
        w_proj,
        b_proj,
        ln2_gain,
        ln2_shift,
        w_fc,
        b_fc,
        w_out,
        b_out,
    ) = params
    (
        hidden,
        normed_low,
        joined_low,
        kept_keys,
        log_total,
        attended_low,
        middle,
        normed_two,
        pre_act,
        activ_low,
    ) = kept
    sample, row_count, width = hidden.shape
    grad_low = d_middle.astype(jnp.bfloat16)
    g_w_proj = weight_grad(attended_low, grad_low)
    g_b_proj = row_sums(grad_low)
    d_att_low = back_dense(grad_low, w_proj).astype(jnp.bfloat16)
    query_rows = joined_low[:, :, :width]
    key_all, value_all = (
        lax.all_gather(kept_keys[0], "seq", axis=1, tiled=True),
        lax.all_gather(kept_keys[1], "seq", axis=1, tiled=True),
    )
    key_count = key_all.shape[1]
    scores = causal_scores(query_rows, key_all, row_start)
    attn_probs = jnp.exp(scores - log_total)
    probs_low = attn_probs.astype(jnp.bfloat16)
    q_heads = query_rows.reshape(sample, row_count, HEADS, HD)
    k_heads = key_all.reshape(sample, key_count, HEADS, HD)
    v_heads = value_all.reshape(sample, key_count, HEADS, HD)
    do_heads = d_att_low.reshape(sample, row_count, HEADS, HD)
    d_probs = jnp.einsum("srhd,sthd->shrt", do_heads, v_heads, preferred_element_type=jnp.float32)
    inner = jnp.sum(d_probs * attn_probs, axis=-1, keepdims=True)
    d_scores = (attn_probs * (d_probs - inner)).astype(jnp.bfloat16)
    scale = HD ** (-0.5)
    d_query = (
        jnp.einsum(
            "shrt,sthd->srhd", d_scores, k_heads, preferred_element_type=jnp.float32
        ).reshape(sample, row_count, width)
        * scale
    )
    d_key_all = (
        jnp.einsum(
            "shrt,srhd->sthd", d_scores, q_heads, preferred_element_type=jnp.float32
        ).reshape(sample, key_count, width)
        * scale
    )
    d_value_all = jnp.einsum(
        "shrt,srhd->sthd", probs_low, do_heads, preferred_element_type=jnp.float32
    ).reshape(sample, key_count, width)
    d_key, d_value = (
        lax.psum_scatter(
            d_key_all.astype(jnp.bfloat16), "seq", scatter_dimension=1, tiled=True
        ).astype(jnp.float32),
        lax.psum_scatter(
            d_value_all.astype(jnp.bfloat16), "seq", scatter_dimension=1, tiled=True
        ).astype(jnp.float32),
    )
    d_joined_low = jnp.concatenate([d_query, d_key, d_value], axis=-1).astype(jnp.bfloat16)
    g_w_qkv = weight_grad(normed_low, d_joined_low)
    g_b_query = row_sums(d_joined_low[:, :, :width])
    g_b_value = row_sums(d_joined_low[:, :, 2 * width :])
    d_normed = back_dense(d_joined_low, w_qkv)
    norm_pull = jax.vjp(layer_norm, hidden, ln1_gain, ln1_shift)[1]
    d_hidden_norm, g_ln1_gain, g_ln1_shift = norm_pull(d_normed)
    terms = (g_ln1_gain, g_ln1_shift, g_w_qkv, g_b_query, g_b_value, g_w_proj, g_b_proj)
    return (terms, d_middle + d_hidden_norm)


def add_terms(accum, terms):
    if accum is None:
        return terms
    return tuple((left_term + right_term for left_term, right_term in zip(accum, terms)))


def on_device(
    tokens,
    out_grad,
    section,
    lengths,
    ln1_gain,
    ln1_shift,
    w_qkv,
    b_query,
    b_value,
    w_proj,
    b_proj,
    ln2_gain,
    ln2_shift,
    w_fc,
    b_fc,
    w_out,
    b_out,
):
    params = (
        ln1_gain,
        ln1_shift,
        w_qkv,
        b_query,
        b_value,
        w_proj,
        b_proj,
        ln2_gain,
        ln2_shift,
        w_fc,
        b_fc,
        w_out,
        b_out,
    )
    sample, row_count, width = tokens.shape
    row_start = lax.axis_index("seq") * row_count
    passes = 2 * section + 1
    position = row_start + lax.broadcasted_iota(jnp.int32, (sample, row_count), 1)
    valid = (position < lengths[:, None]).astype(jnp.float32)
    local_count = jnp.sum(valid)
    hidden = tokens.astype(jnp.float32)
    kept_all = []
    for pass_index in range(MAXP):
        updated, kept = forward_pass(hidden, params, row_start)
        kept_all.append(kept)
        active = (pass_index < passes)[:, None, None]
        hidden = jnp.where(active, updated, hidden)
    mixed = hidden.astype(jnp.bfloat16)
    grad_rows = out_grad.astype(jnp.float32) * valid[:, :, None]
    ffn_acc = None
    attn_acc = None
    for pass_index in reversed(range(MAXP)):
        active_flag = (pass_index < passes).astype(jnp.float32)[:, None, None]
        layer_grad = grad_rows * active_flag
        ffn_terms, d_middle = ffn_back(kept_all[pass_index], layer_grad, params)
        ffn_acc = add_terms(ffn_acc, ffn_terms)
        attn_terms, d_hidden = attn_back(kept_all[pass_index], d_middle, params, row_start)
        attn_acc = add_terms(attn_acc, attn_terms)
        grad_rows = d_hidden + grad_rows * (1.0 - active_flag)
    summed = lax.psum(
        (
            attn_acc[0],
            attn_acc[1],
            attn_acc[2],
            attn_acc[3],
            attn_acc[4],
            attn_acc[5],
            attn_acc[6],
            ffn_acc[0],
            ffn_acc[1],
            ffn_acc[2],
            ffn_acc[3],
            ffn_acc[4],
            ffn_acc[5],
            local_count,
        ),
        ("grp", "seq"),
    )
    attn_sums = summed[0:7]
    ffn_sums = summed[7:13]
    token_total = summed[13]
    return (
        mixed,
        grad_rows / token_total,
        attn_sums[0] / token_total,
        attn_sums[1] / token_total,
        attn_sums[2] / token_total,
        attn_sums[3] / token_total,
        attn_sums[4] / token_total,
        attn_sums[5] / token_total,
        attn_sums[6] / token_total,
        ffn_sums[0] / token_total,
        ffn_sums[1] / token_total,
        ffn_sums[2] / token_total,
        ffn_sums[3] / token_total,
        ffn_sums[4] / token_total,
        ffn_sums[5] / token_total,
    )


BF = jnp.bfloat16
F32 = jnp.float32
MESH_ID = pl.DeviceIdType.MESH
NT = (((1,), (1,)), ((), ()))
TN = (((0,), (0,)), ((), ()))
NN = (((1,), (0,)), ((), ()))
RB = 256
WIDE = 768
HALF = 384
FF = 3072
LEN = 1024
VMEM_BYTES = 60 * 2**20


def mm(left, right, dims):
    return lax.dot_general(left, right, dims, preferred_element_type=F32)


def col_sum(v):
    return jnp.sum(v, axis=0, keepdims=True)


def center(v):
    mean = jnp.mean(v, axis=1, keepdims=True)
    diff = v - mean
    var = jnp.mean(diff * diff, axis=1, keepdims=True)
    return diff, lax.rsqrt(var + EPSILON)


def barrier(partners):
    sem = pltpu.get_barrier_semaphore()
    for seq_index in partners:
        pl.semaphore_signal(sem, inc=1, device_id={"seq": seq_index}, device_id_type=MESH_ID)
    pl.semaphore_wait(sem, len(partners))


def push(src, dst, sems, slot, seq_index):
    return pltpu.make_async_remote_copy(
        src_ref=src,
        dst_ref=dst,
        send_sem=sems.at[0, slot],
        recv_sem=sems.at[1, slot],
        device_id={"seq": seq_index},
        device_id_type=MESH_ID,
    )


def qkv_columns(core, part):
    return pl.ds(pl.multiple_of(part * WIDE + core * HALF, 128), HALF)


def gelu_and_slope(z):
    square = z * z
    t = jnp.tanh(z * (GELU_COEF + (GELU_COEF * 0.044715) * square))
    half = 0.5 + 0.5 * t
    rate = GELU_COEF + (GELU_COEF * 3 * 0.044715) * square
    return z * half, half + (0.5 * z) * (1.0 - t * t) * rate


def norm_back(v, grad, gain):
    diff, inv = center(v)
    xhat = diff * inv
    qv = grad * gain
    mean = jnp.mean(qv, axis=1, keepdims=True)
    cross = jnp.mean(qv * xhat, axis=1, keepdims=True)
    return inv * (qv - mean - xhat * cross), col_sum(grad * xhat), col_sum(grad)


def layer_kernel(
    tokens,
    out_grad,
    section,
    lengths,
    in_ln1_gain,
    in_ln1_shift,
    in_b_query,
    in_b_value,
    in_b_proj,
    in_ln2_gain,
    in_ln2_shift,
    in_b_out,
    in_b_fc,
    w_qkv,
    w_proj,
    w_fc,
    w_out,
    mixed,
    st_norm,
    st_own,
    st_norm2,
    st_act,
    st_e,
    st_dpre,
    st_f,
    st_dfused,
    g_out,
    sums,
    st_h,
    st_q,
    st_k,
    st_v,
    st_att,
    st_lse,
    st_mid,
    st_pre,
    wq,
    wp,
    wf,
    wo,
    tok,
    h,
    norm,
    q,
    k,
    v,
    att,
    own,
    lse,
    mid,
    norm2,
    pre,
    act,
    g,
    glow,
    dmid,
    datt_in,
    dfused,
    dk_acc,
    dv_acc,
    rows_in,
    b_fc,
    wsem,
    ssem,
    lsem,
    bsem,
    nsem,
    asem,
    dsem,
    psem,
    ysem,
):
    me = lax.axis_index("seq")
    core = lax.rem(me, 2)
    chip = me // 2
    partner = me + 1 - 2 * core
    across = lax.rem(me + 2, 4)
    half_lanes = pl.ds(pl.multiple_of(core * HALF, 128), HALF)
    passes = jnp.full((1, WIDE), 2 * section[chip] + 1, jnp.int32)
    length = jnp.full((1, WIDE), lengths[chip], jnp.int32)

    def is_active(p):
        return jnp.full((1, WIDE), p, jnp.int32) < passes

    keep = pltpu.make_async_copy(tokens.at[chip], tok.at[chip], wsem.at[6])
    keep.start()
    loads = [
        pltpu.make_async_copy(
            w_qkv.at[:, qkv_columns(core, third)],
            wq.at[:, pl.ds(third * HALF, HALF)],
            wsem.at[third],
        )
        for third in range(3)
    ]
    loads += [
        pltpu.make_async_copy(w_proj, wp, wsem.at[3]),
        pltpu.make_async_copy(w_fc, wf, wsem.at[4]),
        pltpu.make_async_copy(w_out, wo, wsem.at[5]),
    ]
    for load in loads:
        load.start()
    short = (
        in_ln1_gain,
        in_ln1_shift,
        in_b_query,
        in_b_value,
        in_b_proj,
        in_ln2_gain,
        in_ln2_shift,
        in_b_out,
    )
    for i, ref in enumerate(short):
        rows_in[i : i + 1] = ref[...].reshape(1, WIDE)
    b_fc[...] = in_b_fc[...].reshape(1, FF)
    ln1_gain, ln1_shift, b_query, b_value, b_proj, ln2_gain, ln2_shift, b_out = (
        rows_in.at[pl.ds(i, 1)] for i in range(8)
    )
    barrier((partner, across))
    give = push(tokens.at[1 - chip], tok.at[chip], ysem, 0, across)
    give.start()
    keep.wait()
    give.wait()
    og_keep = pltpu.make_async_copy(out_grad.at[chip], glow.at[chip], wsem.at[6])
    og_give = push(out_grad.at[1 - chip], glow.at[chip], ysem, 1, across)
    og_keep.start()
    og_give.start()
    for j in range(2):
        h[j] = tok[j].astype(F32)
    for load in loads:
        load.wait()

    def forward_pass_step(p, carry):
        norm_send = []
        for j in range(2):
            diff, inv = center(h[j])
            norm[2 * j + core] = (diff * inv * ln1_gain[...] + ln1_shift[...]).astype(BF)
            copy = push(norm.at[2 * j + core], norm.at[2 * j + core], nsem, j, partner)
            copy.start()
            norm_send.append(copy)
        save_h = pltpu.make_async_copy(h, st_h.at[p], ssem.at[0])
        save_h.start()

        def project(block):
            rows = norm[block]
            out = mm(rows, wq[...], NN)
            q[block] = (out[:, :HALF] + b_query[:, half_lanes]).astype(BF)
            k[block] = out[:, HALF : 2 * HALF].astype(BF)
            v[block] = (out[:, 2 * HALF :] + b_value[:, half_lanes]).astype(BF)

        for j in range(2):
            project(2 * j + core)
        for j in range(2):
            norm_send[j].wait()
            project(2 * j + 1 - core)
        saves = [
            pltpu.make_async_copy(norm, st_norm.at[p], ssem.at[1]),
            pltpu.make_async_copy(q, st_q.at[p], ssem.at[2]),
            pltpu.make_async_copy(k, st_k.at[p], ssem.at[3]),
            pltpu.make_async_copy(v, st_v.at[p], ssem.at[4]),
        ]
        for save in saves:
            save.start()
        lane = lax.broadcasted_iota(jnp.int32, (RB, 128), 1)
        row = lax.broadcasted_iota(jnp.int32, (2 * RB, RB), 0) & (RB - 1)
        causal = lax.broadcasted_iota(jnp.int32, (2 * RB, RB), 1) <= row
        zero = jnp.zeros((RB, 128), BF)
        att_send = []
        for i in (3, 2, 0, 1):
            keys = (i + 1) * RB
            for pair in range(3):
                cs = slice(pair * 128, pair * 128 + 128)
                qi = q[i, :, cs] * jnp.asarray(HD**-0.5, BF)
                both = jnp.concatenate(
                    [jnp.where(lane < HD, qi, zero), jnp.where(lane < HD, zero, qi)], 0
                )
                k_all = k[0 : i + 1, :, cs].reshape(keys, 128)
                v_all = v[0 : i + 1, :, cs].reshape(keys, 128)
                s = mm(both, k_all, NT)
                last = jnp.where(causal, s[:, i * RB :], MASKED)
                s = jnp.concatenate([s[:, : i * RB], last], 1) if i else last
                peak = jnp.max(s, axis=1, keepdims=True)
                e = jnp.exp(s - peak).astype(BF)
                ol = mm(e, jnp.concatenate([v_all, jnp.ones((keys, 128), BF)], 1), NN)
                total = ol[:, 128:]
                o = ol[:, :128] / total
                att[i, :, cs] = jnp.where(lane < HD, o[:RB], o[RB:]).astype(BF)
                ls = peak + jnp.log(total)
                ls = jnp.concatenate([ls[:RB], ls[RB:]], 1).T
                lse[pair, 0:1, i * RB : (i + 1) * RB] = ls[0:1]
                lse[pair, 1:2, i * RB : (i + 1) * RB] = ls[128:129]
            if i == 3:
                saves[0].wait()
            copy = push(att.at[i], own.at[i // 2, core], asem, i // 2, partner)

            @pl.when(core == i % 2)
            def _():
                own[i // 2, core] = att[i]

            @pl.when(core != i % 2)
            def _():
                copy.start()

            if i in (2, 1):
                att_send.append(copy)
        save_att = pltpu.make_async_copy(att, st_att.at[p], ssem.at[1])
        save_lse = pltpu.make_async_copy(lse, st_lse.at[p], ssem.at[5])
        save_att.start()
        save_lse.start()
        for j, copy in ((1, att_send[0]), (0, att_send[1])):
            copy.wait()
            out = mm(own[j, 0], wp[0:HALF, :], NN) + mm(own[j, 1], wp[HALF:, :], NN)
            m = h[j] + out + b_proj[...]
            mid[j] = m
            diff, inv = center(m)
            norm2[j] = (diff * inv * ln2_gain[...] + ln2_shift[...]).astype(BF)
        save_rest = [
            pltpu.make_async_copy(own, st_own.at[p], ssem.at[6]),
            pltpu.make_async_copy(mid, st_mid.at[p], ssem.at[7]),
            pltpu.make_async_copy(norm2, st_norm2.at[p], ssem.at[8]),
        ]
        for save in save_rest:
            save.start()
        x = norm2[...].reshape(2 * RB, WIDE)
        for t in range(3):
            cs = slice(t * 1024, (t + 1) * 1024)
            z = mm(x, wf[:, cs], NN) + b_fc[:, cs]
            value, slope = gelu_and_slope(z)
            act[:, cs] = value.astype(BF)
            pre[:, cs] = slope.astype(BF)
        save_ffn = [
            pltpu.make_async_copy(pre, st_pre.at[p], ssem.at[9]),
            pltpu.make_async_copy(act, st_act.at[p], ssem.at[10]),
        ]
        for save in save_ffn:
            save.start()
        out = mm(act[...], wo[...], NN)
        active = is_active(p)
        save_h.wait()
        for j in range(2):
            new = mid[j] + out[j * RB : (j + 1) * RB] + b_out[...]
            h[j] = jnp.where(active, new, h[j])
        for save in saves[1:] + [save_att, save_lse] + save_rest + save_ffn:
            save.wait()
        return carry

    lax.fori_loop(0, MAXP, forward_pass_step, 0)
    for j in range(2):
        tok[j] = h[j].astype(BF)
    mixed_keep = pltpu.make_async_copy(tok.at[chip], mixed.at[chip], wsem.at[7])
    mixed_give = push(tok.at[1 - chip], mixed.at[chip], ysem, 2, across)
    mixed_keep.start()
    mixed_give.start()

    def fetch(p):
        return {
            "pre": pltpu.make_async_copy(st_pre.at[p], pre, lsem.at[0]),
            "mid": pltpu.make_async_copy(st_mid.at[p], mid, lsem.at[1]),
            "q": pltpu.make_async_copy(st_q.at[p], q, lsem.at[2]),
            "k": pltpu.make_async_copy(st_k.at[p], k, lsem.at[3]),
            "v": pltpu.make_async_copy(st_v.at[p], v, lsem.at[4]),
            "att": pltpu.make_async_copy(st_att.at[p], att, lsem.at[5]),
            "lse": pltpu.make_async_copy(st_lse.at[p], lse, lsem.at[6]),
            "h": pltpu.make_async_copy(st_h.at[p], h, lsem.at[7]),
        }

    fetch(MAXP - 1)["h"].start()
    og_keep.wait()
    og_give.wait()
    sums[...] = jnp.zeros_like(sums)
    for j in range(2):
        pos = (2 * j + core) * RB + lax.broadcasted_iota(jnp.int32, (RB, WIDE), 0)
        g[j] = jnp.where(pos < length, glow[j].astype(F32), 0.0)

    def backward_pass_step(step, carry):
        p = MAXP - 1 - step
        here = fetch(p)
        ahead = fetch(jnp.maximum(p - 1, 0))

        def arrive(*names):
            @pl.when(step > 0)
            def _():
                for name in names:
                    here[name].wait()

        def prefetch(*names):
            @pl.when(p > 0)
            def _():
                for name in names:
                    ahead[name].start()

        active = is_active(p)
        for j in range(2):
            glow[j] = jnp.where(active, g[j], 0.0).astype(BF)
        save_e = pltpu.make_async_copy(glow, st_e.at[p], bsem.at[0])
        save_e.start()
        e = glow[...].reshape(2 * RB, WIDE)
        arrive("pre")
        for t in range(3):
            cs = slice(t * 1024, (t + 1) * 1024)
            dact = mm(e, wo[cs, :], NT)
            act[:, cs] = (dact * pre[:, cs].astype(F32)).astype(BF)
        prefetch("pre")
        save_dpre = pltpu.make_async_copy(act, st_dpre.at[p], bsem.at[1])
        save_dpre.start()
        dnorm2 = mm(act[...], wf[...], NT)
        arrive("mid")
        for j in range(2):
            d = dnorm2[j * RB : (j + 1) * RB]
            dv_in, dgain, dshift = norm_back(mid[j], d, ln2_gain[...])
            sums[3:4] += dgain
            sums[4:5] += dshift
            dm = jnp.where(active, g[j], 0.0) + dv_in
            dmid[j] = dm
            low = dm.astype(BF)
            norm2[j] = low
        prefetch("mid")
        save_f = pltpu.make_async_copy(norm2, st_f.at[p], bsem.at[2])
        save_f.start()
        da = mm(norm2[...].reshape(2 * RB, WIDE), wp[...], NT).astype(BF)
        for half in range(2):
            for j in range(2):
                own[half, j] = da[j * RB : (j + 1) * RB, half * HALF : (half + 1) * HALF]
        datt_send = []
        for j in range(2):
            copy = push(
                own.at[1 - core, j], datt_in.at[2 * j + core], dsem, j, partner
            )
            copy.start()
            datt_send.append(copy)
            datt_in[2 * j + core] = own[core, j]
        arrive("q", "k", "v", "att", "lse")
        for copy in datt_send:
            copy.wait()
        lane = lax.broadcasted_iota(jnp.int32, (RB, 128), 1)
        zero = jnp.zeros((RB, 128), BF)
        col = lax.broadcasted_iota(jnp.int32, (RB, 2 * RB), 1) & (RB - 1)
        causal = lax.broadcasted_iota(jnp.int32, (RB, 2 * RB), 0) <= col
        sub = lax.broadcasted_iota(jnp.int32, (128, LEN), 0)
        zero_t = jnp.zeros((128, LEN), BF)
        scale = jnp.asarray(HD**-0.5, BF)

        def split(rows):
            return jnp.concatenate(
                [jnp.where(lane < HD, rows, zero), jnp.where(lane < HD, zero, rows)], 0
            )

        for pair in range(3):
            cs = slice(pair * 128, pair * 128 + 128)
            slot = pair % 2
            k_t = k[:, :, cs].reshape(LEN, 128).T
            k_low = jnp.where(sub < HD, k_t, zero_t)
            k_high = jnp.where(sub < HD, zero_t, k_t)
            for i in (3, 2, 1, 0):
                keys = (i + 1) * RB
                rs = slice(i * RB, (i + 1) * RB)
                qm = split(q[i, :, cs] * scale)
                do = datt_in[i, :, cs]
                dm = split(do)
                inner = (do.astype(F32) * att[i, :, cs].astype(F32)).T
                inner = jnp.concatenate([col_sum(inner[:HD]), col_sum(inner[HD:])], 1)
                total = jnp.concatenate([lse[pair, 0:1, rs], lse[pair, 1:2, rs]], 1)
                s = mm(k[0 : i + 1, :, cs].reshape(keys, 128), qm, NT)
                dp = mm(v[0 : i + 1, :, cs].reshape(keys, 128), dm, NT)
                last = jnp.where(causal, s[i * RB :], MASKED)
                s = jnp.concatenate([s[: i * RB], last], 0) if i else last
                prob = jnp.exp(s - total)
                ds = (prob * (dp - inner)).astype(BF)
                dv = mm(prob.astype(BF), dm, NN)
                dk = mm(ds, qm, NN)
                if i == 3:
                    dv_acc[slot] = dv
                    dk_acc[slot] = dk
                else:
                    dv_acc[slot, 0:keys] += dv
                    dk_acc[slot, 0:keys] += dk
                dq = mm(k_low[:, :keys], ds[:, :RB], NN) + mm(k_high[:, :keys], ds[:, RB:], NN)
                dfused[i, :, cs] = (dq.T * HD**-0.5).astype(BF)
            ks = slice(HALF + pair * 128, HALF + pair * 128 + 128)
            vs = slice(2 * HALF + pair * 128, 2 * HALF + pair * 128 + 128)
            dfused[:, :, ks] = dk_acc[slot].astype(BF).reshape(4, RB, 128)
            dfused[:, :, vs] = dv_acc[slot].astype(BF).reshape(4, RB, 128)
        prefetch("q", "k", "v", "att", "lse")
        save_d = pltpu.make_async_copy(dfused, st_dfused.at[p], bsem.at[3])
        save_d.start()
        part_send = []
        for j in range(2):
            block = 2 * j + 1 - core
            norm[j] = mm(dfused[block], wq[...], NT).astype(BF)
            copy = push(norm.at[j], norm.at[2 + j], psem, j, partner)
            copy.start()
            part_send.append(copy)
        mine = [mm(dfused[2 * j + core], wq[...], NT) for j in range(2)]
        here["h"].wait()
        save_e.wait()
        for j in range(2):
            part_send[j].wait()
            d = mine[j] + norm[2 + j].astype(F32)
            dv_in, dgain, dshift = norm_back(h[j], d, ln1_gain[...])
            sums[0:1] += dgain
            sums[1:2] += dshift
            g[j] = dmid[j] + dv_in + jnp.where(active, 0.0, g[j])
        prefetch("h")
        save_dpre.wait()
        save_f.wait()
        save_d.wait()
        return carry

    lax.fori_loop(0, MAXP, backward_pass_step, 0)
    sums[6:7] = jnp.where(core == 0, length.astype(F32), jnp.zeros((1, WIDE), F32))
    done = pltpu.make_async_copy(g, g_out, bsem.at[0])
    done.start()
    mixed_keep.wait()
    mixed_give.wait()
    done.wait()


def shape(dims, kind=BF):
    return jax.ShapeDtypeStruct(dims, kind)


def layer_call(*operands):
    vmem = pl.BlockSpec(memory_space=pltpu.VMEM)
    smem = pl.BlockSpec(memory_space=pltpu.SMEM)
    hbm = pl.BlockSpec(memory_space=pl.ANY)
    outs = (
        shape((2, RB, WIDE)),
        shape((MAXP, 4, RB, WIDE)),
        shape((MAXP, 2, 2, RB, HALF)),
        shape((MAXP, 2, RB, WIDE)),
        shape((MAXP, 2 * RB, FF)),
        shape((MAXP, 2, RB, WIDE)),
        shape((MAXP, 2 * RB, FF)),
        shape((MAXP, 2, RB, WIDE)),
        shape((MAXP, 4, RB, 3 * HALF)),
        shape((2, RB, WIDE), F32),
        shape((16, WIDE), F32),
        shape((MAXP, 2, RB, WIDE), F32),
        shape((MAXP, 4, RB, HALF)),
        shape((MAXP, 4, RB, HALF)),
        shape((MAXP, 4, RB, HALF)),
        shape((MAXP, 4, RB, HALF)),
        shape((MAXP, 3, 2, LEN), F32),
        shape((MAXP, 2, RB, WIDE), F32),
        shape((MAXP, 2 * RB, FF)),
    )
    scratch = [
        pltpu.VMEM((WIDE, 3 * HALF), BF),
        pltpu.VMEM((WIDE, WIDE), BF),
        pltpu.VMEM((WIDE, FF), BF),
        pltpu.VMEM((FF, WIDE), BF),
        pltpu.VMEM((2, RB, WIDE), BF),
        pltpu.VMEM((2, RB, WIDE), F32),
        pltpu.VMEM((4, RB, WIDE), BF),
        pltpu.VMEM((4, RB, HALF), BF),
        pltpu.VMEM((4, RB, HALF), BF),
        pltpu.VMEM((4, RB, HALF), BF),
        pltpu.VMEM((4, RB, HALF), BF),
        pltpu.VMEM((2, 2, RB, HALF), BF),
        pltpu.VMEM((3, 2, LEN), F32),
        pltpu.VMEM((2, RB, WIDE), F32),
        pltpu.VMEM((2, RB, WIDE), BF),
        pltpu.VMEM((2 * RB, FF), BF),
        pltpu.VMEM((2 * RB, FF), BF),
        pltpu.VMEM((2, RB, WIDE), F32),
        pltpu.VMEM((2, RB, WIDE), BF),
        pltpu.VMEM((2, RB, WIDE), F32),
        pltpu.VMEM((4, RB, HALF), BF),
        pltpu.VMEM((4, RB, 3 * HALF), BF),
        pltpu.VMEM((2, LEN, 128), F32),
        pltpu.VMEM((2, LEN, 128), F32),
        pltpu.VMEM((8, WIDE), F32),
        pltpu.VMEM((1, FF), F32),
        pltpu.SemaphoreType.DMA((8,)),
        pltpu.SemaphoreType.DMA((11,)),
        pltpu.SemaphoreType.DMA((8,)),
        pltpu.SemaphoreType.DMA((4,)),
        pltpu.SemaphoreType.DMA((2, 2)),
        pltpu.SemaphoreType.DMA((2, 2)),
        pltpu.SemaphoreType.DMA((2, 2)),
        pltpu.SemaphoreType.DMA((2, 2)),
        pltpu.SemaphoreType.DMA((2, 3)),
    ]
    return pl.pallas_call(
        layer_kernel,
        out_shape=outs,
        in_specs=[hbm] * 2 + [smem] * 2 + [vmem] * 9 + [hbm] * 4,
        out_specs=(hbm,) * 10 + (vmem,) + (hbm,) * 8,
        scratch_shapes=scratch,
        compiler_params=pltpu.CompilerParams(
            collective_id=1, has_side_effects=True, vmem_limit_bytes=VMEM_BYTES
        ),
        name="layer",
    )(*operands)


CHUNKS = 6
SIDE = 768
ROUTES = (
    "xyzw", "yxzw", "xyzw", "zyxw", "yxzw", "zwyx", "zyxw", "xyzw", "xyzw", "yxzw", "xzyw",
    "yxzw",
)
ORDER = (
    (0, 0), (1, 0), (2, 0, 0, 0), (2, 0, 1, 0), (0, 1), (1, 1), (2, 1, 0, 0), (2, 1, 1, 0),
    (0, 2), (2, 0, 0, 1), (2, 0, 1, 1), (1, 2), (2, 2, 0, 0), (2, 2, 1, 0), (0, 3), (2, 0, 0, 2),
    (2, 1, 0, 1), (2, 1, 1, 1), (1, 3), (2, 0, 1, 2), (2, 3, 0, 0), (2, 3, 1, 0), (0, 4),
    (2, 2, 0, 1), (2, 2, 1, 1), (1, 4), (2, 0, 0, 3), (2, 1, 0, 2), (2, 0, 1, 3), (2, 4, 0, 0),
    (2, 4, 1, 0), (0, 5), (1, 5), (2, 1, 1, 2), (2, 3, 1, 1), (2, 3, 0, 1), (2, 5, 0, 0),
    (2, 5, 1, 0), (2, 2, 0, 2), (2, 2, 1, 2), (2, 0, 0, 4), (2, 4, 1, 1), (2, 1, 0, 3),
    (2, 0, 1, 4), (2, 4, 0, 1), (2, 3, 1, 2), (2, 2, 0, 3), (2, 1, 1, 3), (2, 0, 0, 5),
    (2, 1, 0, 4), (2, 3, 0, 2), (2, 3, 1, 3), (2, 0, 1, 5), (2, 2, 0, 4), (2, 0, 0, 6),
    (2, 1, 1, 4), (2, 5, 0, 1), (2, 1, 0, 5), (2, 5, 1, 1), (2, 0, 1, 6), (2, 3, 1, 4),
    (2, 4, 1, 2), (2, 2, 1, 3), (2, 2, 0, 5), (2, 3, 0, 3), (2, 1, 1, 5), (2, 4, 0, 2),
    (2, 5, 0, 2), (2, 5, 1, 2), (2, 1, 0, 6), (2, 0, 0, 7), (2, 3, 1, 5), (2, 0, 1, 7),
    (2, 4, 1, 3), (2, 5, 0, 3), (2, 2, 1, 4), (2, 2, 0, 6), (2, 1, 1, 6), (2, 3, 0, 4),
    (2, 1, 0, 7), (2, 4, 0, 3), (2, 5, 1, 3), (2, 3, 1, 6), (2, 0, 0, 8), (2, 4, 1, 4),
    (2, 2, 1, 5), (2, 5, 0, 4), (2, 0, 1, 8), (2, 3, 0, 5), (2, 4, 0, 4), (2, 5, 1, 4),
    (2, 2, 0, 7), (2, 1, 1, 7), (2, 4, 1, 5), (2, 5, 0, 5), (2, 3, 1, 7), (2, 4, 0, 5),
    (2, 2, 1, 6), (2, 5, 1, 5), (2, 1, 0, 8), (2, 3, 0, 6), (2, 1, 1, 8), (2, 4, 1, 6),
    (2, 2, 0, 8), (2, 4, 0, 6), (2, 5, 0, 6), (2, 3, 1, 8), (2, 2, 1, 7), (2, 3, 0, 7),
    (2, 5, 1, 6), (2, 4, 1, 7), (2, 4, 0, 7), (2, 5, 0, 7), (2, 5, 1, 7), (2, 4, 1, 8),
    (2, 2, 1, 8), (2, 4, 0, 8), (2, 5, 1, 8), (2, 3, 0, 8), (2, 5, 0, 8),
)


def mesh_push(src, dst, send, recv, where):
    return pltpu.make_async_remote_copy(
        src_ref=src,
        dst_ref=dst,
        send_sem=send,
        recv_sem=recv,
        device_id=where,
        device_id_type=MESH_ID,
    )


def grad_kernel(
    act,
    e,
    norm2,
    dpre,
    own,
    f,
    norm,
    dfused,
    g,
    vec,
    o_qkv,
    o_proj,
    o_fc,
    o_out,
    o_tok,
    o_vec,
    e_v,
    n2_v,
    own_v,
    f_v,
    norm_v,
    third_v,
    pieces,
    give,
    got,
    work,
    rx,
    tok,
    tok_low,
    vsend,
    vgot,
    lsem,
    psem,
    tsem,
    csem,
    xsem,
    rsem,
    vsem,
    ysem,
    osem,
):
    me = lax.axis_index("seq")
    group = lax.axis_index("grp")
    core = lax.rem(me, 2)
    y = me // 2
    x = lax.rem(group, 2)
    z = group // 2
    other = 1 - core
    to_core = {"seq": me + 1 - 2 * core}
    to_y = {"seq": lax.rem(me + 2, 4)}
    to_x = {"grp": group + 1 - 2 * x}

    def to_z_pair(step):
        low = lax.rem(z // step, 2)
        return {"grp": (z + step - 2 * step * low) * 2 + x}

    def half_cols(owner, part):
        return pl.ds(pl.multiple_of(owner * 2 * SIDE + part * SIDE, 128), SIDE)

    stream = []
    for src in (act, dpre):
        for part in range(2):
            for owner in (other, core):
                stream.append((src, half_cols(owner, part)))

    def load_piece(i):
        src, cols = stream[i]
        return pltpu.make_async_copy(src.at[:, :, cols], pieces.at[i % 3], psem.at[i % 3])

    def load_third(i):
        return pltpu.make_async_copy(
            dfused.at[:, :, :, pl.ds(i * HALF, HALF)], third_v.at[i % 2], tsem.at[i % 2]
        )

    load_e = pltpu.make_async_copy(e, e_v, lsem.at[0])
    load_n2 = pltpu.make_async_copy(norm2, n2_v, lsem.at[1])
    load_own = pltpu.make_async_copy(own, own_v, lsem.at[2])
    load_f = pltpu.make_async_copy(f, f_v, lsem.at[3])
    load_norm = pltpu.make_async_copy(norm, norm_v, lsem.at[4])
    load_g = pltpu.make_async_copy(g, tok, lsem.at[5])
    load_piece(0).start()
    load_e.start()
    load_piece(1).start()
    load_g.start()
    load_piece(2).start()
    load_n2.start()
    load_own.start()
    load_f.start()
    load_norm.start()
    load_third(0).start()
    load_third(1).start()

    sem = pltpu.get_barrier_semaphore()
    partners = [to_core, to_y, to_x, to_z_pair(1), to_z_pair(2)]
    for where in partners:
        pl.semaphore_signal(sem, inc=1, device_id=where, device_id_type=MESH_ID)
    pl.semaphore_wait(sem, len(partners))

    load_g.wait()
    tok_low[...] = tok[...].astype(BF)
    tok_give = mesh_push(tok_low.at[1 - y], o_tok.at[y], ysem.at[0], ysem.at[1], to_y)
    tok_keep = pltpu.make_async_copy(tok_low.at[y], o_tok.at[y], lsem.at[5])
    tok_give.start()
    tok_keep.start()

    vec_to = [to_core, to_x, to_y, to_z_pair(1), to_z_pair(2)]

    def vec_copy(k):
        return mesh_push(vsend.at[k], vgot.at[k], vsem.at[0, k], vsem.at[1, k], vec_to[k])

    vsend[0] = vec[...]

    def vec_row(row, v):
        vsend[0, pl.ds(row, 1), :] = v

    def half_row(row, v):
        blank = jnp.zeros((1, HALF), F32)
        vec_row(
            row,
            jnp.concatenate(
                [jnp.where(core == 0, v, blank), jnp.where(core == 0, blank, v)], 1
            ),
        )

    def vec_step(k):
        vec_copy(k).wait()
        vsend[k + 1] = vsend[k] + vgot[k]
        if k < 4:
            vec_copy(k + 1).start()

    def product(n, owner, place):
        if n < 4:
            i = 2 * n + place
            load_piece(i).wait()
            piece = pieces[i % 3].reshape(MAXP * 2 * RB, SIDE)
            if n < 2:
                if i == 0:
                    load_e.wait()
                    vec_row(5, col_sum(e_v[...].reshape(MAXP * 2 * RB, WIDE).astype(F32)))
                out = mm(piece, e_v[...].reshape(MAXP * 2 * RB, WIDE), TN)
            else:
                if i == 4:
                    load_n2.wait()
                out = mm(n2_v[...].reshape(MAXP * 2 * RB, WIDE), piece, TN)
                vec_row(8 + owner * 2 + n - 2, col_sum(piece.astype(F32)))
            return out
        if place == 0:
            load_own.wait()
            load_f.wait()
            vec_row(2, col_sum(f_v[...].reshape(MAXP * 2 * RB, WIDE).astype(F32)))
        right = f_v[:, :, :, pl.ds(pl.multiple_of(owner * HALF, 128), HALF)]
        right = right.reshape(MAXP * 2 * RB, HALF)
        return jnp.concatenate(
            [mm(own_v[:, :, half].reshape(MAXP * 2 * RB, HALF), right, TN) for half in range(2)], 0
        )

    def after_piece(n, place):
        i = 2 * n + place
        if n < 4 and i + 3 < len(stream):
            load_piece(i + 3).start()

    def core_copy(n):
        width = SIDE if n < 4 else HALF
        return mesh_push(
            give.at[n % 2, :, pl.ds(0, width)],
            got.at[n, :, pl.ds(0, width)],
            csem.at[0, n],
            csem.at[1, n],
            to_core,
        )

    def third(i):
        load_third(i).wait()
        right = third_v[i % 2].reshape(MAXP * LEN, HALF)
        if i != 1:
            half_row(12 if i == 0 else 13, col_sum(right.astype(F32)))
        return mm(norm_v[...].reshape(MAXP * LEN, WIDE), right, TN).astype(BF)

    def theirs(n):
        if n >= 2:
            core_copy(n - 2).wait_send()
        out = product(n, other, 0).astype(BF)
        if n < 4:
            give[n % 2] = out
        else:
            give[n % 2, :, 0:HALF] = out
        core_copy(n).start()
        after_piece(n, 0)

    def ours(n):
        if n < 5:
            out = product(n, core, 1)
            after_piece(n, 1)
            core_copy(n).wait_recv()
            if n < 4:
                out = (out + got[n].astype(F32)).astype(BF)
                work[n, 0] = out[:, :HALF]
                work[n, 1] = out[:, HALF:]
            else:
                work[n, 0] = (out + got[n, :, 0:HALF].astype(F32)).astype(BF)
                load_norm.wait()
                work[n, 1] = third(0)
                load_third(2).start()
        else:
            work[n, 1] = third(2)
            vec_copy(0).start()
            work[n, 0] = third(1)

    def rows(start, size):
        return pl.ds(pl.multiple_of(start, 16), size)

    bits = {"x": x, "y": y, "z": lax.rem(z, 2), "w": z // 2}
    pair_of = {"x": to_x, "y": to_y, "z": to_z_pair(1), "w": to_z_pair(2)}

    def first_row(n, s, k):
        row = 0
        for i, name in enumerate(ROUTES[2 * n + s][:k]):
            row = row + bits[name] * (SIDE >> (i + 1))
        return row

    def received(sub, k):
        size = SIDE >> (k + 1)
        return rx.at[sub, pl.ds(SIDE - 2 * size, size)]

    def step_copies(n, s, k):
        route = ROUTES[2 * n + s]
        sub = 2 * n + s

        def copy(src, dst, where):
            return mesh_push(src, dst, xsem.at[sub, k], rsem.at[sub, k], where)

        if k < 4:
            size = SIDE >> (k + 1)
            row = first_row(n, s, k) + (1 - bits[route[k]]) * size
            return [copy(work.at[n, s, rows(row, size)], received(sub, k), pair_of[route[k]])]
        if n < 2:
            out, start, col = o_out, core * 2 * SIDE + n * SIDE, s * HALF
        elif n < 4:
            out, start, col = o_fc, 0, core * 2 * SIDE + (n - 2) * SIDE + s * HALF
        elif n == 4 and s == 0:
            out, start, col = o_proj, 0, core * HALF
        else:
            out, start, col = o_qkv, 0, (0 if n == 4 else 1 + s) * WIDE + core * HALF
        left = 8 - k
        size = SIDE >> left
        row = first_row(n, s, left)
        dst = out.at[rows(start + row, size), pl.ds(pl.multiple_of(col, 128), HALF)]
        if k == 4:
            src = work.at[n, s, rows(row, size)]
            return [copy(src, dst, pair_of[route[3]]), pltpu.make_async_copy(src, dst, osem.at[sub])]
        return [copy(dst, dst, to_core if k == 8 else pair_of[route[left - 1]])]

    def advance(n, s, k):
        if k > 0:
            for copy in step_copies(n, s, k - 1):
                copy.wait()
        if 0 < k < 5:
            sub = 2 * n + s
            size = SIDE >> k
            here = rows(first_row(n, s, k), size)
            more = rx[sub, pl.ds(SIDE - 2 * size, size)]
            work[n, s, here] = (work[n, s, here].astype(F32) + more.astype(F32)).astype(BF)
        for copy in step_copies(n, s, k):
            copy.start()

    tail = ORDER[ORDER.index((1, 5)) + 1 :]
    vec_steps = [tail[i] for i in (6, 12, 18, 24, 30)]
    for entry in ORDER:
        if entry[0] == 0:
            n = entry[1]
            if n < 5:
                theirs(n)
        elif entry[0] == 1:
            ours(entry[1])
        else:
            advance(*entry[1:])
            if entry in vec_steps:
                vec_step(vec_steps.index(entry))
    total = vsend[5]
    inv = 1.0 / total[6:7]
    o_vec[...] = total * inv
    o_vec[7:8] = inv
    for n in range(CHUNKS):
        for s in range(2):
            for copy in step_copies(n, s, 8):
                copy.wait()
    for n in (3, 4):
        core_copy(n).wait_send()
    tok_give.wait()
    tok_keep.wait()


def grad_call(*operands):
    vmem = pl.BlockSpec(memory_space=pltpu.VMEM)
    hbm = pl.BlockSpec(memory_space=pl.ANY)
    outs = (
        shape((WIDE, 3 * WIDE)),
        shape((WIDE, WIDE)),
        shape((WIDE, FF)),
        shape((FF, WIDE)),
        shape((2, RB, WIDE)),
        shape((16, WIDE), F32),
    )
    scratch = [
        pltpu.VMEM((MAXP, 2, RB, WIDE), BF),
        pltpu.VMEM((MAXP, 2, RB, WIDE), BF),
        pltpu.VMEM((MAXP, 2, 2, RB, HALF), BF),
        pltpu.VMEM((MAXP, 2, RB, WIDE), BF),
        pltpu.VMEM((MAXP, 4, RB, WIDE), BF),
        pltpu.VMEM((2, MAXP, 4, RB, HALF), BF),
        pltpu.VMEM((3, MAXP, 2 * RB, SIDE), BF),
        pltpu.VMEM((2, SIDE, SIDE), BF),
        pltpu.VMEM((5, SIDE, SIDE), BF),
        pltpu.VMEM((CHUNKS, 2, SIDE, HALF), BF),
        pltpu.VMEM((2 * CHUNKS, SIDE - 48, HALF), BF),
        pltpu.VMEM((2, RB, WIDE), F32),
        pltpu.VMEM((2, RB, WIDE), BF),
        pltpu.VMEM((6, 16, WIDE), F32),
        pltpu.VMEM((5, 16, WIDE), F32),
        pltpu.SemaphoreType.DMA((6,)),
        pltpu.SemaphoreType.DMA((3,)),
        pltpu.SemaphoreType.DMA((2,)),
        pltpu.SemaphoreType.DMA((2, 5)),
        pltpu.SemaphoreType.DMA((2 * CHUNKS, 9)),
        pltpu.SemaphoreType.DMA((2 * CHUNKS, 9)),
        pltpu.SemaphoreType.DMA((2, 5)),
        pltpu.SemaphoreType.DMA((2,)),
        pltpu.SemaphoreType.DMA((2 * CHUNKS,)),
    ]
    return pl.pallas_call(
        grad_kernel,
        out_shape=outs,
        in_specs=[hbm] * 9 + [vmem],
        out_specs=(hbm,) * 5 + (vmem,),
        scratch_shapes=scratch,
        compiler_params=pltpu.CompilerParams(
            collective_id=2, has_side_effects=True, vmem_limit_bytes=VMEM_BYTES
        ),
        name="gradients",
    )(*operands)


def finish_kernel(
    vec,
    o_qkv,
    o_proj,
    o_fc,
    o_out,
    o_tok,
    f_tok,
    f_ln1_gain,
    f_ln1_shift,
    f_qkv,
    f_bq,
    f_bv,
    f_proj,
    f_b_proj,
    f_ln2_gain,
    f_ln2_shift,
    f_fc,
    f_b_fc,
    f_out,
    f_b_out,
    in_wide,
    out_wide,
    in_tall,
    out_tall,
    isem,
    osem,
):
    inv = vec[7:8, 0:1]
    jobs = []
    for src, dst, size in ((o_fc, f_fc, 128), (o_qkv, f_qkv, 128), (o_out, f_out, 512), (o_proj, f_proj, 384)):
        total, width = src.shape
        for i in range(total // size):
            part = (slice(i * size, (i + 1) * size), slice(0, width))
            jobs.append((src.at[part], dst.at[part], size, width))
    for i in range(2):
        jobs.append((o_tok.at[i], f_tok.at[i], RB, WIDE))

    def parts(n):
        src, dst, size, width = jobs[n]
        slot = n % 4
        wide = size == 128
        here = (in_wide if wide else in_tall).at[slot, pl.ds(0, size), pl.ds(0, width)]
        there = (out_wide if wide else out_tall).at[slot, pl.ds(0, size), pl.ds(0, width)]
        return here, there, src, dst, slot

    def load(n):
        here, _, src, _, slot = parts(n)
        return pltpu.make_async_copy(src, here, isem.at[slot])

    def store(n):
        _, there, _, dst, slot = parts(n)
        return pltpu.make_async_copy(there, dst, osem.at[slot])

    for n in range(3):
        load(n).start()
    f_ln1_gain[...] = vec[0:1].reshape(WIDE)
    f_ln1_shift[...] = vec[1:2].reshape(WIDE)
    f_b_proj[...] = vec[2:3].reshape(WIDE)
    f_ln2_gain[...] = vec[3:4].reshape(WIDE)
    f_ln2_shift[...] = vec[4:5].reshape(WIDE)
    f_b_out[...] = vec[5:6].reshape(WIDE)
    f_bq[...] = vec[12:13].reshape(WIDE)
    f_bv[...] = vec[13:14].reshape(WIDE)
    f_b_fc[...] = jnp.concatenate([vec[8 + i : 9 + i] for i in range(4)], 1).reshape(FF)
    for n in range(len(jobs)):
        here, there = parts(n)[:2]
        load(n).wait()
        if n >= 4:
            store(n - 4).wait()
        there[...] = here[...].astype(F32) * inv
        store(n).start()
        if n + 3 < len(jobs):
            load(n + 3).start()
    for n in range(len(jobs) - 4, len(jobs)):
        store(n).wait()


def finish_call(*operands):
    vmem = pl.BlockSpec(memory_space=pltpu.VMEM)
    hbm = pl.BlockSpec(memory_space=pl.ANY)
    row = shape((WIDE,), F32)
    outs = (
        shape((2, RB, WIDE), F32),
        row,
        row,
        shape((WIDE, 3 * WIDE), F32),
        row,
        row,
        shape((WIDE, WIDE), F32),
        row,
        row,
        row,
        shape((WIDE, FF), F32),
        shape((FF,), F32),
        shape((FF, WIDE), F32),
        row,
    )
    big = {0, 3, 6, 10, 12}
    return pl.pallas_call(
        finish_kernel,
        out_shape=outs,
        in_specs=[vmem] + [hbm] * 5,
        out_specs=tuple(hbm if i in big else vmem for i in range(len(outs))),
        scratch_shapes=[
            pltpu.VMEM((4, 128, FF), BF),
            pltpu.VMEM((4, 128, FF), F32),
            pltpu.VMEM((4, 512, WIDE), BF),
            pltpu.VMEM((4, 512, WIDE), F32),
            pltpu.SemaphoreType.DMA((4,)),
            pltpu.SemaphoreType.DMA((4,)),
        ],
        compiler_params=pltpu.CompilerParams(vmem_limit_bytes=VMEM_BYTES),
        name="finish",
    )(*operands)


def on_chip(
    tokens,
    out_grad,
    section,
    lengths,
    ln1_gain,
    ln1_shift,
    w_qkv,
    b_query,
    b_value,
    w_proj,
    b_proj,
    ln2_gain,
    ln2_shift,
    w_fc,
    b_fc,
    w_out,
    b_out,
):
    (mixed, norm, own, norm2, act, e, dpre, f, dfused, g, sums, *_) = layer_call(
        tokens,
        out_grad,
        section,
        lengths,
        ln1_gain,
        ln1_shift,
        b_query,
        b_value,
        b_proj,
        ln2_gain,
        ln2_shift,
        b_out,
        b_fc,
        w_qkv,
        w_proj,
        w_fc,
        w_out,
    )
    (g_qkv, g_proj, g_fc, g_out, g_tok, vec) = grad_call(
        act, e, norm2, dpre, own, f, norm, dfused, g, sums
    )
    return (mixed, *finish_call(vec, g_qkv, g_proj, g_fc, g_out, g_tok))


def solution(mesh):
    in_specs = (
        P("grp", "seq", None),
        P("grp", "seq", None),
        P("grp"),
        P("grp"),
        P(),
        P(),
        P(),
        P(),
        P(),
        P(),
        P(),
        P(),
        P(),
        P(),
        P(),
        P(),
        P(),
    )
    out_specs = (
        P("grp", "seq", None),
        P("grp", "seq", None),
        P(),
        P(),
        P(),
        P(),
        P(),
        P(),
        P(),
        P(),
        P(),
        P(),
        P(),
        P(),
        P(),
    )
    chosen = on_chip if (mesh.shape["grp"], mesh.shape["seq"]) == (8, 4) else on_device
    return jax.shard_map(
        chosen, mesh=mesh, in_specs=in_specs, out_specs=out_specs, check_vma=False
    )
```

```python
import jax
import jax.numpy as jnp
from jax import lax
from jax.experimental import pallas as pl
from jax.experimental.pallas import tpu as pltpu
from jax.sharding import PartitionSpec as P

HEADS = 12
HD = 64
MAXP = 3


EPSILON = 1e-05
GELU_COEF = 0.7978845608028654
MASKED = -1e30


def layer_norm(hidden, gain, shift):
    average = jnp.mean(hidden, axis=-1, keepdims=True)
    centered = hidden - average
    variance = jnp.mean(centered * centered, axis=-1, keepdims=True)
    return centered * lax.rsqrt(variance + EPSILON) * gain + shift


def gelu_tanh(pre_act):
    return (
        0.5
        * pre_act
        * (1.0 + jnp.tanh(GELU_COEF * (pre_act + 0.044715 * pre_act * pre_act * pre_act)))
    )


def dense(left, right):
    return jnp.einsum("srk,kn->srn", left, right, preferred_element_type=jnp.float32)


def weight_grad(left, right):
    return jnp.einsum("srk,srn->kn", left, right, preferred_element_type=jnp.float32)


def back_dense(grad_rows, right):
    return jnp.einsum("srn,kn->srk", grad_rows, right, preferred_element_type=jnp.float32)


def row_sums(grad_rows):
    return jnp.sum(grad_rows.astype(jnp.float32), axis=(0, 1))


def causal_scores(query_rows, key_all, row_start):
    sample, row_count, width = query_rows.shape
    key_count = key_all.shape[1]
    q_heads = query_rows.reshape(sample, row_count, HEADS, HD)
    k_heads = key_all.reshape(sample, key_count, HEADS, HD)
    scores = jnp.einsum(
        "srhd,sthd->shrt", q_heads, k_heads, preferred_element_type=jnp.float32
    ) * HD ** (-0.5)
    position = row_start + lax.broadcasted_iota(jnp.int32, (row_count, key_count), 0)
    column = lax.broadcasted_iota(jnp.int32, (row_count, key_count), 1)
    return jnp.where(column <= position, scores, MASKED)


def forward_pass(hidden, params, row_start):
    (
        ln1_gain,
        ln1_shift,
        w_qkv,
        b_query,
        b_value,
        w_proj,
        b_proj,
        ln2_gain,
        ln2_shift,
        w_fc,
        b_fc,
        w_out,
        b_out,
    ) = params
    sample, row_count, width = hidden.shape
    normed_low = layer_norm(hidden, ln1_gain, ln1_shift).astype(jnp.bfloat16)
    bias_row = jnp.concatenate([b_query, jnp.zeros_like(b_query), b_value])
    joined_low = (dense(normed_low, w_qkv) + bias_row).astype(jnp.bfloat16)
    query_rows = joined_low[:, :, :width]
    key_rows = joined_low[:, :, width : 2 * width]
    value_rows = joined_low[:, :, 2 * width :]
    key_all, value_all = (
        lax.all_gather(key_rows, "seq", axis=1, tiled=True),
        lax.all_gather(value_rows, "seq", axis=1, tiled=True),
    )
    scores = causal_scores(query_rows, key_all, row_start)
    row_peak = jnp.max(scores, axis=-1, keepdims=True)
    shifted = jnp.exp(scores - row_peak)
    row_total = jnp.sum(shifted, axis=-1, keepdims=True)
    attn_probs = shifted / row_total
    log_total = row_peak + jnp.log(row_total)
    v_heads = value_all.reshape(sample, value_all.shape[1], HEADS, HD)
    attended = jnp.einsum(
        "shrt,sthd->srhd",
        attn_probs.astype(jnp.bfloat16),
        v_heads,
        preferred_element_type=jnp.float32,
    )
    attended_low = attended.reshape(sample, row_count, width).astype(jnp.bfloat16)
    middle = hidden + dense(attended_low, w_proj) + b_proj
    normed_two = layer_norm(middle, ln2_gain, ln2_shift).astype(jnp.bfloat16)
    pre_act = dense(normed_two, w_fc) + b_fc
    activ_low = gelu_tanh(pre_act).astype(jnp.bfloat16)
    output = middle + dense(activ_low, w_out) + b_out
    kept_keys = (key_rows, value_rows)
    kept = (
        hidden,
        normed_low,
        joined_low,
        kept_keys,
        log_total,
        attended_low,
        middle,
        normed_two,
        pre_act,
        activ_low,
    )
    return (output, kept)


def ffn_back(kept, grad_out, params):
    (
        ln1_gain,
        ln1_shift,
        w_qkv,
        b_query,
        b_value,
        w_proj,
        b_proj,
        ln2_gain,
        ln2_shift,
        w_fc,
        b_fc,
        w_out,
        b_out,
    ) = params
    (
        hidden,
        normed_low,
        joined_low,
        kept_keys,
        log_total,
        attended_low,
        middle,
        normed_two,
        pre_act,
        activ_low,
    ) = kept
    grad_low = grad_out.astype(jnp.bfloat16)
    g_w_out = weight_grad(activ_low, grad_low)
    g_b_out = row_sums(grad_low)
    d_activ = back_dense(grad_low, w_out)
    gelu_pull = jax.vjp(gelu_tanh, pre_act)[1]
    d_pre_low = gelu_pull(d_activ)[0].astype(jnp.bfloat16)
    g_w_fc = weight_grad(normed_two, d_pre_low)
    g_b_fc = row_sums(d_pre_low)
    d_normed_two = back_dense(d_pre_low, w_fc)
    norm_pull = jax.vjp(layer_norm, middle, ln2_gain, ln2_shift)[1]
    d_mid_norm, g_ln2_gain, g_ln2_shift = norm_pull(d_normed_two)
    return ((g_ln2_gain, g_ln2_shift, g_w_fc, g_b_fc, g_w_out, g_b_out), grad_out + d_mid_norm)


def attn_back(kept, d_middle, params, row_start):
    (
        ln1_gain,
        ln1_shift,
        w_qkv,
        b_query,
        b_value,
        w_proj,
        b_proj,
        ln2_gain,
        ln2_shift,
        w_fc,
        b_fc,
        w_out,
        b_out,
    ) = params
    (
        hidden,
        normed_low,
        joined_low,
        kept_keys,
        log_total,
        attended_low,
        middle,
        normed_two,
        pre_act,
        activ_low,
    ) = kept
    sample, row_count, width = hidden.shape
    grad_low = d_middle.astype(jnp.bfloat16)
    g_w_proj = weight_grad(attended_low, grad_low)
    g_b_proj = row_sums(grad_low)
    d_att_low = back_dense(grad_low, w_proj).astype(jnp.bfloat16)
    query_rows = joined_low[:, :, :width]
    key_all, value_all = (
        lax.all_gather(kept_keys[0], "seq", axis=1, tiled=True),
        lax.all_gather(kept_keys[1], "seq", axis=1, tiled=True),
    )
    key_count = key_all.shape[1]
    scores = causal_scores(query_rows, key_all, row_start)
    attn_probs = jnp.exp(scores - log_total)
    probs_low = attn_probs.astype(jnp.bfloat16)
    q_heads = query_rows.reshape(sample, row_count, HEADS, HD)
    k_heads = key_all.reshape(sample, key_count, HEADS, HD)
    v_heads = value_all.reshape(sample, key_count, HEADS, HD)
    do_heads = d_att_low.reshape(sample, row_count, HEADS, HD)
    d_probs = jnp.einsum("srhd,sthd->shrt", do_heads, v_heads, preferred_element_type=jnp.float32)
    inner = jnp.sum(d_probs * attn_probs, axis=-1, keepdims=True)
    d_scores = (attn_probs * (d_probs - inner)).astype(jnp.bfloat16)
    scale = HD ** (-0.5)
    d_query = (
        jnp.einsum(
            "shrt,sthd->srhd", d_scores, k_heads, preferred_element_type=jnp.float32
        ).reshape(sample, row_count, width)
        * scale
    )
    d_key_all = (
        jnp.einsum(
            "shrt,srhd->sthd", d_scores, q_heads, preferred_element_type=jnp.float32
        ).reshape(sample, key_count, width)
        * scale
    )
    d_value_all = jnp.einsum(
        "shrt,srhd->sthd", probs_low, do_heads, preferred_element_type=jnp.float32
    ).reshape(sample, key_count, width)
    d_key, d_value = (
        lax.psum_scatter(
            d_key_all.astype(jnp.bfloat16), "seq", scatter_dimension=1, tiled=True
        ).astype(jnp.float32),
        lax.psum_scatter(
            d_value_all.astype(jnp.bfloat16), "seq", scatter_dimension=1, tiled=True
        ).astype(jnp.float32),
    )
    d_joined_low = jnp.concatenate([d_query, d_key, d_value], axis=-1).astype(jnp.bfloat16)
    g_w_qkv = weight_grad(normed_low, d_joined_low)
    g_b_query = row_sums(d_joined_low[:, :, :width])
    g_b_value = row_sums(d_joined_low[:, :, 2 * width :])
    d_normed = back_dense(d_joined_low, w_qkv)
    norm_pull = jax.vjp(layer_norm, hidden, ln1_gain, ln1_shift)[1]
    d_hidden_norm, g_ln1_gain, g_ln1_shift = norm_pull(d_normed)
    terms = (g_ln1_gain, g_ln1_shift, g_w_qkv, g_b_query, g_b_value, g_w_proj, g_b_proj)
    return (terms, d_middle + d_hidden_norm)


def add_terms(accum, terms):
    if accum is None:
        return terms
    return tuple((left_term + right_term for left_term, right_term in zip(accum, terms)))


def on_device(
    tokens,
    out_grad,
    section,
    lengths,
    ln1_gain,
    ln1_shift,
    w_qkv,
    b_query,
    b_value,
    w_proj,
    b_proj,
    ln2_gain,
    ln2_shift,
    w_fc,
    b_fc,
    w_out,
    b_out,
):
    params = (
        ln1_gain,
        ln1_shift,
        w_qkv,
        b_query,
        b_value,
        w_proj,
        b_proj,
        ln2_gain,
        ln2_shift,
        w_fc,
        b_fc,
        w_out,
        b_out,
    )
    sample, row_count, width = tokens.shape
    row_start = lax.axis_index("seq") * row_count
    passes = 2 * section + 1
    position = row_start + lax.broadcasted_iota(jnp.int32, (sample, row_count), 1)
    valid = (position < lengths[:, None]).astype(jnp.float32)
    local_count = jnp.sum(valid)
    hidden = tokens.astype(jnp.float32)
    kept_all = []
    for pass_index in range(MAXP):
        updated, kept = forward_pass(hidden, params, row_start)
        kept_all.append(kept)
        active = (pass_index < passes)[:, None, None]
        hidden = jnp.where(active, updated, hidden)
    mixed = hidden.astype(jnp.bfloat16)
    grad_rows = out_grad.astype(jnp.float32) * valid[:, :, None]
    ffn_acc = None
    attn_acc = None
    for pass_index in reversed(range(MAXP)):
        active_flag = (pass_index < passes).astype(jnp.float32)[:, None, None]
        layer_grad = grad_rows * active_flag
        ffn_terms, d_middle = ffn_back(kept_all[pass_index], layer_grad, params)
        ffn_acc = add_terms(ffn_acc, ffn_terms)
        attn_terms, d_hidden = attn_back(kept_all[pass_index], d_middle, params, row_start)
        attn_acc = add_terms(attn_acc, attn_terms)
        grad_rows = d_hidden + grad_rows * (1.0 - active_flag)
    summed = lax.psum(
        (
            attn_acc[0],
            attn_acc[1],
            attn_acc[2],
            attn_acc[3],
            attn_acc[4],
            attn_acc[5],
            attn_acc[6],
            ffn_acc[0],
            ffn_acc[1],
            ffn_acc[2],
            ffn_acc[3],
            ffn_acc[4],
            ffn_acc[5],
            local_count,
        ),
        ("grp", "seq"),
    )
    attn_sums = summed[0:7]
    ffn_sums = summed[7:13]
    token_total = summed[13]
    return (
        mixed,
        grad_rows / token_total,
        attn_sums[0] / token_total,
        attn_sums[1] / token_total,
        attn_sums[2] / token_total,
        attn_sums[3] / token_total,
        attn_sums[4] / token_total,
        attn_sums[5] / token_total,
        attn_sums[6] / token_total,
        ffn_sums[0] / token_total,
        ffn_sums[1] / token_total,
        ffn_sums[2] / token_total,
        ffn_sums[3] / token_total,
        ffn_sums[4] / token_total,
        ffn_sums[5] / token_total,
    )


BF = jnp.bfloat16
F32 = jnp.float32
MESH_ID = pl.DeviceIdType.MESH
NT = (((1,), (1,)), ((), ()))
TN = (((0,), (0,)), ((), ()))
NN = (((1,), (0,)), ((), ()))
RB = 256
WIDE = 768
HALF = 384
FF = 3072
LEN = 1024
VMEM_BYTES = 60 * 2**20


def mm(left, right, dims):
    return lax.dot_general(left, right, dims, preferred_element_type=F32)


def col_sum(v):
    return jnp.sum(v, axis=0, keepdims=True)


def center(v):
    mean = jnp.mean(v, axis=1, keepdims=True)
    diff = v - mean
    var = jnp.mean(diff * diff, axis=1, keepdims=True)
    return diff, lax.rsqrt(var + EPSILON)


def barrier(partners):
    sem = pltpu.get_barrier_semaphore()
    for seq_index in partners:
        pl.semaphore_signal(sem, inc=1, device_id={"seq": seq_index}, device_id_type=MESH_ID)
    pl.semaphore_wait(sem, len(partners))


def push(src, dst, sems, slot, seq_index):
    return pltpu.make_async_remote_copy(
        src_ref=src,
        dst_ref=dst,
        send_sem=sems.at[0, slot],
        recv_sem=sems.at[1, slot],
        device_id={"seq": seq_index},
        device_id_type=MESH_ID,
    )


def qkv_columns(core, part):
    return pl.ds(pl.multiple_of(part * WIDE + core * HALF, 128), HALF)


def gelu_and_slope(z):
    square = z * z
    t = jnp.tanh(z * (GELU_COEF + (GELU_COEF * 0.044715) * square))
    half = 0.5 + 0.5 * t
    rate = GELU_COEF + (GELU_COEF * 3 * 0.044715) * square
    return z * half, half + (0.5 * z) * (1.0 - t * t) * rate


def norm_back(v, grad, gain):
    diff, inv = center(v)
    xhat = diff * inv
    qv = grad * gain
    mean = jnp.mean(qv, axis=1, keepdims=True)
    cross = jnp.mean(qv * xhat, axis=1, keepdims=True)
    return inv * (qv - mean - xhat * cross), col_sum(grad * xhat), col_sum(grad)


def layer_kernel(
    tokens,
    out_grad,
    section,
    lengths,
    in_ln1_gain,
    in_ln1_shift,
    in_b_query,
    in_b_value,
    in_b_proj,
    in_ln2_gain,
    in_ln2_shift,
    in_b_out,
    in_b_fc,
    w_qkv,
    w_proj,
    w_fc,
    w_out,
    mixed,
    st_norm,
    st_own,
    st_norm2,
    st_act,
    st_e,
    st_dpre,
    st_f,
    st_dfused,
    g_out,
    dnorm2_out,
    sums,
    st_h,
    st_q,
    st_k,
    st_v,
    st_att,
    st_lse,
    st_mid,
    st_pre,
    wq,
    wp,
    wf,
    wo,
    tok,
    h,
    norm,
    q,
    k,
    v,
    att,
    own,
    lse,
    mid,
    norm2,
    pre,
    act,
    g,
    glow,
    dmid,
    datt_in,
    dfused,
    dk_acc,
    dv_acc,
    rows_in,
    b_fc,
    wsem,
    ssem,
    lsem,
    bsem,
    nsem,
    asem,
    dsem,
    psem,
    ysem,
):
    me = lax.axis_index("seq")
    core = lax.rem(me, 2)
    chip = me // 2
    partner = me + 1 - 2 * core
    across = lax.rem(me + 2, 4)
    half_lanes = pl.ds(pl.multiple_of(core * HALF, 128), HALF)
    passes = jnp.full((1, WIDE), 2 * section[chip] + 1, jnp.int32)
    length = jnp.full((1, WIDE), lengths[chip], jnp.int32)

    def is_active(p):
        return jnp.full((1, WIDE), p, jnp.int32) < passes

    keep = pltpu.make_async_copy(tokens.at[chip], tok.at[chip], wsem.at[6])
    keep.start()
    loads = [
        pltpu.make_async_copy(
            w_qkv.at[:, qkv_columns(core, third)],
            wq.at[:, pl.ds(third * HALF, HALF)],
            wsem.at[third],
        )
        for third in range(3)
    ]
    loads += [
        pltpu.make_async_copy(w_proj, wp, wsem.at[3]),
        pltpu.make_async_copy(w_fc, wf, wsem.at[4]),
        pltpu.make_async_copy(w_out, wo, wsem.at[5]),
    ]
    for load in loads:
        load.start()
    short = (
        in_ln1_gain,
        in_ln1_shift,
        in_b_query,
        in_b_value,
        in_b_proj,
        in_ln2_gain,
        in_ln2_shift,
        in_b_out,
    )
    for i, ref in enumerate(short):
        rows_in[i : i + 1] = ref[...].reshape(1, WIDE)
    b_fc[...] = in_b_fc[...].reshape(1, FF)
    ln1_gain, ln1_shift, b_query, b_value, b_proj, ln2_gain, ln2_shift, b_out = (
        rows_in.at[pl.ds(i, 1)] for i in range(8)
    )
    barrier((partner, across))
    give = push(tokens.at[1 - chip], tok.at[chip], ysem, 0, across)
    give.start()
    keep.wait()
    give.wait()
    og_keep = pltpu.make_async_copy(out_grad.at[chip], glow.at[chip], wsem.at[6])
    og_give = push(out_grad.at[1 - chip], glow.at[chip], ysem, 1, across)
    og_keep.start()
    og_give.start()
    for j in range(2):
        h[j] = tok[j].astype(F32)
    for load in loads:
        load.wait()

    def forward_pass_step(p, carry):
        norm_send = []
        for j in range(2):
            diff, inv = center(h[j])
            norm[2 * j + core] = (diff * inv * ln1_gain[...] + ln1_shift[...]).astype(BF)
            copy = push(norm.at[2 * j + core], norm.at[2 * j + core], nsem, j, partner)
            copy.start()
            norm_send.append(copy)
        save_h = pltpu.make_async_copy(h, st_h.at[p], ssem.at[0])
        save_h.start()

        def project(block):
            rows = norm[block]
            out = mm(rows, wq[...], NN)
            q[block] = (out[:, :HALF] + b_query[:, half_lanes]).astype(BF)
            k[block] = out[:, HALF : 2 * HALF].astype(BF)
            v[block] = (out[:, 2 * HALF :] + b_value[:, half_lanes]).astype(BF)

        for j in range(2):
            project(2 * j + core)
        for j in range(2):
            norm_send[j].wait()
            project(2 * j + 1 - core)
        saves = [
            pltpu.make_async_copy(norm, st_norm.at[p], ssem.at[1]),
            pltpu.make_async_copy(q, st_q.at[p], ssem.at[2]),
            pltpu.make_async_copy(k, st_k.at[p], ssem.at[3]),
            pltpu.make_async_copy(v, st_v.at[p], ssem.at[4]),
        ]
        for save in saves:
            save.start()
        lane = lax.broadcasted_iota(jnp.int32, (RB, 128), 1)
        row = lax.broadcasted_iota(jnp.int32, (2 * RB, RB), 0) & (RB - 1)
        causal = lax.broadcasted_iota(jnp.int32, (2 * RB, RB), 1) <= row
        zero = jnp.zeros((RB, 128), BF)
        att_send = []
        for i in (3, 2, 0, 1):
            keys = (i + 1) * RB
            for pair in range(3):
                cs = slice(pair * 128, pair * 128 + 128)
                qi = q[i, :, cs] * jnp.asarray(HD**-0.5, BF)
                both = jnp.concatenate(
                    [jnp.where(lane < HD, qi, zero), jnp.where(lane < HD, zero, qi)], 0
                )
                k_all = k[0 : i + 1, :, cs].reshape(keys, 128)
                v_all = v[0 : i + 1, :, cs].reshape(keys, 128)
                s = mm(both, k_all, NT)
                last = jnp.where(causal, s[:, i * RB :], MASKED)
                s = jnp.concatenate([s[:, : i * RB], last], 1) if i else last
                peak = jnp.max(s, axis=1, keepdims=True)
                e = jnp.exp(s - peak).astype(BF)
                ol = mm(e, jnp.concatenate([v_all, jnp.ones((keys, 128), BF)], 1), NN)
                total = ol[:, 128:]
                o = ol[:, :128] / total
                att[i, :, cs] = jnp.where(lane < HD, o[:RB], o[RB:]).astype(BF)
                ls = peak + jnp.log(total)
                ls = jnp.concatenate([ls[:RB], ls[RB:]], 1).T
                lse[pair, 0:1, i * RB : (i + 1) * RB] = ls[0:1]
                lse[pair, 1:2, i * RB : (i + 1) * RB] = ls[128:129]
            if i == 3:
                saves[0].wait()
            copy = push(att.at[i], own.at[i // 2, core], asem, i // 2, partner)

            @pl.when(core == i % 2)
            def _():
                own[i // 2, core] = att[i]

            @pl.when(core != i % 2)
            def _():
                copy.start()

            if i in (2, 1):
                att_send.append(copy)
        save_att = pltpu.make_async_copy(att, st_att.at[p], ssem.at[1])
        save_lse = pltpu.make_async_copy(lse, st_lse.at[p], ssem.at[5])
        save_att.start()
        save_lse.start()
        for j, copy in ((1, att_send[0]), (0, att_send[1])):
            copy.wait()
            out = mm(own[j, 0], wp[0:HALF, :], NN) + mm(own[j, 1], wp[HALF:, :], NN)
            m = h[j] + out + b_proj[...]
            mid[j] = m
            diff, inv = center(m)
            norm2[j] = (diff * inv * ln2_gain[...] + ln2_shift[...]).astype(BF)
        save_rest = [
            pltpu.make_async_copy(own, st_own.at[p], ssem.at[6]),
            pltpu.make_async_copy(mid, st_mid.at[p], ssem.at[7]),
            pltpu.make_async_copy(norm2, st_norm2.at[p], ssem.at[8]),
        ]
        for save in save_rest:
            save.start()
        x = norm2[...].reshape(2 * RB, WIDE)
        for t in range(3):
            cs = slice(t * 1024, (t + 1) * 1024)
            z = mm(x, wf[:, cs], NN) + b_fc[:, cs]
            value, slope = gelu_and_slope(z)
            act[:, cs] = value.astype(BF)
            pre[:, cs] = slope.astype(BF)
        save_ffn = [
            pltpu.make_async_copy(pre, st_pre.at[p], ssem.at[9]),
            pltpu.make_async_copy(act, st_act.at[p], ssem.at[10]),
        ]
        for save in save_ffn:
            save.start()
        out = mm(act[...], wo[...], NN)
        active = is_active(p)
        save_h.wait()
        for j in range(2):
            new = mid[j] + out[j * RB : (j + 1) * RB] + b_out[...]
            h[j] = jnp.where(active, new, h[j])
        for save in saves[1:] + [save_att, save_lse] + save_rest + save_ffn:
            save.wait()
        return carry

    lax.fori_loop(0, MAXP, forward_pass_step, 0)
    for j in range(2):
        tok[j] = h[j].astype(BF)
    mixed_keep = pltpu.make_async_copy(tok.at[chip], mixed.at[chip], wsem.at[7])
    mixed_give = push(tok.at[1 - chip], mixed.at[chip], ysem, 2, across)
    mixed_keep.start()
    mixed_give.start()

    kept = {
        "pre": (st_pre, pre),
        "mid": (st_mid, mid),
        "q": (st_q, q),
        "k": (st_k, k),
        "v": (st_v, v),
        "att": (st_att, att),
        "lse": (st_lse, lse),
        "h": (st_h, h),
    }

    def fetch(p, name):
        src, dst = kept[name]
        return pltpu.make_async_copy(src.at[p], dst, lsem.at[list(kept).index(name)])

    fetch(MAXP - 1, "h").start()
    og_keep.wait()
    og_give.wait()
    sums[...] = jnp.zeros_like(sums)
    for j in range(2):
        pos = (2 * j + core) * RB + lax.broadcasted_iota(jnp.int32, (RB, WIDE), 0)
        g[j] = jnp.where(pos < length, glow[j].astype(F32), 0.0)

    def feed_forward_back(p, active, arrive, prefetch):
        for j in range(2):
            glow[j] = jnp.where(active, g[j], 0.0).astype(BF)
        save_e = pltpu.make_async_copy(glow, st_e.at[p], bsem.at[0])
        save_e.start()
        e = glow[...].reshape(2 * RB, WIDE)
        arrive("pre")
        for t in range(3):
            cs = slice(t * 1024, (t + 1) * 1024)
            dact = mm(e, wo[cs, :], NT)
            act[:, cs] = (dact * pre[:, cs].astype(F32)).astype(BF)
        prefetch("pre")
        save_dpre = pltpu.make_async_copy(act, st_dpre.at[p], bsem.at[1])
        save_dpre.start()
        dnorm2 = mm(act[...], wf[...], NT)
        return save_e, save_dpre, dnorm2

    def backward_pass_step(step, carry):
        p = MAXP - 1 - step

        def arrive(*names):
            @pl.when(step > 0)
            def _():
                for name in names:
                    fetch(p, name).wait()

        def prefetch(*names):
            for name in names:
                if name == "pre":
                    fetch(p - 1, name).start()
                else:

                    @pl.when(p > 1)
                    def _(name=name):
                        fetch(p - 1, name).start()

        active = is_active(p)
        save_e, save_dpre, dnorm2 = feed_forward_back(p, active, arrive, prefetch)
        arrive("mid")
        for j in range(2):
            d = dnorm2[j * RB : (j + 1) * RB]
            dv_in, dgain, dshift = norm_back(mid[j], d, ln2_gain[...])
            sums[3:4] += dgain
            sums[4:5] += dshift
            dm = jnp.where(active, g[j], 0.0) + dv_in
            dmid[j] = dm
            low = dm.astype(BF)
            norm2[j] = low
        prefetch("mid")
        save_f = pltpu.make_async_copy(norm2, st_f.at[p - 1], bsem.at[2])
        save_f.start()
        da = mm(norm2[...].reshape(2 * RB, WIDE), wp[...], NT).astype(BF)
        for half in range(2):
            for j in range(2):
                own[half, j] = da[j * RB : (j + 1) * RB, half * HALF : (half + 1) * HALF]
        datt_send = []
        for j in range(2):
            copy = push(
                own.at[1 - core, j], datt_in.at[2 * j + core], dsem, j, partner
            )
            copy.start()
            datt_send.append(copy)
            datt_in[2 * j + core] = own[core, j]
        arrive("q", "k", "v", "att", "lse")
        for copy in datt_send:
            copy.wait()
        lane = lax.broadcasted_iota(jnp.int32, (RB, 128), 1)
        zero = jnp.zeros((RB, 128), BF)
        col = lax.broadcasted_iota(jnp.int32, (RB, 2 * RB), 1) & (RB - 1)
        causal = lax.broadcasted_iota(jnp.int32, (RB, 2 * RB), 0) <= col
        sub = lax.broadcasted_iota(jnp.int32, (128, LEN), 0)
        zero_t = jnp.zeros((128, LEN), BF)
        scale = jnp.asarray(HD**-0.5, BF)

        def split(rows):
            return jnp.concatenate(
                [jnp.where(lane < HD, rows, zero), jnp.where(lane < HD, zero, rows)], 0
            )

        for pair in range(3):
            cs = slice(pair * 128, pair * 128 + 128)
            slot = pair % 2
            k_t = k[:, :, cs].reshape(LEN, 128).T
            k_low = jnp.where(sub < HD, k_t, zero_t)
            k_high = jnp.where(sub < HD, zero_t, k_t)
            for i in (3, 2, 1, 0):
                keys = (i + 1) * RB
                rs = slice(i * RB, (i + 1) * RB)
                qm = split(q[i, :, cs] * scale)
                do = datt_in[i, :, cs]
                dm = split(do)
                inner = (do.astype(F32) * att[i, :, cs].astype(F32)).T
                inner = jnp.concatenate([col_sum(inner[:HD]), col_sum(inner[HD:])], 1)
                total = jnp.concatenate([lse[pair, 0:1, rs], lse[pair, 1:2, rs]], 1)
                s = mm(k[0 : i + 1, :, cs].reshape(keys, 128), qm, NT)
                dp = mm(v[0 : i + 1, :, cs].reshape(keys, 128), dm, NT)
                last = jnp.where(causal, s[i * RB :], MASKED)
                s = jnp.concatenate([s[: i * RB], last], 0) if i else last
                prob = jnp.exp(s - total)
                ds = (prob * (dp - inner)).astype(BF)
                dv = mm(prob.astype(BF), dm, NN)
                dk = mm(ds, qm, NN)
                if i == 3:
                    dv_acc[slot] = dv
                    dk_acc[slot] = dk
                else:
                    dv_acc[slot, 0:keys] += dv
                    dk_acc[slot, 0:keys] += dk
                dq = mm(k_low[:, :keys], ds[:, :RB], NN) + mm(k_high[:, :keys], ds[:, RB:], NN)
                dfused[i, :, cs] = (dq.T * HD**-0.5).astype(BF)
            ks = slice(HALF + pair * 128, HALF + pair * 128 + 128)
            vs = slice(2 * HALF + pair * 128, 2 * HALF + pair * 128 + 128)
            dfused[:, :, ks] = dk_acc[slot].astype(BF).reshape(4, RB, 128)
            dfused[:, :, vs] = dv_acc[slot].astype(BF).reshape(4, RB, 128)
        prefetch("q", "k", "v", "att", "lse")
        save_d = pltpu.make_async_copy(dfused, st_dfused.at[p - 1], bsem.at[3])
        save_d.start()
        part_send = []
        for j in range(2):
            block = 2 * j + 1 - core
            norm[j] = mm(dfused[block], wq[...], NT).astype(BF)
            copy = push(norm.at[j], norm.at[2 + j], psem, j, partner)
            copy.start()
            part_send.append(copy)
        mine = [mm(dfused[2 * j + core], wq[...], NT) for j in range(2)]
        fetch(p, "h").wait()
        save_e.wait()
        for j in range(2):
            part_send[j].wait()
            d = mine[j] + norm[2 + j].astype(F32)
            dv_in, dgain, dshift = norm_back(h[j], d, ln1_gain[...])
            sums[0:1] += dgain
            sums[1:2] += dshift
            g[j] = dmid[j] + dv_in + jnp.where(active, 0.0, g[j])
        prefetch("h")
        save_dpre.wait()
        save_f.wait()
        save_d.wait()
        return carry

    lax.fori_loop(0, MAXP - 1, backward_pass_step, 0)
    save_e, save_dpre, dnorm2 = feed_forward_back(
        0, is_active(0), lambda name: fetch(0, name).wait(), lambda name: None
    )
    for j in range(2):
        mid[j] = dnorm2[j * RB : (j + 1) * RB]
    sums[6:7] = jnp.where(core == 0, length.astype(F32), jnp.zeros((1, WIDE), F32))
    done = pltpu.make_async_copy(g, g_out, bsem.at[2])
    done.start()
    done_dnorm2 = pltpu.make_async_copy(mid, dnorm2_out, bsem.at[3])
    done_dnorm2.start()
    save_e.wait()
    save_dpre.wait()
    done_dnorm2.wait()
    mixed_keep.wait()
    mixed_give.wait()
    done.wait()


def shape(dims, kind=BF):
    return jax.ShapeDtypeStruct(dims, kind)


def layer_call(*operands):
    vmem = pl.BlockSpec(memory_space=pltpu.VMEM)
    smem = pl.BlockSpec(memory_space=pltpu.SMEM)
    hbm = pl.BlockSpec(memory_space=pl.ANY)
    outs = (
        shape((2, RB, WIDE)),
        shape((MAXP, 4, RB, WIDE)),
        shape((MAXP, 2, 2, RB, HALF)),
        shape((MAXP, 2, RB, WIDE)),
        shape((MAXP, 2 * RB, FF)),
        shape((MAXP, 2, RB, WIDE)),
        shape((MAXP, 2 * RB, FF)),
        shape((MAXP - 1, 2, RB, WIDE)),
        shape((MAXP - 1, 4, RB, 3 * HALF)),
        shape((2, RB, WIDE), F32),
        shape((2, RB, WIDE), F32),
        shape((16, WIDE), F32),
        shape((MAXP, 2, RB, WIDE), F32),
        shape((MAXP, 4, RB, HALF)),
        shape((MAXP, 4, RB, HALF)),
        shape((MAXP, 4, RB, HALF)),
        shape((MAXP, 4, RB, HALF)),
        shape((MAXP, 3, 2, LEN), F32),
        shape((MAXP, 2, RB, WIDE), F32),
        shape((MAXP, 2 * RB, FF)),
    )
    scratch = [
        pltpu.VMEM((WIDE, 3 * HALF), BF),
        pltpu.VMEM((WIDE, WIDE), BF),
        pltpu.VMEM((WIDE, FF), BF),
        pltpu.VMEM((FF, WIDE), BF),
        pltpu.VMEM((2, RB, WIDE), BF),
        pltpu.VMEM((2, RB, WIDE), F32),
        pltpu.VMEM((4, RB, WIDE), BF),
        pltpu.VMEM((4, RB, HALF), BF),
        pltpu.VMEM((4, RB, HALF), BF),
        pltpu.VMEM((4, RB, HALF), BF),
        pltpu.VMEM((4, RB, HALF), BF),
        pltpu.VMEM((2, 2, RB, HALF), BF),
        pltpu.VMEM((3, 2, LEN), F32),
        pltpu.VMEM((2, RB, WIDE), F32),
        pltpu.VMEM((2, RB, WIDE), BF),
        pltpu.VMEM((2 * RB, FF), BF),
        pltpu.VMEM((2 * RB, FF), BF),
        pltpu.VMEM((2, RB, WIDE), F32),
        pltpu.VMEM((2, RB, WIDE), BF),
        pltpu.VMEM((2, RB, WIDE), F32),
        pltpu.VMEM((4, RB, HALF), BF),
        pltpu.VMEM((4, RB, 3 * HALF), BF),
        pltpu.VMEM((2, LEN, 128), F32),
        pltpu.VMEM((2, LEN, 128), F32),
        pltpu.VMEM((8, WIDE), F32),
        pltpu.VMEM((1, FF), F32),
        pltpu.SemaphoreType.DMA((8,)),
        pltpu.SemaphoreType.DMA((11,)),
        pltpu.SemaphoreType.DMA((8,)),
        pltpu.SemaphoreType.DMA((4,)),
        pltpu.SemaphoreType.DMA((2, 2)),
        pltpu.SemaphoreType.DMA((2, 2)),
        pltpu.SemaphoreType.DMA((2, 2)),
        pltpu.SemaphoreType.DMA((2, 2)),
        pltpu.SemaphoreType.DMA((2, 3)),
    ]
    return pl.pallas_call(
        layer_kernel,
        out_shape=outs,
        in_specs=[hbm] * 2 + [smem] * 2 + [vmem] * 9 + [hbm] * 4,
        out_specs=(hbm,) * 11 + (vmem,) + (hbm,) * 8,
        scratch_shapes=scratch,
        compiler_params=pltpu.CompilerParams(
            collective_id=1, has_side_effects=True, vmem_limit_bytes=VMEM_BYTES
        ),
        name="layer",
    )(*operands)


CHUNKS = 6
SIDE = 768
ROUTES = (
    "xyzw", "yxzw", "xzwy", "yxzw", "yxzw", "xyzw", "yzwx", "xzwy", "zyxw", "xyzw", "yxzw",
    "xzyw",
)
ORDER = (
    ("P", 0), ("O", 0), ("S", 0, 0, 0), ("S", 0, 1, 0), ("L",), ("P", 1), ("A", 0),
    ("S", 0, 0, 1), ("S", 0, 1, 1), ("O", 1), ("S", 1, 0, 0), ("S", 1, 1, 0), ("P", 2),
    ("S", 0, 0, 2), ("S", 0, 1, 2), ("O", 2), ("S", 2, 0, 0), ("S", 2, 1, 0), ("S", 0, 0, 3),
    ("P", 3), ("S", 0, 1, 3), ("S", 1, 1, 1), ("S", 1, 0, 1), ("A", 1), ("S", 0, 0, 4),
    ("S", 0, 1, 4), ("S", 2, 0, 1), ("S", 2, 1, 1), ("S", 1, 0, 2), ("O", 3), ("S", 1, 1, 2),
    ("S", 3, 0, 0), ("S", 3, 1, 0), ("S", 0, 0, 5), ("A", 2), ("S", 0, 1, 5), ("S", 2, 1, 2),
    ("S", 2, 0, 2), ("S", 1, 1, 3), ("S", 1, 0, 3), ("S", 0, 0, 6), ("D",), ("S", 3, 0, 1),
    ("S", 3, 1, 1), ("S", 0, 1, 6), ("S", 1, 0, 4), ("P", 4), ("S", 2, 1, 3), ("N",),
    ("S", 2, 0, 3), ("S", 0, 0, 7), ("S", 1, 1, 4), ("S", 1, 0, 5), ("S", 0, 1, 7),
    ("S", 3, 0, 2), ("O", 4), ("S", 3, 1, 2), ("S", 4, 0, 0), ("S", 4, 1, 0), ("S", 2, 1, 4),
    ("S", 2, 0, 4), ("S", 1, 1, 5), ("O", 5), ("S", 0, 0, 8), ("S", 1, 0, 6), ("S", 5, 0, 0),
    ("S", 5, 1, 0), ("S", 3, 0, 3), ("S", 4, 1, 1), ("S", 3, 1, 3), ("S", 0, 1, 8),
    ("S", 4, 0, 1), ("S", 2, 1, 5), ("S", 2, 0, 5), ("S", 1, 1, 6), ("S", 5, 1, 1),
    ("S", 3, 0, 4), ("S", 5, 0, 1), ("S", 1, 0, 7), ("S", 2, 1, 6), ("S", 4, 1, 2),
    ("S", 1, 1, 7), ("S", 3, 1, 4), ("S", 2, 0, 6), ("S", 3, 0, 5), ("S", 4, 0, 2),
    ("S", 5, 1, 2), ("S", 5, 0, 2), ("S", 4, 1, 3), ("S", 2, 1, 7), ("S", 3, 0, 6),
    ("S", 5, 0, 3), ("S", 4, 1, 4), ("S", 1, 0, 8), ("S", 3, 0, 7), ("S", 1, 1, 8),
    ("S", 2, 0, 7), ("S", 3, 1, 5), ("S", 5, 0, 4), ("S", 4, 0, 3), ("S", 4, 1, 5),
    ("S", 5, 1, 3), ("S", 3, 1, 6), ("S", 4, 1, 6), ("S", 2, 1, 8), ("S", 5, 0, 5),
    ("S", 3, 0, 8), ("S", 4, 0, 4), ("S", 5, 1, 4), ("S", 3, 1, 7), ("S", 5, 0, 6),
    ("S", 2, 0, 8), ("S", 4, 0, 5), ("S", 5, 1, 5), ("S", 4, 1, 7), ("S", 5, 1, 6),
    ("S", 3, 1, 8), ("S", 5, 0, 7), ("S", 5, 1, 7), ("S", 4, 0, 6), ("S", 4, 1, 8),
    ("S", 5, 0, 8), ("S", 4, 0, 7), ("S", 5, 1, 8), ("S", 4, 0, 8),
)


def mesh_push(src, dst, send, recv, where):
    return pltpu.make_async_remote_copy(
        src_ref=src,
        dst_ref=dst,
        send_sem=send,
        recv_sem=recv,
        device_id=where,
        device_id_type=MESH_ID,
    )


def grad_kernel(
    act,
    e,
    norm2,
    dpre,
    own,
    f,
    norm,
    dfused_st,
    st_q,
    st_k,
    st_v,
    st_att,
    st_lse,
    st_mid,
    st_h,
    g_in,
    dnorm2_in,
    w_qkv,
    w_proj,
    section,
    ln1_gain,
    ln2_gain,
    vec,
    o_qkv,
    o_proj,
    o_fc,
    o_out,
    o_tok,
    o_vec,
    wq,
    wp,
    q,
    k,
    v,
    att,
    lse,
    mid,
    h,
    g,
    dn2,
    datt,
    datt_in,
    f0,
    dfused,
    dk_acc,
    dv_acc,
    part,
    part_in,
    slots,
    give,
    got,
    work,
    rx,
    tok_low,
    vsend,
    vgot,
    lsem,
    slsem,
    dsem,
    psem,
    csem,
    xsem,
    rsem,
    vsem,
    ysem,
    osem,
):
    me = lax.axis_index("seq")
    group = lax.axis_index("grp")
    core = lax.rem(me, 2)
    y = me // 2
    x = lax.rem(group, 2)
    z = group // 2
    other = 1 - core
    to_core = {"seq": me + 1 - 2 * core}
    to_y = {"seq": lax.rem(me + 2, 4)}
    to_x = {"grp": group + 1 - 2 * x}

    def to_z_pair(step):
        low = lax.rem(z // step, 2)
        return {"grp": (z + step - 2 * step * low) * 2 + x}

    partner = me + 1 - 2 * core
    passes = jnp.full((1, WIDE), 2 * section[y] + 1, jnp.int32)
    active = jnp.full((1, WIDE), 0, jnp.int32) < passes

    kept = {
        "mid": (st_mid.at[0], mid),
        "g": (g_in, g),
        "dnorm2": (dnorm2_in, dn2),
        "wp": (w_proj, wp),
        "q": (st_q.at[0], q),
        "k": (st_k.at[0], k),
        "v": (st_v.at[0], v),
        "att": (st_att.at[0], att),
        "lse": (st_lse.at[0], lse),
        "h": (st_h.at[0], h),
    }
    for third in range(3):
        kept["wq%d" % third] = (
            w_qkv.at[:, qkv_columns(core, third)],
            wq.at[:, pl.ds(third * HALF, HALF)],
        )

    def kept_copy(name):
        src, dst = kept[name]
        return pltpu.make_async_copy(src, dst, lsem.at[list(kept).index(name)])

    def arrive(*names):
        for name in names:
            kept_copy(name).wait()

    def whole(src):
        return [(src.at[p], (p, slice(None))) for p in range(MAXP)]

    def piece(src, owner, i):
        cols = pl.ds(pl.multiple_of(owner * 2 * SIDE + i * SIDE, 128), SIDE)
        return [(src.at[p, :, :, cols], (p, slice(None))) for p in range(MAXP)]

    def own_rows():
        return [
            (own.at[p, :, half], (p, slice(None), slice(None), pl.ds(half * HALF, HALF)))
            for p in range(MAXP)
            for half in range(2)
        ]

    def f_rows():
        return [(f0, (0, slice(None)))] + [(f.at[p - 1], (p, slice(None))) for p in (1, 2)]

    def dfused_at(p, blocks, cols):
        src = dfused if p == 0 else dfused_st.at[p - 1]
        return src.at[blocks, :, cols]

    def dq_rows():
        return [
            (
                dfused_at(p, pl.ds(2 * i, 2), pl.ds(0, HALF)),
                (p, slice(None), slice(None), pl.ds(i * HALF, HALF)),
            )
            for p in range(MAXP)
            for i in range(2)
        ]

    def kv_rows(i):
        return [
            (dfused_at(p, pl.ds(2 * i, 2), pl.ds(HALF, 2 * HALF)), (p, slice(None)))
            for p in range(MAXP)
        ]

    def norm_rows(i):
        return [(norm.at[p, pl.ds(2 * i, 2)], (p, slice(None))) for p in range(MAXP)]

    other = 1 - core
    operands = {
        "e": (0, lambda: whole(e)),
        "act0": (1, lambda: piece(act, other, 0)),
        "act1": (2, lambda: piece(act, core, 0)),
        "act2": (3, lambda: piece(act, other, 1)),
        "act3": (4, lambda: piece(act, core, 1)),
        "norm2": (1, lambda: whole(norm2)),
        "dpre0": (2, lambda: piece(dpre, other, 0)),
        "dpre1": (3, lambda: piece(dpre, core, 0)),
        "dpre2": (0, lambda: piece(dpre, other, 1)),
        "dpre3": (4, lambda: piece(dpre, core, 1)),
        "own": (2, own_rows),
        "f": (3, f_rows),
        "norm_a": (0, lambda: norm_rows(0)),
        "norm_b": (1, lambda: norm_rows(1)),
        "dq": (4, dq_rows),
        "kv_a": (2, lambda: kv_rows(0)),
        "kv_b": (3, lambda: kv_rows(1)),
    }

    def operand_copies(name):
        slot, copies = operands[name]
        return [
            pltpu.make_async_copy(src, slots.at[(slot, *place)], slsem.at[slot, i])
            for i, (src, place) in enumerate(copies())
        ]

    def begin(*names):
        for name in names:
            for copy in operand_copies(name):
                copy.start()

    def ready(name):
        for copy in operand_copies(name):
            copy.wait()

    def operand(name):
        return slots[operands[name][0]].reshape(MAXP * 2 * RB, SIDE)

    begin("e", "act0", "act1")
    for name in ("mid", "g", "dnorm2", "wp"):
        kept_copy(name).start()
    begin("act2", "act3")
    for name in ("q", "k", "v", "att", "lse", "h", "wq0", "wq1", "wq2"):
        kept_copy(name).start()

    sem = pltpu.get_barrier_semaphore()
    partners = [to_core, to_y, to_x, to_z_pair(1), to_z_pair(2)]
    for where in partners:
        pl.semaphore_signal(sem, inc=1, device_id=where, device_id_type=MESH_ID)
    pl.semaphore_wait(sem, len(partners))

    tok_give = mesh_push(tok_low.at[1 - y], o_tok.at[y], ysem.at[0], ysem.at[1], to_y)
    tok_keep = pltpu.make_async_copy(tok_low.at[y], o_tok.at[y], osem.at[2 * CHUNKS])

    def datt_copy(j):
        return push(datt.at[other, j], datt_in.at[2 * j + core], dsem, j, partner)

    def part_copy(j):
        return push(part.at[j], part_in.at[j], psem, j, partner)

    vec_to = [to_core, to_x, to_y, to_z_pair(1), to_z_pair(2)]

    def vec_copy(k):
        return mesh_push(vsend.at[k], vgot.at[k], vsem.at[0, k], vsem.at[1, k], vec_to[k])

    vsend[0] = vec[...]

    def vec_row(row, v):
        vsend[0, pl.ds(row, 1), :] = v

    def half_row(row, v):
        blank = jnp.zeros((1, HALF), F32)
        vec_row(
            row,
            jnp.concatenate(
                [jnp.where(core == 0, v, blank), jnp.where(core == 0, blank, v)], 1
            ),
        )

    def vec_step(k):
        vec_copy(k).wait()
        vsend[k + 1] = vsend[k] + vgot[k]
        if k < 4:
            vec_copy(k + 1).start()

    def product(n, place):
        owner = core if place else other
        name = ("act%d" if n < 2 else "dpre%d") % (2 * (n % 2) + place)
        if n < 2:
            if n == 0 and place == 0:
                ready("e")
                vec_row(5, col_sum(operand("e").astype(F32)))
            ready(name)
            return mm(operand(name), operand("e"), TN)
        if n < 4:
            if n == 2 and place == 0:
                ready("norm2")
            ready(name)
            right = operand(name)
            vec_row(8 + owner * 2 + n - 2, col_sum(right.astype(F32)))
            return mm(operand("norm2"), right, TN)
        if place == 0:
            ready("own")
            ready("f")
            vec_row(2, col_sum(operand("f").astype(F32)))
        cols = pl.ds(pl.multiple_of(owner * HALF, 128), HALF)
        right = slots[operands["f"][0], :, :, :, cols].reshape(MAXP * 2 * RB, HALF)
        return mm(operand("own"), right, TN)

    def core_copy(n):
        width = SIDE if n < 4 else HALF
        return mesh_push(
            give.at[n % 2, :, pl.ds(0, width)],
            got.at[n % 2, :, pl.ds(0, width)],
            csem.at[0, n],
            csem.at[1, n],
            to_core,
        )

    follow = {
        (0, 0): ("norm2",),
        (0, 1): ("dpre0",),
        (1, 0): ("dpre1",),
        (1, 1): ("dpre2", "dpre3"),
        (2, 0): ("own",),
        (2, 1): ("f",),
        (3, 0): ("norm_a",),
        (3, 1): ("norm_b",),
    }

    def theirs(n):
        if n >= 2:
            core_copy(n - 2).wait_send()
        out = product(n, 0).astype(BF)
        if n < 4:
            give[n % 2] = out
        else:
            give[n % 2, :, 0:HALF] = out
        core_copy(n).start()
        begin(*follow.get((n, 0), ()))

    def ours(n):
        if n < 5:
            out = product(n, 1)
            begin(*follow.get((n, 1), ()))
            core_copy(n).wait_recv()
            if n < 4:
                out = (out + got[n % 2].astype(F32)).astype(BF)
                work[n, 0] = out[:, :HALF]
                work[n, 1] = out[:, HALF:]
                return
            work[n, 0] = (out + got[n % 2, :, 0:HALF].astype(F32)).astype(BF)
            begin("kv_a", "kv_b")
            ready("dq")
            ready("norm_a")
            ready("norm_b")
            right = operand("dq")
            half_row(12, col_sum(right[:, :HALF].astype(F32)) + col_sum(right[:, HALF:].astype(F32)))
            out = mm(operand("norm_a"), right[:, :HALF], TN)
            work[n, 1] = (out + mm(operand("norm_b"), right[:, HALF:], TN)).astype(BF)
            return
        ready("kv_a")
        ready("kv_b")
        right_a, right_b = operand("kv_a"), operand("kv_b")
        half_row(13, col_sum(right_a[:, HALF:].astype(F32)) + col_sum(right_b[:, HALF:].astype(F32)))
        vec_copy(0).start()
        out = mm(operand("norm_a"), right_a, TN) + mm(operand("norm_b"), right_b, TN)
        out = out.astype(BF)
        work[n, 0] = out[:, :HALF]
        work[n, 1] = out[:, HALF:]

    def leave():
        arrive("mid", "g", "dnorm2")
        for j in range(2):
            d = dn2[j]
            dv_in, dgain, dshift = norm_back(mid[j], d, ln2_gain[...].reshape(1, WIDE))
            vsend[0, 3:4] += dgain
            vsend[0, 4:5] += dshift
            dm = jnp.where(active, g[j], 0.0) + dv_in
            mid[j] = dm
            low = dm.astype(BF)
            f0[j] = low
        arrive("wp")
        da = mm(f0[...].reshape(2 * RB, WIDE), wp[...], NT).astype(BF)
        for half in range(2):
            for j in range(2):
                datt[half, j] = da[j * RB : (j + 1) * RB, half * HALF : (half + 1) * HALF]
        for j in range(2):
            datt_copy(j).start()
            datt_in[2 * j + core] = datt[core, j]

    def attend_back(pair):
        if pair == 0:
            arrive("q", "k", "v", "att", "lse")
            for j in range(2):
                datt_copy(j).wait()
        lane = lax.broadcasted_iota(jnp.int32, (RB, 128), 1)
        zero = jnp.zeros((RB, 128), BF)
        col = lax.broadcasted_iota(jnp.int32, (RB, 2 * RB), 1) & (RB - 1)
        causal = lax.broadcasted_iota(jnp.int32, (RB, 2 * RB), 0) <= col
        sub = lax.broadcasted_iota(jnp.int32, (128, LEN), 0)
        zero_t = jnp.zeros((128, LEN), BF)
        scale = jnp.asarray(HD**-0.5, BF)

        def split(rows):
            return jnp.concatenate(
                [jnp.where(lane < HD, rows, zero), jnp.where(lane < HD, zero, rows)], 0
            )

        cs = slice(pair * 128, pair * 128 + 128)
        slot = pair % 2
        k_t = k[:, :, cs].reshape(LEN, 128).T
        k_low = jnp.where(sub < HD, k_t, zero_t)
        k_high = jnp.where(sub < HD, zero_t, k_t)
        for i in (3, 2, 1, 0):
            keys = (i + 1) * RB
            rs = slice(i * RB, (i + 1) * RB)
            qm = split(q[i, :, cs] * scale)
            do = datt_in[i, :, cs]
            dm = split(do)
            inner = (do.astype(F32) * att[i, :, cs].astype(F32)).T
            inner = jnp.concatenate([col_sum(inner[:HD]), col_sum(inner[HD:])], 1)
            total = jnp.concatenate([lse[pair, 0:1, rs], lse[pair, 1:2, rs]], 1)
            s = mm(k[0 : i + 1, :, cs].reshape(keys, 128), qm, NT)
            dp = mm(v[0 : i + 1, :, cs].reshape(keys, 128), dm, NT)
            last = jnp.where(causal, s[i * RB :], MASKED)
            s = jnp.concatenate([s[: i * RB], last], 0) if i else last
            prob = jnp.exp(s - total)
            ds = (prob * (dp - inner)).astype(BF)
            dv = mm(prob.astype(BF), dm, NN)
            dk = mm(ds, qm, NN)
            if i == 3:
                dv_acc[slot] = dv
                dk_acc[slot] = dk
            else:
                dv_acc[slot, 0:keys] += dv
                dk_acc[slot, 0:keys] += dk
            dq = mm(k_low[:, :keys], ds[:, :RB], NN) + mm(k_high[:, :keys], ds[:, RB:], NN)
            dfused[i, :, cs] = (dq.T * HD**-0.5).astype(BF)
        ks = slice(HALF + pair * 128, HALF + pair * 128 + 128)
        vs = slice(2 * HALF + pair * 128, 2 * HALF + pair * 128 + 128)
        dfused[:, :, ks] = dk_acc[slot].astype(BF).reshape(4, RB, 128)
        dfused[:, :, vs] = dv_acc[slot].astype(BF).reshape(4, RB, 128)

    def dense_back():
        arrive("wq0", "wq1", "wq2")
        for j in range(2):
            block = 2 * j + 1 - core
            part[j] = mm(dfused[block], wq[...], NT).astype(BF)
            part_copy(j).start()

    def tokens_back():
        mine = [mm(dfused[2 * j + core], wq[...], NT) for j in range(2)]
        arrive("h")
        for j in range(2):
            part_copy(j).wait()
            d = mine[j] + part_in[j].astype(F32)
            dv_in, dgain, dshift = norm_back(h[j], d, ln1_gain[...].reshape(1, WIDE))
            vsend[0, 0:1] += dgain
            vsend[0, 1:2] += dshift
            tok_low[j] = (mid[j] + dv_in + jnp.where(active, 0.0, g[j])).astype(BF)
        tok_give.start()
        tok_keep.start()

    def rows(start, size):
        return pl.ds(pl.multiple_of(start, 16), size)

    bits = {"x": x, "y": y, "z": lax.rem(z, 2), "w": z // 2}
    pair_of = {"x": to_x, "y": to_y, "z": to_z_pair(1), "w": to_z_pair(2)}

    def first_row(n, s, k):
        row = 0
        for i, name in enumerate(ROUTES[2 * n + s][:k]):
            row = row + bits[name] * (SIDE >> (i + 1))
        return row

    def received(sub, k):
        size = SIDE >> (k + 1)
        return rx.at[sub, pl.ds(SIDE - 2 * size, size)]

    def step_copies(n, s, k):
        route = ROUTES[2 * n + s]
        sub = 2 * n + s

        def copy(src, dst, where):
            return mesh_push(src, dst, xsem.at[sub, k], rsem.at[sub, k], where)

        if k < 4:
            size = SIDE >> (k + 1)
            row = first_row(n, s, k) + (1 - bits[route[k]]) * size
            return [copy(work.at[n, s, rows(row, size)], received(sub, k), pair_of[route[k]])]
        if n < 2:
            out, start, col = o_out, core * 2 * SIDE + n * SIDE, s * HALF
        elif n < 4:
            out, start, col = o_fc, 0, core * 2 * SIDE + (n - 2) * SIDE + s * HALF
        elif n == 4 and s == 0:
            out, start, col = o_proj, 0, core * HALF
        else:
            out, start, col = o_qkv, 0, (0 if n == 4 else 1 + s) * WIDE + core * HALF
        left = 8 - k
        size = SIDE >> left
        row = first_row(n, s, left)
        dst = out.at[rows(start + row, size), pl.ds(pl.multiple_of(col, 128), HALF)]
        if k == 4:
            src = work.at[n, s, rows(row, size)]
            return [copy(src, dst, pair_of[route[3]]), pltpu.make_async_copy(src, dst, osem.at[sub])]
        return [copy(dst, dst, to_core if k == 8 else pair_of[route[left - 1]])]

    def advance(n, s, k):
        if k > 0:
            for copy in step_copies(n, s, k - 1):
                copy.wait()
        if 0 < k < 5:
            sub = 2 * n + s
            size = SIDE >> k
            here = rows(first_row(n, s, k), size)
            more = rx[sub, pl.ds(SIDE - 2 * size, size)]
            work[n, s, here] = (work[n, s, here].astype(F32) + more.astype(F32)).astype(BF)
        for copy in step_copies(n, s, k):
            copy.start()

    tail = ORDER[ORDER.index(("O", 5)) + 1 :]
    vec_steps = [tail[i] for i in (4, 8, 12, 16, 20)]
    for entry in ORDER:
        kind, *which = entry
        if kind == "P":
            theirs(*which)
        elif kind == "O":
            ours(*which)
        elif kind == "L":
            leave()
        elif kind == "A":
            attend_back(*which)
        elif kind == "D":
            dense_back()
            begin("dq")
        elif kind == "N":
            tokens_back()
        else:
            advance(*which)
            if entry in vec_steps:
                vec_step(vec_steps.index(entry))
    total = vsend[5]
    inv = 1.0 / total[6:7]
    o_vec[...] = total * inv
    o_vec[7:8] = inv
    for n in range(CHUNKS):
        for s in range(2):
            for copy in step_copies(n, s, 8):
                copy.wait()
    for n in (3, 4):
        core_copy(n).wait_send()
    tok_give.wait()
    tok_keep.wait()


def grad_call(*operands):
    vmem = pl.BlockSpec(memory_space=pltpu.VMEM)
    hbm = pl.BlockSpec(memory_space=pl.ANY)
    outs = (
        shape((WIDE, 3 * WIDE)),
        shape((WIDE, WIDE)),
        shape((WIDE, FF)),
        shape((FF, WIDE)),
        shape((2, RB, WIDE)),
        shape((16, WIDE), F32),
    )
    scratch = [
        pltpu.VMEM((MAXP, 2, RB, WIDE), BF),
        pltpu.VMEM((MAXP, 2, RB, WIDE), BF),
        pltpu.VMEM((MAXP, 2, 2, RB, HALF), BF),
        pltpu.VMEM((MAXP, 2, RB, WIDE), BF),
        pltpu.VMEM((MAXP, 4, RB, WIDE), BF),
        pltpu.VMEM((2, MAXP, 4, RB, HALF), BF),
        pltpu.VMEM((3, MAXP, 2 * RB, SIDE), BF),
        pltpu.VMEM((2, SIDE, SIDE), BF),
        pltpu.VMEM((5, SIDE, SIDE), BF),
        pltpu.VMEM((CHUNKS, 2, SIDE, HALF), BF),
        pltpu.VMEM((2 * CHUNKS, SIDE - 48, HALF), BF),
        pltpu.VMEM((2, RB, WIDE), F32),
        pltpu.VMEM((2, RB, WIDE), BF),
        pltpu.VMEM((6, 16, WIDE), F32),
        pltpu.VMEM((5, 16, WIDE), F32),
        pltpu.SemaphoreType.DMA((6,)),
        pltpu.SemaphoreType.DMA((3,)),
        pltpu.SemaphoreType.DMA((2,)),
        pltpu.SemaphoreType.DMA((2, 5)),
        pltpu.SemaphoreType.DMA((2 * CHUNKS, 9)),
        pltpu.SemaphoreType.DMA((2 * CHUNKS, 9)),
        pltpu.SemaphoreType.DMA((2, 5)),
        pltpu.SemaphoreType.DMA((2,)),
        pltpu.SemaphoreType.DMA((2 * CHUNKS,)),
    ]
    return pl.pallas_call(
        grad_kernel,
        out_shape=outs,
        in_specs=[hbm] * 9 + [vmem],
        out_specs=(hbm,) * 5 + (vmem,),
        scratch_shapes=scratch,
        compiler_params=pltpu.CompilerParams(
            collective_id=2, has_side_effects=True, vmem_limit_bytes=VMEM_BYTES
        ),
        name="gradients",
    )(*operands)


def grad_call(*operands):
    vmem = pl.BlockSpec(memory_space=pltpu.VMEM)
    hbm = pl.BlockSpec(memory_space=pl.ANY)
    outs = (
        shape((WIDE, 3 * WIDE)),
        shape((WIDE, WIDE)),
        shape((WIDE, FF)),
        shape((FF, WIDE)),
        shape((2, RB, WIDE)),
        shape((16, WIDE), F32),
    )
    rows_f32 = pltpu.VMEM((2, RB, WIDE), F32)
    rows_low = pltpu.VMEM((2, RB, WIDE), BF)
    heads = pltpu.VMEM((4, RB, HALF), BF)
    scratch = [
        pltpu.VMEM((WIDE, 3 * HALF), BF),
        pltpu.VMEM((WIDE, WIDE), BF),
        heads,
        heads,
        heads,
        heads,
        pltpu.VMEM((3, 2, LEN), F32),
        rows_f32,
        rows_f32,
        rows_f32,
        rows_f32,
        pltpu.VMEM((2, 2, RB, HALF), BF),
        heads,
        rows_low,
        pltpu.VMEM((4, RB, 3 * HALF), BF),
        pltpu.VMEM((2, LEN, 128), F32),
        pltpu.VMEM((2, LEN, 128), F32),
        rows_low,
        rows_low,
        pltpu.VMEM((5, MAXP, 2, RB, SIDE), BF),
        pltpu.VMEM((2, SIDE, SIDE), BF),
        pltpu.VMEM((2, SIDE, SIDE), BF),
        pltpu.VMEM((CHUNKS, 2, SIDE, HALF), BF),
        pltpu.VMEM((2 * CHUNKS, SIDE - 48, HALF), BF),
        rows_low,
        pltpu.VMEM((6, 16, WIDE), F32),
        pltpu.VMEM((5, 16, WIDE), F32),
        pltpu.SemaphoreType.DMA((13,)),
        pltpu.SemaphoreType.DMA((5, 6)),
        pltpu.SemaphoreType.DMA((2, 2)),
        pltpu.SemaphoreType.DMA((2, 2)),
        pltpu.SemaphoreType.DMA((2, 5)),
        pltpu.SemaphoreType.DMA((2 * CHUNKS, 9)),
        pltpu.SemaphoreType.DMA((2 * CHUNKS, 9)),
        pltpu.SemaphoreType.DMA((2, 5)),
        pltpu.SemaphoreType.DMA((2,)),
        pltpu.SemaphoreType.DMA((2 * CHUNKS + 1,)),
    ]
    return pl.pallas_call(
        grad_kernel,
        out_shape=outs,
        in_specs=[hbm] * 19 + [pl.BlockSpec(memory_space=pltpu.SMEM)] + [vmem] * 3,
        out_specs=(hbm,) * 5 + (vmem,),
        scratch_shapes=scratch,
        compiler_params=pltpu.CompilerParams(
            collective_id=2, has_side_effects=True, vmem_limit_bytes=VMEM_BYTES
        ),
        name="gradients",
    )(*operands)


def finish_kernel(
    vec,
    o_qkv,
    o_proj,
    o_fc,
    o_out,
    o_tok,
    f_tok,
    f_ln1_gain,
    f_ln1_shift,
    f_qkv,
    f_bq,
    f_bv,
    f_proj,
    f_b_proj,
    f_ln2_gain,
    f_ln2_shift,
    f_fc,
    f_b_fc,
    f_out,
    f_b_out,
    in_wide,
    out_wide,
    in_tall,
    out_tall,
    isem,
    osem,
):
    inv = vec[7:8, 0:1]
    jobs = []
    for src, dst, size in ((o_fc, f_fc, 128), (o_qkv, f_qkv, 128), (o_out, f_out, 512), (o_proj, f_proj, 384)):
        total, width = src.shape
        for i in range(total // size):
            part = (slice(i * size, (i + 1) * size), slice(0, width))
            jobs.append((src.at[part], dst.at[part], size, width))
    for i in range(2):
        jobs.append((o_tok.at[i], f_tok.at[i], RB, WIDE))

    def parts(n):
        src, dst, size, width = jobs[n]
        slot = n % 4
        wide = size == 128
        here = (in_wide if wide else in_tall).at[slot, pl.ds(0, size), pl.ds(0, width)]
        there = (out_wide if wide else out_tall).at[slot, pl.ds(0, size), pl.ds(0, width)]
        return here, there, src, dst, slot

    def load(n):
        here, _, src, _, slot = parts(n)
        return pltpu.make_async_copy(src, here, isem.at[slot])

    def store(n):
        _, there, _, dst, slot = parts(n)
        return pltpu.make_async_copy(there, dst, osem.at[slot])

    for n in range(3):
        load(n).start()
    f_ln1_gain[...] = vec[0:1].reshape(WIDE)
    f_ln1_shift[...] = vec[1:2].reshape(WIDE)
    f_b_proj[...] = vec[2:3].reshape(WIDE)
    f_ln2_gain[...] = vec[3:4].reshape(WIDE)
    f_ln2_shift[...] = vec[4:5].reshape(WIDE)
    f_b_out[...] = vec[5:6].reshape(WIDE)
    f_bq[...] = vec[12:13].reshape(WIDE)
    f_bv[...] = vec[13:14].reshape(WIDE)
    f_b_fc[...] = jnp.concatenate([vec[8 + i : 9 + i] for i in range(4)], 1).reshape(FF)
    for n in range(len(jobs)):
        here, there = parts(n)[:2]
        load(n).wait()
        if n >= 4:
            store(n - 4).wait()
        there[...] = here[...].astype(F32) * inv
        store(n).start()
        if n + 3 < len(jobs):
            load(n + 3).start()
    for n in range(len(jobs) - 4, len(jobs)):
        store(n).wait()


def finish_call(*operands):
    vmem = pl.BlockSpec(memory_space=pltpu.VMEM)
    hbm = pl.BlockSpec(memory_space=pl.ANY)
    row = shape((WIDE,), F32)
    outs = (
        shape((2, RB, WIDE), F32),
        row,
        row,
        shape((WIDE, 3 * WIDE), F32),
        row,
        row,
        shape((WIDE, WIDE), F32),
        row,
        row,
        row,
        shape((WIDE, FF), F32),
        shape((FF,), F32),
        shape((FF, WIDE), F32),
        row,
    )
    big = {0, 3, 6, 10, 12}
    return pl.pallas_call(
        finish_kernel,
        out_shape=outs,
        in_specs=[vmem] + [hbm] * 5,
        out_specs=tuple(hbm if i in big else vmem for i in range(len(outs))),
        scratch_shapes=[
            pltpu.VMEM((4, 128, FF), BF),
            pltpu.VMEM((4, 128, FF), F32),
            pltpu.VMEM((4, 512, WIDE), BF),
            pltpu.VMEM((4, 512, WIDE), F32),
            pltpu.SemaphoreType.DMA((4,)),
            pltpu.SemaphoreType.DMA((4,)),
        ],
        compiler_params=pltpu.CompilerParams(vmem_limit_bytes=VMEM_BYTES),
        name="finish",
    )(*operands)


def on_chip(
    tokens,
    out_grad,
    section,
    lengths,
    ln1_gain,
    ln1_shift,
    w_qkv,
    b_query,
    b_value,
    w_proj,
    b_proj,
    ln2_gain,
    ln2_shift,
    w_fc,
    b_fc,
    w_out,
    b_out,
):
    kept = layer_call(
        tokens,
        out_grad,
        section,
        lengths,
        ln1_gain,
        ln1_shift,
        b_query,
        b_value,
        b_proj,
        ln2_gain,
        ln2_shift,
        b_out,
        b_fc,
        w_qkv,
        w_proj,
        w_fc,
        w_out,
    )
    (mixed, norm, own, norm2, act, e, dpre, f, dfused, g, dnorm2, sums, *heads) = kept
    (h, q, k, v, att, lse, mid, _) = heads
    (g_qkv, g_proj, g_fc, g_out, g_tok, vec) = grad_call(
        act.reshape(MAXP, 2, RB, FF),
        e,
        norm2,
        dpre.reshape(MAXP, 2, RB, FF),
        own,
        f,
        norm,
        dfused,
        q,
        k,
        v,
        att,
        lse,
        mid,
        h,
        g,
        dnorm2,
        w_qkv,
        w_proj,
        section,
        ln1_gain,
        ln2_gain,
        sums,
    )
    return (mixed, *finish_call(vec, g_qkv, g_proj, g_fc, g_out, g_tok))


def solution(mesh):
    in_specs = (
        P("grp", "seq", None),
        P("grp", "seq", None),
        P("grp"),
        P("grp"),
        P(),
        P(),
        P(),
        P(),
        P(),
        P(),
        P(),
        P(),
        P(),
        P(),
        P(),
        P(),
        P(),
    )
    out_specs = (
        P("grp", "seq", None),
        P("grp", "seq", None),
        P(),
        P(),
        P(),
        P(),
        P(),
        P(),
        P(),
        P(),
        P(),
        P(),
        P(),
        P(),
        P(),
    )
    chosen = on_chip if (mesh.shape["grp"], mesh.shape["seq"]) == (8, 4) else on_device
    return jax.shard_map(
        chosen, mesh=mesh, in_specs=in_specs, out_specs=out_specs, check_vma=False
    )
```

```python
import jax
import jax.numpy as jnp
from jax import lax
from jax.experimental import pallas as pl
from jax.experimental.pallas import tpu as pltpu
from jax.sharding import PartitionSpec as P

HEADS = 12
HD = 64
MAXP = 3


EPSILON = 1e-05
GELU_COEF = 0.7978845608028654
MASKED = -1e30


def layer_norm(hidden, gain, shift):
    average = jnp.mean(hidden, axis=-1, keepdims=True)
    centered = hidden - average
    variance = jnp.mean(centered * centered, axis=-1, keepdims=True)
    return centered * lax.rsqrt(variance + EPSILON) * gain + shift


def gelu_tanh(pre_act):
    return (
        0.5
        * pre_act
        * (1.0 + jnp.tanh(GELU_COEF * (pre_act + 0.044715 * pre_act * pre_act * pre_act)))
    )


def dense(left, right):
    return jnp.einsum("srk,kn->srn", left, right, preferred_element_type=jnp.float32)


def weight_grad(left, right):
    return jnp.einsum("srk,srn->kn", left, right, preferred_element_type=jnp.float32)


def back_dense(grad_rows, right):
    return jnp.einsum("srn,kn->srk", grad_rows, right, preferred_element_type=jnp.float32)


def row_sums(grad_rows):
    return jnp.sum(grad_rows.astype(jnp.float32), axis=(0, 1))


def causal_scores(query_rows, key_all, row_start):
    sample, row_count, width = query_rows.shape
    key_count = key_all.shape[1]
    q_heads = query_rows.reshape(sample, row_count, HEADS, HD)
    k_heads = key_all.reshape(sample, key_count, HEADS, HD)
    scores = jnp.einsum(
        "srhd,sthd->shrt", q_heads, k_heads, preferred_element_type=jnp.float32
    ) * HD ** (-0.5)
    position = row_start + lax.broadcasted_iota(jnp.int32, (row_count, key_count), 0)
    column = lax.broadcasted_iota(jnp.int32, (row_count, key_count), 1)
    return jnp.where(column <= position, scores, MASKED)


def forward_pass(hidden, params, row_start):
    (
        ln1_gain,
        ln1_shift,
        w_qkv,
        b_query,
        b_value,
        w_proj,
        b_proj,
        ln2_gain,
        ln2_shift,
        w_fc,
        b_fc,
        w_out,
        b_out,
    ) = params
    sample, row_count, width = hidden.shape
    normed_low = layer_norm(hidden, ln1_gain, ln1_shift).astype(jnp.bfloat16)
    bias_row = jnp.concatenate([b_query, jnp.zeros_like(b_query), b_value])
    joined_low = (dense(normed_low, w_qkv) + bias_row).astype(jnp.bfloat16)
    query_rows = joined_low[:, :, :width]
    key_rows = joined_low[:, :, width : 2 * width]
    value_rows = joined_low[:, :, 2 * width :]
    key_all, value_all = (
        lax.all_gather(key_rows, "seq", axis=1, tiled=True),
        lax.all_gather(value_rows, "seq", axis=1, tiled=True),
    )
    scores = causal_scores(query_rows, key_all, row_start)
    row_peak = jnp.max(scores, axis=-1, keepdims=True)
    shifted = jnp.exp(scores - row_peak)
    row_total = jnp.sum(shifted, axis=-1, keepdims=True)
    attn_probs = shifted / row_total
    log_total = row_peak + jnp.log(row_total)
    v_heads = value_all.reshape(sample, value_all.shape[1], HEADS, HD)
    attended = jnp.einsum(
        "shrt,sthd->srhd",
        attn_probs.astype(jnp.bfloat16),
        v_heads,
        preferred_element_type=jnp.float32,
    )
    attended_low = attended.reshape(sample, row_count, width).astype(jnp.bfloat16)
    middle = hidden + dense(attended_low, w_proj) + b_proj
    normed_two = layer_norm(middle, ln2_gain, ln2_shift).astype(jnp.bfloat16)
    pre_act = dense(normed_two, w_fc) + b_fc
    activ_low = gelu_tanh(pre_act).astype(jnp.bfloat16)
    output = middle + dense(activ_low, w_out) + b_out
    kept_keys = (key_rows, value_rows)
    kept = (
        hidden,
        normed_low,
        joined_low,
        kept_keys,
        log_total,
        attended_low,
        middle,
        normed_two,
        pre_act,
        activ_low,
    )
    return (output, kept)


def ffn_back(kept, grad_out, params):
    (
        ln1_gain,
        ln1_shift,
        w_qkv,
        b_query,
        b_value,
        w_proj,
        b_proj,
        ln2_gain,
        ln2_shift,
        w_fc,
        b_fc,
        w_out,
        b_out,
    ) = params
    (
        hidden,
        normed_low,
        joined_low,
        kept_keys,
        log_total,
        attended_low,
        middle,
        normed_two,
        pre_act,
        activ_low,
    ) = kept
    grad_low = grad_out.astype(jnp.bfloat16)
    g_w_out = weight_grad(activ_low, grad_low)
    g_b_out = row_sums(grad_low)
    d_activ = back_dense(grad_low, w_out)
    gelu_pull = jax.vjp(gelu_tanh, pre_act)[1]
    d_pre_low = gelu_pull(d_activ)[0].astype(jnp.bfloat16)
    g_w_fc = weight_grad(normed_two, d_pre_low)
    g_b_fc = row_sums(d_pre_low)
    d_normed_two = back_dense(d_pre_low, w_fc)
    norm_pull = jax.vjp(layer_norm, middle, ln2_gain, ln2_shift)[1]
    d_mid_norm, g_ln2_gain, g_ln2_shift = norm_pull(d_normed_two)
    return ((g_ln2_gain, g_ln2_shift, g_w_fc, g_b_fc, g_w_out, g_b_out), grad_out + d_mid_norm)


def attn_back(kept, d_middle, params, row_start):
    (
        ln1_gain,
        ln1_shift,
        w_qkv,
        b_query,
        b_value,
        w_proj,
        b_proj,
        ln2_gain,
        ln2_shift,
        w_fc,
        b_fc,
        w_out,
        b_out,
    ) = params
    (
        hidden,
        normed_low,
        joined_low,
        kept_keys,
        log_total,
        attended_low,
        middle,
        normed_two,
        pre_act,
        activ_low,
    ) = kept
    sample, row_count, width = hidden.shape
    grad_low = d_middle.astype(jnp.bfloat16)
    g_w_proj = weight_grad(attended_low, grad_low)
    g_b_proj = row_sums(grad_low)
    d_att_low = back_dense(grad_low, w_proj).astype(jnp.bfloat16)
    query_rows = joined_low[:, :, :width]
    key_all, value_all = (
        lax.all_gather(kept_keys[0], "seq", axis=1, tiled=True),
        lax.all_gather(kept_keys[1], "seq", axis=1, tiled=True),
    )
    key_count = key_all.shape[1]
    scores = causal_scores(query_rows, key_all, row_start)
    attn_probs = jnp.exp(scores - log_total)
    probs_low = attn_probs.astype(jnp.bfloat16)
    q_heads = query_rows.reshape(sample, row_count, HEADS, HD)
    k_heads = key_all.reshape(sample, key_count, HEADS, HD)
    v_heads = value_all.reshape(sample, key_count, HEADS, HD)
    do_heads = d_att_low.reshape(sample, row_count, HEADS, HD)
    d_probs = jnp.einsum("srhd,sthd->shrt", do_heads, v_heads, preferred_element_type=jnp.float32)
    inner = jnp.sum(d_probs * attn_probs, axis=-1, keepdims=True)
    d_scores = (attn_probs * (d_probs - inner)).astype(jnp.bfloat16)
    scale = HD ** (-0.5)
    d_query = (
        jnp.einsum(
            "shrt,sthd->srhd", d_scores, k_heads, preferred_element_type=jnp.float32
        ).reshape(sample, row_count, width)
        * scale
    )
    d_key_all = (
        jnp.einsum(
            "shrt,srhd->sthd", d_scores, q_heads, preferred_element_type=jnp.float32
        ).reshape(sample, key_count, width)
        * scale
    )
    d_value_all = jnp.einsum(
        "shrt,srhd->sthd", probs_low, do_heads, preferred_element_type=jnp.float32
    ).reshape(sample, key_count, width)
    d_key, d_value = (
        lax.psum_scatter(
            d_key_all.astype(jnp.bfloat16), "seq", scatter_dimension=1, tiled=True
        ).astype(jnp.float32),
        lax.psum_scatter(
            d_value_all.astype(jnp.bfloat16), "seq", scatter_dimension=1, tiled=True
        ).astype(jnp.float32),
    )
    d_joined_low = jnp.concatenate([d_query, d_key, d_value], axis=-1).astype(jnp.bfloat16)
    g_w_qkv = weight_grad(normed_low, d_joined_low)
    g_b_query = row_sums(d_joined_low[:, :, :width])
    g_b_value = row_sums(d_joined_low[:, :, 2 * width :])
    d_normed = back_dense(d_joined_low, w_qkv)
    norm_pull = jax.vjp(layer_norm, hidden, ln1_gain, ln1_shift)[1]
    d_hidden_norm, g_ln1_gain, g_ln1_shift = norm_pull(d_normed)
    terms = (g_ln1_gain, g_ln1_shift, g_w_qkv, g_b_query, g_b_value, g_w_proj, g_b_proj)
    return (terms, d_middle + d_hidden_norm)


def add_terms(accum, terms):
    if accum is None:
        return terms
    return tuple((left_term + right_term for left_term, right_term in zip(accum, terms)))


def on_device(
    tokens,
    out_grad,
    section,
    lengths,
    ln1_gain,
    ln1_shift,
    w_qkv,
    b_query,
    b_value,
    w_proj,
    b_proj,
    ln2_gain,
    ln2_shift,
    w_fc,
    b_fc,
    w_out,
    b_out,
):
    params = (
        ln1_gain,
        ln1_shift,
        w_qkv,
        b_query,
        b_value,
        w_proj,
        b_proj,
        ln2_gain,
        ln2_shift,
        w_fc,
        b_fc,
        w_out,
        b_out,
    )
    sample, row_count, width = tokens.shape
    row_start = lax.axis_index("seq") * row_count
    passes = 2 * section + 1
    position = row_start + lax.broadcasted_iota(jnp.int32, (sample, row_count), 1)
    valid = (position < lengths[:, None]).astype(jnp.float32)
    local_count = jnp.sum(valid)
    hidden = tokens.astype(jnp.float32)
    kept_all = []
    for pass_index in range(MAXP):
        updated, kept = forward_pass(hidden, params, row_start)
        kept_all.append(kept)
        active = (pass_index < passes)[:, None, None]
        hidden = jnp.where(active, updated, hidden)
    mixed = hidden.astype(jnp.bfloat16)
    grad_rows = out_grad.astype(jnp.float32) * valid[:, :, None]
    ffn_acc = None
    attn_acc = None
    for pass_index in reversed(range(MAXP)):
        active_flag = (pass_index < passes).astype(jnp.float32)[:, None, None]
        layer_grad = grad_rows * active_flag
        ffn_terms, d_middle = ffn_back(kept_all[pass_index], layer_grad, params)
        ffn_acc = add_terms(ffn_acc, ffn_terms)
        attn_terms, d_hidden = attn_back(kept_all[pass_index], d_middle, params, row_start)
        attn_acc = add_terms(attn_acc, attn_terms)
        grad_rows = d_hidden + grad_rows * (1.0 - active_flag)
    summed = lax.psum(
        (
            attn_acc[0],
            attn_acc[1],
            attn_acc[2],
            attn_acc[3],
            attn_acc[4],
            attn_acc[5],
            attn_acc[6],
            ffn_acc[0],
            ffn_acc[1],
            ffn_acc[2],
            ffn_acc[3],
            ffn_acc[4],
            ffn_acc[5],
            local_count,
        ),
        ("grp", "seq"),
    )
    attn_sums = summed[0:7]
    ffn_sums = summed[7:13]
    token_total = summed[13]
    return (
        mixed,
        grad_rows / token_total,
        attn_sums[0] / token_total,
        attn_sums[1] / token_total,
        attn_sums[2] / token_total,
        attn_sums[3] / token_total,
        attn_sums[4] / token_total,
        attn_sums[5] / token_total,
        attn_sums[6] / token_total,
        ffn_sums[0] / token_total,
        ffn_sums[1] / token_total,
        ffn_sums[2] / token_total,
        ffn_sums[3] / token_total,
        ffn_sums[4] / token_total,
        ffn_sums[5] / token_total,
    )


BF = jnp.bfloat16
F32 = jnp.float32
MESH_ID = pl.DeviceIdType.MESH
NT = (((1,), (1,)), ((), ()))
TN = (((0,), (0,)), ((), ()))
NN = (((1,), (0,)), ((), ()))
RB = 256
WIDE = 768
HALF = 384
FF = 3072
LEN = 1024
VMEM_BYTES = 60 * 2**20


def mm(left, right, dims):
    return lax.dot_general(left, right, dims, preferred_element_type=F32)


def col_sum(v):
    return jnp.sum(v, axis=0, keepdims=True)


def center(v):
    mean = jnp.mean(v, axis=1, keepdims=True)
    diff = v - mean
    var = jnp.mean(diff * diff, axis=1, keepdims=True)
    return diff, lax.rsqrt(var + EPSILON)


def barrier(partners):
    sem = pltpu.get_barrier_semaphore()
    for seq_index in partners:
        pl.semaphore_signal(sem, inc=1, device_id={"seq": seq_index}, device_id_type=MESH_ID)
    pl.semaphore_wait(sem, len(partners))


def push(src, dst, sems, slot, seq_index):
    return pltpu.make_async_remote_copy(
        src_ref=src,
        dst_ref=dst,
        send_sem=sems.at[0, slot],
        recv_sem=sems.at[1, slot],
        device_id={"seq": seq_index},
        device_id_type=MESH_ID,
    )


def qkv_columns(core, part):
    return pl.ds(pl.multiple_of(part * WIDE + core * HALF, 128), HALF)


def gelu_and_slope(z):
    square = z * z
    t = jnp.tanh(z * (GELU_COEF + (GELU_COEF * 0.044715) * square))
    half = 0.5 + 0.5 * t
    rate = GELU_COEF + (GELU_COEF * 3 * 0.044715) * square
    return z * half, half + (0.5 * z) * (1.0 - t * t) * rate


def norm_back(v, grad, gain):
    diff, inv = center(v)
    xhat = diff * inv
    qv = grad * gain
    mean = jnp.mean(qv, axis=1, keepdims=True)
    cross = jnp.mean(qv * xhat, axis=1, keepdims=True)
    return inv * (qv - mean - xhat * cross), col_sum(grad * xhat), col_sum(grad)


def layer_kernel(
    tokens,
    out_grad,
    section,
    lengths,
    in_ln1_gain,
    in_ln1_shift,
    in_b_query,
    in_b_value,
    in_b_proj,
    in_ln2_gain,
    in_ln2_shift,
    in_b_out,
    in_b_fc,
    w_qkv,
    w_proj,
    w_fc,
    w_out,
    mixed,
    st_norm,
    st_own,
    st_norm2,
    st_act,
    st_e,
    st_dpre,
    st_f,
    st_dfused,
    g_out,
    dnorm2_out,
    sums,
    st_h,
    st_q,
    st_k,
    st_v,
    st_att,
    st_lse,
    st_mid,
    st_pre,
    wq,
    wp,
    wf,
    wo,
    tok,
    h,
    norm,
    q,
    k,
    v,
    att,
    own,
    lse,
    mid,
    norm2,
    pre,
    act,
    g,
    glow,
    dmid,
    datt_in,
    dfused,
    dk_acc,
    dv_acc,
    rows_in,
    b_fc,
    wsem,
    ssem,
    lsem,
    bsem,
    nsem,
    asem,
    dsem,
    psem,
    ysem,
):
    me = lax.axis_index("seq")
    core = lax.rem(me, 2)
    chip = me // 2
    partner = me + 1 - 2 * core
    across = lax.rem(me + 2, 4)
    half_lanes = pl.ds(pl.multiple_of(core * HALF, 128), HALF)
    passes = jnp.full((1, WIDE), 2 * section[chip] + 1, jnp.int32)
    length = jnp.full((1, WIDE), lengths[chip], jnp.int32)

    def is_active(p):
        return jnp.full((1, WIDE), p, jnp.int32) < passes

    keep = pltpu.make_async_copy(tokens.at[chip], tok.at[chip], wsem.at[6])
    keep.start()
    loads = [
        pltpu.make_async_copy(
            w_qkv.at[:, qkv_columns(core, third)],
            wq.at[:, pl.ds(third * HALF, HALF)],
            wsem.at[third],
        )
        for third in range(3)
    ]
    loads += [
        pltpu.make_async_copy(w_proj, wp, wsem.at[3]),
        pltpu.make_async_copy(w_fc, wf, wsem.at[4]),
        pltpu.make_async_copy(w_out, wo, wsem.at[5]),
    ]
    for load in loads:
        load.start()
    short = (
        in_ln1_gain,
        in_ln1_shift,
        in_b_query,
        in_b_value,
        in_b_proj,
        in_ln2_gain,
        in_ln2_shift,
        in_b_out,
    )
    for i, ref in enumerate(short):
        rows_in[i : i + 1] = ref[...].reshape(1, WIDE)
    b_fc[...] = in_b_fc[...].reshape(1, FF)
    ln1_gain, ln1_shift, b_query, b_value, b_proj, ln2_gain, ln2_shift, b_out = (
        rows_in.at[pl.ds(i, 1)] for i in range(8)
    )
    barrier((partner, across))
    give = push(tokens.at[1 - chip], tok.at[chip], ysem, 0, across)
    give.start()
    keep.wait()
    give.wait()
    og_keep = pltpu.make_async_copy(out_grad.at[chip], glow.at[chip], wsem.at[6])
    og_give = push(out_grad.at[1 - chip], glow.at[chip], ysem, 1, across)
    og_keep.start()
    og_give.start()
    for j in range(2):
        h[j] = tok[j].astype(F32)
    for load in loads:
        load.wait()

    def saves_of_ffn(p):
        return (
            pltpu.make_async_copy(pre, st_pre.at[p], ssem.at[9]),
            pltpu.make_async_copy(act, st_act.at[p], ssem.at[10]),
        )

    def forward_pass_step(p, carry):
        norm_send = []
        for j in range(2):
            diff, inv = center(h[j])
            norm[2 * j + core] = (diff * inv * ln1_gain[...] + ln1_shift[...]).astype(BF)
            copy = push(norm.at[2 * j + core], norm.at[2 * j + core], nsem, j, partner)
            copy.start()
            norm_send.append(copy)
        save_h = pltpu.make_async_copy(h, st_h.at[p], ssem.at[0])
        save_h.start()

        def project(block):
            rows = norm[block]
            out = mm(rows, wq[...], NN)
            q[block] = (out[:, :HALF] + b_query[:, half_lanes]).astype(BF)
            k[block] = out[:, HALF : 2 * HALF].astype(BF)
            v[block] = (out[:, 2 * HALF :] + b_value[:, half_lanes]).astype(BF)

        for j in range(2):
            project(2 * j + core)
        for j in range(2):
            norm_send[j].wait()
            project(2 * j + 1 - core)
        saves = [
            pltpu.make_async_copy(norm, st_norm.at[p], ssem.at[1]),
            pltpu.make_async_copy(q, st_q.at[p], ssem.at[2]),
            pltpu.make_async_copy(k, st_k.at[p], ssem.at[3]),
            pltpu.make_async_copy(v, st_v.at[p], ssem.at[4]),
        ]
        for save in saves:
            save.start()
        lane = lax.broadcasted_iota(jnp.int32, (RB, 128), 1)
        row = lax.broadcasted_iota(jnp.int32, (2 * RB, RB), 0) & (RB - 1)
        causal = lax.broadcasted_iota(jnp.int32, (2 * RB, RB), 1) <= row
        zero = jnp.zeros((RB, 128), BF)
        att_send = []
        for i in (3, 2, 0, 1):
            keys = (i + 1) * RB
            for pair in range(3):
                cs = slice(pair * 128, pair * 128 + 128)
                qi = q[i, :, cs] * jnp.asarray(HD**-0.5, BF)
                both = jnp.concatenate(
                    [jnp.where(lane < HD, qi, zero), jnp.where(lane < HD, zero, qi)], 0
                )
                k_all = k[0 : i + 1, :, cs].reshape(keys, 128)
                v_all = v[0 : i + 1, :, cs].reshape(keys, 128)
                s = mm(both, k_all, NT)
                last = jnp.where(causal, s[:, i * RB :], MASKED)
                s = jnp.concatenate([s[:, : i * RB], last], 1) if i else last
                peak = jnp.max(s, axis=1, keepdims=True)
                e = jnp.exp(s - peak).astype(BF)
                ol = mm(e, jnp.concatenate([v_all, jnp.ones((keys, 128), BF)], 1), NN)
                total = ol[:, 128:]
                o = ol[:, :128] / total
                att[i, :, cs] = jnp.where(lane < HD, o[:RB], o[RB:]).astype(BF)
                ls = peak + jnp.log(total)
                ls = jnp.concatenate([ls[:RB], ls[RB:]], 1).T
                lse[pair, 0:1, i * RB : (i + 1) * RB] = ls[0:1]
                lse[pair, 1:2, i * RB : (i + 1) * RB] = ls[128:129]
            if i == 3:
                saves[0].wait()
            copy = push(att.at[i], own.at[i // 2, core], asem, i // 2, partner)

            @pl.when(core == i % 2)
            def _():
                own[i // 2, core] = att[i]

            @pl.when(core != i % 2)
            def _():
                copy.start()

            if i in (2, 1):
                att_send.append(copy)
        save_att = pltpu.make_async_copy(att, st_att.at[p], ssem.at[1])
        save_lse = pltpu.make_async_copy(lse, st_lse.at[p], ssem.at[5])
        save_att.start()
        save_lse.start()
        for j, copy in ((1, att_send[0]), (0, att_send[1])):
            copy.wait()
            out = mm(own[j, 0], wp[0:HALF, :], NN) + mm(own[j, 1], wp[HALF:, :], NN)
            m = h[j] + out + b_proj[...]
            mid[j] = m
            diff, inv = center(m)
            norm2[j] = (diff * inv * ln2_gain[...] + ln2_shift[...]).astype(BF)
        save_rest = [
            pltpu.make_async_copy(own, st_own.at[p], ssem.at[6]),
            pltpu.make_async_copy(mid, st_mid.at[p], ssem.at[7]),
            pltpu.make_async_copy(norm2, st_norm2.at[p], ssem.at[8]),
        ]
        for save in save_rest:
            save.start()
        x = norm2[...].reshape(2 * RB, WIDE)

        @pl.when(p > 0)
        def _():
            for save in saves_of_ffn(p - 1):
                save.wait()

        for t in range(3):
            cs = slice(t * 1024, (t + 1) * 1024)
            z = mm(x, wf[:, cs], NN) + b_fc[:, cs]
            value, slope = gelu_and_slope(z)
            act[:, cs] = value.astype(BF)
            pre[:, cs] = slope.astype(BF)
        for save in saves_of_ffn(p):
            save.start()
        out = mm(act[...], wo[...], NN)
        active = is_active(p)
        save_h.wait()
        for j in range(2):
            new = mid[j] + out[j * RB : (j + 1) * RB] + b_out[...]
            h[j] = jnp.where(active, new, h[j])
        for save in saves[1:] + [save_att, save_lse] + save_rest:
            save.wait()
        return carry

    lax.fori_loop(0, MAXP, forward_pass_step, 0)
    for save in saves_of_ffn(MAXP - 1):
        save.wait()
    for j in range(2):
        tok[j] = h[j].astype(BF)
    mixed_keep = pltpu.make_async_copy(tok.at[chip], mixed.at[chip], wsem.at[7])
    mixed_give = push(tok.at[1 - chip], mixed.at[chip], ysem, 2, across)
    mixed_keep.start()
    mixed_give.start()

    kept = {
        "pre": (st_pre, pre),
        "mid": (st_mid, mid),
        "q": (st_q, q),
        "k": (st_k, k),
        "v": (st_v, v),
        "att": (st_att, att),
        "lse": (st_lse, lse),
        "h": (st_h, h),
    }

    def fetch(p, name):
        src, dst = kept[name]
        return pltpu.make_async_copy(src.at[p], dst, lsem.at[list(kept).index(name)])

    fetch(MAXP - 1, "h").start()
    og_keep.wait()
    og_give.wait()
    sums[...] = jnp.zeros_like(sums)
    for j in range(2):
        pos = (2 * j + core) * RB + lax.broadcasted_iota(jnp.int32, (RB, WIDE), 0)
        g[j] = jnp.where(pos < length, glow[j].astype(F32), 0.0)

    def saves_of(p):
        return (
            pltpu.make_async_copy(glow, st_e.at[p], bsem.at[0]),
            pltpu.make_async_copy(act, st_dpre.at[p], bsem.at[1]),
            pltpu.make_async_copy(norm2, st_f.at[jnp.maximum(p - 1, 0)], bsem.at[2]),
            pltpu.make_async_copy(dfused, st_dfused.at[jnp.maximum(p - 1, 0)], bsem.at[3]),
        )

    def feed_forward_back(p, active, arrive):
        for j in range(2):
            glow[j] = jnp.where(active, g[j], 0.0).astype(BF)
        e = glow[...].reshape(2 * RB, WIDE)
        arrive("pre")
        for t in range(3):
            cs = slice(t * 1024, (t + 1) * 1024)
            dact = mm(e, wo[cs, :], NT)
            act[:, cs] = (dact * pre[:, cs].astype(F32)).astype(BF)
        return mm(act[...], wf[...], NT)

    def backward_pass_step(step, carry):
        p = MAXP - 1 - step

        def arrive(*names):
            @pl.when(step > 0)
            def _():
                for name in names:
                    fetch(p, name).wait()

        def prefetch(*names):
            for name in names:
                if name == "pre":
                    fetch(p - 1, name).start()
                else:

                    @pl.when(p > 1)
                    def _(name=name):
                        fetch(p - 1, name).start()

        active = is_active(p)

        @pl.when(step > 0)
        def _():
            for save in saves_of(p + 1)[:3]:
                save.wait()

        dnorm2 = feed_forward_back(p, active, arrive)
        arrive("mid")
        for j in range(2):
            d = dnorm2[j * RB : (j + 1) * RB]
            dv_in, dgain, dshift = norm_back(mid[j], d, ln2_gain[...])
            sums[3:4] += dgain
            sums[4:5] += dshift
            dm = jnp.where(active, g[j], 0.0) + dv_in
            dmid[j] = dm
            low = dm.astype(BF)
            norm2[j] = low
        da = mm(norm2[...].reshape(2 * RB, WIDE), wp[...], NT).astype(BF)
        for half in range(2):
            for j in range(2):
                own[half, j] = da[j * RB : (j + 1) * RB, half * HALF : (half + 1) * HALF]
        datt_send = []
        for j in range(2):
            copy = push(
                own.at[1 - core, j], datt_in.at[2 * j + core], dsem, j, partner
            )
            copy.start()
            datt_send.append(copy)
            datt_in[2 * j + core] = own[core, j]
        for save in saves_of(p)[:3]:
            save.start()
        prefetch("pre", "mid")

        @pl.when(step > 0)
        def _():
            saves_of(p + 1)[3].wait()

        arrive("q", "k", "v", "att", "lse")
        for copy in datt_send:
            copy.wait()
        lane = lax.broadcasted_iota(jnp.int32, (RB, 128), 1)
        zero = jnp.zeros((RB, 128), BF)
        col = lax.broadcasted_iota(jnp.int32, (RB, 2 * RB), 1) & (RB - 1)
        causal = lax.broadcasted_iota(jnp.int32, (RB, 2 * RB), 0) <= col
        sub = lax.broadcasted_iota(jnp.int32, (128, LEN), 0)
        zero_t = jnp.zeros((128, LEN), BF)
        scale = jnp.asarray(HD**-0.5, BF)

        def split(rows):
            return jnp.concatenate(
                [jnp.where(lane < HD, rows, zero), jnp.where(lane < HD, zero, rows)], 0
            )

        def one_pair(pair, carry):
            start = pl.multiple_of(pair * 128, 128)
            cs = pl.ds(start, 128)
            slot = 0
            k_t = k[:, :, cs].reshape(LEN, 128).T
            k_low = jnp.where(sub < HD, k_t, zero_t)
            k_high = jnp.where(sub < HD, zero_t, k_t)
            for i in (3, 2, 1, 0):
                keys = (i + 1) * RB
                rs = slice(i * RB, (i + 1) * RB)
                qm = split(q[i, :, cs] * scale)
                do = datt_in[i, :, cs]
                dm = split(do)
                inner = (do.astype(F32) * att[i, :, cs].astype(F32)).T
                inner = jnp.concatenate([col_sum(inner[:HD]), col_sum(inner[HD:])], 1)
                total = jnp.concatenate([lse[pair, 0:1, rs], lse[pair, 1:2, rs]], 1)
                s = mm(k[0 : i + 1, :, cs].reshape(keys, 128), qm, NT)
                dp = mm(v[0 : i + 1, :, cs].reshape(keys, 128), dm, NT)
                last = jnp.where(causal, s[i * RB :], MASKED)
                s = jnp.concatenate([s[: i * RB], last], 0) if i else last
                prob = jnp.exp(s - total)
                ds = (prob * (dp - inner)).astype(BF)
                dv = mm(prob.astype(BF), dm, NN)
                dk = mm(ds, qm, NN)
                if i == 3:
                    dv_acc[slot] = dv
                    dk_acc[slot] = dk
                else:
                    dv_acc[slot, 0:keys] += dv
                    dk_acc[slot, 0:keys] += dk
                dq = mm(k_low[:, :keys], ds[:, :RB], NN) + mm(k_high[:, :keys], ds[:, RB:], NN)
                dfused[i, :, cs] = (dq.T * HD**-0.5).astype(BF)
            ks = pl.ds(pl.multiple_of(HALF + pair * 128, 128), 128)
            vs = pl.ds(pl.multiple_of(2 * HALF + pair * 128, 128), 128)
            dfused[:, :, ks] = dk_acc[slot].astype(BF).reshape(4, RB, 128)
            dfused[:, :, vs] = dv_acc[slot].astype(BF).reshape(4, RB, 128)
            return carry

        lax.fori_loop(0, 3, one_pair, 0)
        part_send = []
        for j in range(2):
            block = 2 * j + 1 - core
            norm[j] = mm(dfused[block], wq[...], NT).astype(BF)
            copy = push(norm.at[j], norm.at[2 + j], psem, j, partner)
            copy.start()
            part_send.append(copy)
        saves_of(p)[3].start()
        prefetch("q", "k", "v", "att", "lse")
        mine = [mm(dfused[2 * j + core], wq[...], NT) for j in range(2)]
        fetch(p, "h").wait()
        for j in range(2):
            part_send[j].wait()
            d = mine[j] + norm[2 + j].astype(F32)
            dv_in, dgain, dshift = norm_back(h[j], d, ln1_gain[...])
            sums[0:1] += dgain
            sums[1:2] += dshift
            g[j] = dmid[j] + dv_in + jnp.where(active, 0.0, g[j])
        prefetch("h")
        return carry

    lax.fori_loop(0, MAXP - 1, backward_pass_step, 0)
    for save in saves_of(1):
        save.wait()
    dnorm2 = feed_forward_back(0, is_active(0), lambda name: fetch(0, name).wait())
    last = list(saves_of(0)[:2])
    for save in last:
        save.start()
    for j in range(2):
        mid[j] = dnorm2[j * RB : (j + 1) * RB]
    sums[6:7] = jnp.where(core == 0, length.astype(F32), jnp.zeros((1, WIDE), F32))
    done = pltpu.make_async_copy(g, g_out, bsem.at[2])
    done.start()
    done_dnorm2 = pltpu.make_async_copy(mid, dnorm2_out, bsem.at[3])
    done_dnorm2.start()
    for save in last:
        save.wait()
    done_dnorm2.wait()
    mixed_keep.wait()
    mixed_give.wait()
    done.wait()


def shape(dims, kind=BF):
    return jax.ShapeDtypeStruct(dims, kind)


def layer_call(*operands):
    vmem = pl.BlockSpec(memory_space=pltpu.VMEM)
    smem = pl.BlockSpec(memory_space=pltpu.SMEM)
    hbm = pl.BlockSpec(memory_space=pl.ANY)
    outs = (
        shape((2, RB, WIDE)),
        shape((MAXP, 4, RB, WIDE)),
        shape((MAXP, 2, 2, RB, HALF)),
        shape((MAXP, 2, RB, WIDE)),
        shape((MAXP, 2 * RB, FF)),
        shape((MAXP, 2, RB, WIDE)),
        shape((MAXP, 2 * RB, FF)),
        shape((MAXP - 1, 2, RB, WIDE)),
        shape((MAXP - 1, 4, RB, 3 * HALF)),
        shape((2, RB, WIDE), F32),
        shape((2, RB, WIDE), F32),
        shape((16, WIDE), F32),
        shape((MAXP, 2, RB, WIDE), F32),
        shape((MAXP, 4, RB, HALF)),
        shape((MAXP, 4, RB, HALF)),
        shape((MAXP, 4, RB, HALF)),
        shape((MAXP, 4, RB, HALF)),
        shape((MAXP, 3, 2, LEN), F32),
        shape((MAXP, 2, RB, WIDE), F32),
        shape((MAXP, 2 * RB, FF)),
    )
    scratch = [
        pltpu.VMEM((WIDE, 3 * HALF), BF),
        pltpu.VMEM((WIDE, WIDE), BF),
        pltpu.VMEM((WIDE, FF), BF),
        pltpu.VMEM((FF, WIDE), BF),
        pltpu.VMEM((2, RB, WIDE), BF),
        pltpu.VMEM((2, RB, WIDE), F32),
        pltpu.VMEM((4, RB, WIDE), BF),
        pltpu.VMEM((4, RB, HALF), BF),
        pltpu.VMEM((4, RB, HALF), BF),
        pltpu.VMEM((4, RB, HALF), BF),
        pltpu.VMEM((4, RB, HALF), BF),
        pltpu.VMEM((2, 2, RB, HALF), BF),
        pltpu.VMEM((3, 2, LEN), F32),
        pltpu.VMEM((2, RB, WIDE), F32),
        pltpu.VMEM((2, RB, WIDE), BF),
        pltpu.VMEM((2 * RB, FF), BF),
        pltpu.VMEM((2 * RB, FF), BF),
        pltpu.VMEM((2, RB, WIDE), F32),
        pltpu.VMEM((2, RB, WIDE), BF),
        pltpu.VMEM((2, RB, WIDE), F32),
        pltpu.VMEM((4, RB, HALF), BF),
        pltpu.VMEM((4, RB, 3 * HALF), BF),
        pltpu.VMEM((2, LEN, 128), F32),
        pltpu.VMEM((2, LEN, 128), F32),
        pltpu.VMEM((8, WIDE), F32),
        pltpu.VMEM((1, FF), F32),
        pltpu.SemaphoreType.DMA((8,)),
        pltpu.SemaphoreType.DMA((11,)),
        pltpu.SemaphoreType.DMA((8,)),
        pltpu.SemaphoreType.DMA((4,)),
        pltpu.SemaphoreType.DMA((2, 2)),
        pltpu.SemaphoreType.DMA((2, 2)),
        pltpu.SemaphoreType.DMA((2, 2)),
        pltpu.SemaphoreType.DMA((2, 2)),
        pltpu.SemaphoreType.DMA((2, 3)),
    ]
    return pl.pallas_call(
        layer_kernel,
        out_shape=outs,
        in_specs=[hbm] * 2 + [smem] * 2 + [vmem] * 9 + [hbm] * 4,
        out_specs=(hbm,) * 11 + (vmem,) + (hbm,) * 8,
        scratch_shapes=scratch,
        compiler_params=pltpu.CompilerParams(
            collective_id=1, has_side_effects=True, vmem_limit_bytes=VMEM_BYTES
        ),
        name="layer",
    )(*operands)


CHUNKS = 6
SIDE = 768
ROUTES = (
    "yxzw", "xzyw", "yxzw", "yxzw", "xzwy", "zywx", "zxyw", "zxyw", "xyzw", "zxyw", "xyzw",
    "yxzw",
)
ORDER = (
    ("P", 0), ("L",), ("O", 0), ("S", 0, 0, 0), ("S", 0, 1, 0), ("P", 1), ("O", 1),
    ("S", 1, 0, 0), ("S", 1, 1, 0), ("P", 2), ("S", 0, 0, 1), ("S", 0, 1, 1), ("O", 2),
    ("S", 2, 0, 0), ("S", 2, 1, 0), ("P", 3), ("S", 0, 0, 2), ("S", 1, 0, 1), ("S", 0, 1, 2),
    ("O", 3), ("S", 3, 0, 0), ("S", 3, 1, 0), ("A",), ("S", 1, 1, 1), ("S", 2, 0, 1),
    ("S", 2, 1, 1), ("S", 0, 1, 3), ("S", 0, 0, 3), ("S", 1, 0, 2), ("S", 3, 0, 1), ("P", 4),
    ("D",), ("S", 3, 1, 1), ("S", 1, 1, 2), ("N",), ("S", 2, 1, 2), ("S", 2, 0, 2),
    ("S", 0, 1, 4), ("S", 3, 0, 2), ("S", 0, 0, 4), ("O", 4), ("S", 1, 0, 3), ("S", 3, 1, 2),
    ("S", 1, 1, 3), ("S", 4, 0, 0), ("S", 4, 1, 0), ("S", 2, 1, 3), ("O", 5), ("S", 2, 0, 3),
    ("S", 0, 1, 5), ("S", 5, 0, 0), ("S", 5, 1, 0), ("S", 3, 0, 3), ("S", 0, 0, 5),
    ("S", 3, 1, 3), ("S", 1, 0, 4), ("S", 4, 0, 1), ("S", 4, 1, 1), ("S", 1, 1, 4),
    ("S", 2, 1, 4), ("S", 2, 0, 4), ("S", 0, 1, 6), ("S", 3, 0, 4), ("S", 0, 0, 6),
    ("S", 3, 1, 4), ("S", 1, 0, 5), ("S", 5, 0, 1), ("S", 1, 1, 5), ("S", 5, 1, 1),
    ("S", 0, 1, 7), ("S", 3, 0, 5), ("S", 4, 1, 2), ("S", 3, 1, 5), ("S", 2, 1, 5),
    ("S", 4, 0, 2), ("S", 2, 0, 5), ("S", 1, 0, 6), ("S", 0, 0, 7), ("S", 5, 0, 2),
    ("S", 4, 0, 3), ("S", 2, 1, 6), ("S", 1, 1, 6), ("S", 5, 1, 2), ("S", 4, 1, 3),
    ("S", 5, 0, 3), ("S", 2, 0, 6), ("S", 3, 0, 6), ("S", 4, 0, 4), ("S", 5, 1, 3),
    ("S", 4, 1, 4), ("S", 3, 1, 6), ("S", 0, 1, 8), ("S", 5, 0, 4), ("S", 0, 0, 8),
    ("S", 2, 0, 7), ("S", 1, 0, 7), ("S", 4, 0, 5), ("S", 5, 1, 4), ("S", 2, 1, 7),
    ("S", 4, 1, 5), ("S", 1, 1, 7), ("S", 5, 0, 5), ("S", 5, 1, 5), ("S", 3, 0, 7),
    ("S", 4, 0, 6), ("S", 1, 0, 8), ("S", 4, 1, 6), ("S", 3, 1, 7), ("S", 2, 1, 8),
    ("S", 5, 0, 6), ("S", 5, 1, 6), ("S", 2, 0, 8), ("S", 1, 1, 8), ("S", 4, 1, 7),
    ("S", 4, 0, 7), ("S", 3, 0, 8), ("S", 5, 1, 7), ("S", 5, 0, 7), ("S", 3, 1, 8),
    ("S", 4, 0, 8), ("S", 5, 1, 8), ("S", 4, 1, 8), ("S", 5, 0, 8),
)


def mesh_push(src, dst, send, recv, where):
    return pltpu.make_async_remote_copy(
        src_ref=src,
        dst_ref=dst,
        send_sem=send,
        recv_sem=recv,
        device_id=where,
        device_id_type=MESH_ID,
    )


def grad_kernel(
    act,
    e,
    norm2,
    dpre,
    own,
    f,
    norm,
    dfused_st,
    st_q,
    st_k,
    st_v,
    st_att,
    st_lse,
    st_mid,
    st_h,
    g_in,
    dnorm2_in,
    w_qkv,
    w_proj,
    section,
    ln1_gain,
    ln2_gain,
    vec,
    o_qkv,
    o_proj,
    o_fc,
    o_out,
    o_tok,
    o_vec,
    wq,
    wp,
    q,
    k,
    v,
    att,
    lse,
    mid,
    h,
    g,
    dn2,
    datt,
    datt_in,
    f0,
    dfused,
    dk_acc,
    dv_acc,
    part,
    part_in,
    slots,
    give,
    got,
    work,
    rx,
    tok_low,
    vsend,
    vgot,
    lsem,
    slsem,
    dsem,
    psem,
    csem,
    xsem,
    rsem,
    vsem,
    ysem,
    osem,
):
    me = lax.axis_index("seq")
    group = lax.axis_index("grp")
    core = lax.rem(me, 2)
    y = me // 2
    x = lax.rem(group, 2)
    z = group // 2
    other = 1 - core
    to_core = {"seq": me + 1 - 2 * core}
    to_y = {"seq": lax.rem(me + 2, 4)}
    to_x = {"grp": group + 1 - 2 * x}

    def to_z_pair(step):
        low = lax.rem(z // step, 2)
        return {"grp": (z + step - 2 * step * low) * 2 + x}

    partner = me + 1 - 2 * core
    passes = jnp.full((1, WIDE), 2 * section[y] + 1, jnp.int32)
    active = jnp.full((1, WIDE), 0, jnp.int32) < passes

    kept = {
        "mid": (st_mid.at[0], mid),
        "g": (g_in, g),
        "dnorm2": (dnorm2_in, dn2),
        "wp": (w_proj, wp),
        "q": (st_q.at[0], q),
        "k": (st_k.at[0], k),
        "v": (st_v.at[0], v),
        "att": (st_att.at[0], att),
        "lse": (st_lse.at[0], lse),
        "h": (st_h.at[0], h),
    }
    for third in range(3):
        kept["wq%d" % third] = (
            w_qkv.at[:, qkv_columns(core, third)],
            wq.at[:, pl.ds(third * HALF, HALF)],
        )

    def kept_copy(name):
        src, dst = kept[name]
        return pltpu.make_async_copy(src, dst, lsem.at[list(kept).index(name)])

    def arrive(*names):
        for name in names:
            kept_copy(name).wait()

    def whole(src):
        return [(src.at[p], (p, slice(None))) for p in range(MAXP)]

    def piece(src, owner, i):
        cols = pl.ds(pl.multiple_of(owner * 2 * SIDE + i * SIDE, 128), SIDE)
        return [(src.at[p, :, :, cols], (p, slice(None))) for p in range(MAXP)]

    def own_rows():
        return [
            (own.at[p, :, half], (p, slice(None), slice(None), pl.ds(half * HALF, HALF)))
            for p in range(MAXP)
            for half in range(2)
        ]

    def f_rows():
        return [(f0, (0, slice(None)))] + [(f.at[p - 1], (p, slice(None))) for p in (1, 2)]

    def dfused_at(p, blocks, cols):
        src = dfused if p == 0 else dfused_st.at[p - 1]
        return src.at[blocks, :, cols]

    def dq_rows():
        return [
            (
                dfused_at(p, pl.ds(2 * i, 2), pl.ds(0, HALF)),
                (p, slice(None), slice(None), pl.ds(i * HALF, HALF)),
            )
            for p in range(MAXP)
            for i in range(2)
        ]

    def kv_rows(i):
        return [
            (dfused_at(p, pl.ds(2 * i, 2), pl.ds(HALF, 2 * HALF)), (p, slice(None)))
            for p in range(MAXP)
        ]

    def norm_rows(i):
        return [(norm.at[p, pl.ds(2 * i, 2)], (p, slice(None))) for p in range(MAXP)]

    other = 1 - core
    operands = {
        "e": (0, lambda: whole(e)),
        "act0": (1, lambda: piece(act, other, 0)),
        "act1": (2, lambda: piece(act, core, 0)),
        "act2": (3, lambda: piece(act, other, 1)),
        "act3": (4, lambda: piece(act, core, 1)),
        "norm2": (1, lambda: whole(norm2)),
        "dpre0": (2, lambda: piece(dpre, other, 0)),
        "dpre1": (3, lambda: piece(dpre, core, 0)),
        "dpre2": (0, lambda: piece(dpre, other, 1)),
        "dpre3": (4, lambda: piece(dpre, core, 1)),
        "own": (2, own_rows),
        "f": (3, f_rows),
        "norm_a": (0, lambda: norm_rows(0)),
        "norm_b": (1, lambda: norm_rows(1)),
        "dq": (4, dq_rows),
        "kv_a": (2, lambda: kv_rows(0)),
        "kv_b": (3, lambda: kv_rows(1)),
    }

    def operand_copies(name):
        slot, copies = operands[name]
        return [
            pltpu.make_async_copy(src, slots.at[(slot, *place)], slsem.at[slot, i])
            for i, (src, place) in enumerate(copies())
        ]

    def begin(*names):
        for name in names:
            for copy in operand_copies(name):
                copy.start()

    def ready(name):
        for copy in operand_copies(name):
            copy.wait()

    def operand(name):
        return slots[operands[name][0]].reshape(MAXP * 2 * RB, SIDE)

    begin("e", "act0", "act1")
    for name in ("mid", "g", "dnorm2", "wp"):
        kept_copy(name).start()
    begin("act2", "act3")
    for name in ("q", "k", "v", "att", "lse", "h", "wq0", "wq1", "wq2"):
        kept_copy(name).start()

    sem = pltpu.get_barrier_semaphore()
    partners = [to_core, to_y, to_x, to_z_pair(1), to_z_pair(2)]
    for where in partners:
        pl.semaphore_signal(sem, inc=1, device_id=where, device_id_type=MESH_ID)
    pl.semaphore_wait(sem, len(partners))

    tok_give = mesh_push(tok_low.at[1 - y], o_tok.at[y], ysem.at[0], ysem.at[1], to_y)
    tok_keep = pltpu.make_async_copy(tok_low.at[y], o_tok.at[y], osem.at[2 * CHUNKS])

    def datt_copy(j):
        return push(datt.at[other, j], datt_in.at[2 * j + core], dsem, j, partner)

    def part_copy(j):
        return push(part.at[j], part_in.at[j], psem, j, partner)

    vec_to = [to_core, to_x, to_y, to_z_pair(1), to_z_pair(2)]

    def vec_copy(k):
        return mesh_push(vsend.at[k], vgot.at[k], vsem.at[0, k], vsem.at[1, k], vec_to[k])

    vsend[0] = vec[...]

    def vec_row(row, v):
        vsend[0, pl.ds(row, 1), :] = v

    def half_row(row, v):
        blank = jnp.zeros((1, HALF), F32)
        vec_row(
            row,
            jnp.concatenate(
                [jnp.where(core == 0, v, blank), jnp.where(core == 0, blank, v)], 1
            ),
        )

    def vec_step(k):
        vec_copy(k).wait()
        vsend[k + 1] = vsend[k] + vgot[k]
        if k < 4:
            vec_copy(k + 1).start()

    def tiles(lefts, rights, cols, emit):
        def tile(m, carry):
            here = pl.ds(pl.multiple_of(m * 256, 256), 256)
            out = None
            for left, right in zip(lefts, rights):
                left_part = slots[operands[left][0], :, :, :, here].reshape(MAXP * 2 * RB, 256)
                width = SIDE if right[1] is None else HALF
                right_cols = cols if right[1] is None else right[1]
                right_part = slots[operands[right[0]][0], :, :, :, right_cols]
                part_out = mm(left_part, right_part.reshape(MAXP * 2 * RB, width), TN)
                out = part_out if out is None else out + part_out
            emit(m, here, out)
            return carry

        lax.fori_loop(0, SIDE // 256, tile, 0)

    def product(n, place, emit):
        owner = core if place else other
        every = slice(None)
        if n < 4:
            name = ("act%d" if n < 2 else "dpre%d") % (2 * (n % 2) + place)
            if n in (0, 2) and place == 0:
                ready("e" if n == 0 else "norm2")
            ready(name)
            if n < 2:
                if n == 0 and place == 0:
                    vec_row(5, col_sum(operand("e").astype(F32)))
                tiles((name,), (("e", None),), every, emit)
            else:
                vec_row(8 + owner * 2 + n - 2, col_sum(operand(name).astype(F32)))
                tiles(("norm2",), ((name, None),), every, emit)
            return
        if place == 0:
            ready("own")
            ready("f")
            vec_row(2, col_sum(operand("f").astype(F32)))
        cols = pl.ds(pl.multiple_of(owner * HALF, 128), HALF)
        tiles(("own",), (("f", cols),), every, emit)

    def core_copy(n):
        width = SIDE if n < 4 else HALF
        return mesh_push(
            give.at[n % 2, :, pl.ds(0, width)],
            got.at[n % 2, :, pl.ds(0, width)],
            csem.at[0, n],
            csem.at[1, n],
            to_core,
        )

    follow = {
        (0, 0): ("norm2",),
        (0, 1): ("dpre0",),
        (1, 0): ("dpre1",),
        (1, 1): ("dpre2", "dpre3"),
        (2, 0): ("own",),
        (2, 1): ("f",),
        (3, 0): ("norm_a",),
        (3, 1): ("norm_b",),
    }

    def theirs(n):
        if n >= 2:
            core_copy(n - 2).wait_send()

        def emit(m, here, out):
            if n < 4:
                give[n % 2, here] = out.astype(BF)
            else:
                give[n % 2, here, 0:HALF] = out.astype(BF)

        product(n, 0, emit)
        core_copy(n).start()
        begin(*follow.get((n, 0), ()))

    def ours(n):
        if n < 4:
            def emit(m, here, out):
                @pl.when(m == 0)
                def _():
                    core_copy(n).wait_recv()

                out = (out + got[n % 2, here].astype(F32)).astype(BF)
                work[n, 0, here] = out[:, :HALF]
                work[n, 1, here] = out[:, HALF:]

            product(n, 1, emit)
            begin(*follow.get((n, 1), ()))
        elif n == 4:

            def emit_proj(m, here, out):
                work[n, 0, here] = (out + got[n % 2, here, 0:HALF].astype(F32)).astype(BF)

            def emit_dq(m, here, out):
                work[n, 1, here] = out.astype(BF)

            core_copy(n).wait_recv()
            product(n, 1, emit_proj)
            begin("kv_a", "kv_b")
            ready("dq")
            ready("norm_a")
            ready("norm_b")
            right = operand("dq")
            half_row(12, col_sum(right[:, :HALF].astype(F32)) + col_sum(right[:, HALF:].astype(F32)))
            halves = (("dq", slice(0, HALF)), ("dq", slice(HALF, SIDE)))
            tiles(("norm_a", "norm_b"), halves, None, emit_dq)
        else:

            def emit_kv(m, here, out):
                out = out.astype(BF)
                work[n, 0, here] = out[:, :HALF]
                work[n, 1, here] = out[:, HALF:]

            ready("kv_a")
            ready("kv_b")
            right_a, right_b = operand("kv_a")[:, HALF:], operand("kv_b")[:, HALF:]
            half_row(13, col_sum(right_a.astype(F32)) + col_sum(right_b.astype(F32)))
            vec_copy(0).start()
            both = (("kv_a", None), ("kv_b", None))
            tiles(("norm_a", "norm_b"), both, slice(None), emit_kv)

    def leave():
        arrive("mid", "g", "dnorm2")
        for j in range(2):
            d = dn2[j]
            dv_in, dgain, dshift = norm_back(mid[j], d, ln2_gain[...].reshape(1, WIDE))
            vsend[0, 3:4] += dgain
            vsend[0, 4:5] += dshift
            dm = jnp.where(active, g[j], 0.0) + dv_in
            mid[j] = dm
            low = dm.astype(BF)
            f0[j] = low
        arrive("wp")
        da = mm(f0[...].reshape(2 * RB, WIDE), wp[...], NT).astype(BF)
        for half in range(2):
            for j in range(2):
                datt[half, j] = da[j * RB : (j + 1) * RB, half * HALF : (half + 1) * HALF]
        for j in range(2):
            datt_copy(j).start()
            datt_in[2 * j + core] = datt[core, j]

    def attend_back():
        arrive("q", "k", "v", "att", "lse")
        for j in range(2):
            datt_copy(j).wait()
        lane = lax.broadcasted_iota(jnp.int32, (RB, 128), 1)
        zero = jnp.zeros((RB, 128), BF)
        col = lax.broadcasted_iota(jnp.int32, (RB, 2 * RB), 1) & (RB - 1)
        causal = lax.broadcasted_iota(jnp.int32, (RB, 2 * RB), 0) <= col
        sub = lax.broadcasted_iota(jnp.int32, (128, LEN), 0)
        zero_t = jnp.zeros((128, LEN), BF)
        scale = jnp.asarray(HD**-0.5, BF)

        def split(rows):
            return jnp.concatenate(
                [jnp.where(lane < HD, rows, zero), jnp.where(lane < HD, zero, rows)], 0
            )

        def one_pair(pair, carry):
            cs = pl.ds(pl.multiple_of(pair * 128, 128), 128)
            slot = 0
            k_t = k[:, :, cs].reshape(LEN, 128).T
            k_low = jnp.where(sub < HD, k_t, zero_t)
            k_high = jnp.where(sub < HD, zero_t, k_t)
            for i in (3, 2, 1, 0):
                keys = (i + 1) * RB
                rs = slice(i * RB, (i + 1) * RB)
                qm = split(q[i, :, cs] * scale)
                do = datt_in[i, :, cs]
                dm = split(do)
                inner = (do.astype(F32) * att[i, :, cs].astype(F32)).T
                inner = jnp.concatenate([col_sum(inner[:HD]), col_sum(inner[HD:])], 1)
                total = jnp.concatenate([lse[pair, 0:1, rs], lse[pair, 1:2, rs]], 1)
                s = mm(k[0 : i + 1, :, cs].reshape(keys, 128), qm, NT)
                dp = mm(v[0 : i + 1, :, cs].reshape(keys, 128), dm, NT)
                last = jnp.where(causal, s[i * RB :], MASKED)
                s = jnp.concatenate([s[: i * RB], last], 0) if i else last
                prob = jnp.exp(s - total)
                ds = (prob * (dp - inner)).astype(BF)
                dv = mm(prob.astype(BF), dm, NN)
                dk = mm(ds, qm, NN)
                if i == 3:
                    dv_acc[slot] = dv
                    dk_acc[slot] = dk
                else:
                    dv_acc[slot, 0:keys] += dv
                    dk_acc[slot, 0:keys] += dk
                dq = mm(k_low[:, :keys], ds[:, :RB], NN) + mm(k_high[:, :keys], ds[:, RB:], NN)
                dfused[i, :, cs] = (dq.T * HD**-0.5).astype(BF)
            ks = pl.ds(pl.multiple_of(HALF + pair * 128, 128), 128)
            vs = pl.ds(pl.multiple_of(2 * HALF + pair * 128, 128), 128)
            dfused[:, :, ks] = dk_acc[slot].astype(BF).reshape(4, RB, 128)
            dfused[:, :, vs] = dv_acc[slot].astype(BF).reshape(4, RB, 128)
            return carry

        lax.fori_loop(0, 3, one_pair, 0)

    def dense_back():
        arrive("wq0", "wq1", "wq2")
        for j in range(2):
            block = 2 * j + 1 - core
            part[j] = mm(dfused[block], wq[...], NT).astype(BF)
            part_copy(j).start()

    def tokens_back():
        mine = [mm(dfused[2 * j + core], wq[...], NT) for j in range(2)]
        arrive("h")
        for j in range(2):
            part_copy(j).wait()
            d = mine[j] + part_in[j].astype(F32)
            dv_in, dgain, dshift = norm_back(h[j], d, ln1_gain[...].reshape(1, WIDE))
            vsend[0, 0:1] += dgain
            vsend[0, 1:2] += dshift
            tok_low[j] = (mid[j] + dv_in + jnp.where(active, 0.0, g[j])).astype(BF)
        tok_give.start()
        tok_keep.start()

    def rows(start, size):
        return pl.ds(pl.multiple_of(start, 16), size)

    bits = {"x": x, "y": y, "z": lax.rem(z, 2), "w": z // 2}
    pair_of = {"x": to_x, "y": to_y, "z": to_z_pair(1), "w": to_z_pair(2)}

    def first_row(n, s, k):
        row = 0
        for i, name in enumerate(ROUTES[2 * n + s][:k]):
            row = row + bits[name] * (SIDE >> (i + 1))
        return row

    def received(sub, k):
        size = SIDE >> (k + 1)
        return rx.at[sub, pl.ds(SIDE - 2 * size, size)]

    def step_copies(n, s, k):
        route = ROUTES[2 * n + s]
        sub = 2 * n + s

        def copy(src, dst, where):
            return mesh_push(src, dst, xsem.at[sub, k], rsem.at[sub, k], where)

        if k < 4:
            size = SIDE >> (k + 1)
            row = first_row(n, s, k) + (1 - bits[route[k]]) * size
            return [copy(work.at[n, s, rows(row, size)], received(sub, k), pair_of[route[k]])]
        if n < 2:
            out, start, col = o_out, core * 2 * SIDE + n * SIDE, s * HALF
        elif n < 4:
            out, start, col = o_fc, 0, core * 2 * SIDE + (n - 2) * SIDE + s * HALF
        elif n == 4 and s == 0:
            out, start, col = o_proj, 0, core * HALF
        else:
            out, start, col = o_qkv, 0, (0 if n == 4 else 1 + s) * WIDE + core * HALF
        left = 8 - k
        size = SIDE >> left
        row = first_row(n, s, left)
        dst = out.at[rows(start + row, size), pl.ds(pl.multiple_of(col, 128), HALF)]
        if k == 4:
            src = work.at[n, s, rows(row, size)]
            return [copy(src, dst, pair_of[route[3]]), pltpu.make_async_copy(src, dst, osem.at[sub])]
        return [copy(dst, dst, to_core if k == 8 else pair_of[route[left - 1]])]

    def advance(n, s, k):
        if k > 0:
            for copy in step_copies(n, s, k - 1):
                copy.wait()
        if 0 < k < 5:
            sub = 2 * n + s
            size = SIDE >> k
            here = rows(first_row(n, s, k), size)
            more = rx[sub, pl.ds(SIDE - 2 * size, size)]
            work[n, s, here] = (work[n, s, here].astype(F32) + more.astype(F32)).astype(BF)
        for copy in step_copies(n, s, k):
            copy.start()

    tail = ORDER[ORDER.index(("O", 5)) + 1 :]
    vec_steps = [tail[i] for i in (4, 8, 12, 16, 20)]
    for entry in ORDER:
        kind, *which = entry
        if kind == "P":
            theirs(*which)
        elif kind == "O":
            ours(*which)
        elif kind == "L":
            leave()
        elif kind == "A":
            attend_back()
        elif kind == "D":
            dense_back()
            begin("dq")
        elif kind == "N":
            tokens_back()
        else:
            advance(*which)
            if entry in vec_steps:
                vec_step(vec_steps.index(entry))
    total = vsend[5]
    inv = 1.0 / total[6:7]
    o_vec[...] = total * inv
    o_vec[7:8] = inv
    for n in range(CHUNKS):
        for s in range(2):
            for copy in step_copies(n, s, 8):
                copy.wait()
    for n in (3, 4):
        core_copy(n).wait_send()
    tok_give.wait()
    tok_keep.wait()


def grad_call(*operands):
    vmem = pl.BlockSpec(memory_space=pltpu.VMEM)
    hbm = pl.BlockSpec(memory_space=pl.ANY)
    outs = (
        shape((WIDE, 3 * WIDE)),
        shape((WIDE, WIDE)),
        shape((WIDE, FF)),
        shape((FF, WIDE)),
        shape((2, RB, WIDE)),
        shape((16, WIDE), F32),
    )
    scratch = [
        pltpu.VMEM((MAXP, 2, RB, WIDE), BF),
        pltpu.VMEM((MAXP, 2, RB, WIDE), BF),
        pltpu.VMEM((MAXP, 2, 2, RB, HALF), BF),
        pltpu.VMEM((MAXP, 2, RB, WIDE), BF),
        pltpu.VMEM((MAXP, 4, RB, WIDE), BF),
        pltpu.VMEM((2, MAXP, 4, RB, HALF), BF),
        pltpu.VMEM((3, MAXP, 2 * RB, SIDE), BF),
        pltpu.VMEM((2, SIDE, SIDE), BF),
        pltpu.VMEM((5, SIDE, SIDE), BF),
        pltpu.VMEM((CHUNKS, 2, SIDE, HALF), BF),
        pltpu.VMEM((2 * CHUNKS, SIDE - 48, HALF), BF),
        pltpu.VMEM((2, RB, WIDE), F32),
        pltpu.VMEM((2, RB, WIDE), BF),
        pltpu.VMEM((6, 16, WIDE), F32),
        pltpu.VMEM((5, 16, WIDE), F32),
        pltpu.SemaphoreType.DMA((6,)),
        pltpu.SemaphoreType.DMA((3,)),
        pltpu.SemaphoreType.DMA((2,)),
        pltpu.SemaphoreType.DMA((2, 5)),
        pltpu.SemaphoreType.DMA((2 * CHUNKS, 9)),
        pltpu.SemaphoreType.DMA((2 * CHUNKS, 9)),
        pltpu.SemaphoreType.DMA((2, 5)),
        pltpu.SemaphoreType.DMA((2,)),
        pltpu.SemaphoreType.DMA((2 * CHUNKS,)),
    ]
    return pl.pallas_call(
        grad_kernel,
        out_shape=outs,
        in_specs=[hbm] * 9 + [vmem],
        out_specs=(hbm,) * 5 + (vmem,),
        scratch_shapes=scratch,
        compiler_params=pltpu.CompilerParams(
            collective_id=2, has_side_effects=True, vmem_limit_bytes=VMEM_BYTES
        ),
        name="gradients",
    )(*operands)


def grad_call(*operands):
    vmem = pl.BlockSpec(memory_space=pltpu.VMEM)
    hbm = pl.BlockSpec(memory_space=pl.ANY)
    outs = (
        shape((WIDE, 3 * WIDE)),
        shape((WIDE, WIDE)),
        shape((WIDE, FF)),
        shape((FF, WIDE)),
        shape((2, RB, WIDE)),
        shape((16, WIDE), F32),
    )
    rows_f32 = pltpu.VMEM((2, RB, WIDE), F32)
    rows_low = pltpu.VMEM((2, RB, WIDE), BF)
    heads = pltpu.VMEM((4, RB, HALF), BF)
    scratch = [
        pltpu.VMEM((WIDE, 3 * HALF), BF),
        pltpu.VMEM((WIDE, WIDE), BF),
        heads,
        heads,
        heads,
        heads,
        pltpu.VMEM((3, 2, LEN), F32),
        rows_f32,
        rows_f32,
        rows_f32,
        rows_f32,
        pltpu.VMEM((2, 2, RB, HALF), BF),
        heads,
        rows_low,
        pltpu.VMEM((4, RB, 3 * HALF), BF),
        pltpu.VMEM((2, LEN, 128), F32),
        pltpu.VMEM((2, LEN, 128), F32),
        rows_low,
        rows_low,
        pltpu.VMEM((5, MAXP, 2, RB, SIDE), BF),
        pltpu.VMEM((2, SIDE, SIDE), BF),
        pltpu.VMEM((2, SIDE, SIDE), BF),
        pltpu.VMEM((CHUNKS, 2, SIDE, HALF), BF),
        pltpu.VMEM((2 * CHUNKS, SIDE - 48, HALF), BF),
        rows_low,
        pltpu.VMEM((6, 16, WIDE), F32),
        pltpu.VMEM((5, 16, WIDE), F32),
        pltpu.SemaphoreType.DMA((13,)),
        pltpu.SemaphoreType.DMA((5, 6)),
        pltpu.SemaphoreType.DMA((2, 2)),
        pltpu.SemaphoreType.DMA((2, 2)),
        pltpu.SemaphoreType.DMA((2, 5)),
        pltpu.SemaphoreType.DMA((2 * CHUNKS, 9)),
        pltpu.SemaphoreType.DMA((2 * CHUNKS, 9)),
        pltpu.SemaphoreType.DMA((2, 5)),
        pltpu.SemaphoreType.DMA((2,)),
        pltpu.SemaphoreType.DMA((2 * CHUNKS + 1,)),
    ]
    return pl.pallas_call(
        grad_kernel,
        out_shape=outs,
        in_specs=[hbm] * 19 + [pl.BlockSpec(memory_space=pltpu.SMEM)] + [vmem] * 3,
        out_specs=(hbm,) * 5 + (vmem,),
        scratch_shapes=scratch,
        compiler_params=pltpu.CompilerParams(
            collective_id=2, has_side_effects=True, vmem_limit_bytes=VMEM_BYTES
        ),
        name="gradients",
    )(*operands)


def finish_kernel(
    vec,
    o_qkv,
    o_proj,
    o_fc,
    o_out,
    o_tok,
    f_tok,
    f_ln1_gain,
    f_ln1_shift,
    f_qkv,
    f_bq,
    f_bv,
    f_proj,
    f_b_proj,
    f_ln2_gain,
    f_ln2_shift,
    f_fc,
    f_b_fc,
    f_out,
    f_b_out,
    in_wide,
    out_wide,
    in_tall,
    out_tall,
    isem,
    osem,
):
    inv = vec[7:8, 0:1]
    jobs = []
    for src, dst, size in ((o_fc, f_fc, 128), (o_qkv, f_qkv, 128), (o_out, f_out, 512), (o_proj, f_proj, 384)):
        total, width = src.shape
        for i in range(total // size):
            part = (slice(i * size, (i + 1) * size), slice(0, width))
            jobs.append((src.at[part], dst.at[part], size, width))
    for i in range(2):
        jobs.append((o_tok.at[i], f_tok.at[i], RB, WIDE))

    def parts(n):
        src, dst, size, width = jobs[n]
        slot = n % 6
        wide = size == 128
        here = (in_wide if wide else in_tall).at[slot, pl.ds(0, size), pl.ds(0, width)]
        there = (out_wide if wide else out_tall).at[slot, pl.ds(0, size), pl.ds(0, width)]
        return here, there, src, dst, slot

    def load(n):
        here, _, src, _, slot = parts(n)
        return pltpu.make_async_copy(src, here, isem.at[slot])

    def store(n):
        _, there, _, dst, slot = parts(n)
        return pltpu.make_async_copy(there, dst, osem.at[slot])

    for n in range(4):
        load(n).start()
    f_ln1_gain[...] = vec[0:1].reshape(WIDE)
    f_ln1_shift[...] = vec[1:2].reshape(WIDE)
    f_b_proj[...] = vec[2:3].reshape(WIDE)
    f_ln2_gain[...] = vec[3:4].reshape(WIDE)
    f_ln2_shift[...] = vec[4:5].reshape(WIDE)
    f_b_out[...] = vec[5:6].reshape(WIDE)
    f_bq[...] = vec[12:13].reshape(WIDE)
    f_bv[...] = vec[13:14].reshape(WIDE)
    f_b_fc[...] = jnp.concatenate([vec[8 + i : 9 + i] for i in range(4)], 1).reshape(FF)
    for n in range(len(jobs)):
        here, there = parts(n)[:2]
        load(n).wait()
        if n >= 6:
            store(n - 6).wait()
        there[...] = here[...].astype(F32) * inv
        store(n).start()
        if n + 4 < len(jobs):
            load(n + 4).start()
    for n in range(len(jobs) - 6, len(jobs)):
        store(n).wait()


def finish_call(*operands):
    vmem = pl.BlockSpec(memory_space=pltpu.VMEM)
    hbm = pl.BlockSpec(memory_space=pl.ANY)
    row = shape((WIDE,), F32)
    outs = (
        shape((2, RB, WIDE), F32),
        row,
        row,
        shape((WIDE, 3 * WIDE), F32),
        row,
        row,
        shape((WIDE, WIDE), F32),
        row,
        row,
        row,
        shape((WIDE, FF), F32),
        shape((FF,), F32),
        shape((FF, WIDE), F32),
        row,
    )
    big = {0, 3, 6, 10, 12}
    return pl.pallas_call(
        finish_kernel,
        out_shape=outs,
        in_specs=[vmem] + [hbm] * 5,
        out_specs=tuple(hbm if i in big else vmem for i in range(len(outs))),
        scratch_shapes=[
            pltpu.VMEM((6, 128, FF), BF),
            pltpu.VMEM((6, 128, FF), F32),
            pltpu.VMEM((6, 512, WIDE), BF),
            pltpu.VMEM((6, 512, WIDE), F32),
            pltpu.SemaphoreType.DMA((6,)),
            pltpu.SemaphoreType.DMA((6,)),
        ],
        compiler_params=pltpu.CompilerParams(vmem_limit_bytes=VMEM_BYTES),
        name="finish",
    )(*operands)


def on_chip(
    tokens,
    out_grad,
    section,
    lengths,
    ln1_gain,
    ln1_shift,
    w_qkv,
    b_query,
    b_value,
    w_proj,
    b_proj,
    ln2_gain,
    ln2_shift,
    w_fc,
    b_fc,
    w_out,
    b_out,
):
    kept = layer_call(
        tokens,
        out_grad,
        section,
        lengths,
        ln1_gain,
        ln1_shift,
        b_query,
        b_value,
        b_proj,
        ln2_gain,
        ln2_shift,
        b_out,
        b_fc,
        w_qkv,
        w_proj,
        w_fc,
        w_out,
    )
    (mixed, norm, own, norm2, act, e, dpre, f, dfused, g, dnorm2, sums, *heads) = kept
    (h, q, k, v, att, lse, mid, _) = heads
    (g_qkv, g_proj, g_fc, g_out, g_tok, vec) = grad_call(
        act.reshape(MAXP, 2, RB, FF),
        e,
        norm2,
        dpre.reshape(MAXP, 2, RB, FF),
        own,
        f,
        norm,
        dfused,
        q,
        k,
        v,
        att,
        lse,
        mid,
        h,
        g,
        dnorm2,
        w_qkv,
        w_proj,
        section,
        ln1_gain,
        ln2_gain,
        sums,
    )
    return (mixed, *finish_call(vec, g_qkv, g_proj, g_fc, g_out, g_tok))


def solution(mesh):
    in_specs = (
        P("grp", "seq", None),
        P("grp", "seq", None),
        P("grp"),
        P("grp"),
        P(),
        P(),
        P(),
        P(),
        P(),
        P(),
        P(),
        P(),
        P(),
        P(),
        P(),
        P(),
        P(),
    )
    out_specs = (
        P("grp", "seq", None),
        P("grp", "seq", None),
        P(),
        P(),
        P(),
        P(),
        P(),
        P(),
        P(),
        P(),
        P(),
        P(),
        P(),
        P(),
        P(),
    )
    chosen = on_chip if (mesh.shape["grp"], mesh.shape["seq"]) == (8, 4) else on_device
    return jax.shard_map(
        chosen, mesh=mesh, in_specs=in_specs, out_specs=out_specs, check_vma=False
    )
```

```python
import jax
import jax.numpy as jnp
from jax import lax
from jax.experimental import pallas as pl
from jax.experimental.pallas import tpu as pltpu
from jax.sharding import PartitionSpec as P

HEADS = 12
HD = 64
MAXP = 3


EPSILON = 1e-05
GELU_COEF = 0.7978845608028654
MASKED = -1e30


def layer_norm(hidden, gain, shift):
    average = jnp.mean(hidden, axis=-1, keepdims=True)
    centered = hidden - average
    variance = jnp.mean(centered * centered, axis=-1, keepdims=True)
    return centered * lax.rsqrt(variance + EPSILON) * gain + shift


def gelu_tanh(pre_act):
    return (
        0.5
        * pre_act
        * (1.0 + jnp.tanh(GELU_COEF * (pre_act + 0.044715 * pre_act * pre_act * pre_act)))
    )


def dense(left, right):
    return jnp.einsum("srk,kn->srn", left, right, preferred_element_type=jnp.float32)


def weight_grad(left, right):
    return jnp.einsum("srk,srn->kn", left, right, preferred_element_type=jnp.float32)


def back_dense(grad_rows, right):
    return jnp.einsum("srn,kn->srk", grad_rows, right, preferred_element_type=jnp.float32)


def row_sums(grad_rows):
    return jnp.sum(grad_rows.astype(jnp.float32), axis=(0, 1))


def causal_scores(query_rows, key_all, row_start):
    sample, row_count, width = query_rows.shape
    key_count = key_all.shape[1]
    q_heads = query_rows.reshape(sample, row_count, HEADS, HD)
    k_heads = key_all.reshape(sample, key_count, HEADS, HD)
    scores = jnp.einsum(
        "srhd,sthd->shrt", q_heads, k_heads, preferred_element_type=jnp.float32
    ) * HD ** (-0.5)
    position = row_start + lax.broadcasted_iota(jnp.int32, (row_count, key_count), 0)
    column = lax.broadcasted_iota(jnp.int32, (row_count, key_count), 1)
    return jnp.where(column <= position, scores, MASKED)


def forward_pass(hidden, params, row_start):
    (
        ln1_gain,
        ln1_shift,
        w_qkv,
        b_query,
        b_value,
        w_proj,
        b_proj,
        ln2_gain,
        ln2_shift,
        w_fc,
        b_fc,
        w_out,
        b_out,
    ) = params
    sample, row_count, width = hidden.shape
    normed_low = layer_norm(hidden, ln1_gain, ln1_shift).astype(jnp.bfloat16)
    bias_row = jnp.concatenate([b_query, jnp.zeros_like(b_query), b_value])
    joined_low = (dense(normed_low, w_qkv) + bias_row).astype(jnp.bfloat16)
    query_rows = joined_low[:, :, :width]
    key_rows = joined_low[:, :, width : 2 * width]
    value_rows = joined_low[:, :, 2 * width :]
    key_all, value_all = (
        lax.all_gather(key_rows, "seq", axis=1, tiled=True),
        lax.all_gather(value_rows, "seq", axis=1, tiled=True),
    )
    scores = causal_scores(query_rows, key_all, row_start)
    row_peak = jnp.max(scores, axis=-1, keepdims=True)
    shifted = jnp.exp(scores - row_peak)
    row_total = jnp.sum(shifted, axis=-1, keepdims=True)
    attn_probs = shifted / row_total
    log_total = row_peak + jnp.log(row_total)
    v_heads = value_all.reshape(sample, value_all.shape[1], HEADS, HD)
    attended = jnp.einsum(
        "shrt,sthd->srhd",
        attn_probs.astype(jnp.bfloat16),
        v_heads,
        preferred_element_type=jnp.float32,
    )
    attended_low = attended.reshape(sample, row_count, width).astype(jnp.bfloat16)
    middle = hidden + dense(attended_low, w_proj) + b_proj
    normed_two = layer_norm(middle, ln2_gain, ln2_shift).astype(jnp.bfloat16)
    pre_act = dense(normed_two, w_fc) + b_fc
    activ_low = gelu_tanh(pre_act).astype(jnp.bfloat16)
    output = middle + dense(activ_low, w_out) + b_out
    kept_keys = (key_rows, value_rows)
    kept = (
        hidden,
        normed_low,
        joined_low,
        kept_keys,
        log_total,
        attended_low,
        middle,
        normed_two,
        pre_act,
        activ_low,
    )
    return (output, kept)


def ffn_back(kept, grad_out, params):
    (
        ln1_gain,
        ln1_shift,
        w_qkv,
        b_query,
        b_value,
        w_proj,
        b_proj,
        ln2_gain,
        ln2_shift,
        w_fc,
        b_fc,
        w_out,
        b_out,
    ) = params
    (
        hidden,
        normed_low,
        joined_low,
        kept_keys,
        log_total,
        attended_low,
        middle,
        normed_two,
        pre_act,
        activ_low,
    ) = kept
    grad_low = grad_out.astype(jnp.bfloat16)
    g_w_out = weight_grad(activ_low, grad_low)
    g_b_out = row_sums(grad_low)
    d_activ = back_dense(grad_low, w_out)
    gelu_pull = jax.vjp(gelu_tanh, pre_act)[1]
    d_pre_low = gelu_pull(d_activ)[0].astype(jnp.bfloat16)
    g_w_fc = weight_grad(normed_two, d_pre_low)
    g_b_fc = row_sums(d_pre_low)
    d_normed_two = back_dense(d_pre_low, w_fc)
    norm_pull = jax.vjp(layer_norm, middle, ln2_gain, ln2_shift)[1]
    d_mid_norm, g_ln2_gain, g_ln2_shift = norm_pull(d_normed_two)
    return ((g_ln2_gain, g_ln2_shift, g_w_fc, g_b_fc, g_w_out, g_b_out), grad_out + d_mid_norm)


def attn_back(kept, d_middle, params, row_start):
    (
        ln1_gain,
        ln1_shift,
        w_qkv,
        b_query,
        b_value,
        w_proj,
        b_proj,
        ln2_gain,
        ln2_shift,
        w_fc,
        b_fc,
        w_out,
        b_out,
    ) = params
    (
        hidden,
        normed_low,
        joined_low,
        kept_keys,
        log_total,
        attended_low,
        middle,
        normed_two,
        pre_act,
        activ_low,
    ) = kept
    sample, row_count, width = hidden.shape
    grad_low = d_middle.astype(jnp.bfloat16)
    g_w_proj = weight_grad(attended_low, grad_low)
    g_b_proj = row_sums(grad_low)
    d_att_low = back_dense(grad_low, w_proj).astype(jnp.bfloat16)
    query_rows = joined_low[:, :, :width]
    key_all, value_all = (
        lax.all_gather(kept_keys[0], "seq", axis=1, tiled=True),
        lax.all_gather(kept_keys[1], "seq", axis=1, tiled=True),
    )
    key_count = key_all.shape[1]
    scores = causal_scores(query_rows, key_all, row_start)
    attn_probs = jnp.exp(scores - log_total)
    probs_low = attn_probs.astype(jnp.bfloat16)
    q_heads = query_rows.reshape(sample, row_count, HEADS, HD)
    k_heads = key_all.reshape(sample, key_count, HEADS, HD)
    v_heads = value_all.reshape(sample, key_count, HEADS, HD)
    do_heads = d_att_low.reshape(sample, row_count, HEADS, HD)
    d_probs = jnp.einsum("srhd,sthd->shrt", do_heads, v_heads, preferred_element_type=jnp.float32)
    inner = jnp.sum(d_probs * attn_probs, axis=-1, keepdims=True)
    d_scores = (attn_probs * (d_probs - inner)).astype(jnp.bfloat16)
    scale = HD ** (-0.5)
    d_query = (
        jnp.einsum(
            "shrt,sthd->srhd", d_scores, k_heads, preferred_element_type=jnp.float32
        ).reshape(sample, row_count, width)
        * scale
    )
    d_key_all = (
        jnp.einsum(
            "shrt,srhd->sthd", d_scores, q_heads, preferred_element_type=jnp.float32
        ).reshape(sample, key_count, width)
        * scale
    )
    d_value_all = jnp.einsum(
        "shrt,srhd->sthd", probs_low, do_heads, preferred_element_type=jnp.float32
    ).reshape(sample, key_count, width)
    d_key, d_value = (
        lax.psum_scatter(
            d_key_all.astype(jnp.bfloat16), "seq", scatter_dimension=1, tiled=True
        ).astype(jnp.float32),
        lax.psum_scatter(
            d_value_all.astype(jnp.bfloat16), "seq", scatter_dimension=1, tiled=True
        ).astype(jnp.float32),
    )
    d_joined_low = jnp.concatenate([d_query, d_key, d_value], axis=-1).astype(jnp.bfloat16)
    g_w_qkv = weight_grad(normed_low, d_joined_low)
    g_b_query = row_sums(d_joined_low[:, :, :width])
    g_b_value = row_sums(d_joined_low[:, :, 2 * width :])
    d_normed = back_dense(d_joined_low, w_qkv)
    norm_pull = jax.vjp(layer_norm, hidden, ln1_gain, ln1_shift)[1]
    d_hidden_norm, g_ln1_gain, g_ln1_shift = norm_pull(d_normed)
    terms = (g_ln1_gain, g_ln1_shift, g_w_qkv, g_b_query, g_b_value, g_w_proj, g_b_proj)
    return (terms, d_middle + d_hidden_norm)


def add_terms(accum, terms):
    if accum is None:
        return terms
    return tuple((left_term + right_term for left_term, right_term in zip(accum, terms)))


def on_device(
    tokens,
    out_grad,
    section,
    lengths,
    ln1_gain,
    ln1_shift,
    w_qkv,
    b_query,
    b_value,
    w_proj,
    b_proj,
    ln2_gain,
    ln2_shift,
    w_fc,
    b_fc,
    w_out,
    b_out,
):
    params = (
        ln1_gain,
        ln1_shift,
        w_qkv,
        b_query,
        b_value,
        w_proj,
        b_proj,
        ln2_gain,
        ln2_shift,
        w_fc,
        b_fc,
        w_out,
        b_out,
    )
    sample, row_count, width = tokens.shape
    row_start = lax.axis_index("seq") * row_count
    passes = 2 * section + 1
    position = row_start + lax.broadcasted_iota(jnp.int32, (sample, row_count), 1)
    valid = (position < lengths[:, None]).astype(jnp.float32)
    local_count = jnp.sum(valid)
    hidden = tokens.astype(jnp.float32)
    kept_all = []
    for pass_index in range(MAXP):
        updated, kept = forward_pass(hidden, params, row_start)
        kept_all.append(kept)
        active = (pass_index < passes)[:, None, None]
        hidden = jnp.where(active, updated, hidden)
    mixed = hidden.astype(jnp.bfloat16)
    grad_rows = out_grad.astype(jnp.float32) * valid[:, :, None]
    ffn_acc = None
    attn_acc = None
    for pass_index in reversed(range(MAXP)):
        active_flag = (pass_index < passes).astype(jnp.float32)[:, None, None]
        layer_grad = grad_rows * active_flag
        ffn_terms, d_middle = ffn_back(kept_all[pass_index], layer_grad, params)
        ffn_acc = add_terms(ffn_acc, ffn_terms)
        attn_terms, d_hidden = attn_back(kept_all[pass_index], d_middle, params, row_start)
        attn_acc = add_terms(attn_acc, attn_terms)
        grad_rows = d_hidden + grad_rows * (1.0 - active_flag)
    summed = lax.psum(
        (
            attn_acc[0],
            attn_acc[1],
            attn_acc[2],
            attn_acc[3],
            attn_acc[4],
            attn_acc[5],
            attn_acc[6],
            ffn_acc[0],
            ffn_acc[1],
            ffn_acc[2],
            ffn_acc[3],
            ffn_acc[4],
            ffn_acc[5],
            local_count,
        ),
        ("grp", "seq"),
    )
    attn_sums = summed[0:7]
    ffn_sums = summed[7:13]
    token_total = summed[13]
    return (
        mixed,
        grad_rows / token_total,
        attn_sums[0] / token_total,
        attn_sums[1] / token_total,
        attn_sums[2] / token_total,
        attn_sums[3] / token_total,
        attn_sums[4] / token_total,
        attn_sums[5] / token_total,
        attn_sums[6] / token_total,
        ffn_sums[0] / token_total,
        ffn_sums[1] / token_total,
        ffn_sums[2] / token_total,
        ffn_sums[3] / token_total,
        ffn_sums[4] / token_total,
        ffn_sums[5] / token_total,
    )


BF = jnp.bfloat16
F32 = jnp.float32
MESH_ID = pl.DeviceIdType.MESH
NT = (((1,), (1,)), ((), ()))
TN = (((0,), (0,)), ((), ()))
NN = (((1,), (0,)), ((), ()))
RB = 256
WIDE = 768
HALF = 384
FF = 3072
LEN = 1024
VMEM_BYTES = 60 * 2**20


def mm(left, right, dims):
    return lax.dot_general(left, right, dims, preferred_element_type=F32)


def col_sum(v):
    return jnp.sum(v, axis=0, keepdims=True)


def center(v):
    mean = jnp.mean(v, axis=1, keepdims=True)
    diff = v - mean
    var = jnp.mean(diff * diff, axis=1, keepdims=True)
    return diff, lax.rsqrt(var + EPSILON)


def barrier(partners):
    sem = pltpu.get_barrier_semaphore()
    for seq_index in partners:
        pl.semaphore_signal(sem, inc=1, device_id={"seq": seq_index}, device_id_type=MESH_ID)
    pl.semaphore_wait(sem, len(partners))


def push(src, dst, sems, slot, seq_index):
    return pltpu.make_async_remote_copy(
        src_ref=src,
        dst_ref=dst,
        send_sem=sems.at[0, slot],
        recv_sem=sems.at[1, slot],
        device_id={"seq": seq_index},
        device_id_type=MESH_ID,
    )


def qkv_columns(core, part):
    return pl.ds(pl.multiple_of(part * WIDE + core * HALF, 128), HALF)


def gelu_and_slope(z):
    square = z * z
    t = jnp.tanh(z * (GELU_COEF + (GELU_COEF * 0.044715) * square))
    half = 0.5 + 0.5 * t
    rate = GELU_COEF + (GELU_COEF * 3 * 0.044715) * square
    return z * half, half + (0.5 * z) * (1.0 - t * t) * rate


def norm_back(v, grad, gain):
    diff, inv = center(v)
    xhat = diff * inv
    qv = grad * gain
    mean = jnp.mean(qv, axis=1, keepdims=True)
    cross = jnp.mean(qv * xhat, axis=1, keepdims=True)
    return inv * (qv - mean - xhat * cross), col_sum(grad * xhat), col_sum(grad)


def layer_kernel(
    tokens,
    out_grad,
    section,
    lengths,
    in_ln1_gain,
    in_ln1_shift,
    in_b_query,
    in_b_value,
    in_b_proj,
    in_ln2_gain,
    in_ln2_shift,
    in_b_out,
    in_b_fc,
    w_qkv,
    w_proj,
    w_fc,
    w_out,
    mixed,
    st_norm,
    st_own,
    st_norm2,
    st_act,
    st_e,
    st_dpre,
    st_f,
    st_dfused,
    g_out,
    dnorm2_out,
    sums,
    st_h,
    st_q,
    st_k,
    st_v,
    st_att,
    st_lse,
    st_mid,
    st_pre,
    wq,
    wp,
    wf,
    wo,
    tok,
    h,
    norm,
    q,
    k,
    v,
    att,
    own,
    lse,
    mid,
    norm2,
    pre,
    act,
    g,
    glow,
    dmid,
    datt_in,
    dfused,
    dk_acc,
    dv_acc,
    rows_in,
    b_fc,
    wsem,
    ssem,
    lsem,
    bsem,
    nsem,
    asem,
    dsem,
    psem,
    ysem,
):
    me = lax.axis_index("seq")
    core = lax.rem(me, 2)
    chip = me // 2
    partner = me + 1 - 2 * core
    across = lax.rem(me + 2, 4)
    half_lanes = pl.ds(pl.multiple_of(core * HALF, 128), HALF)
    passes = jnp.full((1, WIDE), 2 * section[chip] + 1, jnp.int32)
    length = jnp.full((1, WIDE), lengths[chip], jnp.int32)

    def is_active(p):
        return jnp.full((1, WIDE), p, jnp.int32) < passes

    keep = pltpu.make_async_copy(tokens.at[chip], tok.at[chip], wsem.at[6])
    keep.start()
    loads = [
        pltpu.make_async_copy(
            w_qkv.at[:, qkv_columns(core, third)],
            wq.at[:, pl.ds(third * HALF, HALF)],
            wsem.at[third],
        )
        for third in range(3)
    ]
    loads += [
        pltpu.make_async_copy(w_proj, wp, wsem.at[3]),
        pltpu.make_async_copy(w_fc, wf, wsem.at[4]),
        pltpu.make_async_copy(w_out, wo, wsem.at[5]),
    ]
    for load in loads:
        load.start()
    short = (
        in_ln1_gain,
        in_ln1_shift,
        in_b_query,
        in_b_value,
        in_b_proj,
        in_ln2_gain,
        in_ln2_shift,
        in_b_out,
    )
    for i, ref in enumerate(short):
        rows_in[i : i + 1] = ref[...].reshape(1, WIDE)
    b_fc[...] = in_b_fc[...].reshape(1, FF)
    ln1_gain, ln1_shift, b_query, b_value, b_proj, ln2_gain, ln2_shift, b_out = (
        rows_in.at[pl.ds(i, 1)] for i in range(8)
    )
    barrier((partner, across))
    give = push(tokens.at[1 - chip], tok.at[chip], ysem, 0, across)
    give.start()
    keep.wait()
    give.wait()
    og_keep = pltpu.make_async_copy(out_grad.at[chip], glow.at[chip], wsem.at[6])
    og_give = push(out_grad.at[1 - chip], glow.at[chip], ysem, 1, across)
    og_keep.start()
    og_give.start()
    for j in range(2):
        h[j] = tok[j].astype(F32)
    for load in loads:
        load.wait()

    def saves_of_ffn(p):
        return (
            pltpu.make_async_copy(pre, st_pre.at[p], ssem.at[9]),
            pltpu.make_async_copy(act, st_act.at[p], ssem.at[10]),
        )

    def forward_pass_step(p, carry):
        norm_send = []
        for j in range(2):
            diff, inv = center(h[j])
            norm[2 * j + core] = (diff * inv * ln1_gain[...] + ln1_shift[...]).astype(BF)
            copy = push(norm.at[2 * j + core], norm.at[2 * j + core], nsem, j, partner)
            copy.start()
            norm_send.append(copy)
        save_h = pltpu.make_async_copy(h, st_h.at[p], ssem.at[0])
        save_h.start()

        def project(block):
            rows = norm[block]
            out = mm(rows, wq[...], NN)
            q[block] = (out[:, :HALF] + b_query[:, half_lanes]).astype(BF)
            k[block] = out[:, HALF : 2 * HALF].astype(BF)
            v[block] = (out[:, 2 * HALF :] + b_value[:, half_lanes]).astype(BF)

        for j in range(2):
            project(2 * j + core)
        for j in range(2):
            norm_send[j].wait()
            project(2 * j + 1 - core)
        saves = [
            pltpu.make_async_copy(norm, st_norm.at[p], ssem.at[1]),
            pltpu.make_async_copy(q, st_q.at[p], ssem.at[2]),
            pltpu.make_async_copy(k, st_k.at[p], ssem.at[3]),
            pltpu.make_async_copy(v, st_v.at[p], ssem.at[4]),
        ]
        for save in saves:
            save.start()
        lane = lax.broadcasted_iota(jnp.int32, (RB, 128), 1)
        row = lax.broadcasted_iota(jnp.int32, (2 * RB, RB), 0) & (RB - 1)
        causal = lax.broadcasted_iota(jnp.int32, (2 * RB, RB), 1) <= row
        zero = jnp.zeros((RB, 128), BF)
        att_send = []
        for i in (3, 2, 0, 1):
            keys = (i + 1) * RB
            for pair in range(3):
                cs = slice(pair * 128, pair * 128 + 128)
                qi = q[i, :, cs] * jnp.asarray(HD**-0.5, BF)
                both = jnp.concatenate(
                    [jnp.where(lane < HD, qi, zero), jnp.where(lane < HD, zero, qi)], 0
                )
                k_all = k[0 : i + 1, :, cs].reshape(keys, 128)
                v_all = v[0 : i + 1, :, cs].reshape(keys, 128)
                s = mm(both, k_all, NT)
                last = jnp.where(causal, s[:, i * RB :], MASKED)
                s = jnp.concatenate([s[:, : i * RB], last], 1) if i else last
                peak = jnp.max(s, axis=1, keepdims=True)
                e = jnp.exp(s - peak).astype(BF)
                ol = mm(e, jnp.concatenate([v_all, jnp.ones((keys, 128), BF)], 1), NN)
                total = ol[:, 128:]
                o = ol[:, :128] / total
                att[i, :, cs] = jnp.where(lane < HD, o[:RB], o[RB:]).astype(BF)
                ls = peak + jnp.log(total)
                ls = jnp.concatenate([ls[:RB], ls[RB:]], 1).T
                lse[pair, 0:1, i * RB : (i + 1) * RB] = ls[0:1]
                lse[pair, 1:2, i * RB : (i + 1) * RB] = ls[128:129]
            if i == 3:
                saves[0].wait()
            copy = push(att.at[i], own.at[i // 2, core], asem, i // 2, partner)

            @pl.when(core == i % 2)
            def _():
                own[i // 2, core] = att[i]

            @pl.when(core != i % 2)
            def _():
                copy.start()

            if i in (2, 1):
                att_send.append(copy)
        save_att = pltpu.make_async_copy(att, st_att.at[p], ssem.at[1])
        save_lse = pltpu.make_async_copy(lse, st_lse.at[p], ssem.at[5])
        save_att.start()
        save_lse.start()
        for j, copy in ((1, att_send[0]), (0, att_send[1])):
            copy.wait()
            out = mm(own[j, 0], wp[0:HALF, :], NN) + mm(own[j, 1], wp[HALF:, :], NN)
            m = h[j] + out + b_proj[...]
            mid[j] = m
            diff, inv = center(m)
            norm2[j] = (diff * inv * ln2_gain[...] + ln2_shift[...]).astype(BF)
        save_rest = [
            pltpu.make_async_copy(own, st_own.at[p], ssem.at[6]),
            pltpu.make_async_copy(mid, st_mid.at[p], ssem.at[7]),
            pltpu.make_async_copy(norm2, st_norm2.at[p], ssem.at[8]),
        ]
        for save in save_rest:
            save.start()
        x = norm2[...].reshape(2 * RB, WIDE)

        @pl.when(p > 0)
        def _():
            for save in saves_of_ffn(p - 1):
                save.wait()

        for t in range(3):
            cs = slice(t * 1024, (t + 1) * 1024)
            z = mm(x, wf[:, cs], NN) + b_fc[:, cs]
            value, slope = gelu_and_slope(z)
            act[:, cs] = value.astype(BF)
            pre[:, cs] = slope.astype(BF)
        for save in saves_of_ffn(p):
            save.start()
        out = mm(act[...], wo[...], NN)
        active = is_active(p)
        save_h.wait()
        for j in range(2):
            new = mid[j] + out[j * RB : (j + 1) * RB] + b_out[...]
            h[j] = jnp.where(active, new, h[j])
        for save in saves[1:] + [save_att, save_lse] + save_rest:
            save.wait()
        return carry

    lax.fori_loop(0, MAXP, forward_pass_step, 0)
    for save in saves_of_ffn(MAXP - 1):
        save.wait()
    for j in range(2):
        tok[j] = h[j].astype(BF)
    mixed_keep = pltpu.make_async_copy(tok.at[chip], mixed.at[chip], wsem.at[7])
    mixed_give = push(tok.at[1 - chip], mixed.at[chip], ysem, 2, across)
    mixed_keep.start()
    mixed_give.start()

    kept = {
        "pre": (st_pre, pre),
        "mid": (st_mid, mid),
        "q": (st_q, q),
        "k": (st_k, k),
        "v": (st_v, v),
        "att": (st_att, att),
        "lse": (st_lse, lse),
        "h": (st_h, h),
    }

    def fetch(p, name):
        src, dst = kept[name]
        return pltpu.make_async_copy(src.at[p], dst, lsem.at[list(kept).index(name)])

    fetch(MAXP - 1, "h").start()
    og_keep.wait()
    og_give.wait()
    sums[...] = jnp.zeros_like(sums)
    for j in range(2):
        pos = (2 * j + core) * RB + lax.broadcasted_iota(jnp.int32, (RB, WIDE), 0)
        g[j] = jnp.where(pos < length, glow[j].astype(F32), 0.0)

    def saves_of(p):
        return (
            pltpu.make_async_copy(glow, st_e.at[p], bsem.at[0]),
            pltpu.make_async_copy(act, st_dpre.at[p], bsem.at[1]),
            pltpu.make_async_copy(norm2, st_f.at[jnp.maximum(p - 1, 0)], bsem.at[2]),
            pltpu.make_async_copy(dfused, st_dfused.at[jnp.maximum(p - 1, 0)], bsem.at[3]),
        )

    def feed_forward_back(p, active, arrive):
        for j in range(2):
            glow[j] = jnp.where(active, g[j], 0.0).astype(BF)
        e = glow[...].reshape(2 * RB, WIDE)
        arrive("pre")
        for t in range(3):
            cs = slice(t * 1024, (t + 1) * 1024)
            dact = mm(e, wo[cs, :], NT)
            act[:, cs] = (dact * pre[:, cs].astype(F32)).astype(BF)
        return mm(act[...], wf[...], NT)

    def backward_pass_step(step, carry):
        p = MAXP - 1 - step

        def arrive(*names):
            @pl.when(step > 0)
            def _():
                for name in names:
                    fetch(p, name).wait()

        def prefetch(*names):
            for name in names:
                if name == "pre":
                    fetch(p - 1, name).start()
                else:

                    @pl.when(p > 1)
                    def _(name=name):
                        fetch(p - 1, name).start()

        active = is_active(p)

        @pl.when(step > 0)
        def _():
            for save in saves_of(p + 1)[:3]:
                save.wait()

        dnorm2 = feed_forward_back(p, active, arrive)
        arrive("mid")
        for j in range(2):
            d = dnorm2[j * RB : (j + 1) * RB]
            dv_in, dgain, dshift = norm_back(mid[j], d, ln2_gain[...])
            sums[3:4] += dgain
            sums[4:5] += dshift
            dm = jnp.where(active, g[j], 0.0) + dv_in
            dmid[j] = dm
            low = dm.astype(BF)
            norm2[j] = low
        da = mm(norm2[...].reshape(2 * RB, WIDE), wp[...], NT).astype(BF)
        for half in range(2):
            for j in range(2):
                own[half, j] = da[j * RB : (j + 1) * RB, half * HALF : (half + 1) * HALF]
        datt_send = []
        for j in range(2):
            copy = push(
                own.at[1 - core, j], datt_in.at[2 * j + core], dsem, j, partner
            )
            copy.start()
            datt_send.append(copy)
            datt_in[2 * j + core] = own[core, j]
        for save in saves_of(p)[:3]:
            save.start()
        prefetch("pre", "mid")

        @pl.when(step > 0)
        def _():
            saves_of(p + 1)[3].wait()

        arrive("q", "k", "v", "att", "lse")
        for copy in datt_send:
            copy.wait()
        lane = lax.broadcasted_iota(jnp.int32, (RB, 128), 1)
        zero = jnp.zeros((RB, 128), BF)
        col = lax.broadcasted_iota(jnp.int32, (RB, 2 * RB), 1) & (RB - 1)
        causal = lax.broadcasted_iota(jnp.int32, (RB, 2 * RB), 0) <= col
        sub = lax.broadcasted_iota(jnp.int32, (128, LEN), 0)
        zero_t = jnp.zeros((128, LEN), BF)
        scale = jnp.asarray(HD**-0.5, BF)

        def split(rows):
            return jnp.concatenate(
                [jnp.where(lane < HD, rows, zero), jnp.where(lane < HD, zero, rows)], 0
            )

        def one_pair(pair, carry):
            start = pl.multiple_of(pair * 128, 128)
            cs = pl.ds(start, 128)
            slot = 0
            k_t = k[:, :, cs].reshape(LEN, 128).T
            k_low = jnp.where(sub < HD, k_t, zero_t)
            k_high = jnp.where(sub < HD, zero_t, k_t)
            for i in (3, 2, 1, 0):
                keys = (i + 1) * RB
                rs = slice(i * RB, (i + 1) * RB)
                qm = split(q[i, :, cs] * scale)
                do = datt_in[i, :, cs]
                dm = split(do)
                inner = (do.astype(F32) * att[i, :, cs].astype(F32)).T
                inner = jnp.concatenate([col_sum(inner[:HD]), col_sum(inner[HD:])], 1)
                total = jnp.concatenate([lse[pair, 0:1, rs], lse[pair, 1:2, rs]], 1)
                s = mm(k[0 : i + 1, :, cs].reshape(keys, 128), qm, NT)
                dp = mm(v[0 : i + 1, :, cs].reshape(keys, 128), dm, NT)
                last = jnp.where(causal, s[i * RB :], MASKED)
                s = jnp.concatenate([s[: i * RB], last], 0) if i else last
                prob = jnp.exp(s - total)
                ds = (prob * (dp - inner)).astype(BF)
                dv = mm(prob.astype(BF), dm, NN)
                dk = mm(ds, qm, NN)
                if i == 3:
                    dv_acc[slot] = dv
                    dk_acc[slot] = dk
                else:
                    dv_acc[slot, 0:keys] += dv
                    dk_acc[slot, 0:keys] += dk
                dq = mm(k_low[:, :keys], ds[:, :RB], NN) + mm(k_high[:, :keys], ds[:, RB:], NN)
                dfused[i, :, cs] = (dq.T * HD**-0.5).astype(BF)
            ks = pl.ds(pl.multiple_of(HALF + pair * 128, 128), 128)
            vs = pl.ds(pl.multiple_of(2 * HALF + pair * 128, 128), 128)
            dfused[:, :, ks] = dk_acc[slot].astype(BF).reshape(4, RB, 128)
            dfused[:, :, vs] = dv_acc[slot].astype(BF).reshape(4, RB, 128)
            return carry

        lax.fori_loop(0, 3, one_pair, 0)
        part_send = []
        for j in range(2):
            block = 2 * j + 1 - core
            norm[j] = mm(dfused[block], wq[...], NT).astype(BF)
            copy = push(norm.at[j], norm.at[2 + j], psem, j, partner)
            copy.start()
            part_send.append(copy)
        saves_of(p)[3].start()
        prefetch("q", "k", "v", "att", "lse")
        mine = [mm(dfused[2 * j + core], wq[...], NT) for j in range(2)]
        fetch(p, "h").wait()
        for j in range(2):
            part_send[j].wait()
            d = mine[j] + norm[2 + j].astype(F32)
            dv_in, dgain, dshift = norm_back(h[j], d, ln1_gain[...])
            sums[0:1] += dgain
            sums[1:2] += dshift
            g[j] = dmid[j] + dv_in + jnp.where(active, 0.0, g[j])
        prefetch("h")
        return carry

    lax.fori_loop(0, MAXP - 1, backward_pass_step, 0)
    for save in saves_of(1):
        save.wait()
    dnorm2 = feed_forward_back(0, is_active(0), lambda name: fetch(0, name).wait())
    last = list(saves_of(0)[:2])
    for save in last:
        save.start()
    for j in range(2):
        mid[j] = dnorm2[j * RB : (j + 1) * RB]
    sums[6:7] = jnp.where(core == 0, length.astype(F32), jnp.zeros((1, WIDE), F32))
    done = pltpu.make_async_copy(g, g_out, bsem.at[2])
    done.start()
    done_dnorm2 = pltpu.make_async_copy(mid, dnorm2_out, bsem.at[3])
    done_dnorm2.start()
    for save in last:
        save.wait()
    done_dnorm2.wait()
    mixed_keep.wait()
    mixed_give.wait()
    done.wait()


def shape(dims, kind=BF):
    return jax.ShapeDtypeStruct(dims, kind)


def layer_call(*operands):
    vmem = pl.BlockSpec(memory_space=pltpu.VMEM)
    smem = pl.BlockSpec(memory_space=pltpu.SMEM)
    hbm = pl.BlockSpec(memory_space=pl.ANY)
    outs = (
        shape((2, RB, WIDE)),
        shape((MAXP, 4, RB, WIDE)),
        shape((MAXP, 2, 2, RB, HALF)),
        shape((MAXP, 2, RB, WIDE)),
        shape((MAXP, 2 * RB, FF)),
        shape((MAXP, 2, RB, WIDE)),
        shape((MAXP, 2 * RB, FF)),
        shape((MAXP - 1, 2, RB, WIDE)),
        shape((MAXP - 1, 4, RB, 3 * HALF)),
        shape((2, RB, WIDE), F32),
        shape((2, RB, WIDE), F32),
        shape((16, WIDE), F32),
        shape((MAXP, 2, RB, WIDE), F32),
        shape((MAXP, 4, RB, HALF)),
        shape((MAXP, 4, RB, HALF)),
        shape((MAXP, 4, RB, HALF)),
        shape((MAXP, 4, RB, HALF)),
        shape((MAXP, 3, 2, LEN), F32),
        shape((MAXP, 2, RB, WIDE), F32),
        shape((MAXP, 2 * RB, FF)),
    )
    scratch = [
        pltpu.VMEM((WIDE, 3 * HALF), BF),
        pltpu.VMEM((WIDE, WIDE), BF),
        pltpu.VMEM((WIDE, FF), BF),
        pltpu.VMEM((FF, WIDE), BF),
        pltpu.VMEM((2, RB, WIDE), BF),
        pltpu.VMEM((2, RB, WIDE), F32),
        pltpu.VMEM((4, RB, WIDE), BF),
        pltpu.VMEM((4, RB, HALF), BF),
        pltpu.VMEM((4, RB, HALF), BF),
        pltpu.VMEM((4, RB, HALF), BF),
        pltpu.VMEM((4, RB, HALF), BF),
        pltpu.VMEM((2, 2, RB, HALF), BF),
        pltpu.VMEM((3, 2, LEN), F32),
        pltpu.VMEM((2, RB, WIDE), F32),
        pltpu.VMEM((2, RB, WIDE), BF),
        pltpu.VMEM((2 * RB, FF), BF),
        pltpu.VMEM((2 * RB, FF), BF),
        pltpu.VMEM((2, RB, WIDE), F32),
        pltpu.VMEM((2, RB, WIDE), BF),
        pltpu.VMEM((2, RB, WIDE), F32),
        pltpu.VMEM((4, RB, HALF), BF),
        pltpu.VMEM((4, RB, 3 * HALF), BF),
        pltpu.VMEM((2, LEN, 128), F32),
        pltpu.VMEM((2, LEN, 128), F32),
        pltpu.VMEM((8, WIDE), F32),
        pltpu.VMEM((1, FF), F32),
        pltpu.SemaphoreType.DMA((8,)),
        pltpu.SemaphoreType.DMA((11,)),
        pltpu.SemaphoreType.DMA((8,)),
        pltpu.SemaphoreType.DMA((4,)),
        pltpu.SemaphoreType.DMA((2, 2)),
        pltpu.SemaphoreType.DMA((2, 2)),
        pltpu.SemaphoreType.DMA((2, 2)),
        pltpu.SemaphoreType.DMA((2, 2)),
        pltpu.SemaphoreType.DMA((2, 3)),
    ]
    return pl.pallas_call(
        layer_kernel,
        out_shape=outs,
        in_specs=[hbm] * 2 + [smem] * 2 + [vmem] * 9 + [hbm] * 4,
        out_specs=(hbm,) * 11 + (vmem,) + (hbm,) * 8,
        scratch_shapes=scratch,
        compiler_params=pltpu.CompilerParams(
            collective_id=1, has_side_effects=True, vmem_limit_bytes=VMEM_BYTES
        ),
        name="layer",
    )(*operands)


CHUNKS = 6
SIDE = 768
ROUTES = (
    "yxzw", "xzyw", "yxzw", "xyzw", "zwyx", "yxzw", "yxzw", "zxyw", "xyzw", "zxyw", "xyzw",
    "yxzw",
)
ORDER = (
    ("P", 0), ("L",), ("O", 0), ("S", 0, 0, 0), ("S", 0, 1, 0), ("P", 1), ("O", 1),
    ("S", 1, 0, 0), ("S", 1, 1, 0), ("P", 2), ("S", 0, 0, 1), ("S", 0, 1, 1), ("O", 2),
    ("S", 2, 0, 0), ("S", 2, 1, 0), ("P", 3), ("S", 0, 1, 2), ("S", 1, 0, 1), ("S", 1, 1, 1),
    ("O", 3), ("S", 0, 0, 2), ("S", 3, 0, 0), ("S", 3, 1, 0), ("A",), ("S", 0, 1, 3),
    ("S", 0, 0, 3), ("S", 1, 0, 2), ("S", 1, 1, 2), ("S", 2, 0, 1), ("S", 2, 1, 1),
    ("S", 3, 1, 1), ("D",), ("S", 3, 0, 1), ("P", 4), ("N",), ("S", 1, 0, 3), ("S", 1, 1, 3),
    ("S", 2, 1, 2), ("S", 0, 1, 4), ("S", 0, 0, 4), ("O", 4), ("S", 3, 1, 2), ("S", 2, 0, 2),
    ("S", 4, 0, 0), ("S", 4, 1, 0), ("O", 5), ("V",), ("S", 2, 1, 3), ("S", 3, 0, 2),
    ("S", 5, 0, 0), ("S", 5, 1, 0), ("S", 1, 0, 4), ("S", 1, 1, 4), ("S", 0, 0, 5),
    ("S", 0, 1, 5), ("S", 3, 1, 3), ("S", 4, 0, 1), ("S", 4, 1, 1), ("S", 2, 0, 3),
    ("S", 2, 1, 4), ("S", 3, 0, 3), ("S", 1, 0, 5), ("S", 1, 1, 5), ("S", 0, 0, 6),
    ("S", 5, 0, 1), ("S", 5, 1, 1), ("S", 3, 1, 4), ("S", 2, 1, 5), ("S", 0, 1, 6),
    ("S", 3, 0, 4), ("S", 4, 1, 2), ("S", 1, 0, 6), ("S", 1, 1, 6), ("S", 4, 0, 2),
    ("S", 2, 0, 4), ("S", 3, 1, 5), ("S", 0, 0, 7), ("S", 2, 1, 6), ("S", 5, 0, 2),
    ("S", 4, 1, 3), ("S", 5, 1, 2), ("S", 0, 1, 7), ("S", 3, 0, 5), ("S", 4, 0, 3),
    ("S", 1, 0, 7), ("S", 5, 0, 3), ("S", 1, 1, 7), ("S", 4, 1, 4), ("S", 5, 1, 3),
    ("S", 2, 0, 5), ("S", 4, 0, 4), ("S", 5, 0, 4), ("S", 2, 1, 7), ("S", 0, 0, 8),
    ("S", 3, 1, 6), ("S", 5, 1, 4), ("S", 0, 1, 8), ("S", 4, 0, 5), ("S", 3, 0, 6),
    ("S", 5, 0, 5), ("S", 4, 1, 5), ("S", 1, 0, 8), ("S", 5, 1, 5), ("S", 4, 0, 6),
    ("S", 2, 0, 6), ("S", 1, 1, 8), ("S", 5, 0, 6), ("S", 5, 1, 6), ("S", 3, 1, 7),
    ("S", 2, 1, 8), ("S", 3, 0, 7), ("S", 4, 1, 6), ("S", 2, 0, 7), ("S", 4, 0, 7),
    ("S", 5, 1, 7), ("S", 3, 1, 8), ("S", 4, 1, 7), ("S", 5, 0, 7), ("S", 2, 0, 8),
    ("S", 4, 0, 8), ("S", 3, 0, 8), ("S", 4, 1, 8), ("S", 5, 0, 8), ("S", 5, 1, 8),
)


def mesh_push(src, dst, send, recv, where):
    return pltpu.make_async_remote_copy(
        src_ref=src,
        dst_ref=dst,
        send_sem=send,
        recv_sem=recv,
        device_id=where,
        device_id_type=MESH_ID,
    )


def grad_kernel(
    act,
    e,
    norm2,
    dpre,
    own,
    f,
    norm,
    dfused_st,
    st_q,
    st_k,
    st_v,
    st_att,
    st_lse,
    st_mid,
    st_h,
    g_in,
    dnorm2_in,
    w_qkv,
    w_proj,
    section,
    ln1_gain,
    ln2_gain,
    vec,
    o_qkv,
    o_proj,
    o_fc,
    o_out,
    o_tok,
    o_vec,
    wq,
    wp,
    q,
    k,
    v,
    att,
    lse,
    mid,
    h,
    g,
    dn2,
    datt,
    datt_in,
    f0,
    dfused,
    dk_acc,
    dv_acc,
    part,
    part_in,
    slots,
    give,
    got,
    work,
    rx,
    tok_low,
    vsend,
    vgot,
    lsem,
    slsem,
    dsem,
    psem,
    csem,
    xsem,
    rsem,
    vsem,
    ysem,
    osem,
):
    me = lax.axis_index("seq")
    group = lax.axis_index("grp")
    core = lax.rem(me, 2)
    y = me // 2
    x = lax.rem(group, 2)
    z = group // 2
    other = 1 - core
    to_core = {"seq": me + 1 - 2 * core}
    to_y = {"seq": lax.rem(me + 2, 4)}
    to_x = {"grp": group + 1 - 2 * x}

    def to_z_pair(step):
        low = lax.rem(z // step, 2)
        return {"grp": (z + step - 2 * step * low) * 2 + x}

    partner = me + 1 - 2 * core
    passes = jnp.full((1, WIDE), 2 * section[y] + 1, jnp.int32)
    active = jnp.full((1, WIDE), 0, jnp.int32) < passes

    kept = {
        "mid": (st_mid.at[0], mid),
        "g": (g_in, g),
        "dnorm2": (dnorm2_in, dn2),
        "wp": (w_proj, wp),
        "q": (st_q.at[0], q),
        "k": (st_k.at[0], k),
        "v": (st_v.at[0], v),
        "att": (st_att.at[0], att),
        "lse": (st_lse.at[0], lse),
        "h": (st_h.at[0], h),
    }
    for third in range(3):
        kept["wq%d" % third] = (
            w_qkv.at[:, qkv_columns(core, third)],
            wq.at[:, pl.ds(third * HALF, HALF)],
        )

    def kept_copy(name):
        src, dst = kept[name]
        return pltpu.make_async_copy(src, dst, lsem.at[list(kept).index(name)])

    def arrive(*names):
        for name in names:
            kept_copy(name).wait()

    def whole(src):
        return [(src.at[p], (p, slice(None))) for p in range(MAXP)]

    def piece(src, owner, i):
        cols = pl.ds(pl.multiple_of(owner * 2 * SIDE + i * SIDE, 128), SIDE)
        return [(src.at[p, :, :, cols], (p, slice(None))) for p in range(MAXP)]

    def own_rows():
        return [
            (own.at[p, :, half], (p, slice(None), slice(None), pl.ds(half * HALF, HALF)))
            for p in range(MAXP)
            for half in range(2)
        ]

    def f_rows():
        return [(f0, (0, slice(None)))] + [(f.at[p - 1], (p, slice(None))) for p in (1, 2)]

    def dfused_at(p, blocks, cols):
        src = dfused if p == 0 else dfused_st.at[p - 1]
        return src.at[blocks, :, cols]

    def dq_rows():
        return [
            (
                dfused_at(p, pl.ds(2 * i, 2), pl.ds(0, HALF)),
                (p, slice(None), slice(None), pl.ds(i * HALF, HALF)),
            )
            for p in range(MAXP)
            for i in range(2)
        ]

    def kv_rows(i):
        return [
            (dfused_at(p, pl.ds(2 * i, 2), pl.ds(HALF, 2 * HALF)), (p, slice(None)))
            for p in range(MAXP)
        ]

    def norm_rows(i):
        return [(norm.at[p, pl.ds(2 * i, 2)], (p, slice(None))) for p in range(MAXP)]

    other = 1 - core
    operands = {
        "e": (0, lambda: whole(e)),
        "act0": (1, lambda: piece(act, other, 0)),
        "act1": (2, lambda: piece(act, core, 0)),
        "act2": (3, lambda: piece(act, other, 1)),
        "act3": (4, lambda: piece(act, core, 1)),
        "norm2": (1, lambda: whole(norm2)),
        "dpre0": (2, lambda: piece(dpre, other, 0)),
        "dpre1": (3, lambda: piece(dpre, core, 0)),
        "dpre2": (0, lambda: piece(dpre, other, 1)),
        "dpre3": (4, lambda: piece(dpre, core, 1)),
        "own": (2, own_rows),
        "f": (3, f_rows),
        "norm_a": (0, lambda: norm_rows(0)),
        "norm_b": (1, lambda: norm_rows(1)),
        "dq": (4, dq_rows),
        "kv_a": (2, lambda: kv_rows(0)),
        "kv_b": (3, lambda: kv_rows(1)),
    }

    def operand_copies(name):
        slot, copies = operands[name]
        return [
            pltpu.make_async_copy(src, slots.at[(slot, *place)], slsem.at[slot, i])
            for i, (src, place) in enumerate(copies())
        ]

    def begin(*names):
        for name in names:
            for copy in operand_copies(name):
                copy.start()

    def ready(name):
        for copy in operand_copies(name):
            copy.wait()

    def operand(name):
        return slots[operands[name][0]].reshape(MAXP * 2 * RB, SIDE)

    begin("e", "act0", "act1")
    for name in ("mid", "g", "dnorm2", "wp"):
        kept_copy(name).start()
    begin("act2", "act3")
    for name in ("q", "k", "v", "att", "lse", "h", "wq0", "wq1", "wq2"):
        kept_copy(name).start()

    sem = pltpu.get_barrier_semaphore()
    partners = [to_core, to_y, to_x, to_z_pair(1), to_z_pair(2)]
    for where in partners:
        pl.semaphore_signal(sem, inc=1, device_id=where, device_id_type=MESH_ID)
    pl.semaphore_wait(sem, len(partners))

    tok_give = mesh_push(tok_low.at[1 - y], o_tok.at[y], ysem.at[0], ysem.at[1], to_y)
    tok_keep = pltpu.make_async_copy(tok_low.at[y], o_tok.at[y], osem.at[2 * CHUNKS])

    def datt_copy(j):
        return push(datt.at[other, j], datt_in.at[2 * j + core], dsem, j, partner)

    def part_copy(j):
        return push(part.at[j], part_in.at[j], psem, j, partner)

    vec_to = [to_core, to_x, to_y, to_z_pair(1), to_z_pair(2)]

    def vec_copy(k):
        return mesh_push(vsend.at[k], vgot.at[k], vsem.at[0, k], vsem.at[1, k], vec_to[k])

    vsend[0] = vec[...]

    def vec_row(row, v):
        vsend[0, pl.ds(row, 1), :] += v

    def pass_sum(name, p, cols=slice(None)):
        rows_of = slots[operands[name][0], p].astype(F32).reshape(2 * RB, SIDE)
        return col_sum(rows_of)[:, cols]

    def half_row(row, v):
        blank = jnp.zeros((1, HALF), F32)
        vec_row(
            row,
            jnp.concatenate(
                [jnp.where(core == 0, v, blank), jnp.where(core == 0, blank, v)], 1
            ),
        )

    def vec_step(k):
        vec_copy(k).wait()
        vsend[k + 1] = vsend[k] + vgot[k]
        if k < 4:
            vec_copy(k + 1).start()

    def tiles(lefts, rights, cols, emit, also=None):
        def tile(m, carry):
            here = pl.ds(pl.multiple_of(m * 256, 256), 256)
            out = None
            for left, right in zip(lefts, rights):
                left_part = slots[operands[left][0], :, :, :, here].reshape(MAXP * 2 * RB, 256)
                width = SIDE if right[1] is None else HALF
                right_cols = cols if right[1] is None else right[1]
                right_part = slots[operands[right[0]][0], :, :, :, right_cols]
                part_out = mm(left_part, right_part.reshape(MAXP * 2 * RB, width), TN)
                out = part_out if out is None else out + part_out
            emit(m, here, out)
            if also is not None:
                also(m)
            return carry

        lax.fori_loop(0, SIDE // 256, tile, 0)

    def product(n, place, emit):
        owner = core if place else other
        every = slice(None)
        if n < 4:
            name = ("act%d" if n < 2 else "dpre%d") % (2 * (n % 2) + place)
            if n in (0, 2) and place == 0:
                ready("e" if n == 0 else "norm2")
            ready(name)
            if n < 2:
                also = None
                if n == 0 and place == 0:
                    also = lambda m: vec_row(5, pass_sum("e", m))
                tiles((name,), (("e", None),), every, emit, also)
            else:
                also = lambda m: vec_row(8 + owner * 2 + n - 2, pass_sum(name, m))
                tiles(("norm2",), ((name, None),), every, emit, also)
            return
        if place == 0:
            ready("own")
            ready("f")
        also = (lambda m: vec_row(2, pass_sum("f", m))) if place == 0 else None
        cols = pl.ds(pl.multiple_of(owner * HALF, 128), HALF)
        tiles(("own",), (("f", cols),), every, emit, also)

    def core_copy(n):
        width = SIDE if n < 4 else HALF
        return mesh_push(
            give.at[n % 2, :, pl.ds(0, width)],
            got.at[n % 2, :, pl.ds(0, width)],
            csem.at[0, n],
            csem.at[1, n],
            to_core,
        )

    follow = {
        (0, 0): ("norm2",),
        (0, 1): ("dpre0",),
        (1, 0): ("dpre1",),
        (1, 1): ("dpre2", "dpre3"),
        (2, 0): ("own",),
        (2, 1): ("f",),
        (3, 0): ("norm_a",),
        (3, 1): ("norm_b",),
    }

    def theirs(n):
        if n >= 2:
            core_copy(n - 2).wait_send()

        def emit(m, here, out):
            if n < 4:
                give[n % 2, here] = out.astype(BF)
            else:
                give[n % 2, here, 0:HALF] = out.astype(BF)

        product(n, 0, emit)
        core_copy(n).start()
        begin(*follow.get((n, 0), ()))

    def ours(n):
        if n < 4:
            def emit(m, here, out):
                @pl.when(m == 0)
                def _():
                    core_copy(n).wait_recv()

                out = (out + got[n % 2, here].astype(F32)).astype(BF)
                work[n, 0, here] = out[:, :HALF]
                work[n, 1, here] = out[:, HALF:]

            product(n, 1, emit)
            begin(*follow.get((n, 1), ()))
        elif n == 4:

            def emit_proj(m, here, out):
                work[n, 0, here] = (out + got[n % 2, here, 0:HALF].astype(F32)).astype(BF)

            def emit_dq(m, here, out):
                work[n, 1, here] = out.astype(BF)

            core_copy(n).wait_recv()
            product(n, 1, emit_proj)
            begin("kv_a", "kv_b")
            ready("dq")
            ready("norm_a")
            ready("norm_b")

            def dq_sum(m):
                both = pass_sum("dq", m)
                half_row(12, both[:, :HALF] + both[:, HALF:])

            halves = (("dq", slice(0, HALF)), ("dq", slice(HALF, SIDE)))
            tiles(("norm_a", "norm_b"), halves, None, emit_dq, dq_sum)
        else:

            def emit_kv(m, here, out):
                out = out.astype(BF)
                work[n, 0, here] = out[:, :HALF]
                work[n, 1, here] = out[:, HALF:]

            ready("kv_a")
            ready("kv_b")

            def dv_sum(m):
                half_row(13, (pass_sum("kv_a", m) + pass_sum("kv_b", m))[:, HALF:])

            both = (("kv_a", None), ("kv_b", None))
            tiles(("norm_a", "norm_b"), both, slice(None), emit_kv, dv_sum)

    def leave():
        arrive("mid", "g", "dnorm2")
        for j in range(2):
            d = dn2[j]
            dv_in, dgain, dshift = norm_back(mid[j], d, ln2_gain[...].reshape(1, WIDE))
            vsend[0, 3:4] += dgain
            vsend[0, 4:5] += dshift
            dm = jnp.where(active, g[j], 0.0) + dv_in
            mid[j] = dm
            low = dm.astype(BF)
            f0[j] = low
        arrive("wp")
        da = mm(f0[...].reshape(2 * RB, WIDE), wp[...], NT).astype(BF)
        for half in range(2):
            for j in range(2):
                datt[half, j] = da[j * RB : (j + 1) * RB, half * HALF : (half + 1) * HALF]
        for j in range(2):
            datt_copy(j).start()
            datt_in[2 * j + core] = datt[core, j]

    def attend_back():
        arrive("q", "k", "v", "att", "lse")
        for j in range(2):
            datt_copy(j).wait()
        lane = lax.broadcasted_iota(jnp.int32, (RB, 128), 1)
        zero = jnp.zeros((RB, 128), BF)
        col = lax.broadcasted_iota(jnp.int32, (RB, 2 * RB), 1) & (RB - 1)
        causal = lax.broadcasted_iota(jnp.int32, (RB, 2 * RB), 0) <= col
        sub = lax.broadcasted_iota(jnp.int32, (128, LEN), 0)
        zero_t = jnp.zeros((128, LEN), BF)
        scale = jnp.asarray(HD**-0.5, BF)

        def split(rows):
            return jnp.concatenate(
                [jnp.where(lane < HD, rows, zero), jnp.where(lane < HD, zero, rows)], 0
            )

        def one_pair(pair, carry):
            cs = pl.ds(pl.multiple_of(pair * 128, 128), 128)
            slot = 0
            k_t = k[:, :, cs].reshape(LEN, 128).T
            k_low = jnp.where(sub < HD, k_t, zero_t)
            k_high = jnp.where(sub < HD, zero_t, k_t)
            for i in (3, 2, 1, 0):
                keys = (i + 1) * RB
                rs = slice(i * RB, (i + 1) * RB)
                qm = split(q[i, :, cs] * scale)
                do = datt_in[i, :, cs]
                dm = split(do)
                inner = (do.astype(F32) * att[i, :, cs].astype(F32)).T
                inner = jnp.concatenate([col_sum(inner[:HD]), col_sum(inner[HD:])], 1)
                total = jnp.concatenate([lse[pair, 0:1, rs], lse[pair, 1:2, rs]], 1)
                s = mm(k[0 : i + 1, :, cs].reshape(keys, 128), qm, NT)
                dp = mm(v[0 : i + 1, :, cs].reshape(keys, 128), dm, NT)
                last = jnp.where(causal, s[i * RB :], MASKED)
                s = jnp.concatenate([s[: i * RB], last], 0) if i else last
                prob = jnp.exp(s - total)
                ds = (prob * (dp - inner)).astype(BF)
                dv = mm(prob.astype(BF), dm, NN)
                dk = mm(ds, qm, NN)
                if i == 3:
                    dv_acc[slot] = dv
                    dk_acc[slot] = dk
                else:
                    dv_acc[slot, 0:keys] += dv
                    dk_acc[slot, 0:keys] += dk
                dq = mm(k_low[:, :keys], ds[:, :RB], NN) + mm(k_high[:, :keys], ds[:, RB:], NN)
                dfused[i, :, cs] = (dq.T * HD**-0.5).astype(BF)
            ks = pl.ds(pl.multiple_of(HALF + pair * 128, 128), 128)
            vs = pl.ds(pl.multiple_of(2 * HALF + pair * 128, 128), 128)
            dfused[:, :, ks] = dk_acc[slot].astype(BF).reshape(4, RB, 128)
            dfused[:, :, vs] = dv_acc[slot].astype(BF).reshape(4, RB, 128)
            return carry

        lax.fori_loop(0, 3, one_pair, 0)

    def dense_back():
        arrive("wq0", "wq1", "wq2")
        for j in range(2):
            block = 2 * j + 1 - core
            part[j] = mm(dfused[block], wq[...], NT).astype(BF)
            part_copy(j).start()

    def tokens_back():
        mine = [mm(dfused[2 * j + core], wq[...], NT) for j in range(2)]
        arrive("h")
        for j in range(2):
            part_copy(j).wait()
            d = mine[j] + part_in[j].astype(F32)
            dv_in, dgain, dshift = norm_back(h[j], d, ln1_gain[...].reshape(1, WIDE))
            vsend[0, 0:1] += dgain
            vsend[0, 1:2] += dshift
            tok_low[j] = (mid[j] + dv_in + jnp.where(active, 0.0, g[j])).astype(BF)
        tok_give.start()
        tok_keep.start()

    def rows(start, size):
        return pl.ds(pl.multiple_of(start, 16), size)

    bits = {"x": x, "y": y, "z": lax.rem(z, 2), "w": z // 2}
    pair_of = {"x": to_x, "y": to_y, "z": to_z_pair(1), "w": to_z_pair(2)}

    def first_row(n, s, k):
        row = 0
        for i, name in enumerate(ROUTES[2 * n + s][:k]):
            row = row + bits[name] * (SIDE >> (i + 1))
        return row

    def received(sub, k):
        size = SIDE >> (k + 1)
        return rx.at[sub, pl.ds(SIDE - 2 * size, size)]

    def step_copies(n, s, k):
        route = ROUTES[2 * n + s]
        sub = 2 * n + s

        def copy(src, dst, where):
            return mesh_push(src, dst, xsem.at[sub, k], rsem.at[sub, k], where)

        if k < 4:
            size = SIDE >> (k + 1)
            row = first_row(n, s, k) + (1 - bits[route[k]]) * size
            return [copy(work.at[n, s, rows(row, size)], received(sub, k), pair_of[route[k]])]
        if n < 2:
            out, start, col = o_out, core * 2 * SIDE + n * SIDE, s * HALF
        elif n < 4:
            out, start, col = o_fc, 0, core * 2 * SIDE + (n - 2) * SIDE + s * HALF
        elif n == 4 and s == 0:
            out, start, col = o_proj, 0, core * HALF
        else:
            out, start, col = o_qkv, 0, (0 if n == 4 else 1 + s) * WIDE + core * HALF
        left = 8 - k
        size = SIDE >> left
        row = first_row(n, s, left)
        dst = out.at[rows(start + row, size), pl.ds(pl.multiple_of(col, 128), HALF)]
        if k == 4:
            src = work.at[n, s, rows(row, size)]
            return [copy(src, dst, pair_of[route[3]]), pltpu.make_async_copy(src, dst, osem.at[sub])]
        return [copy(dst, dst, to_core if k == 8 else pair_of[route[left - 1]])]

    def advance(n, s, k):
        if k > 0:
            for copy in step_copies(n, s, k - 1):
                copy.wait()
        if 0 < k < 5:
            sub = 2 * n + s
            size = SIDE >> k
            here = rows(first_row(n, s, k), size)
            more = rx[sub, pl.ds(SIDE - 2 * size, size)]
            work[n, s, here] = (work[n, s, here].astype(F32) + more.astype(F32)).astype(BF)
        for copy in step_copies(n, s, k):
            copy.start()

    tail = ORDER[ORDER.index(("V",)) + 1 :]
    vec_steps = [tail[i] for i in (4, 8, 12, 16, 20)]
    for entry in ORDER:
        kind, *which = entry
        if kind == "P":
            theirs(*which)
        elif kind == "O":
            ours(*which)
        elif kind == "L":
            leave()
        elif kind == "A":
            attend_back()
        elif kind == "D":
            dense_back()
            begin("dq")
        elif kind == "N":
            tokens_back()
        elif kind == "V":
            vec_copy(0).start()
        else:
            advance(*which)
            if entry in vec_steps:
                vec_step(vec_steps.index(entry))
    total = vsend[5]
    inv = 1.0 / total[6:7]
    o_vec[...] = total * inv
    o_vec[7:8] = inv
    for n in range(CHUNKS):
        for s in range(2):
            for copy in step_copies(n, s, 8):
                copy.wait()
    for n in (3, 4):
        core_copy(n).wait_send()
    tok_give.wait()
    tok_keep.wait()


def grad_call(*operands):
    vmem = pl.BlockSpec(memory_space=pltpu.VMEM)
    hbm = pl.BlockSpec(memory_space=pl.ANY)
    outs = (
        shape((WIDE, 3 * WIDE)),
        shape((WIDE, WIDE)),
        shape((WIDE, FF)),
        shape((FF, WIDE)),
        shape((2, RB, WIDE)),
        shape((16, WIDE), F32),
    )
    scratch = [
        pltpu.VMEM((MAXP, 2, RB, WIDE), BF),
        pltpu.VMEM((MAXP, 2, RB, WIDE), BF),
        pltpu.VMEM((MAXP, 2, 2, RB, HALF), BF),
        pltpu.VMEM((MAXP, 2, RB, WIDE), BF),
        pltpu.VMEM((MAXP, 4, RB, WIDE), BF),
        pltpu.VMEM((2, MAXP, 4, RB, HALF), BF),
        pltpu.VMEM((3, MAXP, 2 * RB, SIDE), BF),
        pltpu.VMEM((2, SIDE, SIDE), BF),
        pltpu.VMEM((5, SIDE, SIDE), BF),
        pltpu.VMEM((CHUNKS, 2, SIDE, HALF), BF),
        pltpu.VMEM((2 * CHUNKS, SIDE - 48, HALF), BF),
        pltpu.VMEM((2, RB, WIDE), F32),
        pltpu.VMEM((2, RB, WIDE), BF),
        pltpu.VMEM((6, 16, WIDE), F32),
        pltpu.VMEM((5, 16, WIDE), F32),
        pltpu.SemaphoreType.DMA((6,)),
        pltpu.SemaphoreType.DMA((3,)),
        pltpu.SemaphoreType.DMA((2,)),
        pltpu.SemaphoreType.DMA((2, 5)),
        pltpu.SemaphoreType.DMA((2 * CHUNKS, 9)),
        pltpu.SemaphoreType.DMA((2 * CHUNKS, 9)),
        pltpu.SemaphoreType.DMA((2, 5)),
        pltpu.SemaphoreType.DMA((2,)),
        pltpu.SemaphoreType.DMA((2 * CHUNKS,)),
    ]
    return pl.pallas_call(
        grad_kernel,
        out_shape=outs,
        in_specs=[hbm] * 9 + [vmem],
        out_specs=(hbm,) * 5 + (vmem,),
        scratch_shapes=scratch,
        compiler_params=pltpu.CompilerParams(
            collective_id=2, has_side_effects=True, vmem_limit_bytes=VMEM_BYTES
        ),
        name="gradients",
    )(*operands)


def grad_call(*operands):
    vmem = pl.BlockSpec(memory_space=pltpu.VMEM)
    hbm = pl.BlockSpec(memory_space=pl.ANY)
    outs = (
        shape((WIDE, 3 * WIDE)),
        shape((WIDE, WIDE)),
        shape((WIDE, FF)),
        shape((FF, WIDE)),
        shape((2, RB, WIDE)),
        shape((16, WIDE), F32),
    )
    rows_f32 = pltpu.VMEM((2, RB, WIDE), F32)
    rows_low = pltpu.VMEM((2, RB, WIDE), BF)
    heads = pltpu.VMEM((4, RB, HALF), BF)
    scratch = [
        pltpu.VMEM((WIDE, 3 * HALF), BF),
        pltpu.VMEM((WIDE, WIDE), BF),
        heads,
        heads,
        heads,
        heads,
        pltpu.VMEM((3, 2, LEN), F32),
        rows_f32,
        rows_f32,
        rows_f32,
        rows_f32,
        pltpu.VMEM((2, 2, RB, HALF), BF),
        heads,
        rows_low,
        pltpu.VMEM((4, RB, 3 * HALF), BF),
        pltpu.VMEM((2, LEN, 128), F32),
        pltpu.VMEM((2, LEN, 128), F32),
        rows_low,
        rows_low,
        pltpu.VMEM((5, MAXP, 2, RB, SIDE), BF),
        pltpu.VMEM((2, SIDE, SIDE), BF),
        pltpu.VMEM((2, SIDE, SIDE), BF),
        pltpu.VMEM((CHUNKS, 2, SIDE, HALF), BF),
        pltpu.VMEM((2 * CHUNKS, SIDE - 48, HALF), BF),
        rows_low,
        pltpu.VMEM((6, 16, WIDE), F32),
        pltpu.VMEM((5, 16, WIDE), F32),
        pltpu.SemaphoreType.DMA((13,)),
        pltpu.SemaphoreType.DMA((5, 6)),
        pltpu.SemaphoreType.DMA((2, 2)),
        pltpu.SemaphoreType.DMA((2, 2)),
        pltpu.SemaphoreType.DMA((2, 5)),
        pltpu.SemaphoreType.DMA((2 * CHUNKS, 9)),
        pltpu.SemaphoreType.DMA((2 * CHUNKS, 9)),
        pltpu.SemaphoreType.DMA((2, 5)),
        pltpu.SemaphoreType.DMA((2,)),
        pltpu.SemaphoreType.DMA((2 * CHUNKS + 1,)),
    ]
    return pl.pallas_call(
        grad_kernel,
        out_shape=outs,
        in_specs=[hbm] * 19 + [pl.BlockSpec(memory_space=pltpu.SMEM)] + [vmem] * 3,
        out_specs=(hbm,) * 5 + (vmem,),
        scratch_shapes=scratch,
        compiler_params=pltpu.CompilerParams(
            collective_id=2, has_side_effects=True, vmem_limit_bytes=VMEM_BYTES
        ),
        name="gradients",
    )(*operands)


def finish_kernel(
    vec,
    o_qkv,
    o_proj,
    o_fc,
    o_out,
    o_tok,
    f_tok,
    f_ln1_gain,
    f_ln1_shift,
    f_qkv,
    f_bq,
    f_bv,
    f_proj,
    f_b_proj,
    f_ln2_gain,
    f_ln2_shift,
    f_fc,
    f_b_fc,
    f_out,
    f_b_out,
    in_wide,
    out_wide,
    in_tall,
    out_tall,
    isem,
    osem,
):
    inv = vec[7:8, 0:1]
    jobs = []
    for src, dst, size in ((o_fc, f_fc, 128), (o_qkv, f_qkv, 128), (o_out, f_out, 512), (o_proj, f_proj, 384)):
        total, width = src.shape
        for i in range(total // size):
            part = (slice(i * size, (i + 1) * size), slice(0, width))
            jobs.append((src.at[part], dst.at[part], size, width))
    for i in range(2):
        jobs.append((o_tok.at[i], f_tok.at[i], RB, WIDE))

    def parts(n):
        src, dst, size, width = jobs[n]
        slot = n % 6
        wide = size == 128
        here = (in_wide if wide else in_tall).at[slot, pl.ds(0, size), pl.ds(0, width)]
        there = (out_wide if wide else out_tall).at[slot, pl.ds(0, size), pl.ds(0, width)]
        return here, there, src, dst, slot

    def load(n):
        here, _, src, _, slot = parts(n)
        return pltpu.make_async_copy(src, here, isem.at[slot])

    def store(n):
        _, there, _, dst, slot = parts(n)
        return pltpu.make_async_copy(there, dst, osem.at[slot])

    for n in range(4):
        load(n).start()
    f_ln1_gain[...] = vec[0:1].reshape(WIDE)
    f_ln1_shift[...] = vec[1:2].reshape(WIDE)
    f_b_proj[...] = vec[2:3].reshape(WIDE)
    f_ln2_gain[...] = vec[3:4].reshape(WIDE)
    f_ln2_shift[...] = vec[4:5].reshape(WIDE)
    f_b_out[...] = vec[5:6].reshape(WIDE)
    f_bq[...] = vec[12:13].reshape(WIDE)
    f_bv[...] = vec[13:14].reshape(WIDE)
    f_b_fc[...] = jnp.concatenate([vec[8 + i : 9 + i] for i in range(4)], 1).reshape(FF)
    for n in range(len(jobs)):
        here, there = parts(n)[:2]
        load(n).wait()
        if n >= 6:
            store(n - 6).wait()
        there[...] = here[...].astype(F32) * inv
        store(n).start()
        if n + 4 < len(jobs):
            load(n + 4).start()
    for n in range(len(jobs) - 6, len(jobs)):
        store(n).wait()


def finish_call(*operands):
    vmem = pl.BlockSpec(memory_space=pltpu.VMEM)
    hbm = pl.BlockSpec(memory_space=pl.ANY)
    row = shape((WIDE,), F32)
    outs = (
        shape((2, RB, WIDE), F32),
        row,
        row,
        shape((WIDE, 3 * WIDE), F32),
        row,
        row,
        shape((WIDE, WIDE), F32),
        row,
        row,
        row,
        shape((WIDE, FF), F32),
        shape((FF,), F32),
        shape((FF, WIDE), F32),
        row,
    )
    big = {0, 3, 6, 10, 12}
    return pl.pallas_call(
        finish_kernel,
        out_shape=outs,
        in_specs=[vmem] + [hbm] * 5,
        out_specs=tuple(hbm if i in big else vmem for i in range(len(outs))),
        scratch_shapes=[
            pltpu.VMEM((6, 128, FF), BF),
            pltpu.VMEM((6, 128, FF), F32),
            pltpu.VMEM((6, 512, WIDE), BF),
            pltpu.VMEM((6, 512, WIDE), F32),
            pltpu.SemaphoreType.DMA((6,)),
            pltpu.SemaphoreType.DMA((6,)),
        ],
        compiler_params=pltpu.CompilerParams(vmem_limit_bytes=VMEM_BYTES),
        name="finish",
    )(*operands)


def on_chip(
    tokens,
    out_grad,
    section,
    lengths,
    ln1_gain,
    ln1_shift,
    w_qkv,
    b_query,
    b_value,
    w_proj,
    b_proj,
    ln2_gain,
    ln2_shift,
    w_fc,
    b_fc,
    w_out,
    b_out,
):
    kept = layer_call(
        tokens,
        out_grad,
        section,
        lengths,
        ln1_gain,
        ln1_shift,
        b_query,
        b_value,
        b_proj,
        ln2_gain,
        ln2_shift,
        b_out,
        b_fc,
        w_qkv,
        w_proj,
        w_fc,
        w_out,
    )
    (mixed, norm, own, norm2, act, e, dpre, f, dfused, g, dnorm2, sums, *heads) = kept
    (h, q, k, v, att, lse, mid, _) = heads
    (g_qkv, g_proj, g_fc, g_out, g_tok, vec) = grad_call(
        act.reshape(MAXP, 2, RB, FF),
        e,
        norm2,
        dpre.reshape(MAXP, 2, RB, FF),
        own,
        f,
        norm,
        dfused,
        q,
        k,
        v,
        att,
        lse,
        mid,
        h,
        g,
        dnorm2,
        w_qkv,
        w_proj,
        section,
        ln1_gain,
        ln2_gain,
        sums,
    )
    return (mixed, *finish_call(vec, g_qkv, g_proj, g_fc, g_out, g_tok))


def solution(mesh):
    in_specs = (
        P("grp", "seq", None),
        P("grp", "seq", None),
        P("grp"),
        P("grp"),
        P(),
        P(),
        P(),
        P(),
        P(),
        P(),
        P(),
        P(),
        P(),
        P(),
        P(),
        P(),
        P(),
    )
    out_specs = (
        P("grp", "seq", None),
        P("grp", "seq", None),
        P(),
        P(),
        P(),
        P(),
        P(),
        P(),
        P(),
        P(),
        P(),
        P(),
        P(),
        P(),
        P(),
    )
    chosen = on_chip if (mesh.shape["grp"], mesh.shape["seq"]) == (8, 4) else on_device
    return jax.shard_map(
        chosen, mesh=mesh, in_specs=in_specs, out_specs=out_specs, check_vma=False
    )
```

```python
import jax
import jax.numpy as jnp
from jax import lax
from jax.experimental import pallas as pl
from jax.experimental.pallas import tpu as pltpu
from jax.sharding import PartitionSpec as P

HEADS = 12
HD = 64
MAXP = 3


EPSILON = 1e-05
GELU_COEF = 0.7978845608028654
MASKED = -1e30


def layer_norm(hidden, gain, shift):
    average = jnp.mean(hidden, axis=-1, keepdims=True)
    centered = hidden - average
    variance = jnp.mean(centered * centered, axis=-1, keepdims=True)
    return centered * lax.rsqrt(variance + EPSILON) * gain + shift


def gelu_tanh(pre_act):
    return (
        0.5
        * pre_act
        * (1.0 + jnp.tanh(GELU_COEF * (pre_act + 0.044715 * pre_act * pre_act * pre_act)))
    )


def dense(left, right):
    return jnp.einsum("srk,kn->srn", left, right, preferred_element_type=jnp.float32)


def weight_grad(left, right):
    return jnp.einsum("srk,srn->kn", left, right, preferred_element_type=jnp.float32)


def back_dense(grad_rows, right):
    return jnp.einsum("srn,kn->srk", grad_rows, right, preferred_element_type=jnp.float32)


def row_sums(grad_rows):
    return jnp.sum(grad_rows.astype(jnp.float32), axis=(0, 1))


def causal_scores(query_rows, key_all, row_start):
    sample, row_count, width = query_rows.shape
    key_count = key_all.shape[1]
    q_heads = query_rows.reshape(sample, row_count, HEADS, HD)
    k_heads = key_all.reshape(sample, key_count, HEADS, HD)
    scores = jnp.einsum(
        "srhd,sthd->shrt", q_heads, k_heads, preferred_element_type=jnp.float32
    ) * HD ** (-0.5)
    position = row_start + lax.broadcasted_iota(jnp.int32, (row_count, key_count), 0)
    column = lax.broadcasted_iota(jnp.int32, (row_count, key_count), 1)
    return jnp.where(column <= position, scores, MASKED)


def forward_pass(hidden, params, row_start):
    (
        ln1_gain,
        ln1_shift,
        w_qkv,
        b_query,
        b_value,
        w_proj,
        b_proj,
        ln2_gain,
        ln2_shift,
        w_fc,
        b_fc,
        w_out,
        b_out,
    ) = params
    sample, row_count, width = hidden.shape
    normed_low = layer_norm(hidden, ln1_gain, ln1_shift).astype(jnp.bfloat16)
    bias_row = jnp.concatenate([b_query, jnp.zeros_like(b_query), b_value])
    joined_low = (dense(normed_low, w_qkv) + bias_row).astype(jnp.bfloat16)
    query_rows = joined_low[:, :, :width]
    key_rows = joined_low[:, :, width : 2 * width]
    value_rows = joined_low[:, :, 2 * width :]
    key_all, value_all = (
        lax.all_gather(key_rows, "seq", axis=1, tiled=True),
        lax.all_gather(value_rows, "seq", axis=1, tiled=True),
    )
    scores = causal_scores(query_rows, key_all, row_start)
    row_peak = jnp.max(scores, axis=-1, keepdims=True)
    shifted = jnp.exp(scores - row_peak)
    row_total = jnp.sum(shifted, axis=-1, keepdims=True)
    attn_probs = shifted / row_total
    log_total = row_peak + jnp.log(row_total)
    v_heads = value_all.reshape(sample, value_all.shape[1], HEADS, HD)
    attended = jnp.einsum(
        "shrt,sthd->srhd",
        attn_probs.astype(jnp.bfloat16),
        v_heads,
        preferred_element_type=jnp.float32,
    )
    attended_low = attended.reshape(sample, row_count, width).astype(jnp.bfloat16)
    middle = hidden + dense(attended_low, w_proj) + b_proj
    normed_two = layer_norm(middle, ln2_gain, ln2_shift).astype(jnp.bfloat16)
    pre_act = dense(normed_two, w_fc) + b_fc
    activ_low = gelu_tanh(pre_act).astype(jnp.bfloat16)
    output = middle + dense(activ_low, w_out) + b_out
    kept_keys = (key_rows, value_rows)
    kept = (
        hidden,
        normed_low,
        joined_low,
        kept_keys,
        log_total,
        attended_low,
        middle,
        normed_two,
        pre_act,
        activ_low,
    )
    return (output, kept)


def ffn_back(kept, grad_out, params):
    (
        ln1_gain,
        ln1_shift,
        w_qkv,
        b_query,
        b_value,
        w_proj,
        b_proj,
        ln2_gain,
        ln2_shift,
        w_fc,
        b_fc,
        w_out,
        b_out,
    ) = params
    (
        hidden,
        normed_low,
        joined_low,
        kept_keys,
        log_total,
        attended_low,
        middle,
        normed_two,
        pre_act,
        activ_low,
    ) = kept
    grad_low = grad_out.astype(jnp.bfloat16)
    g_w_out = weight_grad(activ_low, grad_low)
    g_b_out = row_sums(grad_low)
    d_activ = back_dense(grad_low, w_out)
    gelu_pull = jax.vjp(gelu_tanh, pre_act)[1]
    d_pre_low = gelu_pull(d_activ)[0].astype(jnp.bfloat16)
    g_w_fc = weight_grad(normed_two, d_pre_low)
    g_b_fc = row_sums(d_pre_low)
    d_normed_two = back_dense(d_pre_low, w_fc)
    norm_pull = jax.vjp(layer_norm, middle, ln2_gain, ln2_shift)[1]
    d_mid_norm, g_ln2_gain, g_ln2_shift = norm_pull(d_normed_two)
    return ((g_ln2_gain, g_ln2_shift, g_w_fc, g_b_fc, g_w_out, g_b_out), grad_out + d_mid_norm)


def attn_back(kept, d_middle, params, row_start):
    (
        ln1_gain,
        ln1_shift,
        w_qkv,
        b_query,
        b_value,
        w_proj,
        b_proj,
        ln2_gain,
        ln2_shift,
        w_fc,
        b_fc,
        w_out,
        b_out,
    ) = params
    (
        hidden,
        normed_low,
        joined_low,
        kept_keys,
        log_total,
        attended_low,
        middle,
        normed_two,
        pre_act,
        activ_low,
    ) = kept
    sample, row_count, width = hidden.shape
    grad_low = d_middle.astype(jnp.bfloat16)
    g_w_proj = weight_grad(attended_low, grad_low)
    g_b_proj = row_sums(grad_low)
    d_att_low = back_dense(grad_low, w_proj).astype(jnp.bfloat16)
    query_rows = joined_low[:, :, :width]
    key_all, value_all = (
        lax.all_gather(kept_keys[0], "seq", axis=1, tiled=True),
        lax.all_gather(kept_keys[1], "seq", axis=1, tiled=True),
    )
    key_count = key_all.shape[1]
    scores = causal_scores(query_rows, key_all, row_start)
    attn_probs = jnp.exp(scores - log_total)
    probs_low = attn_probs.astype(jnp.bfloat16)
    q_heads = query_rows.reshape(sample, row_count, HEADS, HD)
    k_heads = key_all.reshape(sample, key_count, HEADS, HD)
    v_heads = value_all.reshape(sample, key_count, HEADS, HD)
    do_heads = d_att_low.reshape(sample, row_count, HEADS, HD)
    d_probs = jnp.einsum("srhd,sthd->shrt", do_heads, v_heads, preferred_element_type=jnp.float32)
    inner = jnp.sum(d_probs * attn_probs, axis=-1, keepdims=True)
    d_scores = (attn_probs * (d_probs - inner)).astype(jnp.bfloat16)
    scale = HD ** (-0.5)
    d_query = (
        jnp.einsum(
            "shrt,sthd->srhd", d_scores, k_heads, preferred_element_type=jnp.float32
        ).reshape(sample, row_count, width)
        * scale
    )
    d_key_all = (
        jnp.einsum(
            "shrt,srhd->sthd", d_scores, q_heads, preferred_element_type=jnp.float32
        ).reshape(sample, key_count, width)
        * scale
    )
    d_value_all = jnp.einsum(
        "shrt,srhd->sthd", probs_low, do_heads, preferred_element_type=jnp.float32
    ).reshape(sample, key_count, width)
    d_key, d_value = (
        lax.psum_scatter(
            d_key_all.astype(jnp.bfloat16), "seq", scatter_dimension=1, tiled=True
        ).astype(jnp.float32),
        lax.psum_scatter(
            d_value_all.astype(jnp.bfloat16), "seq", scatter_dimension=1, tiled=True
        ).astype(jnp.float32),
    )
    d_joined_low = jnp.concatenate([d_query, d_key, d_value], axis=-1).astype(jnp.bfloat16)
    g_w_qkv = weight_grad(normed_low, d_joined_low)
    g_b_query = row_sums(d_joined_low[:, :, :width])
    g_b_value = row_sums(d_joined_low[:, :, 2 * width :])
    d_normed = back_dense(d_joined_low, w_qkv)
    norm_pull = jax.vjp(layer_norm, hidden, ln1_gain, ln1_shift)[1]
    d_hidden_norm, g_ln1_gain, g_ln1_shift = norm_pull(d_normed)
    terms = (g_ln1_gain, g_ln1_shift, g_w_qkv, g_b_query, g_b_value, g_w_proj, g_b_proj)
    return (terms, d_middle + d_hidden_norm)


def add_terms(accum, terms):
    if accum is None:
        return terms
    return tuple((left_term + right_term for left_term, right_term in zip(accum, terms)))


def on_device(
    tokens,
    out_grad,
    section,
    lengths,
    ln1_gain,
    ln1_shift,
    w_qkv,
    b_query,
    b_value,
    w_proj,
    b_proj,
    ln2_gain,
    ln2_shift,
    w_fc,
    b_fc,
    w_out,
    b_out,
):
    params = (
        ln1_gain,
        ln1_shift,
        w_qkv,
        b_query,
        b_value,
        w_proj,
        b_proj,
        ln2_gain,
        ln2_shift,
        w_fc,
        b_fc,
        w_out,
        b_out,
    )
    sample, row_count, width = tokens.shape
    row_start = lax.axis_index("seq") * row_count
    passes = 2 * section + 1
    position = row_start + lax.broadcasted_iota(jnp.int32, (sample, row_count), 1)
    valid = (position < lengths[:, None]).astype(jnp.float32)
    local_count = jnp.sum(valid)
    hidden = tokens.astype(jnp.float32)
    kept_all = []
    for pass_index in range(MAXP):
        updated, kept = forward_pass(hidden, params, row_start)
        kept_all.append(kept)
        active = (pass_index < passes)[:, None, None]
        hidden = jnp.where(active, updated, hidden)
    mixed = hidden.astype(jnp.bfloat16)
    grad_rows = out_grad.astype(jnp.float32) * valid[:, :, None]
    ffn_acc = None
    attn_acc = None
    for pass_index in reversed(range(MAXP)):
        active_flag = (pass_index < passes).astype(jnp.float32)[:, None, None]
        layer_grad = grad_rows * active_flag
        ffn_terms, d_middle = ffn_back(kept_all[pass_index], layer_grad, params)
        ffn_acc = add_terms(ffn_acc, ffn_terms)
        attn_terms, d_hidden = attn_back(kept_all[pass_index], d_middle, params, row_start)
        attn_acc = add_terms(attn_acc, attn_terms)
        grad_rows = d_hidden + grad_rows * (1.0 - active_flag)
    summed = lax.psum(
        (
            attn_acc[0],
            attn_acc[1],
            attn_acc[2],
            attn_acc[3],
            attn_acc[4],
            attn_acc[5],
            attn_acc[6],
            ffn_acc[0],
            ffn_acc[1],
            ffn_acc[2],
            ffn_acc[3],
            ffn_acc[4],
            ffn_acc[5],
            local_count,
        ),
        ("grp", "seq"),
    )
    attn_sums = summed[0:7]
    ffn_sums = summed[7:13]
    token_total = summed[13]
    return (
        mixed,
        grad_rows / token_total,
        attn_sums[0] / token_total,
        attn_sums[1] / token_total,
        attn_sums[2] / token_total,
        attn_sums[3] / token_total,
        attn_sums[4] / token_total,
        attn_sums[5] / token_total,
        attn_sums[6] / token_total,
        ffn_sums[0] / token_total,
        ffn_sums[1] / token_total,
        ffn_sums[2] / token_total,
        ffn_sums[3] / token_total,
        ffn_sums[4] / token_total,
        ffn_sums[5] / token_total,
    )


BF = jnp.bfloat16
F32 = jnp.float32
MESH_ID = pl.DeviceIdType.MESH
NT = (((1,), (1,)), ((), ()))
TN = (((0,), (0,)), ((), ()))
NN = (((1,), (0,)), ((), ()))
RB = 256
WIDE = 768
HALF = 384
FF = 3072
LEN = 1024
VMEM_BYTES = 60 * 2**20


def mm(left, right, dims):
    return lax.dot_general(left, right, dims, preferred_element_type=F32)


def col_sum(v):
    return jnp.sum(v, axis=0, keepdims=True)


def center(v):
    mean = jnp.mean(v, axis=1, keepdims=True)
    diff = v - mean
    var = jnp.mean(diff * diff, axis=1, keepdims=True)
    return diff, lax.rsqrt(var + EPSILON)


def barrier(partners):
    sem = pltpu.get_barrier_semaphore()
    for seq_index in partners:
        pl.semaphore_signal(sem, inc=1, device_id={"seq": seq_index}, device_id_type=MESH_ID)
    pl.semaphore_wait(sem, len(partners))


def push(src, dst, sems, slot, seq_index):
    return pltpu.make_async_remote_copy(
        src_ref=src,
        dst_ref=dst,
        send_sem=sems.at[0, slot],
        recv_sem=sems.at[1, slot],
        device_id={"seq": seq_index},
        device_id_type=MESH_ID,
    )


def qkv_columns(core, part):
    return pl.ds(pl.multiple_of(part * WIDE + core * HALF, 128), HALF)


def gelu_and_slope(z):
    square = z * z
    t = jnp.tanh(z * (GELU_COEF + (GELU_COEF * 0.044715) * square))
    half = 0.5 + 0.5 * t
    rate = GELU_COEF + (GELU_COEF * 3 * 0.044715) * square
    return z * half, half + (0.5 * z) * (1.0 - t * t) * rate


def norm_back(v, grad, gain):
    diff, inv = center(v)
    xhat = diff * inv
    qv = grad * gain
    mean = jnp.mean(qv, axis=1, keepdims=True)
    cross = jnp.mean(qv * xhat, axis=1, keepdims=True)
    return inv * (qv - mean - xhat * cross), col_sum(grad * xhat), col_sum(grad)


def layer_kernel(
    tokens,
    out_grad,
    section,
    lengths,
    in_ln1_gain,
    in_ln1_shift,
    in_b_query,
    in_b_value,
    in_b_proj,
    in_ln2_gain,
    in_ln2_shift,
    in_b_out,
    in_b_fc,
    w_qkv,
    w_proj,
    w_fc,
    w_out,
    mixed,
    st_norm,
    st_own,
    st_norm2,
    st_act,
    st_e,
    st_dpre,
    st_f,
    st_dfused,
    g_out,
    dnorm2_out,
    sums,
    st_h,
    st_q,
    st_k,
    st_v,
    st_att,
    st_lse,
    st_mid,
    st_pre,
    wq,
    wp,
    wf,
    wo,
    tok,
    h,
    norm,
    q,
    k,
    v,
    att,
    own,
    lse,
    mid,
    norm2,
    pre,
    act,
    g,
    glow,
    dmid,
    datt_in,
    dfused,
    dk_acc,
    dv_acc,
    rows_in,
    b_fc,
    wsem,
    ssem,
    lsem,
    bsem,
    nsem,
    asem,
    dsem,
    psem,
    ysem,
):
    me = lax.axis_index("seq")
    core = lax.rem(me, 2)
    chip = me // 2
    partner = me + 1 - 2 * core
    across = lax.rem(me + 2, 4)
    half_lanes = pl.ds(pl.multiple_of(core * HALF, 128), HALF)
    passes = jnp.full((1, WIDE), 2 * section[chip] + 1, jnp.int32)
    length = jnp.full((1, WIDE), lengths[chip], jnp.int32)

    def is_active(p):
        return jnp.full((1, WIDE), p, jnp.int32) < passes

    keep = pltpu.make_async_copy(tokens.at[chip], tok.at[chip], wsem.at[6])
    keep.start()
    loads = [
        pltpu.make_async_copy(
            w_qkv.at[:, qkv_columns(core, third)],
            wq.at[:, pl.ds(third * HALF, HALF)],
            wsem.at[third],
        )
        for third in range(3)
    ]
    loads += [
        pltpu.make_async_copy(w_proj, wp, wsem.at[3]),
        pltpu.make_async_copy(w_fc, wf, wsem.at[4]),
        pltpu.make_async_copy(w_out, wo, wsem.at[5]),
    ]
    for load in loads:
        load.start()
    short = (
        in_ln1_gain,
        in_ln1_shift,
        in_b_query,
        in_b_value,
        in_b_proj,
        in_ln2_gain,
        in_ln2_shift,
        in_b_out,
    )
    for i, ref in enumerate(short):
        rows_in[i : i + 1] = ref[...].reshape(1, WIDE)
    b_fc[...] = in_b_fc[...].reshape(1, FF)
    ln1_gain, ln1_shift, b_query, b_value, b_proj, ln2_gain, ln2_shift, b_out = (
        rows_in.at[pl.ds(i, 1)] for i in range(8)
    )
    barrier((partner, across))
    give = push(tokens.at[1 - chip], tok.at[chip], ysem, 0, across)
    give.start()
    keep.wait()
    give.wait()
    og_keep = pltpu.make_async_copy(out_grad.at[chip], glow.at[chip], wsem.at[6])
    og_give = push(out_grad.at[1 - chip], glow.at[chip], ysem, 1, across)
    og_keep.start()
    og_give.start()
    for j in range(2):
        h[j] = tok[j].astype(F32)
    for load in loads:
        load.wait()

    def saves_of_ffn(p):
        return (
            pltpu.make_async_copy(pre, st_pre.at[p], ssem.at[9]),
            pltpu.make_async_copy(act, st_act.at[p], ssem.at[10]),
        )

    def forward_pass_step(p, carry):
        norm_send = []
        for j in range(2):
            diff, inv = center(h[j])
            norm[2 * j + core] = (diff * inv * ln1_gain[...] + ln1_shift[...]).astype(BF)
            copy = push(norm.at[2 * j + core], norm.at[2 * j + core], nsem, j, partner)
            copy.start()
            norm_send.append(copy)
        save_h = pltpu.make_async_copy(h, st_h.at[p], ssem.at[0])
        save_h.start()

        def project(block):
            rows = norm[block]
            out = mm(rows, wq[...], NN)
            q[block] = (out[:, :HALF] + b_query[:, half_lanes]).astype(BF)
            k[block] = out[:, HALF : 2 * HALF].astype(BF)
            v[block] = (out[:, 2 * HALF :] + b_value[:, half_lanes]).astype(BF)

        for j in range(2):
            project(2 * j + core)
        for j in range(2):
            norm_send[j].wait()
            project(2 * j + 1 - core)
        saves = [
            pltpu.make_async_copy(norm, st_norm.at[p], ssem.at[1]),
            pltpu.make_async_copy(q, st_q.at[p], ssem.at[2]),
            pltpu.make_async_copy(k, st_k.at[p], ssem.at[3]),
            pltpu.make_async_copy(v, st_v.at[p], ssem.at[4]),
        ]
        for save in saves:
            save.start()
        lane = lax.broadcasted_iota(jnp.int32, (RB, 128), 1)
        row = lax.broadcasted_iota(jnp.int32, (2 * RB, RB), 0) & (RB - 1)
        causal = lax.broadcasted_iota(jnp.int32, (2 * RB, RB), 1) <= row
        zero = jnp.zeros((RB, 128), BF)
        att_send = []
        for i in (3, 2, 0, 1):
            keys = (i + 1) * RB
            for pair in range(3):
                cs = slice(pair * 128, pair * 128 + 128)
                qi = q[i, :, cs] * jnp.asarray(HD**-0.5, BF)
                both = jnp.concatenate(
                    [jnp.where(lane < HD, qi, zero), jnp.where(lane < HD, zero, qi)], 0
                )
                k_all = k[0 : i + 1, :, cs].reshape(keys, 128)
                v_all = v[0 : i + 1, :, cs].reshape(keys, 128)
                s = mm(both, k_all, NT)
                last = jnp.where(causal, s[:, i * RB :], MASKED)
                s = jnp.concatenate([s[:, : i * RB], last], 1) if i else last
                peak = jnp.max(s, axis=1, keepdims=True)
                e = jnp.exp(s - peak).astype(BF)
                ol = mm(e, jnp.concatenate([v_all, jnp.ones((keys, 128), BF)], 1), NN)
                total = ol[:, 128:]
                o = ol[:, :128] / total
                att[i, :, cs] = jnp.where(lane < HD, o[:RB], o[RB:]).astype(BF)
                ls = peak + jnp.log(total)
                ls = jnp.concatenate([ls[:RB], ls[RB:]], 1).T
                lse[pair, 0:1, i * RB : (i + 1) * RB] = ls[0:1]
                lse[pair, 1:2, i * RB : (i + 1) * RB] = ls[128:129]
            if i == 3:
                saves[0].wait()
            copy = push(att.at[i], own.at[i // 2, core], asem, i // 2, partner)

            @pl.when(core == i % 2)
            def _():
                own[i // 2, core] = att[i]

            @pl.when(core != i % 2)
            def _():
                copy.start()

            if i in (2, 1):
                att_send.append(copy)
        save_att = pltpu.make_async_copy(att, st_att.at[p], ssem.at[1])
        save_lse = pltpu.make_async_copy(lse, st_lse.at[p], ssem.at[5])
        save_att.start()
        save_lse.start()
        for j, copy in ((1, att_send[0]), (0, att_send[1])):
            copy.wait()
            out = mm(own[j, 0], wp[0:HALF, :], NN) + mm(own[j, 1], wp[HALF:, :], NN)
            m = h[j] + out + b_proj[...]
            mid[j] = m
            diff, inv = center(m)
            norm2[j] = (diff * inv * ln2_gain[...] + ln2_shift[...]).astype(BF)
        save_rest = [
            pltpu.make_async_copy(own, st_own.at[p], ssem.at[6]),
            pltpu.make_async_copy(mid, st_mid.at[p], ssem.at[7]),
            pltpu.make_async_copy(norm2, st_norm2.at[p], ssem.at[8]),
        ]
        for save in save_rest:
            save.start()
        x = norm2[...].reshape(2 * RB, WIDE)

        @pl.when(p > 0)
        def _():
            for save in saves_of_ffn(p - 1):
                save.wait()

        for t in range(3):
            cs = slice(t * 1024, (t + 1) * 1024)
            z = mm(x, wf[:, cs], NN) + b_fc[:, cs]
            value, slope = gelu_and_slope(z)
            act[:, cs] = value.astype(BF)
            pre[:, cs] = slope.astype(BF)
        for save in saves_of_ffn(p):
            save.start()
        out = mm(act[...], wo[...], NN)
        active = is_active(p)
        save_h.wait()
        for j in range(2):
            new = mid[j] + out[j * RB : (j + 1) * RB] + b_out[...]
            h[j] = jnp.where(active, new, h[j])
        for save in saves[1:] + [save_att, save_lse] + save_rest:
            save.wait()
        return carry

    lax.fori_loop(0, MAXP, forward_pass_step, 0)
    for save in saves_of_ffn(MAXP - 1):
        save.wait()
    for j in range(2):
        tok[j] = h[j].astype(BF)
    mixed_keep = pltpu.make_async_copy(tok.at[chip], mixed.at[chip], wsem.at[7])
    mixed_give = push(tok.at[1 - chip], mixed.at[chip], ysem, 2, across)
    mixed_keep.start()
    mixed_give.start()

    kept = {
        "pre": (st_pre, pre),
        "mid": (st_mid, mid),
        "q": (st_q, q),
        "k": (st_k, k),
        "v": (st_v, v),
        "att": (st_att, att),
        "lse": (st_lse, lse),
        "h": (st_h, h),
    }

    def fetch(p, name):
        src, dst = kept[name]
        return pltpu.make_async_copy(src.at[p], dst, lsem.at[list(kept).index(name)])

    fetch(MAXP - 1, "h").start()
    og_keep.wait()
    og_give.wait()
    sums[...] = jnp.zeros_like(sums)
    for j in range(2):
        pos = (2 * j + core) * RB + lax.broadcasted_iota(jnp.int32, (RB, WIDE), 0)
        g[j] = jnp.where(pos < length, glow[j].astype(F32), 0.0)

    def saves_of(p):
        return (
            pltpu.make_async_copy(glow, st_e.at[p], bsem.at[0]),
            pltpu.make_async_copy(act, st_dpre.at[p], bsem.at[1]),
            pltpu.make_async_copy(norm2, st_f.at[jnp.maximum(p - 1, 0)], bsem.at[2]),
            pltpu.make_async_copy(dfused, st_dfused.at[jnp.maximum(p - 1, 0)], bsem.at[3]),
        )

    def feed_forward_back(p, active, arrive):
        for j in range(2):
            glow[j] = jnp.where(active, g[j], 0.0).astype(BF)
        e = glow[...].reshape(2 * RB, WIDE)
        arrive("pre")
        for t in range(3):
            cs = slice(t * 1024, (t + 1) * 1024)
            dact = mm(e, wo[cs, :], NT)
            act[:, cs] = (dact * pre[:, cs].astype(F32)).astype(BF)
        return mm(act[...], wf[...], NT)

    def backward_pass_step(step, carry):
        p = MAXP - 1 - step

        def arrive(*names):
            @pl.when(step > 0)
            def _():
                for name in names:
                    fetch(p, name).wait()

        def prefetch(*names):
            for name in names:
                if name == "pre":
                    fetch(p - 1, name).start()
                else:

                    @pl.when(p > 1)
                    def _(name=name):
                        fetch(p - 1, name).start()

        active = is_active(p)

        @pl.when(step > 0)
        def _():
            for save in saves_of(p + 1)[:3]:
                save.wait()

        dnorm2 = feed_forward_back(p, active, arrive)
        arrive("mid")
        for j in range(2):
            d = dnorm2[j * RB : (j + 1) * RB]
            dv_in, dgain, dshift = norm_back(mid[j], d, ln2_gain[...])
            sums[3:4] += dgain
            sums[4:5] += dshift
            dm = jnp.where(active, g[j], 0.0) + dv_in
            dmid[j] = dm
            low = dm.astype(BF)
            norm2[j] = low
        da = mm(norm2[...].reshape(2 * RB, WIDE), wp[...], NT).astype(BF)
        for half in range(2):
            for j in range(2):
                own[half, j] = da[j * RB : (j + 1) * RB, half * HALF : (half + 1) * HALF]
        datt_send = []
        for j in range(2):
            copy = push(
                own.at[1 - core, j], datt_in.at[2 * j + core], dsem, j, partner
            )
            copy.start()
            datt_send.append(copy)
            datt_in[2 * j + core] = own[core, j]
        for save in saves_of(p)[:3]:
            save.start()
        prefetch("pre", "mid")

        @pl.when(step > 0)
        def _():
            saves_of(p + 1)[3].wait()

        arrive("q", "k", "v", "att", "lse")
        for copy in datt_send:
            copy.wait()
        lane = lax.broadcasted_iota(jnp.int32, (RB, 128), 1)
        zero = jnp.zeros((RB, 128), BF)
        col = lax.broadcasted_iota(jnp.int32, (RB, 2 * RB), 1) & (RB - 1)
        causal = lax.broadcasted_iota(jnp.int32, (RB, 2 * RB), 0) <= col
        sub = lax.broadcasted_iota(jnp.int32, (128, LEN), 0)
        zero_t = jnp.zeros((128, LEN), BF)
        scale = jnp.asarray(HD**-0.5, BF)

        def split(rows):
            return jnp.concatenate(
                [jnp.where(lane < HD, rows, zero), jnp.where(lane < HD, zero, rows)], 0
            )

        def one_pair(pair, carry):
            start = pl.multiple_of(pair * 128, 128)
            cs = pl.ds(start, 128)
            slot = 0
            k_t = k[:, :, cs].reshape(LEN, 128).T
            k_low = jnp.where(sub < HD, k_t, zero_t)
            k_high = jnp.where(sub < HD, zero_t, k_t)
            for i in (3, 2, 1, 0):
                keys = (i + 1) * RB
                rs = slice(i * RB, (i + 1) * RB)
                qm = split(q[i, :, cs] * scale)
                do = datt_in[i, :, cs]
                dm = split(do)
                inner = (do.astype(F32) * att[i, :, cs].astype(F32)).T
                inner = jnp.concatenate([col_sum(inner[:HD]), col_sum(inner[HD:])], 1)
                total = jnp.concatenate([lse[pair, 0:1, rs], lse[pair, 1:2, rs]], 1)
                s = mm(k[0 : i + 1, :, cs].reshape(keys, 128), qm, NT)
                dp = mm(v[0 : i + 1, :, cs].reshape(keys, 128), dm, NT)
                last = jnp.where(causal, s[i * RB :], MASKED)
                s = jnp.concatenate([s[: i * RB], last], 0) if i else last
                prob = jnp.exp(s - total)
                ds = (prob * (dp - inner)).astype(BF)
                dv = mm(prob.astype(BF), dm, NN)
                dk = mm(ds, qm, NN)
                if i == 3:
                    dv_acc[slot] = dv
                    dk_acc[slot] = dk
                else:
                    dv_acc[slot, 0:keys] += dv
                    dk_acc[slot, 0:keys] += dk
                dq = mm(k_low[:, :keys], ds[:, :RB], NN) + mm(k_high[:, :keys], ds[:, RB:], NN)
                dfused[i, :, cs] = (dq.T * HD**-0.5).astype(BF)
            ks = pl.ds(pl.multiple_of(HALF + pair * 128, 128), 128)
            vs = pl.ds(pl.multiple_of(2 * HALF + pair * 128, 128), 128)
            dfused[:, :, ks] = dk_acc[slot].astype(BF).reshape(4, RB, 128)
            dfused[:, :, vs] = dv_acc[slot].astype(BF).reshape(4, RB, 128)
            return carry

        lax.fori_loop(0, 3, one_pair, 0)
        part_send = []
        for j in range(2):
            block = 2 * j + 1 - core
            norm[j] = mm(dfused[block], wq[...], NT).astype(BF)
            copy = push(norm.at[j], norm.at[2 + j], psem, j, partner)
            copy.start()
            part_send.append(copy)
        saves_of(p)[3].start()
        prefetch("q", "k", "v", "att", "lse")
        mine = [mm(dfused[2 * j + core], wq[...], NT) for j in range(2)]
        fetch(p, "h").wait()
        for j in range(2):
            part_send[j].wait()
            d = mine[j] + norm[2 + j].astype(F32)
            dv_in, dgain, dshift = norm_back(h[j], d, ln1_gain[...])
            sums[0:1] += dgain
            sums[1:2] += dshift
            g[j] = dmid[j] + dv_in + jnp.where(active, 0.0, g[j])
        prefetch("h")
        return carry

    lax.fori_loop(0, MAXP - 1, backward_pass_step, 0)
    for save in saves_of(1):
        save.wait()
    dnorm2 = feed_forward_back(0, is_active(0), lambda name: fetch(0, name).wait())
    last = list(saves_of(0)[:2])
    for save in last:
        save.start()
    for j in range(2):
        mid[j] = dnorm2[j * RB : (j + 1) * RB]
    sums[6:7] = jnp.where(core == 0, length.astype(F32), jnp.zeros((1, WIDE), F32))
    done = pltpu.make_async_copy(g, g_out, bsem.at[2])
    done.start()
    done_dnorm2 = pltpu.make_async_copy(mid, dnorm2_out, bsem.at[3])
    done_dnorm2.start()
    for save in last:
        save.wait()
    done_dnorm2.wait()
    mixed_keep.wait()
    mixed_give.wait()
    done.wait()


def shape(dims, kind=BF):
    return jax.ShapeDtypeStruct(dims, kind)


def layer_call(*operands):
    vmem = pl.BlockSpec(memory_space=pltpu.VMEM)
    smem = pl.BlockSpec(memory_space=pltpu.SMEM)
    hbm = pl.BlockSpec(memory_space=pl.ANY)
    outs = (
        shape((2, RB, WIDE)),
        shape((MAXP, 4, RB, WIDE)),
        shape((MAXP, 2, 2, RB, HALF)),
        shape((MAXP, 2, RB, WIDE)),
        shape((MAXP, 2 * RB, FF)),
        shape((MAXP, 2, RB, WIDE)),
        shape((MAXP, 2 * RB, FF)),
        shape((MAXP - 1, 2, RB, WIDE)),
        shape((MAXP - 1, 4, RB, 3 * HALF)),
        shape((2, RB, WIDE), F32),
        shape((2, RB, WIDE), F32),
        shape((16, WIDE), F32),
        shape((MAXP, 2, RB, WIDE), F32),
        shape((MAXP, 4, RB, HALF)),
        shape((MAXP, 4, RB, HALF)),
        shape((MAXP, 4, RB, HALF)),
        shape((MAXP, 4, RB, HALF)),
        shape((MAXP, 3, 2, LEN), F32),
        shape((MAXP, 2, RB, WIDE), F32),
        shape((MAXP, 2 * RB, FF)),
    )
    scratch = [
        pltpu.VMEM((WIDE, 3 * HALF), BF),
        pltpu.VMEM((WIDE, WIDE), BF),
        pltpu.VMEM((WIDE, FF), BF),
        pltpu.VMEM((FF, WIDE), BF),
        pltpu.VMEM((2, RB, WIDE), BF),
        pltpu.VMEM((2, RB, WIDE), F32),
        pltpu.VMEM((4, RB, WIDE), BF),
        pltpu.VMEM((4, RB, HALF), BF),
        pltpu.VMEM((4, RB, HALF), BF),
        pltpu.VMEM((4, RB, HALF), BF),
        pltpu.VMEM((4, RB, HALF), BF),
        pltpu.VMEM((2, 2, RB, HALF), BF),
        pltpu.VMEM((3, 2, LEN), F32),
        pltpu.VMEM((2, RB, WIDE), F32),
        pltpu.VMEM((2, RB, WIDE), BF),
        pltpu.VMEM((2 * RB, FF), BF),
        pltpu.VMEM((2 * RB, FF), BF),
        pltpu.VMEM((2, RB, WIDE), F32),
        pltpu.VMEM((2, RB, WIDE), BF),
        pltpu.VMEM((2, RB, WIDE), F32),
        pltpu.VMEM((4, RB, HALF), BF),
        pltpu.VMEM((4, RB, 3 * HALF), BF),
        pltpu.VMEM((2, LEN, 128), F32),
        pltpu.VMEM((2, LEN, 128), F32),
        pltpu.VMEM((8, WIDE), F32),
        pltpu.VMEM((1, FF), F32),
        pltpu.SemaphoreType.DMA((8,)),
        pltpu.SemaphoreType.DMA((11,)),
        pltpu.SemaphoreType.DMA((8,)),
        pltpu.SemaphoreType.DMA((4,)),
        pltpu.SemaphoreType.DMA((2, 2)),
        pltpu.SemaphoreType.DMA((2, 2)),
        pltpu.SemaphoreType.DMA((2, 2)),
        pltpu.SemaphoreType.DMA((2, 2)),
        pltpu.SemaphoreType.DMA((2, 3)),
    ]
    return pl.pallas_call(
        layer_kernel,
        out_shape=outs,
        in_specs=[hbm] * 2 + [smem] * 2 + [vmem] * 9 + [hbm] * 4,
        out_specs=(hbm,) * 11 + (vmem,) + (hbm,) * 8,
        scratch_shapes=scratch,
        compiler_params=pltpu.CompilerParams(
            collective_id=1, has_side_effects=True, vmem_limit_bytes=VMEM_BYTES
        ),
        name="layer",
    )(*operands)


CHUNKS = 6
SIDE = 768
ROUTES = (
    "yxzw", "xzyw", "yxzw", "xyzw", "zwyx", "yxzw", "yxzw", "zxyw", "xyzw", "zxyw", "xyzw",
    "yxzw",
)
ORDER = (
    ("P", 0), ("L",), ("O", 0), ("S", 0, 0, 0), ("S", 0, 1, 0), ("P", 1), ("O", 1),
    ("S", 1, 0, 0), ("S", 1, 1, 0), ("P", 2), ("S", 0, 0, 1), ("S", 0, 1, 1), ("O", 2),
    ("S", 2, 0, 0), ("S", 2, 1, 0), ("P", 3), ("S", 0, 1, 2), ("S", 1, 0, 1), ("S", 1, 1, 1),
    ("O", 3), ("S", 0, 0, 2), ("S", 3, 0, 0), ("S", 3, 1, 0), ("A",), ("S", 0, 1, 3),
    ("S", 0, 0, 3), ("S", 1, 0, 2), ("S", 1, 1, 2), ("S", 2, 0, 1), ("S", 2, 1, 1),
    ("S", 3, 1, 1), ("D",), ("S", 3, 0, 1), ("P", 4), ("N",), ("S", 1, 0, 3), ("S", 1, 1, 3),
    ("S", 2, 1, 2), ("S", 0, 1, 4), ("S", 0, 0, 4), ("O", 4), ("S", 3, 1, 2), ("S", 2, 0, 2),
    ("S", 4, 0, 0), ("S", 4, 1, 0), ("O", 5), ("V",), ("S", 2, 1, 3), ("S", 3, 0, 2),
    ("S", 5, 0, 0), ("S", 5, 1, 0), ("S", 1, 0, 4), ("S", 1, 1, 4), ("S", 0, 0, 5),
    ("S", 0, 1, 5), ("S", 3, 1, 3), ("S", 4, 0, 1), ("S", 4, 1, 1), ("S", 2, 0, 3),
    ("S", 2, 1, 4), ("S", 3, 0, 3), ("S", 1, 0, 5), ("S", 1, 1, 5), ("S", 0, 0, 6),
    ("S", 5, 0, 1), ("S", 5, 1, 1), ("S", 3, 1, 4), ("S", 2, 1, 5), ("S", 0, 1, 6),
    ("S", 3, 0, 4), ("S", 4, 1, 2), ("S", 1, 0, 6), ("S", 1, 1, 6), ("S", 4, 0, 2),
    ("S", 2, 0, 4), ("S", 3, 1, 5), ("S", 0, 0, 7), ("S", 2, 1, 6), ("S", 5, 0, 2),
    ("S", 4, 1, 3), ("S", 5, 1, 2), ("S", 0, 1, 7), ("S", 3, 0, 5), ("S", 4, 0, 3),
    ("S", 1, 0, 7), ("S", 5, 0, 3), ("S", 1, 1, 7), ("S", 4, 1, 4), ("S", 5, 1, 3),
    ("S", 2, 0, 5), ("S", 4, 0, 4), ("S", 5, 0, 4), ("S", 2, 1, 7), ("S", 0, 0, 8),
    ("S", 3, 1, 6), ("S", 5, 1, 4), ("S", 0, 1, 8), ("S", 4, 0, 5), ("S", 3, 0, 6),
    ("S", 5, 0, 5), ("S", 4, 1, 5), ("S", 1, 0, 8), ("S", 5, 1, 5), ("S", 4, 0, 6),
    ("S", 2, 0, 6), ("S", 1, 1, 8), ("S", 5, 0, 6), ("S", 5, 1, 6), ("S", 3, 1, 7),
    ("S", 2, 1, 8), ("S", 3, 0, 7), ("S", 4, 1, 6), ("S", 2, 0, 7), ("S", 4, 0, 7),
    ("S", 5, 1, 7), ("S", 3, 1, 8), ("S", 4, 1, 7), ("S", 5, 0, 7), ("S", 2, 0, 8),
    ("S", 4, 0, 8), ("S", 3, 0, 8), ("S", 4, 1, 8), ("S", 5, 0, 8), ("S", 5, 1, 8),
)


def mesh_push(src, dst, send, recv, where):
    return pltpu.make_async_remote_copy(
        src_ref=src,
        dst_ref=dst,
        send_sem=send,
        recv_sem=recv,
        device_id=where,
        device_id_type=MESH_ID,
    )


def grad_kernel(
    act,
    e,
    norm2,
    dpre,
    own,
    f,
    norm,
    dfused_st,
    st_q,
    st_k,
    st_v,
    st_att,
    st_lse,
    st_mid,
    st_h,
    g_in,
    dnorm2_in,
    w_qkv,
    w_proj,
    section,
    ln1_gain,
    ln2_gain,
    vec,
    o_qkv,
    o_proj,
    o_fc,
    o_out,
    o_tok,
    o_vec,
    wq,
    wp,
    q,
    k,
    v,
    att,
    lse,
    mid,
    h,
    g,
    dn2,
    datt,
    datt_in,
    f0,
    dfused,
    dk_acc,
    dv_acc,
    part,
    part_in,
    slots,
    give,
    got,
    work,
    rx,
    tok_low,
    vsend,
    vgot,
    lsem,
    slsem,
    dsem,
    psem,
    csem,
    xsem,
    rsem,
    vsem,
    ysem,
    osem,
):
    me = lax.axis_index("seq")
    group = lax.axis_index("grp")
    core = lax.rem(me, 2)
    y = me // 2
    x = lax.rem(group, 2)
    z = group // 2
    other = 1 - core
    to_core = {"seq": me + 1 - 2 * core}
    to_y = {"seq": lax.rem(me + 2, 4)}
    to_x = {"grp": group + 1 - 2 * x}

    def to_z_pair(step):
        low = lax.rem(z // step, 2)
        return {"grp": (z + step - 2 * step * low) * 2 + x}

    partner = me + 1 - 2 * core
    passes = jnp.full((1, WIDE), 2 * section[y] + 1, jnp.int32)
    active = jnp.full((1, WIDE), 0, jnp.int32) < passes

    kept = {
        "mid": (st_mid.at[0], mid),
        "g": (g_in, g),
        "dnorm2": (dnorm2_in, dn2),
        "wp": (w_proj, wp),
        "q": (st_q.at[0], q),
        "k": (st_k.at[0], k),
        "v": (st_v.at[0], v),
        "att": (st_att.at[0], att),
        "lse": (st_lse.at[0], lse),
        "h": (st_h.at[0], h),
    }
    for third in range(3):
        kept["wq%d" % third] = (
            w_qkv.at[:, qkv_columns(core, third)],
            wq.at[:, pl.ds(third * HALF, HALF)],
        )

    def kept_copy(name):
        src, dst = kept[name]
        return pltpu.make_async_copy(src, dst, lsem.at[list(kept).index(name)])

    def arrive(*names):
        for name in names:
            kept_copy(name).wait()

    def whole(src):
        return [(src.at[p], (p, slice(None))) for p in range(MAXP)]

    def piece(src, owner, i):
        cols = pl.ds(pl.multiple_of(owner * 2 * SIDE + i * SIDE, 128), SIDE)
        return [(src.at[p, :, :, cols], (p, slice(None))) for p in range(MAXP)]

    def own_rows():
        return [
            (own.at[p, :, half], (p, slice(None), slice(None), pl.ds(half * HALF, HALF)))
            for p in range(MAXP)
            for half in range(2)
        ]

    def f_rows():
        return [(f0, (0, slice(None)))] + [(f.at[p - 1], (p, slice(None))) for p in (1, 2)]

    def dfused_at(p, blocks, cols):
        src = dfused if p == 0 else dfused_st.at[p - 1]
        return src.at[blocks, :, cols]

    def dq_rows():
        return [
            (
                dfused_at(p, pl.ds(2 * i, 2), pl.ds(0, HALF)),
                (p, slice(None), slice(None), pl.ds(i * HALF, HALF)),
            )
            for p in range(MAXP)
            for i in range(2)
        ]

    def kv_rows(i):
        return [
            (dfused_at(p, pl.ds(2 * i, 2), pl.ds(HALF, 2 * HALF)), (p, slice(None)))
            for p in range(MAXP)
        ]

    def norm_rows(i):
        return [(norm.at[p, pl.ds(2 * i, 2)], (p, slice(None))) for p in range(MAXP)]

    other = 1 - core
    operands = {
        "e": (0, lambda: whole(e)),
        "act0": (1, lambda: piece(act, other, 0)),
        "act1": (2, lambda: piece(act, core, 0)),
        "act2": (3, lambda: piece(act, other, 1)),
        "act3": (4, lambda: piece(act, core, 1)),
        "norm2": (1, lambda: whole(norm2)),
        "dpre0": (2, lambda: piece(dpre, other, 0)),
        "dpre1": (3, lambda: piece(dpre, core, 0)),
        "dpre2": (0, lambda: piece(dpre, other, 1)),
        "dpre3": (4, lambda: piece(dpre, core, 1)),
        "own": (2, own_rows),
        "f": (3, f_rows),
        "norm_a": (0, lambda: norm_rows(0)),
        "norm_b": (1, lambda: norm_rows(1)),
        "dq": (4, dq_rows),
        "kv_a": (2, lambda: kv_rows(0)),
        "kv_b": (3, lambda: kv_rows(1)),
    }

    def operand_copies(name):
        slot, copies = operands[name]
        return [
            pltpu.make_async_copy(src, slots.at[(slot, *place)], slsem.at[slot, i])
            for i, (src, place) in enumerate(copies())
        ]

    def begin(*names):
        for name in names:
            for copy in operand_copies(name):
                copy.start()

    def ready(name):
        for copy in operand_copies(name):
            copy.wait()

    def operand(name):
        return slots[operands[name][0]].reshape(MAXP * 2 * RB, SIDE)

    begin("e", "act0", "act1")
    for name in ("mid", "g", "dnorm2", "wp"):
        kept_copy(name).start()
    begin("act2", "act3")
    for name in ("q", "k", "v", "att", "lse", "h", "wq0", "wq1", "wq2"):
        kept_copy(name).start()

    sem = pltpu.get_barrier_semaphore()
    partners = [to_core, to_y, to_x, to_z_pair(1), to_z_pair(2)]
    for where in partners:
        pl.semaphore_signal(sem, inc=1, device_id=where, device_id_type=MESH_ID)
    pl.semaphore_wait(sem, len(partners))

    tok_give = mesh_push(tok_low.at[1 - y], o_tok.at[y], ysem.at[0], ysem.at[1], to_y)
    tok_keep = pltpu.make_async_copy(tok_low.at[y], o_tok.at[y], osem.at[2 * CHUNKS])

    def datt_copy(j):
        return push(datt.at[other, j], datt_in.at[2 * j + core], dsem, j, partner)

    def part_copy(j):
        return push(part.at[j], part_in.at[j], psem, j, partner)

    vec_to = [to_core, to_x, to_y, to_z_pair(1), to_z_pair(2)]

    def vec_copy(k):
        return mesh_push(vsend.at[k], vgot.at[k], vsem.at[0, k], vsem.at[1, k], vec_to[k])

    vsend[0] = vec[...]

    def vec_row(row, v):
        vsend[0, pl.ds(row, 1), :] += v

    def pass_sum(name, p, cols=slice(None)):
        rows_of = slots[operands[name][0], p].astype(F32).reshape(2 * RB, SIDE)
        return col_sum(rows_of)[:, cols]

    def half_row(row, v):
        blank = jnp.zeros((1, HALF), F32)
        vec_row(
            row,
            jnp.concatenate(
                [jnp.where(core == 0, v, blank), jnp.where(core == 0, blank, v)], 1
            ),
        )

    def vec_step(k):
        vec_copy(k).wait()
        vsend[k + 1] = vsend[k] + vgot[k]
        if k < 4:
            vec_copy(k + 1).start()

    def tiles(lefts, rights, cols, emit, also=None):
        def tile(m, carry):
            here = pl.ds(pl.multiple_of(m * 256, 256), 256)
            out = None
            for left, right in zip(lefts, rights):
                left_part = slots[operands[left][0], :, :, :, here].reshape(MAXP * 2 * RB, 256)
                width = SIDE if right[1] is None else HALF
                right_cols = cols if right[1] is None else right[1]
                right_part = slots[operands[right[0]][0], :, :, :, right_cols]
                part_out = mm(left_part, right_part.reshape(MAXP * 2 * RB, width), TN)
                out = part_out if out is None else out + part_out
            emit(m, here, out)
            if also is not None:
                also(m)
            return carry

        lax.fori_loop(0, SIDE // 256, tile, 0)

    def product(n, place, emit):
        owner = core if place else other
        every = slice(None)
        if n < 4:
            name = ("act%d" if n < 2 else "dpre%d") % (2 * (n % 2) + place)
            if n in (0, 2) and place == 0:
                ready("e" if n == 0 else "norm2")
            ready(name)
            if n < 2:
                also = None
                if n == 0 and place == 0:
                    also = lambda m: vec_row(5, pass_sum("e", m))
                tiles((name,), (("e", None),), every, emit, also)
            else:
                also = lambda m: vec_row(8 + owner * 2 + n - 2, pass_sum(name, m))
                tiles(("norm2",), ((name, None),), every, emit, also)
            return
        if place == 0:
            ready("own")
            ready("f")
        also = (lambda m: vec_row(2, pass_sum("f", m))) if place == 0 else None
        cols = pl.ds(pl.multiple_of(owner * HALF, 128), HALF)
        tiles(("own",), (("f", cols),), every, emit, also)

    def core_copy(n):
        width = SIDE if n < 4 else HALF
        return mesh_push(
            give.at[n % 2, :, pl.ds(0, width)],
            got.at[n % 2, :, pl.ds(0, width)],
            csem.at[0, n],
            csem.at[1, n],
            to_core,
        )

    follow = {
        (0, 0): ("norm2",),
        (0, 1): ("dpre0",),
        (1, 0): ("dpre1",),
        (1, 1): ("dpre2", "dpre3"),
        (2, 0): ("own",),
        (2, 1): ("f",),
        (3, 0): ("norm_a",),
        (3, 1): ("norm_b",),
    }

    def theirs(n):
        if n >= 2:
            core_copy(n - 2).wait_send()

        def emit(m, here, out):
            if n < 4:
                give[n % 2, here] = out.astype(BF)
            else:
                give[n % 2, here, 0:HALF] = out.astype(BF)

        product(n, 0, emit)
        core_copy(n).start()
        begin(*follow.get((n, 0), ()))

    def ours(n):
        if n < 4:
            def emit(m, here, out):
                @pl.when(m == 0)
                def _():
                    core_copy(n).wait_recv()

                out = (out + got[n % 2, here].astype(F32)).astype(BF)
                work[n, 0, here] = out[:, :HALF]
                work[n, 1, here] = out[:, HALF:]

            product(n, 1, emit)
            begin(*follow.get((n, 1), ()))
        elif n == 4:

            def emit_proj(m, here, out):
                work[n, 0, here] = (out + got[n % 2, here, 0:HALF].astype(F32)).astype(BF)

            def emit_dq(m, here, out):
                work[n, 1, here] = out.astype(BF)

            core_copy(n).wait_recv()
            product(n, 1, emit_proj)
            begin("kv_a", "kv_b")
            ready("dq")
            ready("norm_a")
            ready("norm_b")

            def dq_sum(m):
                both = pass_sum("dq", m)
                half_row(12, both[:, :HALF] + both[:, HALF:])

            halves = (("dq", slice(0, HALF)), ("dq", slice(HALF, SIDE)))
            tiles(("norm_a", "norm_b"), halves, None, emit_dq, dq_sum)
        else:

            def emit_kv(m, here, out):
                out = out.astype(BF)
                work[n, 0, here] = out[:, :HALF]
                work[n, 1, here] = out[:, HALF:]

            ready("kv_a")
            ready("kv_b")

            def dv_sum(m):
                half_row(13, (pass_sum("kv_a", m) + pass_sum("kv_b", m))[:, HALF:])

            both = (("kv_a", None), ("kv_b", None))
            tiles(("norm_a", "norm_b"), both, slice(None), emit_kv, dv_sum)

    def leave():
        arrive("mid", "g", "dnorm2")
        for j in range(2):
            d = dn2[j]
            dv_in, dgain, dshift = norm_back(mid[j], d, ln2_gain[...].reshape(1, WIDE))
            vsend[0, 3:4] += dgain
            vsend[0, 4:5] += dshift
            dm = jnp.where(active, g[j], 0.0) + dv_in
            mid[j] = dm
            low = dm.astype(BF)
            f0[j] = low
        arrive("wp")
        da = mm(f0[...].reshape(2 * RB, WIDE), wp[...], NT).astype(BF)
        for half in range(2):
            for j in range(2):
                datt[half, j] = da[j * RB : (j + 1) * RB, half * HALF : (half + 1) * HALF]
        for j in range(2):
            datt_copy(j).start()
            datt_in[2 * j + core] = datt[core, j]

    def attend_back():
        arrive("q", "k", "v", "att", "lse")
        for j in range(2):
            datt_copy(j).wait()
        lane = lax.broadcasted_iota(jnp.int32, (RB, 128), 1)
        zero = jnp.zeros((RB, 128), BF)
        col = lax.broadcasted_iota(jnp.int32, (RB, 2 * RB), 1) & (RB - 1)
        causal = lax.broadcasted_iota(jnp.int32, (RB, 2 * RB), 0) <= col
        sub = lax.broadcasted_iota(jnp.int32, (128, LEN), 0)
        zero_t = jnp.zeros((128, LEN), BF)
        scale = jnp.asarray(HD**-0.5, BF)

        def split(rows):
            return jnp.concatenate(
                [jnp.where(lane < HD, rows, zero), jnp.where(lane < HD, zero, rows)], 0
            )

        def one_pair(pair, carry):
            cs = pl.ds(pl.multiple_of(pair * 128, 128), 128)
            slot = 0
            k_t = k[:, :, cs].reshape(LEN, 128).T
            k_low = jnp.where(sub < HD, k_t, zero_t)
            k_high = jnp.where(sub < HD, zero_t, k_t)
            for i in (3, 2, 1, 0):
                keys = (i + 1) * RB
                rs = slice(i * RB, (i + 1) * RB)
                qm = split(q[i, :, cs] * scale)
                do = datt_in[i, :, cs]
                dm = split(do)
                inner = (do.astype(F32) * att[i, :, cs].astype(F32)).T
                inner = jnp.concatenate([col_sum(inner[:HD]), col_sum(inner[HD:])], 1)
                total = jnp.concatenate([lse[pair, 0:1, rs], lse[pair, 1:2, rs]], 1)
                s = mm(k[0 : i + 1, :, cs].reshape(keys, 128), qm, NT)
                dp = mm(v[0 : i + 1, :, cs].reshape(keys, 128), dm, NT)
                last = jnp.where(causal, s[i * RB :], MASKED)
                s = jnp.concatenate([s[: i * RB], last], 0) if i else last
                prob = jnp.exp(s - total)
                ds = (prob * (dp - inner)).astype(BF)
                dv = mm(prob.astype(BF), dm, NN)
                dk = mm(ds, qm, NN)
                if i == 3:
                    dv_acc[slot] = dv
                    dk_acc[slot] = dk
                else:
                    dv_acc[slot, 0:keys] += dv
                    dk_acc[slot, 0:keys] += dk
                dq = mm(k_low[:, :keys], ds[:, :RB], NN) + mm(k_high[:, :keys], ds[:, RB:], NN)
                dfused[i, :, cs] = (dq.T * HD**-0.5).astype(BF)
            ks = pl.ds(pl.multiple_of(HALF + pair * 128, 128), 128)
            vs = pl.ds(pl.multiple_of(2 * HALF + pair * 128, 128), 128)
            dfused[:, :, ks] = dk_acc[slot].astype(BF).reshape(4, RB, 128)
            dfused[:, :, vs] = dv_acc[slot].astype(BF).reshape(4, RB, 128)
            return carry

        lax.fori_loop(0, 3, one_pair, 0)

    def dense_back():
        arrive("wq0", "wq1", "wq2")
        for j in range(2):
            block = 2 * j + 1 - core
            part[j] = mm(dfused[block], wq[...], NT).astype(BF)
            part_copy(j).start()

    def tokens_back():
        mine = [mm(dfused[2 * j + core], wq[...], NT) for j in range(2)]
        arrive("h")
        for j in range(2):
            part_copy(j).wait()
            d = mine[j] + part_in[j].astype(F32)
            dv_in, dgain, dshift = norm_back(h[j], d, ln1_gain[...].reshape(1, WIDE))
            vsend[0, 0:1] += dgain
            vsend[0, 1:2] += dshift
            tok_low[j] = (mid[j] + dv_in + jnp.where(active, 0.0, g[j])).astype(BF)
        tok_give.start()
        tok_keep.start()

    def rows(start, size):
        return pl.ds(pl.multiple_of(start, 16), size)

    bits = {"x": x, "y": y, "z": lax.rem(z, 2), "w": z // 2}
    pair_of = {"x": to_x, "y": to_y, "z": to_z_pair(1), "w": to_z_pair(2)}

    def first_row(n, s, k):
        row = 0
        for i, name in enumerate(ROUTES[2 * n + s][:k]):
            row = row + bits[name] * (SIDE >> (i + 1))
        return row

    def received(sub, k):
        size = SIDE >> (k + 1)
        return rx.at[sub, pl.ds(SIDE - 2 * size, size)]

    def step_copies(n, s, k):
        route = ROUTES[2 * n + s]
        sub = 2 * n + s

        def copy(src, dst, where):
            return mesh_push(src, dst, xsem.at[sub, k], rsem.at[sub, k], where)

        if k < 4:
            size = SIDE >> (k + 1)
            row = first_row(n, s, k) + (1 - bits[route[k]]) * size
            return [copy(work.at[n, s, rows(row, size)], received(sub, k), pair_of[route[k]])]
        if n < 2:
            out, start, col = o_out, core * 2 * SIDE + n * SIDE, s * HALF
        elif n < 4:
            out, start, col = o_fc, 0, core * 2 * SIDE + (n - 2) * SIDE + s * HALF
        elif n == 4 and s == 0:
            out, start, col = o_proj, 0, core * HALF
        else:
            out, start, col = o_qkv, 0, (0 if n == 4 else 1 + s) * WIDE + core * HALF
        left = 8 - k
        size = SIDE >> left
        row = first_row(n, s, left)
        dst = out.at[rows(start + row, size), pl.ds(pl.multiple_of(col, 128), HALF)]
        if k == 4:
            src = work.at[n, s, rows(row, size)]
            return [copy(src, dst, pair_of[route[3]]), pltpu.make_async_copy(src, dst, osem.at[sub])]
        return [copy(dst, dst, to_core if k == 8 else pair_of[route[left - 1]])]

    def advance(n, s, k):
        if k > 0:
            for copy in step_copies(n, s, k - 1):
                copy.wait()
        if 0 < k < 5:
            sub = 2 * n + s
            size = SIDE >> k
            here = rows(first_row(n, s, k), size)
            more = rx[sub, pl.ds(SIDE - 2 * size, size)]
            work[n, s, here] = (work[n, s, here].astype(F32) + more.astype(F32)).astype(BF)
        for copy in step_copies(n, s, k):
            copy.start()

    tail = ORDER[ORDER.index(("V",)) + 1 :]
    vec_steps = [tail[i] for i in (4, 8, 12, 16, 20)]
    for entry in ORDER:
        kind, *which = entry
        if kind == "P":
            theirs(*which)
        elif kind == "O":
            ours(*which)
        elif kind == "L":
            leave()
        elif kind == "A":
            attend_back()
        elif kind == "D":
            dense_back()
            begin("dq")
        elif kind == "N":
            tokens_back()
        elif kind == "V":
            vec_copy(0).start()
        else:
            advance(*which)
            if entry in vec_steps:
                vec_step(vec_steps.index(entry))
    total = vsend[5]
    inv = 1.0 / total[6:7]
    o_vec[...] = total * inv
    o_vec[7:8] = inv
    for n in range(CHUNKS):
        for s in range(2):
            for copy in step_copies(n, s, 8):
                copy.wait()
    for n in (3, 4):
        core_copy(n).wait_send()
    tok_give.wait()
    tok_keep.wait()


def grad_call(*operands):
    vmem = pl.BlockSpec(memory_space=pltpu.VMEM)
    hbm = pl.BlockSpec(memory_space=pl.ANY)
    outs = (
        shape((WIDE, 3 * WIDE)),
        shape((WIDE, WIDE)),
        shape((WIDE, FF)),
        shape((FF, WIDE)),
        shape((2, RB, WIDE)),
        shape((16, WIDE), F32),
    )
    scratch = [
        pltpu.VMEM((MAXP, 2, RB, WIDE), BF),
        pltpu.VMEM((MAXP, 2, RB, WIDE), BF),
        pltpu.VMEM((MAXP, 2, 2, RB, HALF), BF),
        pltpu.VMEM((MAXP, 2, RB, WIDE), BF),
        pltpu.VMEM((MAXP, 4, RB, WIDE), BF),
        pltpu.VMEM((2, MAXP, 4, RB, HALF), BF),
        pltpu.VMEM((3, MAXP, 2 * RB, SIDE), BF),
        pltpu.VMEM((2, SIDE, SIDE), BF),
        pltpu.VMEM((5, SIDE, SIDE), BF),
        pltpu.VMEM((CHUNKS, 2, SIDE, HALF), BF),
        pltpu.VMEM((2 * CHUNKS, SIDE - 48, HALF), BF),
        pltpu.VMEM((2, RB, WIDE), F32),
        pltpu.VMEM((2, RB, WIDE), BF),
        pltpu.VMEM((6, 16, WIDE), F32),
        pltpu.VMEM((5, 16, WIDE), F32),
        pltpu.SemaphoreType.DMA((6,)),
        pltpu.SemaphoreType.DMA((3,)),
        pltpu.SemaphoreType.DMA((2,)),
        pltpu.SemaphoreType.DMA((2, 5)),
        pltpu.SemaphoreType.DMA((2 * CHUNKS, 9)),
        pltpu.SemaphoreType.DMA((2 * CHUNKS, 9)),
        pltpu.SemaphoreType.DMA((2, 5)),
        pltpu.SemaphoreType.DMA((2,)),
        pltpu.SemaphoreType.DMA((2 * CHUNKS,)),
    ]
    return pl.pallas_call(
        grad_kernel,
        out_shape=outs,
        in_specs=[hbm] * 9 + [vmem],
        out_specs=(hbm,) * 5 + (vmem,),
        scratch_shapes=scratch,
        compiler_params=pltpu.CompilerParams(
            collective_id=2, has_side_effects=True, vmem_limit_bytes=VMEM_BYTES
        ),
        name="gradients",
    )(*operands)


def grad_call(*operands):
    vmem = pl.BlockSpec(memory_space=pltpu.VMEM)
    hbm = pl.BlockSpec(memory_space=pl.ANY)
    outs = (
        shape((WIDE, 3 * WIDE)),
        shape((WIDE, WIDE)),
        shape((WIDE, FF)),
        shape((FF, WIDE)),
        shape((2, RB, WIDE)),
        shape((16, WIDE), F32),
    )
    rows_f32 = pltpu.VMEM((2, RB, WIDE), F32)
    rows_low = pltpu.VMEM((2, RB, WIDE), BF)
    heads = pltpu.VMEM((4, RB, HALF), BF)
    scratch = [
        pltpu.VMEM((WIDE, 3 * HALF), BF),
        pltpu.VMEM((WIDE, WIDE), BF),
        heads,
        heads,
        heads,
        heads,
        pltpu.VMEM((3, 2, LEN), F32),
        rows_f32,
        rows_f32,
        rows_f32,
        rows_f32,
        pltpu.VMEM((2, 2, RB, HALF), BF),
        heads,
        rows_low,
        pltpu.VMEM((4, RB, 3 * HALF), BF),
        pltpu.VMEM((2, LEN, 128), F32),
        pltpu.VMEM((2, LEN, 128), F32),
        rows_low,
        rows_low,
        pltpu.VMEM((5, MAXP, 2, RB, SIDE), BF),
        pltpu.VMEM((2, SIDE, SIDE), BF),
        pltpu.VMEM((2, SIDE, SIDE), BF),
        pltpu.VMEM((CHUNKS, 2, SIDE, HALF), BF),
        pltpu.VMEM((2 * CHUNKS, SIDE - 48, HALF), BF),
        rows_low,
        pltpu.VMEM((6, 16, WIDE), F32),
        pltpu.VMEM((5, 16, WIDE), F32),
        pltpu.SemaphoreType.DMA((13,)),
        pltpu.SemaphoreType.DMA((5, 6)),
        pltpu.SemaphoreType.DMA((2, 2)),
        pltpu.SemaphoreType.DMA((2, 2)),
        pltpu.SemaphoreType.DMA((2, 5)),
        pltpu.SemaphoreType.DMA((2 * CHUNKS, 9)),
        pltpu.SemaphoreType.DMA((2 * CHUNKS, 9)),
        pltpu.SemaphoreType.DMA((2, 5)),
        pltpu.SemaphoreType.DMA((2,)),
        pltpu.SemaphoreType.DMA((2 * CHUNKS + 1,)),
    ]
    return pl.pallas_call(
        grad_kernel,
        out_shape=outs,
        in_specs=[hbm] * 19 + [pl.BlockSpec(memory_space=pltpu.SMEM)] + [vmem] * 3,
        out_specs=(hbm,) * 5 + (vmem,),
        scratch_shapes=scratch,
        compiler_params=pltpu.CompilerParams(
            collective_id=2, has_side_effects=True, vmem_limit_bytes=VMEM_BYTES
        ),
        name="gradients",
    )(*operands)


def finish_kernel(
    vec,
    o_qkv,
    o_proj,
    o_fc,
    o_out,
    o_tok,
    o_mixed,
    f_mixed,
    f_tok,
    f_ln1_gain,
    f_ln1_shift,
    f_qkv,
    f_bq,
    f_bv,
    f_proj,
    f_b_proj,
    f_ln2_gain,
    f_ln2_shift,
    f_fc,
    f_b_fc,
    f_out,
    f_b_out,
    in_wide,
    out_wide,
    in_tall,
    out_tall,
    mixed_v,
    isem,
    osem,
    msem,
):
    mixed_in = pltpu.make_async_copy(o_mixed, mixed_v, msem.at[0])
    mixed_out = pltpu.make_async_copy(mixed_v, f_mixed, msem.at[1])
    mixed_in.start()
    inv = vec[7:8, 0:1]
    jobs = []
    for src, dst, size in ((o_fc, f_fc, 128), (o_qkv, f_qkv, 128), (o_out, f_out, 512), (o_proj, f_proj, 384)):
        total, width = src.shape
        for i in range(total // size):
            part = (slice(i * size, (i + 1) * size), slice(0, width))
            jobs.append((src.at[part], dst.at[part], size, width))
    for i in range(2):
        jobs.append((o_tok.at[i], f_tok.at[i], RB, WIDE))

    def parts(n):
        src, dst, size, width = jobs[n]
        slot = n % 6
        wide = size == 128
        here = (in_wide if wide else in_tall).at[slot, pl.ds(0, size), pl.ds(0, width)]
        there = (out_wide if wide else out_tall).at[slot, pl.ds(0, size), pl.ds(0, width)]
        return here, there, src, dst, slot

    def load(n):
        here, _, src, _, slot = parts(n)
        return pltpu.make_async_copy(src, here, isem.at[slot])

    def store(n):
        _, there, _, dst, slot = parts(n)
        return pltpu.make_async_copy(there, dst, osem.at[slot])

    for n in range(4):
        load(n).start()
    f_ln1_gain[...] = vec[0:1].reshape(WIDE)
    f_ln1_shift[...] = vec[1:2].reshape(WIDE)
    f_b_proj[...] = vec[2:3].reshape(WIDE)
    f_ln2_gain[...] = vec[3:4].reshape(WIDE)
    f_ln2_shift[...] = vec[4:5].reshape(WIDE)
    f_b_out[...] = vec[5:6].reshape(WIDE)
    f_bq[...] = vec[12:13].reshape(WIDE)
    f_bv[...] = vec[13:14].reshape(WIDE)
    f_b_fc[...] = jnp.concatenate([vec[8 + i : 9 + i] for i in range(4)], 1).reshape(FF)
    mixed_in.wait()
    mixed_out.start()
    for n in range(len(jobs)):
        here, there = parts(n)[:2]
        load(n).wait()
        if n >= 6:
            store(n - 6).wait()
        there[...] = here[...].astype(F32) * inv
        store(n).start()
        if n + 4 < len(jobs):
            load(n + 4).start()
    for n in range(len(jobs) - 6, len(jobs)):
        store(n).wait()
    mixed_out.wait()


def finish_call(*operands):
    vmem = pl.BlockSpec(memory_space=pltpu.VMEM)
    hbm = pl.BlockSpec(memory_space=pl.ANY)
    row = shape((WIDE,), F32)
    outs = (
        shape((2, RB, WIDE)),
        shape((2, RB, WIDE), F32),
        row,
        row,
        shape((WIDE, 3 * WIDE), F32),
        row,
        row,
        shape((WIDE, WIDE), F32),
        row,
        row,
        row,
        shape((WIDE, FF), F32),
        shape((FF,), F32),
        shape((FF, WIDE), F32),
        row,
    )
    big = {0, 1, 4, 7, 11, 13}
    return pl.pallas_call(
        finish_kernel,
        out_shape=outs,
        in_specs=[vmem] + [hbm] * 6,
        out_specs=tuple(hbm if i in big else vmem for i in range(len(outs))),
        scratch_shapes=[
            pltpu.VMEM((6, 128, FF), BF),
            pltpu.VMEM((6, 128, FF), F32),
            pltpu.VMEM((6, 512, WIDE), BF),
            pltpu.VMEM((6, 512, WIDE), F32),
            pltpu.VMEM((2, RB, WIDE), BF),
            pltpu.SemaphoreType.DMA((6,)),
            pltpu.SemaphoreType.DMA((6,)),
            pltpu.SemaphoreType.DMA((2,)),
        ],
        compiler_params=pltpu.CompilerParams(vmem_limit_bytes=VMEM_BYTES),
        name="finish",
    )(*operands)


def on_chip(
    tokens,
    out_grad,
    section,
    lengths,
    ln1_gain,
    ln1_shift,
    w_qkv,
    b_query,
    b_value,
    w_proj,
    b_proj,
    ln2_gain,
    ln2_shift,
    w_fc,
    b_fc,
    w_out,
    b_out,
):
    kept = layer_call(
        tokens,
        out_grad,
        section,
        lengths,
        ln1_gain,
        ln1_shift,
        b_query,
        b_value,
        b_proj,
        ln2_gain,
        ln2_shift,
        b_out,
        b_fc,
        w_qkv,
        w_proj,
        w_fc,
        w_out,
    )
    (mixed, norm, own, norm2, act, e, dpre, f, dfused, g, dnorm2, sums, *heads) = kept
    (h, q, k, v, att, lse, mid, _) = heads
    (g_qkv, g_proj, g_fc, g_out, g_tok, vec) = grad_call(
        act.reshape(MAXP, 2, RB, FF),
        e,
        norm2,
        dpre.reshape(MAXP, 2, RB, FF),
        own,
        f,
        norm,
        dfused,
        q,
        k,
        v,
        att,
        lse,
        mid,
        h,
        g,
        dnorm2,
        w_qkv,
        w_proj,
        section,
        ln1_gain,
        ln2_gain,
        sums,
    )
    return finish_call(vec, g_qkv, g_proj, g_fc, g_out, g_tok, mixed)


def solution(mesh):
    in_specs = (
        P("grp", "seq", None),
        P("grp", "seq", None),
        P("grp"),
        P("grp"),
        P(),
        P(),
        P(),
        P(),
        P(),
        P(),
        P(),
        P(),
        P(),
        P(),
        P(),
        P(),
        P(),
    )
    out_specs = (
        P("grp", "seq", None),
        P("grp", "seq", None),
        P(),
        P(),
        P(),
        P(),
        P(),
        P(),
        P(),
        P(),
        P(),
        P(),
        P(),
        P(),
        P(),
    )
    chosen = on_chip if (mesh.shape["grp"], mesh.shape["seq"]) == (8, 4) else on_device
    return jax.shard_map(
        chosen, mesh=mesh, in_specs=in_specs, out_specs=out_specs, check_vma=False
    )
```
